32 devices in a mesh: dp: 4 (over y, x), ctx: 8 (over z, core).
Axes of the slice: x: 2, y: 2, z: 4, core: 2. Of those that a mesh axis runs over, the one named last changes fastest.
Arguments:
- queries: bfloat16 [4, 2048, 512], P('dp', 'ctx'), may hold values from -6 to 6
- keys: bfloat16 [4, 2048, 512], P('dp', 'ctx'), may hold values from -6 to 6
- values: bfloat16 [4, 2048, 512], P('dp', 'ctx'), may hold values from -24 to 24
- out_grad: bfloat16 [4, 2048, 1024], P('dp', 'ctx'), may hold values from -6 to 6
- w_out: bfloat16 [512, 1024], replicated, may hold values from -0.25 to 0.25
- block_mask: int32 [4, 16, 3], P('dp'), may hold values 0 or 1
Outputs:
- output: bfloat16 [4, 2048, 1024], P('dp', 'ctx')
- query_grad: bfloat16 [4, 2048, 512], P('dp', 'ctx')
- key_grad: bfloat16 [4, 2048, 512], P('dp', 'ctx')
- value_grad: bfloat16 [4, 2048, 512], P('dp', 'ctx')
- weight_grad: float32 [512, 1024], P('ctx')
The draws below stay inside these ranges and needn't reach their ends.
All inputs are finite; a program needn't handle non-finite values. No bound on the sum of `block_mask` on one device may be relied on, other than what follows from the above.
Results may differ from the reference program's by a relative error of at most 0.038.
Values may be sent and summed in bfloat16 or wider, within the bound.
No kernel may reach another device: no remote copies, remote signals or barrier semaphores. Data moves between devices by JAX's collectives and lax.ppermute only.
A program may use at most 64 MiB of HBM per device.

```python
import jax
import jax.numpy as jnp
from jax import lax

D = 1024
HEADS = 8
HD = 64
BLK = 128
RAD = 1
DA = 512
CAND = 3
TOKENS = 2048
NBLK = 16
VOLUMES = 4


def draw_queries(key, part):
    own_key = jax.random.fold_in(key, 1)
    dims_all = (VOLUMES, TOKENS, DA)
    return (1.5 * jax.random.truncated_normal(own_key, -4.0, 4.0, dims_all, jnp.float32)).astype(jnp.bfloat16)


def draw_keys(key, part):
    own_key = jax.random.fold_in(key, 2)
    dims_all = (VOLUMES, TOKENS, DA)
    return jax.random.truncated_normal(own_key, -6.0, 6.0, dims_all, jnp.float32).astype(jnp.bfloat16)


def place_ends(values, stream_key, smallest, top_value):
    index_at = [jax.random.randint(jax.random.fold_in(stream_key, axis), (), 0, length) for axis, length in enumerate(values.shape)]
    longest = values.shape.index(max(values.shape))
    next_to = index_at[:longest] + [(index_at[longest] + 1) % values.shape[longest]] + index_at[longest + 1:]
    return values.at[tuple(index_at)].set(smallest).at[tuple(next_to)].set(top_value)


def shard_levels(stream_key, dims, cuts, low, top_value):
    def one(axis_at, blocks):
        draws = jax.random.uniform(jax.random.fold_in(jax.random.fold_in(stream_key, 6), axis_at), (blocks,), jnp.float32, low / len(cuts), top_value / len(cuts))
        return jnp.repeat(jnp.exp(draws), dims[axis_at] // blocks).reshape((-1,) + (1,) * (len(dims) - axis_at - 1))

    level = one(*cuts[0])
    for cut in cuts[1:]:
        level = level * one(*cut)
    return level


def scatter_about(rng, shape, spread, limit, pieces=(), held_as=jnp.bfloat16):
    values = spread * jax.random.normal(rng, shape, jnp.float32)
    if pieces:
        values = values * shard_levels(rng, shape, pieces, -0.22, 0.18)
    return jnp.clip(values, -limit, limit).astype(held_as)


def setup_inputs(seed: int = 0) -> dict:
    splits = jax.random.split(jax.random.key(seed), 7)
    return {
        "queries": draw_queries(jax.random.fold_in(splits[6], 71), 0),
        "keys": draw_keys(jax.random.fold_in(splits[6], 71), 0),
        "values": scatter_about(splits[2], (VOLUMES, TOKENS, DA), 4.0, 24.0, ((0, 4), (1, 8))),
        "out_grad": scatter_about(splits[3], (VOLUMES, TOKENS, D), 1.0, 6.0, ((0, 4), (1, 8))),
        "w_out": scatter_about(splits[4], (DA, D), DA ** -0.5, 0.25),
        "block_mask": place_ends((jax.random.randint(splits[5], (VOLUMES, NBLK, CAND), 0, 5) < 3).astype(jnp.int32), jax.random.fold_in(splits[5], 1), 0, 1),
    }


big_negative = -1e30


def allowed_keys(mask_row):
    centre = jnp.arange(2 * RAD + 1) == RAD
    allowed = (mask_row == 1) | centre
    return jnp.repeat(allowed, BLK)


def one_volume(query_rows, key_rows, value_rows, grad_rows, w_out, pattern):
    rim_rows = RAD * BLK
    span_rows = (2 * RAD + 1) * BLK
    score_scale = HD ** -0.5
    key_pad = jnp.concatenate([key_rows[-rim_rows:], key_rows, key_rows[:rim_rows]], axis=0)
    value_pad = jnp.concatenate([value_rows[-rim_rows:], value_rows, value_rows[:rim_rows]], axis=0)

    def step(carry, row_block):
        key_acc, value_acc, weight_acc = carry
        first_row = (row_block * BLK).astype(jnp.int32)
        q_block = lax.dynamic_slice_in_dim(query_rows, first_row, BLK, 0)
        g_block = lax.dynamic_slice_in_dim(grad_rows, first_row, BLK, 0)
        k_window = lax.dynamic_slice_in_dim(key_pad, first_row, span_rows, 0)
        v_window = lax.dynamic_slice_in_dim(value_pad, first_row, span_rows, 0)
        allowed = allowed_keys(lax.dynamic_index_in_dim(pattern, row_block, 0, keepdims=False))
        q_heads = q_block.astype(jnp.float32).reshape(BLK, HEADS, HD)
        k_heads = k_window.astype(jnp.float32).reshape(span_rows, HEADS, HD)
        v_heads = v_window.astype(jnp.float32).reshape(span_rows, HEADS, HD)
        scores = jnp.einsum("qhd,khd->hqk", q_heads, k_heads) * score_scale
        scores = jnp.where(allowed[None, None, :], scores, big_negative)
        row_max = jnp.max(scores, axis=-1, keepdims=True)
        log_total = row_max + jnp.log(jnp.sum(jnp.exp(scores - row_max), axis=-1, keepdims=True))
        probs = jnp.exp(scores - log_total)
        probs_bf = lax.optimization_barrier(probs.astype(jnp.bfloat16)).astype(jnp.float32)
        attn_block = jnp.einsum("hqk,khd->qhd", probs_bf, v_heads).reshape(BLK, HEADS * HD).astype(jnp.bfloat16)
        out_block = jnp.dot(attn_block, w_out, preferred_element_type=jnp.float32).astype(jnp.bfloat16)
        attn_grad = lax.dot_general(g_block, w_out, (((1,), (1,)), ((), ())), preferred_element_type=jnp.float32).astype(jnp.bfloat16)
        grad_heads = attn_grad.astype(jnp.float32).reshape(BLK, HEADS, HD)
        row_delta = jnp.sum(grad_heads * attn_block.astype(jnp.float32).reshape(BLK, HEADS, HD), axis=-1).T
        dprob = jnp.einsum("qhd,khd->hqk", grad_heads, v_heads)
        dscore = (probs * (dprob - row_delta[:, :, None]) * score_scale).astype(jnp.bfloat16)
        dscore = lax.optimization_barrier(dscore).astype(jnp.float32)
        query_block = jnp.einsum("hqk,khd->qhd", dscore, k_heads).reshape(BLK, HEADS * HD).astype(jnp.bfloat16)
        key_window = jnp.einsum("hqk,qhd->khd", dscore, q_heads).reshape(span_rows, HEADS * HD)
        value_window = jnp.einsum("hqk,qhd->khd", probs_bf, grad_heads).reshape(span_rows, HEADS * HD)
        key_acc = lax.dynamic_update_slice_in_dim(key_acc, lax.dynamic_slice_in_dim(key_acc, first_row, span_rows, 0) + key_window, first_row, 0)
        value_acc = lax.dynamic_update_slice_in_dim(value_acc, lax.dynamic_slice_in_dim(value_acc, first_row, span_rows, 0) + value_window, first_row, 0)
        weight_acc = weight_acc + lax.dot_general(attn_block, g_block, (((0,), (0,)), ((), ())), preferred_element_type=jnp.float32)
        return (key_acc, value_acc, weight_acc), (out_block, query_block)

    start_acc = jnp.zeros((TOKENS + 2 * rim_rows, HEADS * HD), jnp.float32)
    start_weight = jnp.zeros((HEADS * HD, D), jnp.float32)
    (key_acc, value_acc, weight_acc), (out_rows, query_out) = lax.scan(step, (start_acc, start_acc, start_weight), jnp.arange(NBLK, dtype=jnp.int32))

    def fold(acc):
        own_sums = acc[rim_rows:rim_rows + TOKENS]
        own_sums = own_sums.at[TOKENS - rim_rows:].add(acc[:rim_rows])
        own_sums = own_sums.at[:rim_rows].add(acc[rim_rows + TOKENS:])
        return own_sums.astype(jnp.bfloat16)

    return out_rows.reshape(TOKENS, D), query_out.reshape(TOKENS, HEADS * HD), fold(key_acc), fold(value_acc), weight_acc


def reference(queries, keys, values, out_grad, w_out, block_mask):
    def per_volume(weight_sum, items):
        query_rows, key_rows, value_rows, grad_rows, pattern = items
        out_rows, query_out, key_out, value_out, weight_acc = one_volume(query_rows, key_rows, value_rows, grad_rows, w_out, pattern)
        return weight_sum + weight_acc, (out_rows, query_out, key_out, value_out)

    weight_sum, stacked = lax.scan(per_volume, jnp.zeros((HEADS * HD, D), jnp.float32), (queries, keys, values, out_grad, block_mask))
    weight_grad = weight_sum * (VOLUMES * TOKENS) ** -0.5
    return (stacked[0], stacked[1], stacked[2], stacked[3], weight_grad)
```

```python
import functools

import jax
import jax.numpy as jnp
from jax import lax
from jax.experimental import pallas as pl
from jax.experimental.pallas import tpu as pltpu
from jax.sharding import PartitionSpec as P

HEADS = 8
HD = 64
BLK = 128
RAD = 1
PAIR = 2 * HD
SPAN = (2 * RAD + 1) * BLK
RIM = RAD * BLK
BIG_NEGATIVE = -1e30
SCALE = HD ** (-0.5)
BF16 = jnp.bfloat16
F32 = jnp.float32


def dot(a, b, contract):
    return lax.dot_general(a, b, (contract, ((), ())), preferred_element_type=F32)


def two_heads(block):
    lane = lax.broadcasted_iota(jnp.int32, block.shape, 1)
    zero = jnp.zeros_like(block)
    return jnp.concatenate(
        [jnp.where(lane < HD, block, zero), jnp.where(lane < HD, zero, block)], axis=0
    )


def own_features(both):
    return jnp.concatenate([both[:HD, :BLK], both[HD:, BLK:]], axis=0)


def extend(ext, own, low, high, which):
    rows = own.shape[0]
    ext[:RIM] = low[which]
    ext[RIM : RIM + rows] = own[...]
    ext[RIM + rows :] = high[which]


def probabilities(mask, b, q2, k_win):
    scores = dot(k_win, q2, ((1,), (1,)))
    parts = []
    for c in range(2 * RAD + 1):
        part = scores[c * BLK : (c + 1) * BLK]
        if c != RAD:
            part = jnp.where(mask[b, c] == 1, part, BIG_NEGATIVE)
        parts.append(part)
    scores = jnp.concatenate(parts, axis=0)
    top = jnp.max(scores, axis=0, keepdims=True)
    e = jnp.exp(scores - top)
    return e * (1.0 / jnp.sum(e, axis=0, keepdims=True))


def forward_kernel(mask, q, k, v, low, high, g, attn_t, part, k_ext, v_ext):
    extend(k_ext, k, low, high, 0)
    extend(v_ext, v, low, high, 1)
    for b in range(q.shape[0] // BLK):
        rows = slice(b * BLK, (b + 1) * BLK)
        window = slice(b * BLK, b * BLK + SPAN)
        for p in range(HEADS // 2):
            cols = slice(p * PAIR, (p + 1) * PAIR)
            q2 = two_heads(q[rows, cols] * SCALE)
            probs = probabilities(mask, b, q2, k_ext[window, cols]).astype(BF16)
            both = dot(v_ext[window, cols], probs, ((0,), (0,)))
            attn_t[cols, rows] = own_features(both).astype(BF16)
    part[...] = dot(attn_t[...], g[...], ((1,), (0,))).astype(BF16)


def backward_kernel(
    mask, q, k, v, low, high, ag, q_grad, k_own, v_own, to_low, to_high, k_ext, v_ext, dk, dv
):
    extend(k_ext, k, low, high, 0)
    extend(v_ext, v, low, high, 1)
    tokens = q.shape[0]
    for b in range(tokens // BLK):
        rows = slice(b * BLK, (b + 1) * BLK)
        window = slice(b * BLK, b * BLK + SPAN)
        old = slice(b * BLK, b * BLK + SPAN - BLK)
        new = slice(b * BLK + SPAN - BLK, b * BLK + SPAN)
        for p in range(HEADS // 2):
            cols = slice(p * PAIR, (p + 1) * PAIR)
            q2 = two_heads(q[rows, cols] * SCALE)
            g2 = two_heads(ag[rows, cols])
            k_win = k_ext[window, cols]
            v_win = v_ext[window, cols]
            probs = probabilities(mask, b, q2, k_win)
            dprob = dot(v_win, g2, ((1,), (1,)))
            delta = jnp.sum(probs * dprob, axis=0, keepdims=True)
            dscore = (probs * (dprob - delta)).astype(BF16)
            dq_t = dot(k_win, dscore, ((0,), (0,)))
            q_grad[rows, cols] = (own_features(dq_t) * SCALE).T.astype(BF16)
            k_part = dot(dscore, q2, ((1,), (0,)))
            v_part = dot(probs.astype(BF16), g2, ((1,), (0,)))
            if b == 0:
                dk[window, cols] = k_part
                dv[window, cols] = v_part
            else:
                dk[old, cols] += k_part[: SPAN - BLK]
                dv[old, cols] += v_part[: SPAN - BLK]
                dk[new, cols] = k_part[SPAN - BLK :]
                dv[new, cols] = v_part[SPAN - BLK :]
    k_own[...] = dk[RIM : RIM + tokens]
    v_own[...] = dv[RIM : RIM + tokens]
    to_low[0] = dk[:RIM].astype(BF16)
    to_low[1] = dv[:RIM].astype(BF16)
    to_high[0] = dk[RIM + tokens :].astype(BF16)
    to_high[1] = dv[RIM + tokens :].astype(BF16)


def call(kernel, outs, scratch, flops, *args):
    in_vmem = pl.BlockSpec(memory_space=pltpu.VMEM)
    return pl.pallas_call(
        kernel,
        out_shape=[jax.ShapeDtypeStruct(s, d) for s, d in outs],
        in_specs=[pl.BlockSpec(memory_space=pltpu.SMEM)] + [in_vmem] * (len(args) - 1),
        out_specs=[in_vmem] * len(outs),
        scratch_shapes=[pltpu.VMEM(s, d) for s, d in scratch],
        compiler_params=pltpu.CompilerParams(vmem_limit_bytes=32 * 1024 * 1024),
        cost_estimate=pl.CostEstimate(flops=flops, bytes_accessed=4 << 20, transcendentals=0),
    )(*args)


def ring(count, step):
    return [(i, (i + step) % count) for i in range(count)]


def swap(count, bits):
    return [(i, i ^ bits) for i in range(count)]


def total(parts):
    return functools.reduce(jnp.add, [p.astype(F32) for p in parts])


def body(queries, keys, values, out_grad, w_out, block_mask):
    q, k, v, g = queries[0], keys[0], values[0], out_grad[0]
    tokens, feats = q.shape
    width = g.shape[1]
    blocks = tokens // BLK
    ctx, dp = lax.axis_size("ctx"), lax.axis_size("dp")
    chips = ctx // 2
    at_ctx, at_dp = lax.axis_index("ctx"), lax.axis_index("dp")
    core, chip = at_ctx % 2, at_ctx // 2

    low = lax.ppermute(jnp.stack([k[-RIM:], v[-RIM:]]), "ctx", ring(ctx, 1))
    high = lax.ppermute(jnp.stack([k[:RIM], v[:RIM]]), "ctx", ring(ctx, -1))
    mask = lax.dynamic_slice_in_dim(block_mask[0], at_ctx * blocks, blocks, 0)
    ag = dot(g, w_out, ((1,), (1,))).astype(BF16)

    ext = (tokens + 2 * RIM, feats)
    attn_t, part = call(
        forward_kernel,
        [((feats, tokens), BF16), ((feats, width), BF16)],
        [(ext, BF16)] * 2,
        10**9,
        mask, q, k, v, low, high, g,
    )

    rows, cols = feats // ctx, width // dp
    part = part.reshape(chips, 2, rows, width)
    mine = lax.dynamic_index_in_dim(part, core, 1, keepdims=False)
    other = lax.dynamic_index_in_dim(part, 1 - core, 1, keepdims=False)
    other = lax.ppermute(other, "ctx", swap(ctx, 1))
    half = total([mine, other]).astype(BF16)

    q_grad, k_own, v_own, to_low, to_high = call(
        backward_kernel,
        [((tokens, feats), BF16)]
        + [((tokens, feats), F32)] * 2
        + [((2, RIM, feats), BF16)] * 2,
        [(ext, BF16)] * 2 + [(ext, F32)] * 2,
        2 * 10**9,
        mask, q, k, v, low, high, ag,
    )
    from_high = lax.ppermute(to_low, "ctx", ring(ctx, -1))
    from_low = lax.ppermute(to_high, "ctx", ring(ctx, 1))

    def columns(step):
        return lax.dynamic_slice_in_dim(half, (at_dp ^ step) * cols, cols, 2)

    quarter = total(
        [columns(0)] + [lax.ppermute(columns(s), "dp", swap(dp, s)) for s in range(1, dp)]
    ).astype(BF16)

    def of_chip(step):
        return lax.dynamic_index_in_dim(quarter, chip ^ step, 0, keepdims=False)

    piece = total(
        [of_chip(0)]
        + [lax.ppermute(of_chip(s), "ctx", swap(ctx, 2 * s)) for s in range(1, chips)]
    )
    piece = (piece * (dp * tokens * ctx) ** (-0.5)).astype(BF16)
    pieces = jnp.stack(
        [piece] + [lax.ppermute(piece, "dp", swap(dp, s)) for s in range(1, dp)]
    )
    step = 1
    while step < dp:
        turned = pieces[jnp.arange(dp) ^ step]
        pieces = jnp.where((at_dp & step) != 0, turned, pieces)
        step *= 2
    weight_grad = jnp.concatenate([pieces[d] for d in range(dp)], axis=1).astype(F32)

    output = dot(attn_t, w_out, ((0,), (0,))).astype(BF16)
    grads = []
    for which, own in enumerate((k_own, v_own)):
        own = own.at[:RIM].add(from_low[which].astype(F32))
        own = own.at[tokens - RIM :].add(from_high[which].astype(F32))
        grads.append(own.astype(BF16))
    return (output[None], q_grad[None], grads[0][None], grads[1][None], weight_grad)


def solution(mesh):
    rows = P("dp", "ctx", None)
    return jax.shard_map(
        body,
        mesh=mesh,
        in_specs=(rows, rows, rows, rows, P(), P("dp", None, None)),
        out_specs=(rows, rows, rows, rows, P("ctx", None)),
        check_vma=False,
    )
```

```python
import functools

import jax
import jax.numpy as jnp
from jax import lax
from jax.experimental import pallas as pl
from jax.experimental.pallas import tpu as pltpu
from jax.sharding import PartitionSpec as P

HEADS = 8
HD = 64
BLK = 128
RAD = 1
PAIR = 2 * HD
SPAN = (2 * RAD + 1) * BLK
RIM = RAD * BLK
BIG_NEGATIVE = -1e30
SCALE = HD ** (-0.5)
BF16 = jnp.bfloat16
F32 = jnp.float32


def dot(a, b, contract):
    return lax.dot_general(a, b, (contract, ((), ())), preferred_element_type=F32)


def two_heads(block):
    lane = lax.broadcasted_iota(jnp.int32, block.shape, 1)
    zero = jnp.zeros_like(block)
    return jnp.concatenate(
        [jnp.where(lane < HD, block, zero), jnp.where(lane < HD, zero, block)], axis=0
    )


def own_features(both):
    return jnp.concatenate([both[:HD, :BLK], both[HD:, BLK:]], axis=0)


def extend(ext, own, low, high, which):
    rows = own.shape[0]
    ext[:RIM] = low[which]
    ext[RIM : RIM + rows] = own[...]
    ext[RIM + rows :] = high[which]


def probabilities(mask, b, q2, k_win):
    scores = dot(k_win, q2, ((1,), (1,)))
    scores = jnp.concatenate(
        [masked(mask, b, c, scores[c * BLK : (c + 1) * BLK]) for c in range(2 * RAD + 1)], axis=0
    )
    top = jnp.max(scores, axis=0, keepdims=True)
    e = jnp.exp(scores - top)
    return e * (1.0 / jnp.sum(e, axis=0, keepdims=True))


def own_candidates(b, blocks):
    return max(0, RAD - b), min(2 * RAD, blocks - 1 - b + RAD)


def masked(mask, b, c, part):
    return part if c == RAD else jnp.where(mask[b, c] == 1, part, BIG_NEGATIVE)


def own_kernel(mask, q, k, v, own_t, stats):
    blocks = q.shape[0] // BLK
    pairs = HEADS // 2
    for b in range(blocks):
        rows = slice(b * BLK, (b + 1) * BLK)
        first, last = own_candidates(b, blocks)
        here = slice((b + first - RAD) * BLK, (b + last - RAD + 1) * BLK)
        for p in range(pairs):
            cols = slice(p * PAIR, (p + 1) * PAIR)
            scores = dot(k[here, cols], two_heads(q[rows, cols] * SCALE), ((1,), (1,)))
            scores = jnp.concatenate(
                [
                    masked(mask, b, c, scores[(c - first) * BLK : (c - first + 1) * BLK])
                    for c in range(first, last + 1)
                ],
                axis=0,
            )
            top = jnp.max(scores, axis=0, keepdims=True)
            e = jnp.exp(scores - top)
            stats[0, b * pairs + p : b * pairs + p + 1] = top
            stats[1, b * pairs + p : b * pairs + p + 1] = jnp.sum(e, axis=0, keepdims=True)
            own_t[cols, rows] = own_features(dot(v[here, cols], e.astype(BF16), ((0,), (0,))))


def spread(row):
    return jnp.concatenate(
        [
            jnp.broadcast_to(row[:, :BLK], (HD, BLK)),
            jnp.broadcast_to(row[:, BLK:], (HD, BLK)),
        ],
        axis=0,
    )


def forward_kernel(mask, q, low, high, own_t, stats, g, attn_t, part):
    blocks = q.shape[0] // BLK
    pairs = HEADS // 2
    for b in range(blocks):
        rows = slice(b * BLK, (b + 1) * BLK)
        first, last = own_candidates(b, blocks)
        rims = [(low, c) for c in range(first)] + [(high, c) for c in range(last + 1, 3)]
        for p in range(pairs):
            cols = slice(p * PAIR, (p + 1) * PAIR)
            old = stats[0, b * pairs + p : b * pairs + p + 1]
            q2 = two_heads(q[rows, cols] * SCALE)
            scores = [
                masked(mask, b, c, dot(rim[0, :, cols], q2, ((1,), (1,)))) for rim, c in rims
            ]
            top = old
            for part_scores in scores:
                top = jnp.maximum(top, jnp.max(part_scores, axis=0, keepdims=True))
            kept = jnp.exp(old - top)
            count = stats[1, b * pairs + p : b * pairs + p + 1] * kept
            both = None
            for (rim, _), part_scores in zip(rims, scores):
                e = jnp.exp(part_scores - top)
                count = count + jnp.sum(e, axis=0, keepdims=True)
                more = dot(rim[1, :, cols], e.astype(BF16), ((0,), (0,)))
                both = more if both is None else both + more
            share = 1.0 / count
            attn = own_t[cols, rows] * spread(kept * share)
            if both is not None:
                attn = attn + own_features(both) * spread(share)
            attn_t[cols, rows] = attn.astype(BF16)
    part[...] = dot(attn_t[...], g[...], ((1,), (0,))).astype(BF16)


def backward_kernel(
    mask, q, k, v, low, high, ag, after, q_grad, k_own, v_own, to_low, to_high, k_ext, v_ext, dk, dv
):
    extend(k_ext, k, low, high, 0)
    extend(v_ext, v, low, high, 1)
    tokens = q.shape[0]
    for b in range(tokens // BLK):
        rows = slice(b * BLK, (b + 1) * BLK)
        window = slice(b * BLK, b * BLK + SPAN)
        old = slice(b * BLK, b * BLK + SPAN - BLK)
        new = slice(b * BLK + SPAN - BLK, b * BLK + SPAN)
        for p in range(HEADS // 2):
            cols = slice(p * PAIR, (p + 1) * PAIR)
            q2 = two_heads(q[rows, cols] * SCALE)
            g2 = two_heads(ag[rows, cols])
            k_win = k_ext[window, cols]
            v_win = v_ext[window, cols]
            probs = probabilities(mask, b, q2, k_win)
            dprob = dot(v_win, g2, ((1,), (1,)))
            delta = jnp.sum(probs * dprob, axis=0, keepdims=True)
            dscore = (probs * (dprob - delta)).astype(BF16)
            dq_t = dot(k_win, dscore, ((0,), (0,)))
            q_grad[rows, cols] = (own_features(dq_t) * SCALE).T.astype(BF16)
            k_part = dot(dscore, q2, ((1,), (0,)))
            v_part = dot(probs.astype(BF16), g2, ((1,), (0,)))
            if b == 0:
                dk[window, cols] = k_part
                dv[window, cols] = v_part
            else:
                dk[old, cols] += k_part[: SPAN - BLK]
                dv[old, cols] += v_part[: SPAN - BLK]
                dk[new, cols] = k_part[SPAN - BLK :]
                dv[new, cols] = v_part[SPAN - BLK :]
    k_own[...] = dk[RIM : RIM + tokens]
    v_own[...] = dv[RIM : RIM + tokens]
    to_low[0] = dk[:RIM].astype(BF16)
    to_low[1] = dv[:RIM].astype(BF16)
    to_high[0] = dk[RIM + tokens :].astype(BF16)
    to_high[1] = dv[RIM + tokens :].astype(BF16)


def rims_kernel(at, k_own, v_own, from_link, from_chip, after, k_grad, v_grad):
    tokens = k_own.shape[0]
    core = at[0]
    for which, (own, grad) in enumerate(((k_own, k_grad), (v_own, v_grad))):
        link = from_link[which].astype(F32)
        chip = from_chip[which].astype(F32)
        low = jnp.where(core == 0, link, chip)
        high = jnp.where(core == 0, chip, link)
        if tokens == RIM:
            grad[...] = (own[...] + low + high).astype(BF16)
        else:
            grad[:RIM] = (own[:RIM] + low).astype(BF16)
            if tokens > 2 * RIM:
                grad[RIM : tokens - RIM] = own[RIM : tokens - RIM].astype(BF16)
            grad[tokens - RIM :] = (own[tokens - RIM :] + high).astype(BF16)


def columns_kernel(at, *refs):
    pieces, out = refs[:-1], refs[-1]
    cols = pieces[0].shape[1]
    for d in range(len(pieces)):
        value = pieces[0][...]
        for s in range(1, len(pieces)):
            value = jnp.where((at[1] ^ s) == d, pieces[s][...], value)
        out[:, d * cols : (d + 1) * cols] = value.astype(F32)


def call(kernel, outs, scratch, flops, *args, after=()):
    in_vmem = pl.BlockSpec(memory_space=pltpu.VMEM)
    anywhere = pl.BlockSpec(memory_space=pl.ANY)
    return pl.pallas_call(
        kernel,
        out_shape=[jax.ShapeDtypeStruct(s, d) for s, d in outs],
        in_specs=[pl.BlockSpec(memory_space=pltpu.SMEM)]
        + [in_vmem] * (len(args) - 1)
        + [anywhere] * len(after),
        out_specs=[in_vmem] * len(outs),
        scratch_shapes=[pltpu.VMEM(s, d) for s, d in scratch],
        compiler_params=pltpu.CompilerParams(vmem_limit_bytes=32 * 1024 * 1024),
        cost_estimate=pl.CostEstimate(flops=flops, bytes_accessed=4 << 20, transcendentals=0),
    )(*args, *after)


def swap(count, bits):
    return [(i, i ^ bits) for i in range(count)]


def over_links(count):
    return [(i, (i - 1 if i % 2 == 0 else i + 1) % count) for i in range(count)]


def total(parts):
    return functools.reduce(jnp.add, [p.astype(F32) for p in parts])


def body(queries, keys, values, out_grad, w_out, block_mask):
    q, k, v, g = queries[0], keys[0], values[0], out_grad[0]
    tokens, feats = q.shape
    width = g.shape[1]
    blocks = tokens // BLK
    ctx, dp = lax.axis_size("ctx"), lax.axis_size("dp")
    chips = ctx // 2
    at_ctx, at_dp = lax.axis_index("ctx"), lax.axis_index("dp")
    core, chip = at_ctx % 2, at_ctx // 2
    at = jnp.stack([core, at_dp])

    link_row = core * (tokens - RIM)
    chip_row = tokens - RIM - link_row

    def rim(row):
        return jnp.stack([lax.dynamic_slice_in_dim(x, row, RIM, 0) for x in (k, v)])

    from_link = lax.ppermute(rim(link_row), "ctx", over_links(ctx))
    from_chip = lax.ppermute(rim(chip_row), "ctx", swap(ctx, 1))
    low = jnp.where(core == 0, from_link, from_chip)
    high = jnp.where(core == 0, from_chip, from_link)

    mask = lax.dynamic_slice_in_dim(block_mask[0], at_ctx * blocks, blocks, 0)
    ag = dot(g, w_out, ((1,), (1,))).astype(BF16)
    own_t, stats = call(
        own_kernel,
        [((feats, tokens), F32), ((2, blocks * HEADS // 2, 2 * BLK), F32)],
        [],
        5 * 10**8,
        mask, q, k, v,
    )
    attn_t, part = call(
        forward_kernel,
        [((feats, tokens), BF16), ((feats, width), BF16)],
        [],
        10**9,
        mask, q, low, high, own_t, stats, g,
    )

    rows, cols = feats // ctx, width // dp
    part = part.reshape(chips, 2, rows, width)
    mine = lax.dynamic_index_in_dim(part, core, 1, keepdims=False)
    other = lax.dynamic_index_in_dim(part, 1 - core, 1, keepdims=False)
    other = lax.ppermute(other, "ctx", swap(ctx, 1))
    half = total([mine, other]).astype(BF16)

    ext = (tokens + 2 * RIM, feats)
    q_grad, k_own, v_own, to_low, to_high = call(
        backward_kernel,
        [((tokens, feats), BF16)]
        + [((tokens, feats), F32)] * 2
        + [((2, RIM, feats), BF16)] * 2,
        [(ext, BF16)] * 2 + [(ext, F32)] * 2,
        2 * 10**9,
        mask, q, k, v, low, high, ag,
        after=(half,),
    )

    def columns(step):
        return lax.dynamic_slice_in_dim(half, (at_dp ^ step) * cols, cols, 2)

    quarter = total(
        [columns(0)] + [lax.ppermute(columns(s), "dp", swap(dp, s)) for s in range(1, dp)]
    ).astype(BF16)

    grad_link = lax.ppermute(jnp.where(core == 0, to_low, to_high), "ctx", over_links(ctx))
    grad_chip = lax.ppermute(jnp.where(core == 0, to_high, to_low), "ctx", swap(ctx, 1))

    def of_chip(step):
        return lax.dynamic_index_in_dim(quarter, chip ^ step, 0, keepdims=False)

    piece = total(
        [of_chip(0)]
        + [lax.ppermute(of_chip(s), "ctx", swap(ctx, 2 * s)) for s in range(1, chips)]
    )
    piece = (piece * (dp * tokens * ctx) ** (-0.5)).astype(BF16)
    pieces = [piece] + [lax.ppermute(piece, "dp", swap(dp, s)) for s in range(1, dp)]
    (weight_grad,) = call(columns_kernel, [((rows, width), F32)], [], 10**6, at, *pieces)

    output = dot(attn_t, w_out, ((0,), (0,))).astype(BF16)
    k_grad, v_grad = call(
        rims_kernel,
        [((tokens, feats), BF16)] * 2,
        [],
        10**6,
        at, k_own, v_own, grad_link, grad_chip,
        after=(piece,),
    )
    return (output[None], q_grad[None], k_grad[None], v_grad[None], weight_grad)


def solution(mesh):
    rows = P("dp", "ctx", None)
    return jax.shard_map(
        body,
        mesh=mesh,
        in_specs=(rows, rows, rows, rows, P(), P("dp", None, None)),
        out_specs=(rows, rows, rows, rows, P("ctx", None)),
        check_vma=False,
    )
```

```python
import functools

import jax
import jax.numpy as jnp
from jax import lax
from jax.experimental import pallas as pl
from jax.experimental.pallas import tpu as pltpu
from jax.sharding import PartitionSpec as P

HEADS = 8
HD = 64
BLK = 128
RAD = 1
PAIR = 2 * HD
SPAN = (2 * RAD + 1) * BLK
RIM = RAD * BLK
BIG_NEGATIVE = -1e30
SCALE = HD ** (-0.5)
BF16 = jnp.bfloat16
F32 = jnp.float32


def dot(a, b, contract):
    return lax.dot_general(a, b, (contract, ((), ())), preferred_element_type=F32)


def two_heads(block):
    lane = lax.broadcasted_iota(jnp.int32, block.shape, 1)
    zero = jnp.zeros_like(block)
    return jnp.concatenate(
        [jnp.where(lane < HD, block, zero), jnp.where(lane < HD, zero, block)], axis=0
    )


def own_features(both):
    return jnp.concatenate([both[:HD, :BLK], both[HD:, BLK:]], axis=0)


def extend(ext, own, low, high, which):
    rows = own.shape[0]
    ext[:RIM] = low[which]
    ext[RIM : RIM + rows] = own[...]
    ext[RIM + rows :] = high[which]


def probabilities(mask, b, q2, k_win):
    scores = dot(k_win, q2, ((1,), (1,)))
    scores = jnp.concatenate(
        [masked(mask, b, c, scores[c * BLK : (c + 1) * BLK]) for c in range(2 * RAD + 1)], axis=0
    )
    top = jnp.max(scores, axis=0, keepdims=True)
    e = jnp.exp(scores - top)
    return e * (1.0 / jnp.sum(e, axis=0, keepdims=True))


def own_candidates(b, blocks):
    return max(0, RAD - b), min(2 * RAD, blocks - 1 - b + RAD)


def masked(mask, b, c, part):
    return part if c == RAD else jnp.where(mask[b, c] == 1, part, BIG_NEGATIVE)


def own_kernel(mask, q, k, v, own_t, stats):
    blocks = q.shape[0] // BLK
    pairs = HEADS // 2
    for b in range(blocks):
        rows = slice(b * BLK, (b + 1) * BLK)
        first, last = own_candidates(b, blocks)
        here = slice((b + first - RAD) * BLK, (b + last - RAD + 1) * BLK)
        for p in range(pairs):
            cols = slice(p * PAIR, (p + 1) * PAIR)
            scores = dot(k[here, cols], two_heads(q[rows, cols] * SCALE), ((1,), (1,)))
            scores = jnp.concatenate(
                [
                    masked(mask, b, c, scores[(c - first) * BLK : (c - first + 1) * BLK])
                    for c in range(first, last + 1)
                ],
                axis=0,
            )
            top = jnp.max(scores, axis=0, keepdims=True)
            e = jnp.exp(scores - top)
            stats[0, b * pairs + p : b * pairs + p + 1] = top
            stats[1, b * pairs + p : b * pairs + p + 1] = jnp.sum(e, axis=0, keepdims=True)
            own_t[cols, rows] = own_features(dot(v[here, cols], e.astype(BF16), ((0,), (0,))))


def spread(row):
    return jnp.concatenate(
        [
            jnp.broadcast_to(row[:, :BLK], (HD, BLK)),
            jnp.broadcast_to(row[:, BLK:], (HD, BLK)),
        ],
        axis=0,
    )


def pack_kernel(k, v, to_link, to_chip, sems):
    tokens = k.shape[0]
    link_row = lax.rem(lax.axis_index("ctx"), 2) * (tokens - RIM)
    chip_row = tokens - RIM - link_row
    copies = []
    for which, source in enumerate((k, v)):
        for out, row in ((to_link, link_row), (to_chip, chip_row)):
            rows = pl.ds(pl.multiple_of(row, RIM), RIM)
            copies.append(
                pltpu.make_async_copy(source.at[rows], out.at[which], sems.at[len(copies)])
            )
            copies[-1].start()
    for copy in copies:
        copy.wait()


def forward_kernel(mask, q, low, high, own_t, stats, g, attn_t, mine, other):
    blocks = q.shape[0] // BLK
    pairs = HEADS // 2
    for b in range(blocks):
        rows = slice(b * BLK, (b + 1) * BLK)
        first, last = own_candidates(b, blocks)
        rims = [(low, c) for c in range(first)] + [(high, c) for c in range(last + 1, 3)]
        for p in range(pairs):
            cols = slice(p * PAIR, (p + 1) * PAIR)
            old = stats[0, b * pairs + p : b * pairs + p + 1]
            q2 = two_heads(q[rows, cols] * SCALE)
            scores = [
                masked(mask, b, c, dot(rim[0, :, cols], q2, ((1,), (1,)))) for rim, c in rims
            ]
            top = old
            for part_scores in scores:
                top = jnp.maximum(top, jnp.max(part_scores, axis=0, keepdims=True))
            kept = jnp.exp(old - top)
            count = stats[1, b * pairs + p : b * pairs + p + 1] * kept
            both = None
            for (rim, _), part_scores in zip(rims, scores):
                e = jnp.exp(part_scores - top)
                count = count + jnp.sum(e, axis=0, keepdims=True)
                more = dot(rim[1, :, cols], e.astype(BF16), ((0,), (0,)))
                both = more if both is None else both + more
            share = 1.0 / count
            attn = own_t[cols, rows] * spread(kept * share)
            if both is not None:
                attn = attn + own_features(both) * spread(share)
            attn_t[cols, rows] = attn.astype(BF16)
    part = dot(attn_t[...], g[...], ((1,), (0,))).astype(BF16)
    core = lax.rem(lax.axis_index("ctx"), 2)
    chips, rows, _ = mine.shape
    for c in range(2 * chips):
        value = part[c * rows : (c + 1) * rows]

        @pl.when(core == c % 2)
        def _():
            mine[c // 2] = value

        @pl.when(core != c % 2)
        def _():
            other[c // 2] = value


def backward_kernel(
    mask, q, k, v, low, high, ag, after, q_grad, k_own, v_own, to_low, to_high, k_ext, v_ext, dk, dv
):
    extend(k_ext, k, low, high, 0)
    extend(v_ext, v, low, high, 1)
    tokens = q.shape[0]
    for b in range(tokens // BLK):
        rows = slice(b * BLK, (b + 1) * BLK)
        window = slice(b * BLK, b * BLK + SPAN)
        old = slice(b * BLK, b * BLK + SPAN - BLK)
        new = slice(b * BLK + SPAN - BLK, b * BLK + SPAN)
        for p in range(HEADS // 2):
            cols = slice(p * PAIR, (p + 1) * PAIR)
            q2 = two_heads(q[rows, cols] * SCALE)
            g2 = two_heads(ag[rows, cols])
            k_win = k_ext[window, cols]
            v_win = v_ext[window, cols]
            probs = probabilities(mask, b, q2, k_win)
            dprob = dot(v_win, g2, ((1,), (1,)))
            delta = jnp.sum(probs * dprob, axis=0, keepdims=True)
            dscore = (probs * (dprob - delta)).astype(BF16)
            dq_t = dot(k_win, dscore, ((0,), (0,)))
            q_grad[rows, cols] = (own_features(dq_t) * SCALE).T.astype(BF16)
            k_part = dot(dscore, q2, ((1,), (0,)))
            v_part = dot(probs.astype(BF16), g2, ((1,), (0,)))
            if b == 0:
                dk[window, cols] = k_part
                dv[window, cols] = v_part
            else:
                dk[old, cols] += k_part[: SPAN - BLK]
                dv[old, cols] += v_part[: SPAN - BLK]
                dk[new, cols] = k_part[SPAN - BLK :]
                dv[new, cols] = v_part[SPAN - BLK :]
    k_own[...] = dk[RIM : RIM + tokens]
    v_own[...] = dv[RIM : RIM + tokens]
    to_low[0] = dk[:RIM].astype(BF16)
    to_low[1] = dv[:RIM].astype(BF16)
    to_high[0] = dk[RIM + tokens :].astype(BF16)
    to_high[1] = dv[RIM + tokens :].astype(BF16)


def last_kernel(k_own, v_own, from_link, from_chip, pieces, k_grad, v_grad, weight_grad):
    tokens = k_own.shape[0]
    core = lax.rem(lax.axis_index("ctx"), 2)
    for which, (own, grad) in enumerate(((k_own, k_grad), (v_own, v_grad))):
        link = from_link[which].astype(F32)
        chip = from_chip[which].astype(F32)
        low = jnp.where(core == 0, link, chip)
        high = jnp.where(core == 0, chip, link)
        if tokens == RIM:
            grad[...] = (own[...] + low + high).astype(BF16)
        else:
            grad[:RIM] = (own[:RIM] + low).astype(BF16)
            if tokens > 2 * RIM:
                grad[RIM : tokens - RIM] = own[RIM : tokens - RIM].astype(BF16)
            grad[tokens - RIM :] = (own[tokens - RIM :] + high).astype(BF16)
    cols = pieces.shape[2]
    for d in range(pieces.shape[0]):
        weight_grad[:, d * cols : (d + 1) * cols] = pieces[d].astype(F32)


def call(kernel, outs, scratch, flops, *args, first=pltpu.VMEM):
    in_vmem = pl.BlockSpec(memory_space=pltpu.VMEM)
    return pl.pallas_call(
        kernel,
        out_shape=[jax.ShapeDtypeStruct(s, d) for s, d in outs],
        in_specs=[pl.BlockSpec(memory_space=first)] + [in_vmem] * (len(args) - 1),
        out_specs=[in_vmem] * len(outs),
        scratch_shapes=[pltpu.VMEM(s, d) for s, d in scratch],
        compiler_params=pltpu.CompilerParams(vmem_limit_bytes=16 * 1024 * 1024),
        cost_estimate=pl.CostEstimate(flops=flops, bytes_accessed=4 << 20, transcendentals=0),
    )(*args)


def pack(k, v):
    in_hbm = pl.BlockSpec(memory_space=pltpu.HBM)
    in_vmem = pl.BlockSpec(memory_space=pltpu.VMEM)
    rim = jax.ShapeDtypeStruct((2, RIM, k.shape[1]), k.dtype)
    return pl.pallas_call(
        pack_kernel,
        out_shape=[rim, rim],
        in_specs=[in_hbm, in_hbm],
        out_specs=[in_vmem, in_vmem],
        scratch_shapes=[pltpu.SemaphoreType.DMA((4,))],
    )(k, v)


def swap(count, bits):
    return [(i, i ^ bits) for i in range(count)]


def over_links(count):
    return [(i, (i - 1 if i % 2 == 0 else i + 1) % count) for i in range(count)]


def total(parts):
    return functools.reduce(jnp.add, [p.astype(F32) for p in parts])


def body(queries, keys, values, out_grad, w_out, block_mask):
    q, k, v, g = queries[0], keys[0], values[0], out_grad[0]
    tokens, feats = q.shape
    width = g.shape[1]
    blocks = tokens // BLK
    ctx, dp = lax.axis_size("ctx"), lax.axis_size("dp")
    chips = ctx // 2
    at_ctx, at_dp = lax.axis_index("ctx"), lax.axis_index("dp")
    core = at_ctx % 2

    to_link, to_chip = pack(k, v)
    from_link = lax.ppermute(to_link, "ctx", over_links(ctx))
    from_chip = lax.ppermute(to_chip, "ctx", swap(ctx, 1))
    low = jnp.where(core == 0, from_link, from_chip)
    high = jnp.where(core == 0, from_chip, from_link)

    mask = lax.dynamic_slice_in_dim(block_mask[0], at_ctx * blocks, blocks, 0)
    ag = dot(g, w_out, ((1,), (1,))).astype(BF16)
    own_t, stats = call(
        own_kernel,
        [((feats, tokens), F32), ((2, blocks * HEADS // 2, 2 * BLK), F32)],
        [],
        5 * 10**8,
        mask, q, k, v,
        first=pltpu.SMEM,
    )
    rows, cols = feats // ctx, width // dp
    attn_t, mine, other = call(
        forward_kernel,
        [((feats, tokens), BF16)] + [((chips, rows, width), BF16)] * 2,
        [],
        10**9,
        mask, q, low, high, own_t, stats, g,
        first=pltpu.SMEM,
    )

    other = lax.ppermute(other, "ctx", swap(ctx, 1))
    half = total([mine, other]).astype(BF16)

    ext = (tokens + 2 * RIM, feats)
    q_grad, k_own, v_own, to_low, to_high = call(
        backward_kernel,
        [((tokens, feats), BF16)]
        + [((tokens, feats), F32)] * 2
        + [((2, RIM, feats), BF16)] * 2,
        [(ext, BF16)] * 2 + [(ext, F32)] * 2,
        2 * 10**9,
        mask, q, k, v, low, high, ag, half[0, :16, :128],
        first=pltpu.SMEM,
    )

    def columns(step):
        return lax.dynamic_slice_in_dim(half, (at_dp ^ step) * cols, cols, 2)

    quarter = total(
        [columns(0)] + [lax.ppermute(columns(s), "dp", swap(dp, s)) for s in range(1, dp)]
    ).astype(BF16)

    grad_link = lax.ppermute(jnp.where(core == 0, to_low, to_high), "ctx", over_links(ctx))
    grad_chip = lax.ppermute(jnp.where(core == 0, to_high, to_low), "ctx", swap(ctx, 1))

    groups = [list(range(c, ctx, 2)) for c in range(2)]
    over_chips = lax.all_to_all(quarter, "ctx", 0, 0, axis_index_groups=groups)
    piece = total([over_chips[i] for i in range(chips)])
    piece = (piece * (dp * tokens * ctx) ** (-0.5)).astype(BF16)
    pieces = lax.all_to_all(jnp.broadcast_to(piece[None], (dp, rows, cols)), "dp", 0, 0)

    output = dot(attn_t, w_out, ((0,), (0,))).astype(BF16)
    k_grad, v_grad, weight_grad = call(
        last_kernel,
        [((tokens, feats), BF16)] * 2 + [((rows, width), F32)],
        [],
        10**6,
        k_own, v_own, grad_link, grad_chip, pieces,
    )
    return (output[None], q_grad[None], k_grad[None], v_grad[None], weight_grad)


def solution(mesh):
    rows = P("dp", "ctx", None)
    return jax.shard_map(
        body,
        mesh=mesh,
        in_specs=(rows, rows, rows, rows, P(), P("dp", None, None)),
        out_specs=(rows, rows, rows, rows, P("ctx", None)),
        check_vma=False,
    )
```

```python
import functools

import jax
import jax.numpy as jnp
from jax import lax
from jax.experimental import pallas as pl
from jax.experimental.pallas import tpu as pltpu
from jax.sharding import PartitionSpec as P

HEADS = 8
HD = 64
BLK = 128
RAD = 1
CAND = 2 * RAD + 1
PAIRS = HEADS // 2
PAIR = 2 * HD
RIM = RAD * BLK
BIG_NEGATIVE = -1e30
SCALE = HD ** (-0.5)
BF16 = jnp.bfloat16
F32 = jnp.float32


def dot(a, b, contract):
    return lax.dot_general(a, b, (contract, ((), ())), preferred_element_type=F32)


def two_heads(block, axis):
    feature = lax.broadcasted_iota(jnp.int32, block.shape, axis)
    zero = jnp.zeros_like(block)
    return jnp.concatenate(
        [jnp.where(feature < HD, block, zero), jnp.where(feature < HD, zero, block)], axis=1 - axis
    )


def own_features(both):
    return jnp.concatenate([both[:HD, :BLK], both[HD:, BLK:]], axis=0)


def spread(row):
    return jnp.concatenate(
        [
            jnp.broadcast_to(row[:, :BLK], (HD, BLK)),
            jnp.broadcast_to(row[:, BLK:], (HD, BLK)),
        ],
        axis=0,
    )


def own_candidates(b, blocks):
    return max(0, RAD - b), min(CAND - 1, blocks - 1 - b + RAD)


def own_rows(b, blocks):
    first, last = own_candidates(b, blocks)
    return slice((b + first - RAD) * BLK, (b + last - RAD + 1) * BLK)


def rim_candidates(b, blocks):
    first, last = own_candidates(b, blocks)
    return [(0, c) for c in range(first)] + [(1, c) for c in range(last + 1, CAND)]


def masked(mask, b, c, part):
    return part if c == RAD else jnp.where(mask[b, c] == 1, part, BIG_NEGATIVE)


def pairs_of(blocks):
    for b in range(blocks):
        for p in range(PAIRS):
            yield b, slice(b * BLK, (b + 1) * BLK), slice(p * PAIR, (p + 1) * PAIR), b * PAIRS + p


def at_core():
    return lax.rem(lax.axis_index("ctx"), 2)


def own_kernel(mask, q, k, v, g, w_out, own_t, stats, exps, grad_t):
    blocks = q.shape[0] // BLK
    for b, rows, cols, at in pairs_of(blocks):
        first, last = own_candidates(b, blocks)
        here = own_rows(b, blocks)
        scores = dot(k[here, cols], two_heads(q[rows, cols] * SCALE, 1), ((1,), (1,)))
        scores = jnp.concatenate(
            [
                masked(mask, b, c, scores[(c - first) * BLK : (c - first + 1) * BLK])
                for c in range(first, last + 1)
            ],
            axis=0,
        )
        top = jnp.max(scores, axis=0, keepdims=True)
        e = jnp.exp(scores - top)
        exps[at, : e.shape[0]] = e
        stats[0, at : at + 1] = top
        stats[1, at : at + 1] = jnp.sum(e, axis=0, keepdims=True)
        own_t[cols, rows] = own_features(dot(v[here, cols], e.astype(BF16), ((0,), (0,))))
    grad_t[...] = dot(w_out[...], g[...], ((1,), (1,))).astype(BF16)


def forward_kernel(mask, q, low, high, own_t, stats, g, attn_t, mine, other, exps, factors):
    blocks = q.shape[0] // BLK
    sides = (low, high)
    for b, rows, cols, at in pairs_of(blocks):
        rims = rim_candidates(b, blocks)
        old = stats[0, at : at + 1]
        q2 = two_heads(q[rows, cols] * SCALE, 1)
        scores = [masked(mask, b, c, dot(sides[s][0, :, cols], q2, ((1,), (1,)))) for s, c in rims]
        top = old
        for part in scores:
            top = jnp.maximum(top, jnp.max(part, axis=0, keepdims=True))
        kept = jnp.exp(old - top)
        count = stats[1, at : at + 1] * kept
        both = None
        for (s, _), part in zip(rims, scores):
            e = jnp.exp(part - top)
            exps[s, at % PAIRS] = e
            count = count + jnp.sum(e, axis=0, keepdims=True)
            more = dot(sides[s][1, :, cols], e.astype(BF16), ((0,), (0,)))
            both = more if both is None else both + more
        share = 1.0 / count
        factors[0, at : at + 1] = kept * share
        factors[1, at : at + 1] = share
        attn = own_t[cols, rows] * spread(kept * share)
        if both is not None:
            attn = attn + own_features(both) * spread(share)
        attn_t[cols, rows] = attn.astype(BF16)
    part = dot(attn_t[...], g[...], ((1,), (0,))).astype(BF16)
    core = at_core()
    chips, rows, _ = mine.shape
    for c in range(2 * chips):
        value = part[c * rows : (c + 1) * rows]

        @pl.when(core == c % 2)
        def _():
            mine[c // 2] = value

        @pl.when(core != c % 2)
        def _():
            other[c // 2] = value


def backward(probs, delta, k, v, q2, g2_t):
    dprob = dot(v, g2_t, ((1,), (0,)))
    dscore = (probs * (dprob - delta)).astype(BF16)
    query_t = own_features(dot(k, dscore, ((0,), (0,)))) * SCALE
    return query_t, dot(dscore, q2, ((1,), (0,))), dot(probs.astype(BF16), g2_t, ((1,), (1,)))


def rim_kernel(q, low, high, grad_t, attn_t, exps, factors, to_link, to_chip, deltas, query_t):
    blocks = q.shape[0] // BLK
    first_core = at_core() == 0
    parts = {}
    for b, rows, cols, at in pairs_of(blocks):
        product = grad_t[cols, rows].astype(F32) * attn_t[cols, rows].astype(F32)
        delta = jnp.concatenate(
            [
                jnp.sum(product[:HD], axis=0, keepdims=True),
                jnp.sum(product[HD:], axis=0, keepdims=True),
            ],
            axis=1,
        )
        deltas[at : at + 1] = delta
        q2 = two_heads(q[rows, cols] * SCALE, 1)
        g2_t = two_heads(grad_t[cols, rows], 0)
        total_t = jnp.zeros((PAIR, BLK), F32)
        for s, _ in rim_candidates(b, blocks):
            rim = (low, high)[s]
            probs = exps[s, at % PAIRS] * factors[1, at : at + 1]
            part_t, k_part, v_part = backward(
                probs, delta, rim[0, :, cols], rim[1, :, cols], q2, g2_t
            )
            total_t = total_t + part_t
            parts[s, at % PAIRS] = (k_part.astype(BF16), v_part.astype(BF16))
            if len(parts) > PAIRS and (1 - s, at % PAIRS) in parts:
                for which in range(2):
                    below = parts[0, at % PAIRS][which]
                    above = parts[1, at % PAIRS][which]
                    to_link[which, :, cols] = jnp.where(first_core, below, above)
                    to_chip[which, :, cols] = jnp.where(first_core, above, below)
        query_t[cols, rows] = total_t


def own_backward_kernel(
    q, k, v, grad_t, attn_t, exps, factors, deltas, rim_t, w_out, before,
    q_grad, k_own, v_own, output, after,
):
    blocks = q.shape[0] // BLK
    k_own[...] = jnp.zeros_like(k_own)
    v_own[...] = jnp.zeros_like(v_own)
    for b, rows, cols, at in pairs_of(blocks):
        here = own_rows(b, blocks)
        probs = exps[at, : here.stop - here.start] * factors[0, at : at + 1]
        q2 = two_heads(q[rows, cols] * SCALE, 1)
        g2_t = two_heads(grad_t[cols, rows], 0)
        part_t, k_part, v_part = backward(
            probs, deltas[at : at + 1], k[here, cols], v[here, cols], q2, g2_t
        )
        q_grad[rows, cols] = (part_t + rim_t[cols, rows]).T.astype(BF16)
        k_own[here, cols] += k_part
        v_own[here, cols] += v_part
    output[...] = dot(attn_t[...], w_out[...], ((0,), (0,))).astype(BF16)
    after[...] = jnp.zeros_like(after)


def halves_kernel(mine, other, before, *outs):
    pieces, after = outs[:-1], outs[-1]
    at_dp = lax.axis_index("dp")
    cols = pieces[0].shape[2]
    for d in range(len(pieces)):
        at = slice(d * cols, (d + 1) * cols)
        value = (mine[:, :, at].astype(F32) + other[:, :, at].astype(F32)).astype(BF16)
        for s in range(len(pieces)):

            @pl.when((at_dp ^ s) == d)
            def _(s=s, value=value):
                pieces[s][...] = value

    after[...] = jnp.zeros_like(after)


def chips_kernel(*refs):
    parts, outs = refs[: lax.axis_size("dp")], refs[lax.axis_size("dp") + 3 :]
    chip = lax.div(lax.axis_index("ctx"), 2)
    for s, out in enumerate(outs):
        out[...] = total([part[chip ^ s] for part in parts]).astype(BF16)


def rim_sum_kernel(k_own, v_own, from_link, from_chip, before, k_grad, v_grad):
    tokens = k_own.shape[0]
    first_core = at_core() == 0
    for which, (own, grad) in enumerate(((k_own, k_grad), (v_own, v_grad))):
        link = from_link[which].astype(F32)
        chip = from_chip[which].astype(F32)
        low = jnp.where(first_core, link, chip)
        high = jnp.where(first_core, chip, link)
        if tokens == RIM:
            grad[...] = (own[...] + low + high).astype(BF16)
        else:
            grad[:RIM] = (own[:RIM] + low).astype(BF16)
            if tokens > 2 * RIM:
                grad[RIM : tokens - RIM] = own[RIM : tokens - RIM].astype(BF16)
            grad[tokens - RIM :] = (own[tokens - RIM :] + high).astype(BF16)


def columns_kernel(*refs):
    pieces, out = refs[:-1], refs[-1]
    at_dp = lax.axis_index("dp")
    cols = pieces[0].shape[1]
    for d in range(len(pieces)):
        value = pieces[0][...]
        for s in range(1, len(pieces)):
            value = jnp.where((at_dp ^ s) == d, pieces[s][...], value)
        out[:, d * cols : (d + 1) * cols] = value.astype(F32)


def vmem(*shape, dtype=BF16):
    return pltpu.VMEM(shape, dtype)


def hbm(*shape, dtype=BF16):
    return jax.ShapeDtypeStruct(shape, dtype)


def call(kernel, outs, flops, *args, mask=None):
    in_vmem = pl.BlockSpec(memory_space=pltpu.VMEM)
    in_smem = pl.BlockSpec(memory_space=pltpu.SMEM)
    masks = () if mask is None else (mask,)
    return pl.pallas_call(
        kernel,
        out_shape=outs,
        in_specs=[in_smem] * len(masks) + [in_vmem] * len(args),
        out_specs=[in_vmem] * len(outs),
        compiler_params=pltpu.CompilerParams(vmem_limit_bytes=24 * 1024 * 1024),
        cost_estimate=pl.CostEstimate(flops=flops, bytes_accessed=4 << 20, transcendentals=0),
    )(*masks, *args)


def swap(count, bits):
    return [(i, i ^ bits) for i in range(count)]


def over_links(count):
    return [(i, (i - 1 if i % 2 == 0 else i + 1) % count) for i in range(count)]


def total(parts):
    return functools.reduce(jnp.add, [p.astype(F32) for p in parts])


def body(queries, keys, values, out_grad, w_out, block_mask):
    q, k, v, g = queries[0], keys[0], values[0], out_grad[0]
    tokens, feats = q.shape
    width = g.shape[1]
    blocks = tokens // BLK
    ctx, dp = lax.axis_size("ctx"), lax.axis_size("dp")
    chips = ctx // 2
    at_ctx = lax.axis_index("ctx")
    core = at_ctx % 2
    rows, cols = feats // ctx, width // dp
    groups = blocks * PAIRS

    link_row = core * (tokens - RIM)
    chip_row = tokens - RIM - link_row

    def rim(row):
        return jnp.stack([lax.dynamic_slice_in_dim(x, row, RIM, 0) for x in (k, v)])

    from_link = lax.ppermute(rim(link_row), "ctx", over_links(ctx))
    from_chip = lax.ppermute(rim(chip_row), "ctx", swap(ctx, 1))
    low = jnp.where(core == 0, from_link, from_chip)
    high = jnp.where(core == 0, from_chip, from_link)

    mask = lax.dynamic_slice_in_dim(block_mask[0], at_ctx * blocks, blocks, 0)
    own_t, stats, own_exps, grad_t = call(
        own_kernel,
        [
            vmem(feats, tokens, dtype=F32),
            vmem(2, groups, 2 * BLK, dtype=F32),
            vmem(groups, min(CAND, blocks) * BLK, 2 * BLK, dtype=F32),
            vmem(feats, tokens),
        ],
        10**9,
        q, k, v, g, w_out,
        mask=mask,
    )
    attn_t, mine, other, rim_exps, factors = call(
        forward_kernel,
        [
            vmem(feats, tokens),
            vmem(chips, rows, width),
            vmem(chips, rows, width),
            vmem(2, PAIRS, RIM, 2 * BLK, dtype=F32),
            vmem(2, groups, 2 * BLK, dtype=F32),
        ],
        10**9,
        q, low, high, own_t, stats, g,
        mask=mask,
    )

    other = lax.ppermute(other, "ctx", swap(ctx, 1))
    other = pltpu.with_memory_space_constraint(other, pltpu.VMEM)
    to_link, to_chip, deltas, rim_t = call(
        rim_kernel,
        [
            vmem(2, RIM, feats),
            vmem(2, RIM, feats),
            vmem(groups, 2 * BLK, dtype=F32),
            vmem(feats, tokens, dtype=F32),
        ],
        10**9,
        q, low, high, grad_t, attn_t, rim_exps, factors,
    )
    *halves, after = call(
        halves_kernel,
        [vmem(chips, rows, cols)] * dp + [vmem(8, 128, dtype=F32)],
        10**6,
        mine, other, deltas,
    )
    grad_link = lax.ppermute(to_link, "ctx", over_links(ctx))
    grad_chip = lax.ppermute(to_chip, "ctx", swap(ctx, 1))

    q_grad, k_own, v_own, output, after = call(
        own_backward_kernel,
        [
            hbm(tokens, feats),
            vmem(tokens, feats, dtype=F32),
            vmem(tokens, feats, dtype=F32),
            hbm(tokens, width),
            vmem(8, 128, dtype=F32),
        ],
        2 * 10**9,
        q, k, v, grad_t, attn_t, own_exps, factors, deltas, rim_t, w_out, after,
    )

    halves = [halves[0]] + [lax.ppermute(halves[s], "dp", swap(dp, s)) for s in range(1, dp)]
    quarters = call(chips_kernel, [vmem(rows, cols)] * chips, 10**6, *halves, after, grad_link, grad_chip)
    k_grad, v_grad = call(
        rim_sum_kernel,
        [hbm(tokens, feats), hbm(tokens, feats)],
        10**6,
        k_own, v_own, grad_link, grad_chip, quarters[0],
    )
    piece = total(
        [quarters[0]]
        + [lax.ppermute(quarters[s], "ctx", swap(ctx, 2 * s)) for s in range(1, chips)]
    )
    piece = (piece * (dp * tokens * ctx) ** (-0.5)).astype(BF16)
    pieces = [piece] + [lax.ppermute(piece, "dp", swap(dp, s)) for s in range(1, dp)]
    (weight_grad,) = call(columns_kernel, [hbm(rows, width, dtype=F32)], 10**6, *pieces)
    return (output[None], q_grad[None], k_grad[None], v_grad[None], weight_grad)


def solution(mesh):
    rows = P("dp", "ctx", None)
    return jax.shard_map(
        body,
        mesh=mesh,
        in_specs=(rows, rows, rows, rows, P(), P("dp", None, None)),
        out_specs=(rows, rows, rows, rows, P("ctx", None)),
        check_vma=False,
    )
```

```python
import functools

import jax
import jax.numpy as jnp
from jax import lax
from jax.experimental import pallas as pl
from jax.experimental.pallas import tpu as pltpu
from jax.sharding import PartitionSpec as P

HEADS = 8
HD = 64
BLK = 128
RAD = 1
CAND = 2 * RAD + 1
PAIRS = HEADS // 2
PAIR = 2 * HD
RIM = RAD * BLK
BIG_NEGATIVE = -1e30
SCALE = HD ** (-0.5)
BF16 = jnp.bfloat16
F32 = jnp.float32


def dot(a, b, contract):
    return lax.dot_general(a, b, (contract, ((), ())), preferred_element_type=F32)


def two_heads(block, axis):
    feature = lax.broadcasted_iota(jnp.int32, block.shape, axis)
    zero = jnp.zeros_like(block)
    return jnp.concatenate(
        [jnp.where(feature < HD, block, zero), jnp.where(feature < HD, zero, block)], axis=1 - axis
    )


def own_features(both):
    return jnp.concatenate([both[:HD, :BLK], both[HD:, BLK:]], axis=0)


def spread(row):
    return jnp.concatenate(
        [
            jnp.broadcast_to(row[:, :BLK], (HD, BLK)),
            jnp.broadcast_to(row[:, BLK:], (HD, BLK)),
        ],
        axis=0,
    )


def own_candidates(b, blocks):
    return max(0, RAD - b), min(CAND - 1, blocks - 1 - b + RAD)


def own_rows(b, blocks):
    first, last = own_candidates(b, blocks)
    return slice((b + first - RAD) * BLK, (b + last - RAD + 1) * BLK)


def rim_candidates(b, blocks):
    first, last = own_candidates(b, blocks)
    return [(0, c) for c in range(first)] + [(1, c) for c in range(last + 1, CAND)]


def masked(mask, b, c, part):
    return part if c == RAD else jnp.where(mask[b, c] == 1, part, BIG_NEGATIVE)


def pairs_of(blocks):
    for b in range(blocks):
        for p in range(PAIRS):
            yield b, slice(b * BLK, (b + 1) * BLK), slice(p * PAIR, (p + 1) * PAIR), b * PAIRS + p


def at_core():
    return lax.rem(lax.axis_index("ctx"), 2)


def own_kernel(mask, q, k, v, g, w_out, own_t, stats, exps, grad_t):
    blocks = q.shape[0] // BLK
    for b, rows, cols, at in pairs_of(blocks):
        first, last = own_candidates(b, blocks)
        here = own_rows(b, blocks)
        scores = dot(k[here, cols], two_heads(q[rows, cols] * SCALE, 1), ((1,), (1,)))
        scores = jnp.concatenate(
            [
                masked(mask, b, c, scores[(c - first) * BLK : (c - first + 1) * BLK])
                for c in range(first, last + 1)
            ],
            axis=0,
        )
        top = jnp.max(scores, axis=0, keepdims=True)
        e = jnp.exp(scores - top)
        exps[at, : e.shape[0]] = e
        stats[0, at : at + 1] = top
        stats[1, at : at + 1] = jnp.sum(e, axis=0, keepdims=True)
        own_t[cols, rows] = own_features(dot(v[here, cols], e.astype(BF16), ((0,), (0,))))
    grad_t[...] = dot(w_out[...], g[...], ((1,), (1,))).astype(BF16)


def forward_kernel(mask, q, low, high, own_t, stats, g, attn_t, mine, other, exps, factors):
    blocks = q.shape[0] // BLK
    sides = (low, high)
    for b, rows, cols, at in pairs_of(blocks):
        rims = rim_candidates(b, blocks)
        old = stats[0, at : at + 1]
        q2 = two_heads(q[rows, cols] * SCALE, 1)
        scores = [masked(mask, b, c, dot(sides[s][0, :, cols], q2, ((1,), (1,)))) for s, c in rims]
        top = old
        for part in scores:
            top = jnp.maximum(top, jnp.max(part, axis=0, keepdims=True))
        kept = jnp.exp(old - top)
        count = stats[1, at : at + 1] * kept
        both = None
        for (s, _), part in zip(rims, scores):
            e = jnp.exp(part - top)
            exps[s, at % PAIRS] = e
            count = count + jnp.sum(e, axis=0, keepdims=True)
            more = dot(sides[s][1, :, cols], e.astype(BF16), ((0,), (0,)))
            both = more if both is None else both + more
        share = 1.0 / count
        factors[0, at : at + 1] = kept * share
        factors[1, at : at + 1] = share
        attn = own_t[cols, rows] * spread(kept * share)
        if both is not None:
            attn = attn + own_features(both) * spread(share)
        attn_t[cols, rows] = attn.astype(BF16)
    part = dot(attn_t[...], g[...], ((1,), (0,))).astype(BF16)
    core = at_core()
    chips, rows, _ = mine.shape
    for c in range(2 * chips):
        value = part[c * rows : (c + 1) * rows]

        @pl.when(core == c % 2)
        def _():
            mine[c // 2] = value

        @pl.when(core != c % 2)
        def _():
            other[c // 2] = value


def backward(probs, delta, k, v, q2, g2_t):
    dprob = dot(v, g2_t, ((1,), (0,)))
    dscore = (probs * (dprob - delta)).astype(BF16)
    query_t = own_features(dot(k, dscore, ((0,), (0,)))) * SCALE
    return query_t, dot(dscore, q2, ((1,), (0,))), dot(probs.astype(BF16), g2_t, ((1,), (1,)))


def rim_kernel(q, low, high, grad_t, attn_t, exps, factors, to_link, to_chip, deltas, query_t):
    blocks = q.shape[0] // BLK
    first_core = at_core() == 0
    parts = {}
    for b, rows, cols, at in pairs_of(blocks):
        product = grad_t[cols, rows].astype(F32) * attn_t[cols, rows].astype(F32)
        delta = jnp.concatenate(
            [
                jnp.sum(product[:HD], axis=0, keepdims=True),
                jnp.sum(product[HD:], axis=0, keepdims=True),
            ],
            axis=1,
        )
        deltas[at : at + 1] = delta
        q2 = two_heads(q[rows, cols] * SCALE, 1)
        g2_t = two_heads(grad_t[cols, rows], 0)
        total_t = jnp.zeros((PAIR, BLK), F32)
        for s, _ in rim_candidates(b, blocks):
            rim = (low, high)[s]
            probs = exps[s, at % PAIRS] * factors[1, at : at + 1]
            part_t, k_part, v_part = backward(
                probs, delta, rim[0, :, cols], rim[1, :, cols], q2, g2_t
            )
            total_t = total_t + part_t
            parts[s, at % PAIRS] = (k_part.astype(BF16), v_part.astype(BF16))
            if len(parts) > PAIRS and (1 - s, at % PAIRS) in parts:
                for which in range(2):
                    below = parts[0, at % PAIRS][which]
                    above = parts[1, at % PAIRS][which]
                    to_link[which, :, cols] = jnp.where(first_core, below, above)
                    to_chip[which, :, cols] = jnp.where(first_core, above, below)
        query_t[cols, rows] = total_t


def own_backward_kernel(
    q, k, v, grad_t, attn_t, exps, factors, deltas, rim_t, w_out, before,
    q_grad, k_own, v_own, output, after,
):
    blocks = q.shape[0] // BLK
    k_own[...] = jnp.zeros_like(k_own)
    v_own[...] = jnp.zeros_like(v_own)
    for b, rows, cols, at in pairs_of(blocks):
        here = own_rows(b, blocks)
        probs = exps[at, : here.stop - here.start] * factors[0, at : at + 1]
        q2 = two_heads(q[rows, cols] * SCALE, 1)
        g2_t = two_heads(grad_t[cols, rows], 0)
        part_t, k_part, v_part = backward(
            probs, deltas[at : at + 1], k[here, cols], v[here, cols], q2, g2_t
        )
        q_grad[rows, cols] = (part_t + rim_t[cols, rows]).T.astype(BF16)
        k_own[here, cols] += k_part
        v_own[here, cols] += v_part
    output[...] = dot(attn_t[...], w_out[...], ((0,), (0,))).astype(BF16)
    after[...] = jnp.zeros_like(after)


def halves_kernel(mine, other, before, *outs):
    pieces, after = outs[:-1], outs[-1]
    at_dp = lax.axis_index("dp")
    cols = pieces[0].shape[2]
    for d in range(len(pieces)):
        at = slice(d * cols, (d + 1) * cols)
        value = (mine[:, :, at].astype(F32) + other[:, :, at].astype(F32)).astype(BF16)
        for s in range(len(pieces)):

            @pl.when((at_dp ^ s) == d)
            def _(s=s, value=value):
                pieces[s][...] = value

    after[...] = jnp.zeros_like(after)


def cut_chips(parts, kept, sent):
    left = parts[0].shape[0]
    bit = lax.rem(lax.div(lax.axis_index("ctx"), lax.axis_size("ctx") // left), 2)
    for i in range(left // 2):
        kept[i] = total([part[2 * i + bit] for part in parts]).astype(BF16)
        sent[i] = total([part[2 * i + 1 - bit] for part in parts]).astype(BF16)


def chips_kernel(*refs):
    cut_chips(refs[: lax.axis_size("dp")], *refs[-2:])


def chips_step_kernel(kept, got, *outs):
    cut_chips((kept, got), *outs)


def piece_kernel(scale, kept, got, piece):
    piece[...] = (total([kept[0], got[0]]) * scale).astype(BF16)[None]


def join_kernel(held, got, out):
    count = held.shape[0]
    out[:count] = held[...]
    out[count:] = got[...]


def rim_sum_kernel(k_own, v_own, from_link, from_chip, before, k_grad, v_grad):
    tokens = k_own.shape[0]
    first_core = at_core() == 0
    for which, (own, grad) in enumerate(((k_own, k_grad), (v_own, v_grad))):
        link = from_link[which].astype(F32)
        chip = from_chip[which].astype(F32)
        low = jnp.where(first_core, link, chip)
        high = jnp.where(first_core, chip, link)
        if tokens == RIM:
            grad[...] = (own[...] + low + high).astype(BF16)
        else:
            grad[:RIM] = (own[:RIM] + low).astype(BF16)
            if tokens > 2 * RIM:
                grad[RIM : tokens - RIM] = own[RIM : tokens - RIM].astype(BF16)
            grad[tokens - RIM :] = (own[tokens - RIM :] + high).astype(BF16)


def columns_kernel(held, got, out):
    at_dp = lax.axis_index("dp")
    pieces = [part[i] for part in (held, got) for i in range(part.shape[0])]
    cols = held.shape[2]
    for d in range(len(pieces)):
        value = pieces[0]
        for s in range(1, len(pieces)):
            value = jnp.where((at_dp ^ s) == d, pieces[s], value)
        out[:, d * cols : (d + 1) * cols] = value.astype(F32)


def vmem(*shape, dtype=BF16):
    return pltpu.VMEM(shape, dtype)


def hbm(*shape, dtype=BF16):
    return jax.ShapeDtypeStruct(shape, dtype)


def call(kernel, outs, flops, *args, mask=None):
    in_vmem = pl.BlockSpec(memory_space=pltpu.VMEM)
    in_smem = pl.BlockSpec(memory_space=pltpu.SMEM)
    masks = () if mask is None else (mask,)
    return pl.pallas_call(
        kernel,
        out_shape=outs,
        in_specs=[in_smem] * len(masks) + [in_vmem] * len(args),
        out_specs=[in_vmem] * len(outs),
        compiler_params=pltpu.CompilerParams(vmem_limit_bytes=24 * 1024 * 1024),
        cost_estimate=pl.CostEstimate(flops=flops, bytes_accessed=4 << 20, transcendentals=0),
    )(*masks, *args)


def swap(count, bits):
    return [(i, i ^ bits) for i in range(count)]


def over_links(count):
    return [(i, (i - 1 if i % 2 == 0 else i + 1) % count) for i in range(count)]


def total(parts):
    return functools.reduce(jnp.add, [p.astype(F32) for p in parts])


def body(queries, keys, values, out_grad, w_out, block_mask):
    q, k, v, g = queries[0], keys[0], values[0], out_grad[0]
    tokens, feats = q.shape
    width = g.shape[1]
    blocks = tokens // BLK
    ctx, dp = lax.axis_size("ctx"), lax.axis_size("dp")
    chips = ctx // 2
    at_ctx = lax.axis_index("ctx")
    core = at_ctx % 2
    rows, cols = feats // ctx, width // dp
    groups = blocks * PAIRS

    link_row = core * (tokens - RIM)
    chip_row = tokens - RIM - link_row

    def rim(row):
        return jnp.stack([lax.dynamic_slice_in_dim(x, row, RIM, 0) for x in (k, v)])

    from_link = lax.ppermute(rim(link_row), "ctx", over_links(ctx))
    from_chip = lax.ppermute(rim(chip_row), "ctx", swap(ctx, 1))
    low = jnp.where(core == 0, from_link, from_chip)
    high = jnp.where(core == 0, from_chip, from_link)

    mask = lax.dynamic_slice_in_dim(block_mask[0], at_ctx * blocks, blocks, 0)
    own_t, stats, own_exps, grad_t = call(
        own_kernel,
        [
            vmem(feats, tokens, dtype=F32),
            vmem(2, groups, 2 * BLK, dtype=F32),
            vmem(groups, min(CAND, blocks) * BLK, 2 * BLK, dtype=F32),
            vmem(feats, tokens),
        ],
        10**9,
        q, k, v, g, w_out,
        mask=mask,
    )
    attn_t, mine, other, rim_exps, factors = call(
        forward_kernel,
        [
            vmem(feats, tokens),
            vmem(chips, rows, width),
            vmem(chips, rows, width),
            vmem(2, PAIRS, RIM, 2 * BLK, dtype=F32),
            vmem(2, groups, 2 * BLK, dtype=F32),
        ],
        10**9,
        q, low, high, own_t, stats, g,
        mask=mask,
    )

    other = lax.ppermute(other, "ctx", swap(ctx, 1))
    other = pltpu.with_memory_space_constraint(other, pltpu.VMEM)
    to_link, to_chip, deltas, rim_t = call(
        rim_kernel,
        [
            vmem(2, RIM, feats),
            vmem(2, RIM, feats),
            vmem(groups, 2 * BLK, dtype=F32),
            vmem(feats, tokens, dtype=F32),
        ],
        10**9,
        q, low, high, grad_t, attn_t, rim_exps, factors,
    )
    *halves, after = call(
        halves_kernel,
        [vmem(chips, rows, cols)] * dp + [vmem(8, 128, dtype=F32)],
        10**6,
        mine, other, deltas,
    )
    grad_link = lax.ppermute(to_link, "ctx", over_links(ctx))
    grad_chip = lax.ppermute(to_chip, "ctx", swap(ctx, 1))

    q_grad, k_own, v_own, output, after = call(
        own_backward_kernel,
        [
            hbm(tokens, feats),
            vmem(tokens, feats, dtype=F32),
            vmem(tokens, feats, dtype=F32),
            hbm(tokens, width),
            vmem(8, 128, dtype=F32),
        ],
        2 * 10**9,
        q, k, v, grad_t, attn_t, own_exps, factors, deltas, rim_t, w_out, after,
    )

    halves = [halves[0]] + [lax.ppermute(halves[s], "dp", swap(dp, s)) for s in range(1, dp)]
    kept, sent = call(
        chips_kernel,
        [vmem(chips // 2, rows, cols)] * 2,
        10**6,
        *halves, after, grad_link, grad_chip,
    )
    k_grad, v_grad = call(
        rim_sum_kernel,
        [hbm(tokens, feats), hbm(tokens, feats)],
        10**6,
        k_own, v_own, grad_link, grad_chip, kept,
    )
    bits = 2
    while 2 * bits < ctx:
        got = lax.ppermute(sent, "ctx", swap(ctx, bits))
        kept, sent = call(
            chips_step_kernel, [vmem(kept.shape[0] // 2, rows, cols)] * 2, 10**6, kept, got
        )
        bits *= 2
    got = lax.ppermute(sent, "ctx", swap(ctx, bits))
    (held,) = call(
        functools.partial(piece_kernel, (dp * tokens * ctx) ** (-0.5)),
        [vmem(1, rows, cols)],
        10**6,
        kept, got,
    )
    bits = 1
    while 2 * bits < dp:
        got = lax.ppermute(held, "dp", swap(dp, bits))
        (held,) = call(join_kernel, [vmem(2 * bits, rows, cols)], 10**6, held, got)
        bits *= 2
    got = lax.ppermute(held, "dp", swap(dp, bits))
    (weight_grad,) = call(columns_kernel, [hbm(rows, width, dtype=F32)], 10**6, held, got)
    return (output[None], q_grad[None], k_grad[None], v_grad[None], weight_grad)


def solution(mesh):
    rows = P("dp", "ctx", None)
    return jax.shard_map(
        body,
        mesh=mesh,
        in_specs=(rows, rows, rows, rows, P(), P("dp", None, None)),
        out_specs=(rows, rows, rows, rows, P("ctx", None)),
        check_vma=False,
    )
```

```python
import functools

import jax
import jax.numpy as jnp
from jax import lax
from jax.experimental import pallas as pl
from jax.experimental.pallas import tpu as pltpu
from jax.sharding import PartitionSpec as P

HEADS = 8
HD = 64
BLK = 128
RAD = 1
CAND = 2 * RAD + 1
PAIRS = HEADS // 2
PAIR = 2 * HD
RIM = RAD * BLK
BIG_NEGATIVE = -1e30
SCALE = HD ** (-0.5)
BF16 = jnp.bfloat16
F32 = jnp.float32


def dot(a, b, contract):
    return lax.dot_general(a, b, (contract, ((), ())), preferred_element_type=F32)


def two_heads(block, axis):
    feature = lax.broadcasted_iota(jnp.int32, block.shape, axis)
    zero = jnp.zeros_like(block)
    return jnp.concatenate(
        [jnp.where(feature < HD, block, zero), jnp.where(feature < HD, zero, block)], axis=1 - axis
    )


def own_features(both):
    return jnp.concatenate([both[:HD, :BLK], both[HD:, BLK:]], axis=0)


def spread(row):
    return jnp.concatenate(
        [
            jnp.broadcast_to(row[:, :BLK], (HD, BLK)),
            jnp.broadcast_to(row[:, BLK:], (HD, BLK)),
        ],
        axis=0,
    )


def own_candidates(b, blocks):
    return max(0, RAD - b), min(CAND - 1, blocks - 1 - b + RAD)


def own_rows(b, blocks):
    first, last = own_candidates(b, blocks)
    return slice((b + first - RAD) * BLK, (b + last - RAD + 1) * BLK)


def rim_candidates(b, blocks):
    first, last = own_candidates(b, blocks)
    return [(0, c) for c in range(first)] + [(1, c) for c in range(last + 1, CAND)]


def masked(mask, b, c, part):
    return part if c == RAD else jnp.where(mask[b, c] == 1, part, BIG_NEGATIVE)


def pairs_of(blocks):
    for b in range(blocks):
        for p in range(PAIRS):
            yield b, slice(b * BLK, (b + 1) * BLK), slice(p * PAIR, (p + 1) * PAIR), b * PAIRS + p


def at_core():
    return lax.rem(lax.axis_index("ctx"), 2)


def own_kernel(mask, q, k, v, g, w_out, own_t, stats, exps, grad_t):
    blocks = q.shape[0] // BLK
    for b, rows, cols, at in pairs_of(blocks):
        first, last = own_candidates(b, blocks)
        here = own_rows(b, blocks)
        scores = dot(k[here, cols], two_heads(q[rows, cols] * SCALE, 1), ((1,), (1,)))
        scores = jnp.concatenate(
            [
                masked(mask, b, c, scores[(c - first) * BLK : (c - first + 1) * BLK])
                for c in range(first, last + 1)
            ],
            axis=0,
        )
        top = jnp.max(scores, axis=0, keepdims=True)
        e = jnp.exp(scores - top)
        exps[at, : e.shape[0]] = e
        stats[0, at : at + 1] = top
        stats[1, at : at + 1] = jnp.sum(e, axis=0, keepdims=True)
        own_t[cols, rows] = own_features(dot(v[here, cols], e.astype(BF16), ((0,), (0,))))
    grad_t[...] = dot(w_out[...], g[...], ((1,), (1,))).astype(BF16)


def forward_kernel(mask, q, low, high, own_t, stats, g, attn_t, mine, other, exps, factors):
    blocks = q.shape[0] // BLK
    sides = (low, high)
    for b, rows, cols, at in pairs_of(blocks):
        rims = rim_candidates(b, blocks)
        old = stats[0, at : at + 1]
        q2 = two_heads(q[rows, cols] * SCALE, 1)
        scores = [masked(mask, b, c, dot(sides[s][0, :, cols], q2, ((1,), (1,)))) for s, c in rims]
        top = old
        for part in scores:
            top = jnp.maximum(top, jnp.max(part, axis=0, keepdims=True))
        kept = jnp.exp(old - top)
        count = stats[1, at : at + 1] * kept
        both = None
        for (s, _), part in zip(rims, scores):
            e = jnp.exp(part - top)
            exps[s, at % PAIRS] = e
            count = count + jnp.sum(e, axis=0, keepdims=True)
            more = dot(sides[s][1, :, cols], e.astype(BF16), ((0,), (0,)))
            both = more if both is None else both + more
        share = 1.0 / count
        factors[0, at : at + 1] = kept * share
        factors[1, at : at + 1] = share
        attn = own_t[cols, rows] * spread(kept * share)
        if both is not None:
            attn = attn + own_features(both) * spread(share)
        attn_t[cols, rows] = attn.astype(BF16)
    part = dot(attn_t[...], g[...], ((1,), (0,))).astype(BF16)
    core = at_core()
    chips, rows, _ = mine.shape
    for c in range(2 * chips):
        value = part[c * rows : (c + 1) * rows]

        @pl.when(core == c % 2)
        def _():
            mine[c // 2] = value

        @pl.when(core != c % 2)
        def _():
            other[c // 2] = value


def backward(probs, delta, k, v, q2, g2_t):
    dprob = dot(v, g2_t, ((1,), (0,)))
    dscore = (probs * (dprob - delta)).astype(BF16)
    query_t = own_features(dot(k, dscore, ((0,), (0,)))) * SCALE
    return query_t, dot(dscore, q2, ((1,), (0,))), dot(probs.astype(BF16), g2_t, ((1,), (1,)))


def rim_kernel(
    q, low, high, grad_t, attn_t, exps, factors, before, to_link, to_chip, deltas, query_t
):
    blocks = q.shape[0] // BLK
    first_core = at_core() == 0
    parts = {}
    for b, rows, cols, at in pairs_of(blocks):
        product = grad_t[cols, rows].astype(F32) * attn_t[cols, rows].astype(F32)
        delta = jnp.concatenate(
            [
                jnp.sum(product[:HD], axis=0, keepdims=True),
                jnp.sum(product[HD:], axis=0, keepdims=True),
            ],
            axis=1,
        )
        deltas[at : at + 1] = delta
        q2 = two_heads(q[rows, cols] * SCALE, 1)
        g2_t = two_heads(grad_t[cols, rows], 0)
        total_t = jnp.zeros((PAIR, BLK), F32)
        for s, _ in rim_candidates(b, blocks):
            rim = (low, high)[s]
            probs = exps[s, at % PAIRS] * factors[1, at : at + 1]
            part_t, k_part, v_part = backward(
                probs, delta, rim[0, :, cols], rim[1, :, cols], q2, g2_t
            )
            total_t = total_t + part_t
            parts[s, at % PAIRS] = (k_part.astype(BF16), v_part.astype(BF16))
            if len(parts) > PAIRS and (1 - s, at % PAIRS) in parts:
                for which in range(2):
                    below = parts[0, at % PAIRS][which]
                    above = parts[1, at % PAIRS][which]
                    to_link[which, :, cols] = jnp.where(first_core, below, above)
                    to_chip[which, :, cols] = jnp.where(first_core, above, below)
        query_t[cols, rows] = total_t


def own_backward_kernel(
    q, k, v, grad_t, attn_t, exps, factors, deltas, rim_t, w_out, before,
    q_grad, k_own, v_own, output, after,
):
    blocks = q.shape[0] // BLK
    k_own[...] = jnp.zeros_like(k_own)
    v_own[...] = jnp.zeros_like(v_own)
    for b, rows, cols, at in pairs_of(blocks):
        here = own_rows(b, blocks)
        probs = exps[at, : here.stop - here.start] * factors[0, at : at + 1]
        q2 = two_heads(q[rows, cols] * SCALE, 1)
        g2_t = two_heads(grad_t[cols, rows], 0)
        part_t, k_part, v_part = backward(
            probs, deltas[at : at + 1], k[here, cols], v[here, cols], q2, g2_t
        )
        q_grad[rows, cols] = (part_t + rim_t[cols, rows]).T.astype(BF16)
        k_own[here, cols] += k_part
        v_own[here, cols] += v_part
    output[...] = dot(attn_t[...], w_out[...], ((0,), (0,))).astype(BF16)
    after[...] = jnp.zeros_like(after)


def halves_kernel(mine, other, *outs):
    pieces, after = outs[:-1], outs[-1]
    at_dp = lax.axis_index("dp")
    cols = pieces[0].shape[2]
    for d in range(len(pieces)):
        at = slice(d * cols, (d + 1) * cols)
        value = (mine[:, :, at].astype(F32) + other[:, :, at].astype(F32)).astype(BF16)
        for s in range(len(pieces)):

            @pl.when((at_dp ^ s) == d)
            def _(s=s, value=value):
                pieces[s][...] = value

    after[...] = jnp.zeros_like(after)


def chips_kernel(*refs):
    parts, outs = refs[: lax.axis_size("dp")], refs[lax.axis_size("dp") + 1 :]
    chip = lax.div(lax.axis_index("ctx"), 2)
    for s, out in enumerate(outs):
        out[...] = total([part[chip ^ s] for part in parts]).astype(BF16)


def last_kernel(k_own, v_own, from_link, from_chip, *refs):
    pieces, (k_grad, v_grad, weight_grad) = refs[:-3], refs[-3:]
    tokens = k_own.shape[0]
    first_core = at_core() == 0
    for which, (own, grad) in enumerate(((k_own, k_grad), (v_own, v_grad))):
        link = from_link[which].astype(F32)
        chip = from_chip[which].astype(F32)
        low = jnp.where(first_core, link, chip)
        high = jnp.where(first_core, chip, link)
        if tokens == RIM:
            grad[...] = (own[...] + low + high).astype(BF16)
        else:
            grad[:RIM] = (own[:RIM] + low).astype(BF16)
            if tokens > 2 * RIM:
                grad[RIM : tokens - RIM] = own[RIM : tokens - RIM].astype(BF16)
            grad[tokens - RIM :] = (own[tokens - RIM :] + high).astype(BF16)
    at_dp = lax.axis_index("dp")
    cols = pieces[0].shape[1]
    for d in range(len(pieces)):
        value = pieces[0][...]
        for s in range(1, len(pieces)):
            value = jnp.where((at_dp ^ s) == d, pieces[s][...], value)
        weight_grad[:, d * cols : (d + 1) * cols] = value.astype(F32)


def vmem(*shape, dtype=BF16):
    return pltpu.VMEM(shape, dtype)


def hbm(*shape, dtype=BF16):
    return jax.ShapeDtypeStruct(shape, dtype)


def call(kernel, outs, flops, *args, mask=None):
    in_vmem = pl.BlockSpec(memory_space=pltpu.VMEM)
    in_smem = pl.BlockSpec(memory_space=pltpu.SMEM)
    masks = () if mask is None else (mask,)
    return pl.pallas_call(
        kernel,
        out_shape=outs,
        in_specs=[in_smem] * len(masks) + [in_vmem] * len(args),
        out_specs=[in_vmem] * len(outs),
        compiler_params=pltpu.CompilerParams(vmem_limit_bytes=24 * 1024 * 1024),
        cost_estimate=pl.CostEstimate(flops=flops, bytes_accessed=flops // 250, transcendentals=0),
    )(*masks, *args)


def swap(count, bits):
    return [(i, i ^ bits) for i in range(count)]


def over_links(count):
    return [(i, (i - 1 if i % 2 == 0 else i + 1) % count) for i in range(count)]


def total(parts):
    return functools.reduce(jnp.add, [p.astype(F32) for p in parts])


def body(queries, keys, values, out_grad, w_out, block_mask):
    q, k, v, g = queries[0], keys[0], values[0], out_grad[0]
    tokens, feats = q.shape
    width = g.shape[1]
    blocks = tokens // BLK
    ctx, dp = lax.axis_size("ctx"), lax.axis_size("dp")
    chips = ctx // 2
    at_ctx = lax.axis_index("ctx")
    core = at_ctx % 2
    rows, cols = feats // ctx, width // dp
    groups = blocks * PAIRS

    link_row = core * (tokens - RIM)
    chip_row = tokens - RIM - link_row

    def rim(row):
        return jnp.stack([lax.dynamic_slice_in_dim(x, row, RIM, 0) for x in (k, v)])

    from_link = lax.ppermute(rim(link_row), "ctx", over_links(ctx))
    from_chip = lax.ppermute(rim(chip_row), "ctx", swap(ctx, 1))
    low = jnp.where(core == 0, from_link, from_chip)
    high = jnp.where(core == 0, from_chip, from_link)

    mask = lax.dynamic_slice_in_dim(block_mask[0], at_ctx * blocks, blocks, 0)
    own_t, stats, own_exps, grad_t = call(
        own_kernel,
        [
            vmem(feats, tokens, dtype=F32),
            vmem(2, groups, 2 * BLK, dtype=F32),
            vmem(groups, min(CAND, blocks) * BLK, 2 * BLK, dtype=F32),
            vmem(feats, tokens),
        ],
        10**9,
        q, k, v, g, w_out,
        mask=mask,
    )
    attn_t, mine, other, rim_exps, factors = call(
        forward_kernel,
        [
            vmem(feats, tokens),
            vmem(chips, rows, width),
            vmem(chips, rows, width),
            vmem(2, PAIRS, RIM, 2 * BLK, dtype=F32),
            vmem(2, groups, 2 * BLK, dtype=F32),
        ],
        10**9,
        q, low, high, own_t, stats, g,
        mask=mask,
    )

    other = lax.ppermute(other, "ctx", swap(ctx, 1))
    other = pltpu.with_memory_space_constraint(other, pltpu.VMEM)
    *halves, after = call(
        halves_kernel,
        [vmem(chips, rows, cols)] * dp + [vmem(8, 128, dtype=F32)],
        10**6,
        mine, other,
    )
    to_link, to_chip, deltas, rim_t = call(
        rim_kernel,
        [
            vmem(2, RIM, feats),
            vmem(2, RIM, feats),
            vmem(groups, 2 * BLK, dtype=F32),
            vmem(feats, tokens, dtype=F32),
        ],
        10**6,
        q, low, high, grad_t, attn_t, rim_exps, factors, after,
    )
    grad_link = lax.ppermute(to_link, "ctx", over_links(ctx))
    grad_chip = lax.ppermute(to_chip, "ctx", swap(ctx, 1))

    q_grad, k_own, v_own, output, after = call(
        own_backward_kernel,
        [
            hbm(tokens, feats),
            vmem(tokens, feats, dtype=F32),
            vmem(tokens, feats, dtype=F32),
            hbm(tokens, width),
            vmem(8, 128, dtype=F32),
        ],
        10**6,
        q, k, v, grad_t, attn_t, own_exps, factors, deltas, rim_t, w_out, after,
    )

    halves = [halves[0]] + [lax.ppermute(halves[s], "dp", swap(dp, s)) for s in range(1, dp)]
    quarters = call(chips_kernel, [vmem(rows, cols)] * chips, 10**6, *halves, after)
    piece = total(
        [quarters[0]]
        + [lax.ppermute(quarters[s], "ctx", swap(ctx, 2 * s)) for s in range(1, chips)]
    )
    piece = (piece * (dp * tokens * ctx) ** (-0.5)).astype(BF16)
    pieces = [piece] + [lax.ppermute(piece, "dp", swap(dp, s)) for s in range(1, dp)]
    k_grad, v_grad, weight_grad = call(
        last_kernel,
        [hbm(tokens, feats), hbm(tokens, feats), hbm(rows, width, dtype=F32)],
        10**6,
        k_own, v_own, grad_link, grad_chip, *pieces,
    )
    return (output[None], q_grad[None], k_grad[None], v_grad[None], weight_grad)


def solution(mesh):
    rows = P("dp", "ctx", None)
    return jax.shard_map(
        body,
        mesh=mesh,
        in_specs=(rows, rows, rows, rows, P(), P("dp", None, None)),
        out_specs=(rows, rows, rows, rows, P("ctx", None)),
        check_vma=False,
    )
```

```python
import functools

import jax
import jax.numpy as jnp
from jax import lax
from jax.experimental import pallas as pl
from jax.experimental.pallas import tpu as pltpu
from jax.sharding import PartitionSpec as P

HEADS = 8
HD = 64
BLK = 128
RAD = 1
CAND = 2 * RAD + 1
PAIRS = HEADS // 2
PAIR = 2 * HD
RIM = RAD * BLK
BIG_NEGATIVE = -1e30
SCALE = HD ** (-0.5)
BF16 = jnp.bfloat16
F32 = jnp.float32


def dot(a, b, contract):
    return lax.dot_general(a, b, (contract, ((), ())), preferred_element_type=F32)


def two_heads(block, axis):
    feature = lax.broadcasted_iota(jnp.int32, block.shape, axis)
    zero = jnp.zeros_like(block)
    return jnp.concatenate(
        [jnp.where(feature < HD, block, zero), jnp.where(feature < HD, zero, block)], axis=1 - axis
    )


def own_features(both):
    return jnp.concatenate([both[:HD, :BLK], both[HD:, BLK:]], axis=0)


def spread(row):
    return jnp.concatenate(
        [
            jnp.broadcast_to(row[:, :BLK], (HD, BLK)),
            jnp.broadcast_to(row[:, BLK:], (HD, BLK)),
        ],
        axis=0,
    )


def own_candidates(b, blocks):
    return max(0, RAD - b), min(CAND - 1, blocks - 1 - b + RAD)


def own_rows(b, blocks):
    first, last = own_candidates(b, blocks)
    return slice((b + first - RAD) * BLK, (b + last - RAD + 1) * BLK)


def rim_candidates(b, blocks):
    first, last = own_candidates(b, blocks)
    return [(0, c) for c in range(first)] + [(1, c) for c in range(last + 1, CAND)]


def masked(mask, b, c, part):
    return part if c == RAD else jnp.where(mask[b, c] == 1, part, BIG_NEGATIVE)


def pairs_of(blocks):
    for b in range(blocks):
        for p in range(PAIRS):
            yield b, slice(b * BLK, (b + 1) * BLK), slice(p * PAIR, (p + 1) * PAIR), b * PAIRS + p


def at_core():
    return lax.rem(lax.axis_index("ctx"), 2)


def own_kernel(mask, q, k, v, g, w_out, own_t, stats, exps, grad_t):
    blocks = q.shape[0] // BLK
    for b, rows, cols, at in pairs_of(blocks):
        first, last = own_candidates(b, blocks)
        here = own_rows(b, blocks)
        scores = dot(k[here, cols], two_heads(q[rows, cols] * SCALE, 1), ((1,), (1,)))
        scores = jnp.concatenate(
            [
                masked(mask, b, c, scores[(c - first) * BLK : (c - first + 1) * BLK])
                for c in range(first, last + 1)
            ],
            axis=0,
        )
        top = jnp.max(scores, axis=0, keepdims=True)
        e = jnp.exp(scores - top)
        exps[at, : e.shape[0]] = e
        stats[0, at : at + 1] = top
        stats[1, at : at + 1] = jnp.sum(e, axis=0, keepdims=True)
        own_t[cols, rows] = own_features(dot(v[here, cols], e.astype(BF16), ((0,), (0,))))
    grad_t[...] = dot(w_out[...], g[...], ((1,), (1,))).astype(BF16)


def forward_kernel(
    mask, q, low, high, own_t, stats, before, attn_t, mine, other, exps, factors
):
    blocks = q.shape[0] // BLK
    sides = (low, high)
    for b, rows, cols, at in pairs_of(blocks):
        rims = rim_candidates(b, blocks)
        old = stats[0, at : at + 1]
        q2 = two_heads(q[rows, cols] * SCALE, 1)
        scores = [masked(mask, b, c, dot(sides[s][0, :, cols], q2, ((1,), (1,)))) for s, c in rims]
        top = old
        for part in scores:
            top = jnp.maximum(top, jnp.max(part, axis=0, keepdims=True))
        kept = jnp.exp(old - top)
        count = stats[1, at : at + 1] * kept
        both = None
        for (s, _), part in zip(rims, scores):
            e = jnp.exp(part - top)
            exps[s, at % PAIRS] = e
            count = count + jnp.sum(e, axis=0, keepdims=True)
            more = dot(sides[s][1, :, cols], e.astype(BF16), ((0,), (0,)))
            both = more if both is None else both + more
        share = 1.0 / count
        factors[0, at : at + 1] = kept * share
        factors[1, at : at + 1] = share
        attn = own_t[cols, rows] * spread(kept * share)
        if both is not None:
            attn = attn + own_features(both) * spread(share)
        attn_t[cols, rows] = attn.astype(BF16)
    core = at_core()
    chips, rows, _ = mine.shape
    for c in range(2 * chips):
        value = attn_t[c * rows : (c + 1) * rows]

        @pl.when(core == c % 2)
        def _(c=c, value=value):
            mine[c // 2] = value

        @pl.when(core != c % 2)
        def _(c=c, value=value):
            other[c // 2] = value


def flat_dot(attn, g):
    chips, rows, tokens = attn.shape
    return dot(attn[...].reshape(chips * rows, tokens), g[...], ((1,), (0,)))


def product_kernel(mine, g, product):
    product[...] = flat_dot(mine, g)


def backward(probs, delta, k, v, q2, g2_t):
    dprob = dot(v, g2_t, ((1,), (0,)))
    dscore = (probs * (dprob - delta)).astype(BF16)
    query_t = own_features(dot(k, dscore, ((0,), (0,)))) * SCALE
    return query_t, dot(dscore, q2, ((1,), (0,))), dot(probs.astype(BF16), g2_t, ((1,), (1,)))


def rim_kernel(
    q, low, high, grad_t, attn_t, exps, factors, before, to_link, to_chip, deltas, query_t
):
    blocks = q.shape[0] // BLK
    first_core = at_core() == 0
    parts = {}
    for b, rows, cols, at in pairs_of(blocks):
        product = grad_t[cols, rows].astype(F32) * attn_t[cols, rows].astype(F32)
        delta = jnp.concatenate(
            [
                jnp.sum(product[:HD], axis=0, keepdims=True),
                jnp.sum(product[HD:], axis=0, keepdims=True),
            ],
            axis=1,
        )
        deltas[at : at + 1] = delta
        q2 = two_heads(q[rows, cols] * SCALE, 1)
        g2_t = two_heads(grad_t[cols, rows], 0)
        total_t = jnp.zeros((PAIR, BLK), F32)
        for s, _ in rim_candidates(b, blocks):
            rim = (low, high)[s]
            probs = exps[s, at % PAIRS] * factors[1, at : at + 1]
            part_t, k_part, v_part = backward(
                probs, delta, rim[0, :, cols], rim[1, :, cols], q2, g2_t
            )
            total_t = total_t + part_t
            parts[s, at % PAIRS] = (k_part.astype(BF16), v_part.astype(BF16))
            if len(parts) > PAIRS and (1 - s, at % PAIRS) in parts:
                for which in range(2):
                    below = parts[0, at % PAIRS][which]
                    above = parts[1, at % PAIRS][which]
                    to_link[which, :, cols] = jnp.where(first_core, below, above)
                    to_chip[which, :, cols] = jnp.where(first_core, above, below)
        query_t[cols, rows] = total_t


def own_backward_kernel(
    q, k, v, grad_t, attn_t, exps, factors, deltas, rim_t, w_out, before,
    q_grad, k_own, v_own, output, after,
):
    blocks = q.shape[0] // BLK
    k_own[...] = jnp.zeros_like(k_own)
    v_own[...] = jnp.zeros_like(v_own)
    for b, rows, cols, at in pairs_of(blocks):
        here = own_rows(b, blocks)
        probs = exps[at, : here.stop - here.start] * factors[0, at : at + 1]
        q2 = two_heads(q[rows, cols] * SCALE, 1)
        g2_t = two_heads(grad_t[cols, rows], 0)
        part_t, k_part, v_part = backward(
            probs, deltas[at : at + 1], k[here, cols], v[here, cols], q2, g2_t
        )
        q_grad[rows, cols] = (part_t + rim_t[cols, rows]).T.astype(BF16)
        k_own[here, cols] += k_part
        v_own[here, cols] += v_part
    output[...] = dot(attn_t[...], w_out[...], ((0,), (0,))).astype(BF16)
    after[...] = jnp.zeros_like(after)


def halves_kernel(product, other, g, *outs):
    pieces, after = outs[:-1], outs[-1]
    at_dp = lax.axis_index("dp")
    chips, rows, cols = pieces[0].shape
    both = (product[...] + flat_dot(other, g)).astype(BF16)
    for d in range(len(pieces)):
        value = both[:, d * cols : (d + 1) * cols].reshape(chips, rows, cols)
        for s in range(len(pieces)):

            @pl.when((at_dp ^ s) == d)
            def _(s=s, value=value):
                pieces[s][...] = value

    after[...] = jnp.zeros_like(after)


def chips_kernel(*refs):
    parts, outs = refs[: lax.axis_size("dp")], refs[lax.axis_size("dp") + 1 :]
    chip = lax.div(lax.axis_index("ctx"), 2)
    for s, out in enumerate(outs):
        out[...] = total([part[chip ^ s] for part in parts]).astype(BF16)


def last_kernel(k_own, v_own, from_link, from_chip, *refs):
    pieces, (k_grad, v_grad, weight_grad) = refs[:-3], refs[-3:]
    tokens = k_own.shape[0]
    first_core = at_core() == 0
    for which, (own, grad) in enumerate(((k_own, k_grad), (v_own, v_grad))):
        link = from_link[which].astype(F32)
        chip = from_chip[which].astype(F32)
        low = jnp.where(first_core, link, chip)
        high = jnp.where(first_core, chip, link)
        if tokens == RIM:
            grad[...] = (own[...] + low + high).astype(BF16)
        else:
            grad[:RIM] = (own[:RIM] + low).astype(BF16)
            if tokens > 2 * RIM:
                grad[RIM : tokens - RIM] = own[RIM : tokens - RIM].astype(BF16)
            grad[tokens - RIM :] = (own[tokens - RIM :] + high).astype(BF16)
    at_dp = lax.axis_index("dp")
    cols = pieces[0].shape[1]
    for d in range(len(pieces)):
        value = pieces[0][...]
        for s in range(1, len(pieces)):
            value = jnp.where((at_dp ^ s) == d, pieces[s][...], value)
        weight_grad[:, d * cols : (d + 1) * cols] = value.astype(F32)


def vmem(*shape, dtype=BF16):
    return pltpu.VMEM(shape, dtype)


def hbm(*shape, dtype=BF16):
    return jax.ShapeDtypeStruct(shape, dtype)


def call(kernel, outs, flops, *args, mask=None):
    in_vmem = pl.BlockSpec(memory_space=pltpu.VMEM)
    in_smem = pl.BlockSpec(memory_space=pltpu.SMEM)
    masks = () if mask is None else (mask,)
    return pl.pallas_call(
        kernel,
        out_shape=outs,
        in_specs=[in_smem] * len(masks) + [in_vmem] * len(args),
        out_specs=[in_vmem] * len(outs),
        compiler_params=pltpu.CompilerParams(vmem_limit_bytes=24 * 1024 * 1024),
        cost_estimate=pl.CostEstimate(flops=flops, bytes_accessed=flops // 250, transcendentals=0),
    )(*masks, *args)


def swap(count, bits):
    return [(i, i ^ bits) for i in range(count)]


def over_links(count):
    return [(i, (i - 1 if i % 2 == 0 else i + 1) % count) for i in range(count)]


def total(parts):
    return functools.reduce(jnp.add, [p.astype(F32) for p in parts])


def body(queries, keys, values, out_grad, w_out, block_mask):
    q, k, v, g = queries[0], keys[0], values[0], out_grad[0]
    tokens, feats = q.shape
    width = g.shape[1]
    blocks = tokens // BLK
    ctx, dp = lax.axis_size("ctx"), lax.axis_size("dp")
    chips = ctx // 2
    at_ctx = lax.axis_index("ctx")
    core = at_ctx % 2
    rows, cols = feats // ctx, width // dp
    groups = blocks * PAIRS

    link_row = core * (tokens - RIM)
    chip_row = tokens - RIM - link_row

    def rim(row):
        return jnp.stack([lax.dynamic_slice_in_dim(x, row, RIM, 0) for x in (k, v)])

    from_link = lax.ppermute(rim(link_row), "ctx", over_links(ctx))
    from_chip = lax.ppermute(rim(chip_row), "ctx", swap(ctx, 1))
    sibling_g = lax.ppermute(g, "ctx", swap(ctx, 1))
    sibling_g = pltpu.with_memory_space_constraint(sibling_g, pltpu.VMEM)
    low = jnp.where(core == 0, from_link, from_chip)
    high = jnp.where(core == 0, from_chip, from_link)

    mask = lax.dynamic_slice_in_dim(block_mask[0], at_ctx * blocks, blocks, 0)
    own_t, stats, own_exps, grad_t = call(
        own_kernel,
        [
            vmem(feats, tokens, dtype=F32),
            vmem(2, groups, 2 * BLK, dtype=F32),
            vmem(groups, min(CAND, blocks) * BLK, 2 * BLK, dtype=F32),
            vmem(feats, tokens),
        ],
        10**9,
        q, k, v, g, w_out,
        mask=mask,
    )
    attn_t, mine, other, rim_exps, factors = call(
        forward_kernel,
        [
            vmem(feats, tokens),
            vmem(chips, rows, tokens),
            vmem(chips, rows, tokens),
            vmem(2, PAIRS, RIM, 2 * BLK, dtype=F32),
            vmem(2, groups, 2 * BLK, dtype=F32),
        ],
        10**9,
        q, low, high, own_t, stats, sibling_g,
        mask=mask,
    )

    other = lax.ppermute(other, "ctx", swap(ctx, 1))
    other = pltpu.with_memory_space_constraint(other, pltpu.VMEM)
    (product,) = call(product_kernel, [vmem(chips * rows, width, dtype=F32)], 10**6, mine, g)
    *halves, after = call(
        halves_kernel,
        [vmem(chips, rows, cols)] * dp + [vmem(8, 128, dtype=F32)],
        10**6,
        product, other, sibling_g,
    )
    to_link, to_chip, deltas, rim_t = call(
        rim_kernel,
        [
            vmem(2, RIM, feats),
            vmem(2, RIM, feats),
            vmem(groups, 2 * BLK, dtype=F32),
            vmem(feats, tokens, dtype=F32),
        ],
        10**6,
        q, low, high, grad_t, attn_t, rim_exps, factors, after,
    )
    grad_link = lax.ppermute(to_link, "ctx", over_links(ctx))
    grad_chip = lax.ppermute(to_chip, "ctx", swap(ctx, 1))

    q_grad, k_own, v_own, output, after = call(
        own_backward_kernel,
        [
            hbm(tokens, feats),
            vmem(tokens, feats, dtype=F32),
            vmem(tokens, feats, dtype=F32),
            hbm(tokens, width),
            vmem(8, 128, dtype=F32),
        ],
        10**6,
        q, k, v, grad_t, attn_t, own_exps, factors, deltas, rim_t, w_out, after,
    )

    halves = [halves[0]] + [lax.ppermute(halves[s], "dp", swap(dp, s)) for s in range(1, dp)]
    quarters = call(chips_kernel, [vmem(rows, cols)] * chips, 10**6, *halves, after)
    piece = total(
        [quarters[0]]
        + [lax.ppermute(quarters[s], "ctx", swap(ctx, 2 * s)) for s in range(chips - 1, 0, -1)]
    )
    piece = (piece * (dp * tokens * ctx) ** (-0.5)).astype(BF16)
    pieces = [piece] + [lax.ppermute(piece, "dp", swap(dp, s)) for s in range(1, dp)]
    k_grad, v_grad, weight_grad = call(
        last_kernel,
        [hbm(tokens, feats), hbm(tokens, feats), hbm(rows, width, dtype=F32)],
        10**6,
        k_own, v_own, grad_link, grad_chip, *pieces,
    )
    return (output[None], q_grad[None], k_grad[None], v_grad[None], weight_grad)


def solution(mesh):
    rows = P("dp", "ctx", None)
    return jax.shard_map(
        body,
        mesh=mesh,
        in_specs=(rows, rows, rows, rows, P(), P("dp", None, None)),
        out_specs=(rows, rows, rows, rows, P("ctx", None)),
        check_vma=False,
    )
```

```python
import functools

import jax
import jax.numpy as jnp
from jax import lax
from jax.experimental import pallas as pl
from jax.experimental.pallas import tpu as pltpu
from jax.sharding import PartitionSpec as P

HEADS = 8
HD = 64
BLK = 128
RAD = 1
CAND = 2 * RAD + 1
PAIRS = HEADS // 2
PAIR = 2 * HD
RIM = RAD * BLK
BIG_NEGATIVE = -1e30
SCALE = HD ** (-0.5)
BF16 = jnp.bfloat16
F32 = jnp.float32


def dot(a, b, contract):
    return lax.dot_general(a, b, (contract, ((), ())), preferred_element_type=F32)


def two_heads(block, axis):
    feature = lax.broadcasted_iota(jnp.int32, block.shape, axis)
    zero = jnp.zeros_like(block)
    return jnp.concatenate(
        [jnp.where(feature < HD, block, zero), jnp.where(feature < HD, zero, block)], axis=1 - axis
    )


def own_features(both):
    return jnp.concatenate([both[:HD, :BLK], both[HD:, BLK:]], axis=0)


def spread(row):
    return jnp.concatenate(
        [
            jnp.broadcast_to(row[:, :BLK], (HD, BLK)),
            jnp.broadcast_to(row[:, BLK:], (HD, BLK)),
        ],
        axis=0,
    )


def own_candidates(b, blocks):
    return max(0, RAD - b), min(CAND - 1, blocks - 1 - b + RAD)


def own_rows(b, blocks):
    first, last = own_candidates(b, blocks)
    return slice((b + first - RAD) * BLK, (b + last - RAD + 1) * BLK)


def rim_candidates(b, blocks):
    first, last = own_candidates(b, blocks)
    return [(0, c) for c in range(first)] + [(1, c) for c in range(last + 1, CAND)]


def masked(mask, b, c, part):
    return part if c == RAD else jnp.where(mask[b, c] == 1, part, BIG_NEGATIVE)


def pairs_of(blocks):
    for b in range(blocks):
        for p in range(PAIRS):
            yield b, slice(b * BLK, (b + 1) * BLK), slice(p * PAIR, (p + 1) * PAIR), b * PAIRS + p


def at_core():
    return lax.rem(lax.axis_index("ctx"), 2)


def own_kernel(mask, q, k, v, g, w_out, own_t, stats, exps, grad_t):
    blocks = q.shape[0] // BLK
    for b, rows, cols, at in pairs_of(blocks):
        first, last = own_candidates(b, blocks)
        here = own_rows(b, blocks)
        scores = dot(k[here, cols], two_heads(q[rows, cols] * SCALE, 1), ((1,), (1,)))
        scores = jnp.concatenate(
            [
                masked(mask, b, c, scores[(c - first) * BLK : (c - first + 1) * BLK])
                for c in range(first, last + 1)
            ],
            axis=0,
        )
        top = jnp.max(scores, axis=0, keepdims=True)
        e = jnp.exp(scores - top)
        exps[at, : e.shape[0]] = e
        stats[0, at : at + 1] = top
        stats[1, at : at + 1] = jnp.sum(e, axis=0, keepdims=True)
        own_t[cols, rows] = own_features(dot(v[here, cols], e.astype(BF16), ((0,), (0,))))
    grad_t[...] = dot(w_out[...], g[...], ((1,), (1,))).astype(BF16)


def forward_kernel(
    mask, q, low, high, own_t, stats, before, attn_t, mine, other, exps, factors
):
    blocks = q.shape[0] // BLK
    sides = (low, high)
    for b, rows, cols, at in pairs_of(blocks):
        rims = rim_candidates(b, blocks)
        old = stats[0, at : at + 1]
        q2 = two_heads(q[rows, cols] * SCALE, 1)
        scores = [masked(mask, b, c, dot(sides[s][0, :, cols], q2, ((1,), (1,)))) for s, c in rims]
        top = old
        for part in scores:
            top = jnp.maximum(top, jnp.max(part, axis=0, keepdims=True))
        kept = jnp.exp(old - top)
        count = stats[1, at : at + 1] * kept
        both = None
        for (s, _), part in zip(rims, scores):
            e = jnp.exp(part - top)
            exps[s, at % PAIRS] = e
            count = count + jnp.sum(e, axis=0, keepdims=True)
            more = dot(sides[s][1, :, cols], e.astype(BF16), ((0,), (0,)))
            both = more if both is None else both + more
        share = 1.0 / count
        factors[0, at : at + 1] = kept * share
        factors[1, at : at + 1] = share
        attn = own_t[cols, rows] * spread(kept * share)
        if both is not None:
            attn = attn + own_features(both) * spread(share)
        attn_t[cols, rows] = attn.astype(BF16)
    core = at_core()
    chips, rows, _ = mine.shape
    for c in range(2 * chips):
        value = attn_t[c * rows : (c + 1) * rows]

        @pl.when(core == c % 2)
        def _(c=c, value=value):
            mine[c // 2] = value

        @pl.when(core != c % 2)
        def _(c=c, value=value):
            other[c // 2] = value


def flat_dot(attn, g):
    chips, rows, tokens = attn.shape
    return dot(attn[...].reshape(chips * rows, tokens), g[...], ((1,), (0,)))


def product_kernel(mine, g, product):
    product[...] = flat_dot(mine, g)


def backward(probs, delta, k, v, q2, g2_t):
    dprob = dot(v, g2_t, ((1,), (0,)))
    dscore = (probs * (dprob - delta)).astype(BF16)
    query_t = own_features(dot(k, dscore, ((0,), (0,)))) * SCALE
    return query_t, dot(dscore, q2, ((1,), (0,))), dot(probs.astype(BF16), g2_t, ((1,), (1,)))


def rim_kernel(
    q, low, high, grad_t, attn_t, exps, factors, before, to_link, to_chip, deltas, query_t
):
    blocks = q.shape[0] // BLK
    first_core = at_core() == 0
    parts = {}
    for b, rows, cols, at in pairs_of(blocks):
        product = grad_t[cols, rows].astype(F32) * attn_t[cols, rows].astype(F32)
        delta = jnp.concatenate(
            [
                jnp.sum(product[:HD], axis=0, keepdims=True),
                jnp.sum(product[HD:], axis=0, keepdims=True),
            ],
            axis=1,
        )
        deltas[at : at + 1] = delta
        q2 = two_heads(q[rows, cols] * SCALE, 1)
        g2_t = two_heads(grad_t[cols, rows], 0)
        total_t = jnp.zeros((PAIR, BLK), F32)
        for s, _ in rim_candidates(b, blocks):
            rim = (low, high)[s]
            probs = exps[s, at % PAIRS] * factors[1, at : at + 1]
            part_t, k_part, v_part = backward(
                probs, delta, rim[0, :, cols], rim[1, :, cols], q2, g2_t
            )
            total_t = total_t + part_t
            parts[s, at % PAIRS] = (k_part.astype(BF16), v_part.astype(BF16))
            if len(parts) > PAIRS and (1 - s, at % PAIRS) in parts:
                for which in range(2):
                    below = parts[0, at % PAIRS][which]
                    above = parts[1, at % PAIRS][which]
                    to_link[which, :, cols] = jnp.where(first_core, below, above)
                    to_chip[which, :, cols] = jnp.where(first_core, above, below)
        query_t[cols, rows] = total_t


def own_backward_kernel(
    q, k, v, grad_t, exps, factors, deltas, rim_t, before, q_grad, k_own, v_own, after
):
    blocks = q.shape[0] // BLK
    k_own[...] = jnp.zeros_like(k_own)
    v_own[...] = jnp.zeros_like(v_own)
    for b, rows, cols, at in pairs_of(blocks):
        here = own_rows(b, blocks)
        probs = exps[at, : here.stop - here.start] * factors[0, at : at + 1]
        q2 = two_heads(q[rows, cols] * SCALE, 1)
        g2_t = two_heads(grad_t[cols, rows], 0)
        part_t, k_part, v_part = backward(
            probs, deltas[at : at + 1], k[here, cols], v[here, cols], q2, g2_t
        )
        q_grad[rows, cols] = (part_t + rim_t[cols, rows]).T.astype(BF16)
        k_own[here, cols] += k_part
        v_own[here, cols] += v_part
    after[...] = jnp.zeros_like(after)


def output_kernel(attn_t, w_out, before, output):
    output[...] = dot(attn_t[...], w_out[...], ((0,), (0,))).astype(BF16)


def halves_kernel(product, other, g, *outs):
    pieces, after = outs[:-1], outs[-1]
    at_dp = lax.axis_index("dp")
    chips, rows, cols = pieces[0].shape
    both = (product[...] + flat_dot(other, g)).astype(BF16)
    for d in range(len(pieces)):
        value = both[:, d * cols : (d + 1) * cols].reshape(chips, rows, cols)
        for s in range(len(pieces)):

            @pl.when((at_dp ^ s) == d)
            def _(s=s, value=value):
                pieces[s][...] = value

    after[...] = jnp.zeros_like(after)


def chips_kernel(*refs):
    parts, outs = refs[: lax.axis_size("dp")], refs[lax.axis_size("dp") + 1 :]
    chip = lax.div(lax.axis_index("ctx"), 2)
    for s, out in enumerate(outs):
        out[...] = total([part[chip ^ s] for part in parts]).astype(BF16)


def last_kernel(k_own, v_own, from_link, from_chip, *refs):
    pieces, (k_grad, v_grad, weight_grad) = refs[:-3], refs[-3:]
    tokens = k_own.shape[0]
    first_core = at_core() == 0
    for which, (own, grad) in enumerate(((k_own, k_grad), (v_own, v_grad))):
        link = from_link[which].astype(F32)
        chip = from_chip[which].astype(F32)
        low = jnp.where(first_core, link, chip)
        high = jnp.where(first_core, chip, link)
        if tokens == RIM:
            grad[...] = (own[...] + low + high).astype(BF16)
        else:
            grad[:RIM] = (own[:RIM] + low).astype(BF16)
            if tokens > 2 * RIM:
                grad[RIM : tokens - RIM] = own[RIM : tokens - RIM].astype(BF16)
            grad[tokens - RIM :] = (own[tokens - RIM :] + high).astype(BF16)
    at_dp = lax.axis_index("dp")
    cols = pieces[0].shape[1]
    for d in range(len(pieces)):
        value = pieces[0][...]
        for s in range(1, len(pieces)):
            value = jnp.where((at_dp ^ s) == d, pieces[s][...], value)
        weight_grad[:, d * cols : (d + 1) * cols] = value.astype(F32)


def vmem(*shape, dtype=BF16):
    return pltpu.VMEM(shape, dtype)


def hbm(*shape, dtype=BF16):
    return jax.ShapeDtypeStruct(shape, dtype)


def call(kernel, outs, flops, *args, mask=None):
    in_vmem = pl.BlockSpec(memory_space=pltpu.VMEM)
    in_smem = pl.BlockSpec(memory_space=pltpu.SMEM)
    masks = () if mask is None else (mask,)
    return pl.pallas_call(
        kernel,
        out_shape=outs,
        in_specs=[in_smem] * len(masks) + [in_vmem] * len(args),
        out_specs=[in_vmem] * len(outs),
        compiler_params=pltpu.CompilerParams(vmem_limit_bytes=24 * 1024 * 1024),
        cost_estimate=pl.CostEstimate(flops=flops, bytes_accessed=flops // 250, transcendentals=0),
    )(*masks, *args)


def swap(count, bits):
    return [(i, i ^ bits) for i in range(count)]


def over_links(count):
    return [(i, (i - 1 if i % 2 == 0 else i + 1) % count) for i in range(count)]


def total(parts):
    return functools.reduce(jnp.add, [p.astype(F32) for p in parts])


def body(queries, keys, values, out_grad, w_out, block_mask):
    q, k, v, g = queries[0], keys[0], values[0], out_grad[0]
    tokens, feats = q.shape
    width = g.shape[1]
    blocks = tokens // BLK
    ctx, dp = lax.axis_size("ctx"), lax.axis_size("dp")
    chips = ctx // 2
    at_ctx = lax.axis_index("ctx")
    core = at_ctx % 2
    rows, cols = feats // ctx, width // dp
    groups = blocks * PAIRS

    link_row = core * (tokens - RIM)
    chip_row = tokens - RIM - link_row

    def rim(row):
        return jnp.stack([lax.dynamic_slice_in_dim(x, row, RIM, 0) for x in (k, v)])

    from_link = lax.ppermute(rim(link_row), "ctx", over_links(ctx))
    from_chip = lax.ppermute(rim(chip_row), "ctx", swap(ctx, 1))
    sibling_g = lax.ppermute(g, "ctx", swap(ctx, 1))
    sibling_g = pltpu.with_memory_space_constraint(sibling_g, pltpu.VMEM)
    low = jnp.where(core == 0, from_link, from_chip)
    high = jnp.where(core == 0, from_chip, from_link)

    mask = lax.dynamic_slice_in_dim(block_mask[0], at_ctx * blocks, blocks, 0)
    own_t, stats, own_exps, grad_t = call(
        own_kernel,
        [
            vmem(feats, tokens, dtype=F32),
            vmem(2, groups, 2 * BLK, dtype=F32),
            vmem(groups, min(CAND, blocks) * BLK, 2 * BLK, dtype=F32),
            vmem(feats, tokens),
        ],
        10**9,
        q, k, v, g, w_out,
        mask=mask,
    )
    attn_t, mine, other, rim_exps, factors = call(
        forward_kernel,
        [
            vmem(feats, tokens),
            vmem(chips, rows, tokens),
            vmem(chips, rows, tokens),
            vmem(2, PAIRS, RIM, 2 * BLK, dtype=F32),
            vmem(2, groups, 2 * BLK, dtype=F32),
        ],
        10**9,
        q, low, high, own_t, stats, sibling_g,
        mask=mask,
    )

    other = lax.ppermute(other, "ctx", swap(ctx, 1))
    other = pltpu.with_memory_space_constraint(other, pltpu.VMEM)
    (product,) = call(product_kernel, [vmem(chips * rows, width, dtype=F32)], 10**6, mine, g)
    *halves, after = call(
        halves_kernel,
        [vmem(chips, rows, cols)] * dp + [vmem(8, 128, dtype=F32)],
        10**6,
        product, other, sibling_g,
    )
    to_link, to_chip, deltas, rim_t = call(
        rim_kernel,
        [
            vmem(2, RIM, feats),
            vmem(2, RIM, feats),
            vmem(groups, 2 * BLK, dtype=F32),
            vmem(feats, tokens, dtype=F32),
        ],
        10**6,
        q, low, high, grad_t, attn_t, rim_exps, factors, after,
    )
    grad_link = lax.ppermute(to_link, "ctx", over_links(ctx))
    grad_chip = lax.ppermute(to_chip, "ctx", swap(ctx, 1))

    q_grad, k_own, v_own, after = call(
        own_backward_kernel,
        [
            hbm(tokens, feats),
            vmem(tokens, feats, dtype=F32),
            vmem(tokens, feats, dtype=F32),
            vmem(8, 128, dtype=F32),
        ],
        10**6,
        q, k, v, grad_t, own_exps, factors, deltas, rim_t, after,
    )

    halves = [halves[0]] + [lax.ppermute(halves[s], "dp", swap(dp, s)) for s in range(dp - 1, 0, -1)]
    quarters = call(chips_kernel, [vmem(rows, cols)] * chips, 10**6, *halves, after)
    (output,) = call(output_kernel, [hbm(tokens, width)], 10**6, attn_t, w_out, quarters[0])
    piece = total(
        [quarters[0]]
        + [lax.ppermute(quarters[s], "ctx", swap(ctx, 2 * s)) for s in range(chips - 1, 0, -1)]
    )
    piece = (piece * (dp * tokens * ctx) ** (-0.5)).astype(BF16)
    pieces = [piece] + [lax.ppermute(piece, "dp", swap(dp, s)) for s in range(1, dp)]
    k_grad, v_grad, weight_grad = call(
        last_kernel,
        [hbm(tokens, feats), hbm(tokens, feats), hbm(rows, width, dtype=F32)],
        10**6,
        k_own, v_own, grad_link, grad_chip, *pieces,
    )
    return (output[None], q_grad[None], k_grad[None], v_grad[None], weight_grad)


def solution(mesh):
    rows = P("dp", "ctx", None)
    return jax.shard_map(
        body,
        mesh=mesh,
        in_specs=(rows, rows, rows, rows, P(), P("dp", None, None)),
        out_specs=(rows, rows, rows, rows, P("ctx", None)),
        check_vma=False,
    )
```

```python
import functools

import jax
import jax.numpy as jnp
from jax import lax
from jax.experimental import pallas as pl
from jax.experimental.pallas import tpu as pltpu
from jax.sharding import PartitionSpec as P

HEADS = 8
HD = 64
BLK = 128
RAD = 1
CAND = 2 * RAD + 1
PAIRS = HEADS // 2
PAIR = 2 * HD
RIM = RAD * BLK
BIG_NEGATIVE = -1e30
SCALE = HD ** (-0.5)
BF16 = jnp.bfloat16
F32 = jnp.float32


def dot(a, b, contract):
    return lax.dot_general(a, b, (contract, ((), ())), preferred_element_type=F32)


def two_heads(block, axis):
    feature = lax.broadcasted_iota(jnp.int32, block.shape, axis)
    zero = jnp.zeros_like(block)
    return jnp.concatenate(
        [jnp.where(feature < HD, block, zero), jnp.where(feature < HD, zero, block)], axis=1 - axis
    )


def own_features(both):
    return jnp.concatenate([both[:HD, :BLK], both[HD:, BLK:]], axis=0)


def spread(row):
    return jnp.concatenate(
        [
            jnp.broadcast_to(row[:, :BLK], (HD, BLK)),
            jnp.broadcast_to(row[:, BLK:], (HD, BLK)),
        ],
        axis=0,
    )


def own_candidates(b, blocks):
    return max(0, RAD - b), min(CAND - 1, blocks - 1 - b + RAD)


def own_rows(b, blocks):
    first, last = own_candidates(b, blocks)
    return slice((b + first - RAD) * BLK, (b + last - RAD + 1) * BLK)


def masked(mask, b, c, part):
    return part if c == RAD else jnp.where(mask[b, c] == 1, part, BIG_NEGATIVE)


def pairs_of(blocks):
    for b in range(blocks):
        for p in range(PAIRS):
            yield b, slice(b * BLK, (b + 1) * BLK), slice(p * PAIR, (p + 1) * PAIR), p


def at_core():
    return lax.rem(lax.axis_index("ctx"), 2)


def rim_block(blocks, over_link):
    core = at_core()
    upper = core if over_link else 1 - core
    return upper * (blocks - 1), upper * (CAND - 1)


def rows_of(b):
    return pl.ds(pl.multiple_of(b * BLK, BLK), BLK)


def copy_all(pairs, sems):
    copies = [pltpu.make_async_copy(a, b, sems.at[i]) for i, (a, b) in enumerate(pairs)]
    for copy in copies:
        copy.start()
    for copy in copies:
        copy.wait()


def pack_link_kernel(k, v, out, sems):
    rows = rows_of(rim_block(k.shape[0] // BLK, True)[0])
    copy_all([(k.at[rows], out.at[0]), (v.at[rows], out.at[1])], sems)


def pack_chip_kernel(k, v, k_out, v_out, sems):
    rows = rows_of(rim_block(k.shape[0] // BLK, False)[0])
    copy_all([(k.at[rows], k_out), (v.at[rows], v_out)], sems)


def load_kernel(*refs):
    count = len(refs) // 2
    copy_all(list(zip(refs[:count], refs[count:-1])), refs[-1])


def own_kernel(mask, q, k, v, g, w_out, own_t, stats, exps, grad_t):
    blocks = q.shape[0] // BLK
    for b, rows, cols, p in pairs_of(blocks):
        first, last = own_candidates(b, blocks)
        here = own_rows(b, blocks)
        scores = dot(k[here, cols], two_heads(q[rows, cols] * SCALE, 1), ((1,), (1,)))
        scores = jnp.concatenate(
            [
                masked(mask, b, c, scores[(c - first) * BLK : (c - first + 1) * BLK])
                for c in range(first, last + 1)
            ],
            axis=0,
        )
        top = jnp.max(scores, axis=0, keepdims=True)
        e = jnp.exp(scores - top)
        exps[b, p, : e.shape[0]] = e
        stats[0, b, p : p + 1] = top
        stats[1, b, p : p + 1] = jnp.sum(e, axis=0, keepdims=True)
        own_t[b, cols] = own_features(dot(v[here, cols], e.astype(BF16), ((0,), (0,))))
    for b in range(blocks):
        rows = slice(b * BLK, (b + 1) * BLK)
        grad_t[b] = dot(w_out[...], g[rows], ((1,), (1,))).astype(BF16)


def with_rim(mask, q, rim_k, rim_v, b, c, p, old_top, old_sum):
    cols = slice(p * PAIR, (p + 1) * PAIR)
    scores = dot(rim_k[:, cols], two_heads(q[rows_of(b), cols] * SCALE, 1), ((1,), (1,)))
    scores = jnp.where(mask[b, c] == 1, scores, BIG_NEGATIVE)
    top = jnp.maximum(old_top, jnp.max(scores, axis=0, keepdims=True))
    kept = jnp.exp(old_top - top)
    e = jnp.exp(scores - top)
    count = old_sum * kept + jnp.sum(e, axis=0, keepdims=True)
    part = own_features(dot(rim_v[:, cols], e.astype(BF16), ((0,), (0,))))
    return top, kept, count, e, part


def chip_kernel(mask, q, rim_k, rim_v, own_t, stats, chip_t, chip_stats, exps):
    b, c = rim_block(q.shape[0] // BLK, False)
    for p in range(PAIRS):
        cols = slice(p * PAIR, (p + 1) * PAIR)
        top, kept, count, e, part = with_rim(
            mask, q, rim_k, rim_v, b, c, p, stats[0, b, p : p + 1], stats[1, b, p : p + 1]
        )
        chip_t[cols] = own_t[b, cols] * spread(kept) + part
        chip_stats[0, p : p + 1] = top
        chip_stats[1, p : p + 1] = count
        exps[p] = e


def forward_kernel(
    mask, q, rim, own_t, stats, chip_t, chip_stats,
    attn_t, mine, other, exps, own_factors, rim_factors,
):
    blocks = q.shape[0] // BLK
    b, c = rim_block(blocks, True)
    at_chip, _ = rim_block(blocks, False)
    for p in range(PAIRS):
        at = slice(p, p + 1)
        cols = slice(p * PAIR, (p + 1) * PAIR)
        if blocks == 1:
            base, old_top, old_sum = chip_t[cols], chip_stats[0, at], chip_stats[1, at]
        else:
            base, old_top, old_sum = own_t[b, cols], stats[0, b, at], stats[1, b, at]
        top, kept, count, e, part = with_rim(
            mask, q, rim.at[0], rim.at[1], b, c, p, old_top, old_sum
        )
        share = 1.0 / count
        attn_t[b, cols] = (base * spread(kept * share) + part * spread(share)).astype(BF16)
        exps[p] = e
        rim_factors[0, at] = share
        if blocks == 1:
            rim_factors[1, at] = kept * share
            own_factors[0, at] = jnp.exp(stats[0, 0, at] - top) * share
        else:
            own_factors[b, at] = kept * share
            share = 1.0 / chip_stats[1, at]
            attn_t[at_chip, cols] = (chip_t[cols] * spread(share)).astype(BF16)
            rim_factors[1, at] = share
            own_factors[at_chip, at] = jnp.exp(stats[0, at_chip, at] - chip_stats[0, at]) * share
        for inner in range(1, blocks - 1):
            share = 1.0 / stats[1, inner, at]
            attn_t[inner, cols] = (own_t[inner, cols] * spread(share)).astype(BF16)
            own_factors[inner, at] = share
    core = at_core()
    chips, rows, _ = mine.shape
    for c in range(2 * chips):
        for i in range(blocks):
            value = attn_t[i, c * rows : (c + 1) * rows]
            tokens = slice(i * BLK, (i + 1) * BLK)

            @pl.when(core == c % 2)
            def _(c=c, value=value, tokens=tokens):
                mine[c // 2, :, tokens] = value

            @pl.when(core != c % 2)
            def _(c=c, value=value, tokens=tokens):
                other[c // 2, :, tokens] = value


def flat_dot(attn, g):
    chips, rows, tokens = attn.shape
    return dot(attn[...].reshape(chips * rows, tokens), g[...], ((1,), (0,)))


def product_kernel(mine, g, product):
    product[...] = flat_dot(mine, g)


def backward(probs, delta, k, v, q2, g2_t):
    dprob = dot(v, g2_t, ((1,), (0,)))
    dscore = (probs * (dprob - delta)).astype(BF16)
    query_t = own_features(dot(k, dscore, ((0,), (0,)))) * SCALE
    return query_t, dot(dscore, q2, ((1,), (0,))), dot(probs.astype(BF16), g2_t, ((1,), (1,)))


def rim_kernel(
    q, link, chip_k, chip_v, grad_t, attn_t, link_exps, chip_exps, rim_factors, before,
    to_link, to_chip, deltas, query_t,
):
    blocks = q.shape[0] // BLK
    for b, _, cols, p in pairs_of(blocks):
        product = grad_t[b, cols].astype(F32) * attn_t[b, cols].astype(F32)
        deltas[b, p : p + 1] = jnp.concatenate(
            [
                jnp.sum(product[:HD], axis=0, keepdims=True),
                jnp.sum(product[HD:], axis=0, keepdims=True),
            ],
            axis=1,
        )
    query_t[...] = jnp.zeros_like(query_t)
    link_side = (link.at[0], link.at[1], link_exps, to_link)
    for i, (rim_k, rim_v, exps, back) in enumerate(
        (link_side, (chip_k, chip_v, chip_exps, to_chip))
    ):
        b, _ = rim_block(blocks, i == 0)
        for p in range(PAIRS):
            cols = slice(p * PAIR, (p + 1) * PAIR)
            part_t, k_part, v_part = backward(
                exps[p] * rim_factors[i, p : p + 1],
                deltas[b, p : p + 1],
                rim_k[:, cols],
                rim_v[:, cols],
                two_heads(q[rows_of(b), cols] * SCALE, 1),
                two_heads(grad_t[b, cols], 0),
            )
            query_t[b, cols] += part_t
            back[0, :, cols] = k_part.astype(BF16)
            back[1, :, cols] = v_part.astype(BF16)


def own_backward_kernel(
    q, k, v, grad_t, exps, factors, deltas, rim_t, before, q_grad, k_own, v_own, after
):
    blocks = q.shape[0] // BLK
    k_own[...] = jnp.zeros_like(k_own)
    v_own[...] = jnp.zeros_like(v_own)
    for b, rows, cols, p in pairs_of(blocks):
        here = own_rows(b, blocks)
        part_t, k_part, v_part = backward(
            exps[b, p, : here.stop - here.start] * factors[b, p : p + 1],
            deltas[b, p : p + 1],
            k[here, cols],
            v[here, cols],
            two_heads(q[rows, cols] * SCALE, 1),
            two_heads(grad_t[b, cols], 0),
        )
        q_grad[rows, cols] = (part_t + rim_t[b, cols]).T.astype(BF16)
        k_own[here, cols] += k_part
        v_own[here, cols] += v_part
    after[...] = jnp.zeros_like(after)


def output_kernel(attn_t, w_out, before, output):
    for b in range(attn_t.shape[0]):
        part = dot(attn_t[b], w_out[...], ((0,), (0,)))
        output[b * BLK : (b + 1) * BLK] = part.astype(BF16)


def halves_kernel(product, other, g, *outs):
    pieces, after = outs[:-1], outs[-1]
    at_dp = lax.axis_index("dp")
    chips, rows, cols = pieces[0].shape
    both = (product[...] + flat_dot(other, g)).astype(BF16)
    for d in range(len(pieces)):
        value = both[:, d * cols : (d + 1) * cols].reshape(chips, rows, cols)
        for s in range(len(pieces)):

            @pl.when((at_dp ^ s) == d)
            def _(s=s, value=value):
                pieces[s][...] = value

    after[...] = jnp.zeros_like(after)


def chips_kernel(*refs):
    parts, outs = refs[: lax.axis_size("dp")], refs[lax.axis_size("dp") + 1 :]
    chip = lax.div(lax.axis_index("ctx"), 2)
    for s, out in enumerate(outs):
        out[...] = total([part[chip ^ s] for part in parts]).astype(BF16)


def last_kernel(k_own, v_own, from_link, from_chip, *refs):
    pieces, (k_grad, v_grad, weight_grad) = refs[:1] + refs[-4:0:-1], refs[-3:]
    tokens = k_own.shape[0]
    first_core = at_core() == 0
    for which, (own, grad) in enumerate(((k_own, k_grad), (v_own, v_grad))):
        link = from_link[which].astype(F32)
        chip = from_chip[which].astype(F32)
        low = jnp.where(first_core, link, chip)
        high = jnp.where(first_core, chip, link)
        if tokens == RIM:
            grad[...] = (own[...] + low + high).astype(BF16)
        else:
            grad[:RIM] = (own[:RIM] + low).astype(BF16)
            if tokens > 2 * RIM:
                grad[RIM : tokens - RIM] = own[RIM : tokens - RIM].astype(BF16)
            grad[tokens - RIM :] = (own[tokens - RIM :] + high).astype(BF16)
    at_dp = lax.axis_index("dp")
    cols = pieces[0].shape[1]
    for d in range(len(pieces)):
        value = pieces[0][...]
        for s in range(1, len(pieces)):
            value = jnp.where((at_dp ^ s) == d, pieces[s][...], value)
        weight_grad[:, d * cols : (d + 1) * cols] = value.astype(F32)


def vmem(*shape, dtype=BF16):
    return pltpu.VMEM(shape, dtype)


def hbm(*shape, dtype=BF16):
    return jax.ShapeDtypeStruct(shape, dtype)


def call(kernel, outs, flops, *args, mask=None):
    in_vmem = pl.BlockSpec(memory_space=pltpu.VMEM)
    in_smem = pl.BlockSpec(memory_space=pltpu.SMEM)
    masks = () if mask is None else (mask,)
    return pl.pallas_call(
        kernel,
        out_shape=outs,
        in_specs=[in_smem] * len(masks) + [in_vmem] * len(args),
        out_specs=[in_vmem] * len(outs),
        compiler_params=pltpu.CompilerParams(vmem_limit_bytes=24 * 1024 * 1024),
        cost_estimate=pl.CostEstimate(flops=flops, bytes_accessed=flops // 250, transcendentals=0),
    )(*masks, *args)


def from_hbm(kernel, outs, *args):
    return pl.pallas_call(
        kernel,
        out_shape=outs,
        in_specs=[pl.BlockSpec(memory_space=pltpu.HBM)] * len(args),
        out_specs=[pl.BlockSpec(memory_space=pltpu.VMEM)] * len(outs),
        scratch_shapes=[pltpu.SemaphoreType.DMA((len(args),))],
        compiler_params=pltpu.CompilerParams(vmem_limit_bytes=1024 * 1024),
        cost_estimate=pl.CostEstimate(flops=0, bytes_accessed=4096, transcendentals=0),
    )(*(pltpu.with_memory_space_constraint(x, pltpu.HBM) for x in args))


def swap(count, bits):
    return [(i, i ^ bits) for i in range(count)]


def over_links(count):
    return [(i, (i - 1 if i % 2 == 0 else i + 1) % count) for i in range(count)]


def total(parts):
    return functools.reduce(jnp.add, [p.astype(F32) for p in parts])


def body(queries, keys, values, out_grad, w_out, block_mask):
    q, k, v, g = queries[0], keys[0], values[0], out_grad[0]
    tokens, feats = q.shape
    width = g.shape[1]
    blocks = tokens // BLK
    ctx, dp = lax.axis_size("ctx"), lax.axis_size("dp")
    chips = ctx // 2
    at_ctx = lax.axis_index("ctx")
    rows, cols = feats // ctx, width // dp

    (to_link,) = from_hbm(pack_link_kernel, [vmem(2, RIM, feats)], k, v)
    link = lax.ppermute(to_link, "ctx", over_links(ctx))
    to_chip = from_hbm(pack_chip_kernel, [vmem(RIM, feats)] * 2, k, v)
    chip_k, chip_v = (lax.ppermute(x, "ctx", swap(ctx, 1)) for x in to_chip)
    sibling_g = lax.ppermute(g, "ctx", swap(ctx, 1))
    sibling_g = pltpu.with_memory_space_constraint(sibling_g, pltpu.VMEM)
    args = (q, k, v, g, w_out)
    q, k, v, g, w_out = from_hbm(load_kernel, [vmem(*x.shape) for x in args], *args)

    mask = lax.dynamic_slice_in_dim(block_mask[0], at_ctx * blocks, blocks, 0)
    own_t, stats, own_exps, grad_t = call(
        own_kernel,
        [
            vmem(blocks, feats, BLK, dtype=F32),
            vmem(2, blocks, PAIRS, 2 * BLK, dtype=F32),
            vmem(blocks, PAIRS, min(CAND, blocks) * BLK, 2 * BLK, dtype=F32),
            vmem(blocks, feats, BLK),
        ],
        10**6,
        q, k, v, g, w_out,
        mask=mask,
    )
    chip_t, chip_stats, chip_exps = call(
        chip_kernel,
        [
            vmem(feats, BLK, dtype=F32),
            vmem(2, PAIRS, 2 * BLK, dtype=F32),
            vmem(PAIRS, RIM, 2 * BLK, dtype=F32),
        ],
        10**6,
        q, chip_k, chip_v, own_t, stats,
        mask=mask,
    )
    attn_t, mine, other, link_exps, own_factors, rim_factors = call(
        forward_kernel,
        [
            vmem(blocks, feats, BLK),
            vmem(chips, rows, tokens),
            vmem(chips, rows, tokens),
            vmem(PAIRS, RIM, 2 * BLK, dtype=F32),
            vmem(blocks, PAIRS, 2 * BLK, dtype=F32),
            vmem(2, PAIRS, 2 * BLK, dtype=F32),
        ],
        10**6,
        q, link, own_t, stats, chip_t, chip_stats,
        mask=mask,
    )

    other = lax.ppermute(other, "ctx", swap(ctx, 1))
    other = pltpu.with_memory_space_constraint(other, pltpu.VMEM)
    (product,) = call(product_kernel, [vmem(chips * rows, width, dtype=F32)], 10**6, mine, g)
    *halves, after = call(
        halves_kernel,
        [vmem(chips, rows, cols)] * dp + [vmem(8, 128, dtype=F32)],
        10**6,
        product, other, sibling_g,
    )
    to_link, to_chip, deltas, rim_t = call(
        rim_kernel,
        [
            vmem(2, RIM, feats),
            vmem(2, RIM, feats),
            vmem(blocks, PAIRS, 2 * BLK, dtype=F32),
            vmem(blocks, feats, BLK, dtype=F32),
        ],
        10**6,
        q, link, chip_k, chip_v, grad_t, attn_t, link_exps, chip_exps, rim_factors, after,
    )
    grad_link = lax.ppermute(to_link, "ctx", over_links(ctx))
    grad_chip = lax.ppermute(to_chip, "ctx", swap(ctx, 1))

    q_grad, k_own, v_own, after = call(
        own_backward_kernel,
        [
            hbm(tokens, feats),
            vmem(tokens, feats, dtype=F32),
            vmem(tokens, feats, dtype=F32),
            vmem(8, 128, dtype=F32),
        ],
        10**6,
        q, k, v, grad_t, own_exps, own_factors, deltas, rim_t, after,
    )

    halves = [halves[0]] + [lax.ppermute(halves[s], "dp", swap(dp, s)) for s in range(dp - 1, 0, -1)]
    quarters = call(chips_kernel, [vmem(rows, cols)] * chips, 10**6, *halves, after)
    (output,) = call(output_kernel, [hbm(tokens, width)], 10**6, attn_t, w_out, quarters[0])
    piece = total(
        [quarters[0]]
        + [lax.ppermute(quarters[s], "ctx", swap(ctx, 2 * s)) for s in range(chips - 1, 0, -1)]
    )
    piece = (piece * (dp * tokens * ctx) ** (-0.5)).astype(BF16)
    pieces = [piece] + [lax.ppermute(piece, "dp", swap(dp, s)) for s in range(dp - 1, 0, -1)]
    k_grad, v_grad, weight_grad = call(
        last_kernel,
        [hbm(tokens, feats), hbm(tokens, feats), hbm(rows, width, dtype=F32)],
        10**6,
        k_own, v_own, grad_link, grad_chip, *pieces,
    )
    return (output[None], q_grad[None], k_grad[None], v_grad[None], weight_grad)


def solution(mesh):
    rows = P("dp", "ctx", None)
    return jax.shard_map(
        body,
        mesh=mesh,
        in_specs=(rows, rows, rows, rows, P(), P("dp", None, None)),
        out_specs=(rows, rows, rows, rows, P("ctx", None)),
        check_vma=False,
    )
```

```python
import functools

import jax
import jax.numpy as jnp
from jax import lax
from jax.experimental import pallas as pl
from jax.experimental.pallas import tpu as pltpu
from jax.sharding import PartitionSpec as P

HEADS = 8
HD = 64
BLK = 128
RAD = 1
CAND = 2 * RAD + 1
PAIRS = HEADS // 2
PAIR = 2 * HD
RIM = RAD * BLK
BIG_NEGATIVE = -1e30
SCALE = HD ** (-0.5)
BF16 = jnp.bfloat16
F32 = jnp.float32


def dot(a, b, contract):
    return lax.dot_general(a, b, (contract, ((), ())), preferred_element_type=F32)


def two_heads(block, axis):
    feature = lax.broadcasted_iota(jnp.int32, block.shape, axis)
    zero = jnp.zeros_like(block)
    return jnp.concatenate(
        [jnp.where(feature < HD, block, zero), jnp.where(feature < HD, zero, block)], axis=1 - axis
    )


def own_features(both):
    return jnp.concatenate([both[:HD, :BLK], both[HD:, BLK:]], axis=0)


def spread(row):
    return jnp.concatenate(
        [
            jnp.broadcast_to(row[:, :BLK], (HD, BLK)),
            jnp.broadcast_to(row[:, BLK:], (HD, BLK)),
        ],
        axis=0,
    )


def own_candidates(b, blocks):
    return max(0, RAD - b), min(CAND - 1, blocks - 1 - b + RAD)


def own_rows(b, blocks):
    first, last = own_candidates(b, blocks)
    return slice((b + first - RAD) * BLK, (b + last - RAD + 1) * BLK)


def masked(mask, b, c, part):
    return part if c == RAD else jnp.where(mask[b, c] == 1, part, BIG_NEGATIVE)


def pairs_of(blocks):
    for b in range(blocks):
        for p in range(PAIRS):
            yield b, slice(b * BLK, (b + 1) * BLK), slice(p * PAIR, (p + 1) * PAIR), p


def at_core():
    return lax.rem(lax.axis_index("ctx"), 2)


def rim_block(blocks, over_link):
    core = at_core()
    upper = core if over_link else 1 - core
    return upper * (blocks - 1), upper * (CAND - 1)


def rows_of(b):
    return pl.ds(pl.multiple_of(b * BLK, BLK), BLK)


def pack_kernel(k, v, to_link, chip_k, chip_v, sems):
    blocks = k.shape[0] // BLK
    link_rows = rows_of(rim_block(blocks, True)[0])
    chip_rows = rows_of(rim_block(blocks, False)[0])
    pairs = (
        (k.at[link_rows], to_link.at[0]),
        (v.at[link_rows], to_link.at[1]),
        (k.at[chip_rows], chip_k),
        (v.at[chip_rows], chip_v),
    )
    copies = [pltpu.make_async_copy(x, y, sems.at[i]) for i, (x, y) in enumerate(pairs)]
    for copy in copies:
        copy.start()
    for copy in copies:
        copy.wait()


def own_kernel(
    mask, q_arg, k_arg, v_arg, g_arg, w_arg,
    q, k, v, g, w_out, own_t, stats, exps, grad_t, rounded, sems,
):
    pairs = ((q_arg, q), (k_arg, k), (v_arg, v), (g_arg, g), (w_arg, w_out))
    copies = [pltpu.make_async_copy(x, y, sems.at[i]) for i, (x, y) in enumerate(pairs)]
    for copy in copies:
        copy.start()
    copies[0].wait()
    copies[1].wait()
    blocks = q.shape[0] // BLK
    for b, rows, cols, p in pairs_of(blocks):
        first, last = own_candidates(b, blocks)
        here = own_rows(b, blocks)
        scores = dot(k[here, cols], two_heads(q[rows, cols] * SCALE, 1), ((1,), (1,)))
        for c in range(first, last + 1):
            part = slice((c - first) * BLK, (c - first + 1) * BLK)
            exps[b, p, part] = masked(mask, b, c, scores[part])
    for b, rows, cols, p in pairs_of(blocks):
        here = own_rows(b, blocks)
        keys = slice(0, here.stop - here.start)
        scores = exps[b, p, keys]
        top = jnp.max(scores, axis=0, keepdims=True)
        e = jnp.exp(scores - top)
        exps[b, p, keys] = e
        rounded[b, p, keys] = e.astype(BF16)
        stats[0, b, p : p + 1] = top
        stats[1, b, p : p + 1] = jnp.sum(e, axis=0, keepdims=True)
    copies[2].wait()
    for b, rows, cols, p in pairs_of(blocks):
        here = own_rows(b, blocks)
        e = rounded[b, p, : here.stop - here.start]
        own_t[b, cols] = own_features(dot(v[here, cols], e, ((0,), (0,))))
    copies[3].wait()
    copies[4].wait()
    for b in range(blocks):
        rows = slice(b * BLK, (b + 1) * BLK)
        grad_t[b] = dot(w_out[...], g[rows], ((1,), (1,))).astype(BF16)


def pair_cols(p):
    return slice(p * PAIR, (p + 1) * PAIR)


def with_rim(mask, q, rim_k, rim_v, b, c, old, exps, rounded):
    for p in range(PAIRS):
        q2 = two_heads(q[rows_of(b), pair_cols(p)] * SCALE, 1)
        scores = dot(rim_k[:, pair_cols(p)], q2, ((1,), (1,)))
        exps[p] = jnp.where(mask[b, c] == 1, scores, BIG_NEGATIVE)
    results = []
    for p in range(PAIRS):
        old_top, old_sum = old(p)
        scores = exps[p]
        top = jnp.maximum(old_top, jnp.max(scores, axis=0, keepdims=True))
        kept = jnp.exp(old_top - top)
        e = jnp.exp(scores - top)
        exps[p] = e
        rounded[p] = e.astype(BF16)
        results.append((top, kept, old_sum * kept + jnp.sum(e, axis=0, keepdims=True)))
    parts = [
        own_features(dot(rim_v[:, pair_cols(p)], rounded[p], ((0,), (0,)))) for p in range(PAIRS)
    ]
    return [(*result, part) for result, part in zip(results, parts)]


def chip_kernel(mask, q, rim_k, rim_v, own_t, stats, chip_t, chip_stats, exps, rounded):
    b, c = rim_block(q.shape[0] // BLK, False)

    def old(p):
        return stats[0, b, p : p + 1], stats[1, b, p : p + 1]

    results = with_rim(mask, q, rim_k, rim_v, b, c, old, exps, rounded)
    for p, (top, kept, count, part) in enumerate(results):
        chip_t[pair_cols(p)] = own_t[b, pair_cols(p)] * spread(kept) + part
        chip_stats[0, p : p + 1] = top
        chip_stats[1, p : p + 1] = count


def forward_kernel(
    mask, q, rim, own_t, stats, chip_t, chip_stats,
    attn_t, mine, other, exps, own_factors, rim_factors, rounded,
):
    blocks = q.shape[0] // BLK
    b, c = rim_block(blocks, True)
    at_chip, _ = rim_block(blocks, False)

    def old(p):
        at = slice(p, p + 1)
        if blocks == 1:
            return chip_stats[0, at], chip_stats[1, at]
        return stats[0, b, at], stats[1, b, at]

    results = with_rim(mask, q, rim.at[0], rim.at[1], b, c, old, exps, rounded)
    for p, (top, kept, count, part) in enumerate(results):
        at = slice(p, p + 1)
        cols = pair_cols(p)
        base = chip_t[cols] if blocks == 1 else own_t[b, cols]
        share = 1.0 / count
        attn_t[b, cols] = (base * spread(kept * share) + part * spread(share)).astype(BF16)
        rim_factors[0, at] = share
        if blocks == 1:
            rim_factors[1, at] = kept * share
            own_factors[0, at] = jnp.exp(stats[0, 0, at] - top) * share
        else:
            own_factors[b, at] = kept * share
            share = 1.0 / chip_stats[1, at]
            attn_t[at_chip, cols] = (chip_t[cols] * spread(share)).astype(BF16)
            rim_factors[1, at] = share
            own_factors[at_chip, at] = jnp.exp(stats[0, at_chip, at] - chip_stats[0, at]) * share
        for inner in range(1, blocks - 1):
            share = 1.0 / stats[1, inner, at]
            attn_t[inner, cols] = (own_t[inner, cols] * spread(share)).astype(BF16)
            own_factors[inner, at] = share
    first_core = at_core() == 0
    chips, rows, _ = mine.shape
    for i in range(chips):
        for block in range(blocks):
            tokens = slice(block * BLK, (block + 1) * BLK)
            even = attn_t[block, 2 * i * rows : (2 * i + 1) * rows]
            odd = attn_t[block, (2 * i + 1) * rows : (2 * i + 2) * rows]
            mine[i, :, tokens] = jnp.where(first_core, even, odd)
            other[i, :, tokens] = jnp.where(first_core, odd, even)


def flat_dot(attn, g):
    chips, rows, tokens = attn.shape
    return dot(attn[...].reshape(chips * rows, tokens), g[...], ((1,), (0,)))


def product_kernel(mine, g, product):
    product[...] = flat_dot(mine, g)


def score_grads(probs, dprob, delta):
    return (probs * (dprob - delta)).astype(BF16), probs.astype(BF16)


def rim_kernel(
    q, link, chip_k, chip_v, grad_t, attn_t, link_exps, chip_exps, rim_factors, before,
    to_link, to_chip, deltas, query_t, dprobs, dscores, rounded,
):
    blocks = q.shape[0] // BLK
    sides = (
        (rim_block(blocks, True)[0], link.at[0], link.at[1], link_exps, to_link),
        (rim_block(blocks, False)[0], chip_k, chip_v, chip_exps, to_chip),
    )
    for i, (b, _, rim_v, _, _) in enumerate(sides):
        for p in range(PAIRS):
            g2_t = two_heads(grad_t[b, pair_cols(p)], 0)
            dprobs[i, p] = dot(rim_v[:, pair_cols(p)], g2_t, ((1,), (0,)))
    for b, _, cols, p in pairs_of(blocks):
        product = grad_t[b, cols].astype(F32) * attn_t[b, cols].astype(F32)
        deltas[b, p : p + 1] = jnp.concatenate(
            [
                jnp.sum(product[:HD], axis=0, keepdims=True),
                jnp.sum(product[HD:], axis=0, keepdims=True),
            ],
            axis=1,
        )
    query_t[...] = jnp.zeros_like(query_t)
    for i, (b, _, _, exps, _) in enumerate(sides):
        for p in range(PAIRS):
            at = slice(p, p + 1)
            dscores[i, p], rounded[i, p] = score_grads(
                exps[p] * rim_factors[i, at], dprobs[i, p], deltas[b, at]
            )
    for i, (b, rim_k, _, _, back) in enumerate(sides):
        for p in range(PAIRS):
            cols = pair_cols(p)
            q2 = two_heads(q[rows_of(b), cols] * SCALE, 1)
            g2_t = two_heads(grad_t[b, cols], 0)
            back[0, :, cols] = dot(dscores[i, p], q2, ((1,), (0,))).astype(BF16)
            back[1, :, cols] = dot(rounded[i, p], g2_t, ((1,), (1,))).astype(BF16)
            query_t[b, cols] += own_features(dot(rim_k[:, cols], dscores[i, p], ((0,), (0,))))


def own_backward_kernel(
    q, k, v, grad_t, exps, factors, deltas, rim_t, before,
    q_grad, k_own, v_own, after, dprobs, dscores, rounded,
):
    blocks = q.shape[0] // BLK
    for b, _, cols, p in pairs_of(blocks):
        here = own_rows(b, blocks)
        g2_t = two_heads(grad_t[b, cols], 0)
        dprobs[b, p, : here.stop - here.start] = dot(v[here, cols], g2_t, ((1,), (0,)))
    for b, _, _, p in pairs_of(blocks):
        here = own_rows(b, blocks)
        keys = slice(0, here.stop - here.start)
        dscores[b, p, keys], rounded[b, p, keys] = score_grads(
            exps[b, p, keys] * factors[b, p : p + 1], dprobs[b, p, keys], deltas[b, p : p + 1]
        )
    k_sums, v_sums = {}, {}
    for b, rows, cols, p in pairs_of(blocks):
        here = own_rows(b, blocks)
        keys = slice(0, here.stop - here.start)
        q2 = two_heads(q[rows, cols] * SCALE, 1)
        g2_t = two_heads(grad_t[b, cols], 0)
        dscore = dscores[b, p, keys]
        k_part = dot(dscore, q2, ((1,), (0,)))
        v_part = dot(rounded[b, p, keys], g2_t, ((1,), (1,)))
        for at in range(here.start, here.stop, BLK):
            part = slice(at - here.start, at - here.start + BLK)
            for sums, value in ((k_sums, k_part), (v_sums, v_part)):
                sums.setdefault((at, p), []).append(value[part])
        query_t = own_features(dot(k[here, cols], dscore, ((0,), (0,)))) + rim_t[b, cols]
        q_grad[rows, cols] = (query_t * SCALE).T.astype(BF16)
    for out, sums in ((k_own, k_sums), (v_own, v_sums)):
        for (at, p), values in sums.items():
            out[at : at + BLK, pair_cols(p)] = functools.reduce(jnp.add, values)
    after[...] = jnp.zeros_like(after)


def output_kernel(attn_t, w_out, before, output):
    for b in range(attn_t.shape[0]):
        part = dot(attn_t[b], w_out[...], ((0,), (0,)))
        output[b * BLK : (b + 1) * BLK] = part.astype(BF16)


def halves_kernel(product, other, g, *outs):
    pieces, after = outs[:-1], outs[-1]
    at_dp = lax.axis_index("dp")
    chips, rows, cols = pieces[0].shape
    both = (product[...] + flat_dot(other, g)).astype(BF16)
    for d in range(len(pieces)):
        value = both[:, d * cols : (d + 1) * cols].reshape(chips, rows, cols)
        for s in range(len(pieces)):

            @pl.when((at_dp ^ s) == d)
            def _(s=s, value=value):
                pieces[s][...] = value

    after[...] = jnp.zeros_like(after)


def chips_kernel(*refs):
    parts, outs = refs[: lax.axis_size("dp")], refs[lax.axis_size("dp") + 1 :]
    chip = lax.div(lax.axis_index("ctx"), 2)
    for s, out in enumerate(outs):
        out[...] = total([part[chip ^ s] for part in parts]).astype(BF16)


def last_kernel(k_own, v_own, from_link, from_chip, *refs):
    pieces, (k_grad, v_grad, weight_grad) = refs[:1] + refs[-4:0:-1], refs[-3:]
    tokens = k_own.shape[0]
    first_core = at_core() == 0
    for which, (own, grad) in enumerate(((k_own, k_grad), (v_own, v_grad))):
        link = from_link[which].astype(F32)
        chip = from_chip[which].astype(F32)
        low = jnp.where(first_core, link, chip)
        high = jnp.where(first_core, chip, link)
        if tokens == RIM:
            grad[...] = (own[...] + low + high).astype(BF16)
        else:
            grad[:RIM] = (own[:RIM] + low).astype(BF16)
            if tokens > 2 * RIM:
                grad[RIM : tokens - RIM] = own[RIM : tokens - RIM].astype(BF16)
            grad[tokens - RIM :] = (own[tokens - RIM :] + high).astype(BF16)
    at_dp = lax.axis_index("dp")
    cols = pieces[0].shape[1]
    for d in range(len(pieces)):
        value = pieces[0][...]
        for s in range(1, len(pieces)):
            value = jnp.where((at_dp ^ s) == d, pieces[s][...], value)
        weight_grad[:, d * cols : (d + 1) * cols] = value.astype(F32)


def vmem(*shape, dtype=BF16):
    return pltpu.VMEM(shape, dtype)


def hbm(*shape, dtype=BF16):
    return jax.ShapeDtypeStruct(shape, dtype)


def call(kernel, outs, flops, *args, mask=None, scratch=()):
    in_vmem = pl.BlockSpec(memory_space=pltpu.VMEM)
    in_smem = pl.BlockSpec(memory_space=pltpu.SMEM)
    masks = () if mask is None else (mask,)
    return pl.pallas_call(
        kernel,
        out_shape=outs,
        in_specs=[in_smem] * len(masks) + [in_vmem] * len(args),
        out_specs=[in_vmem] * len(outs),
        scratch_shapes=list(scratch),
        compiler_params=pltpu.CompilerParams(vmem_limit_bytes=24 * 1024 * 1024),
        cost_estimate=pl.CostEstimate(flops=flops, bytes_accessed=flops // 250, transcendentals=0),
    )(*masks, *args)


def call_on_hbm(kernel, outs, *args, mask=None, scratch=()):
    masks = () if mask is None else (mask,)
    return pl.pallas_call(
        kernel,
        out_shape=outs,
        in_specs=[pl.BlockSpec(memory_space=pltpu.SMEM)] * len(masks)
        + [pl.BlockSpec(memory_space=pltpu.HBM)] * len(args),
        out_specs=[pl.BlockSpec(memory_space=pltpu.VMEM)] * len(outs),
        scratch_shapes=list(scratch),
        compiler_params=pltpu.CompilerParams(vmem_limit_bytes=8 * 1024 * 1024),
        cost_estimate=pl.CostEstimate(flops=10**6, bytes_accessed=4096, transcendentals=0),
    )(*masks, *(pltpu.with_memory_space_constraint(x, pltpu.HBM) for x in args))


def swap(count, bits):
    return [(i, i ^ bits) for i in range(count)]


def over_links(count):
    return [(i, (i - 1 if i % 2 == 0 else i + 1) % count) for i in range(count)]


def total(parts):
    return functools.reduce(jnp.add, [p.astype(F32) for p in parts])


def body(queries, keys, values, out_grad, w_out, block_mask):
    q, k, v, g = queries[0], keys[0], values[0], out_grad[0]
    tokens, feats = q.shape
    width = g.shape[1]
    blocks = tokens // BLK
    ctx, dp = lax.axis_size("ctx"), lax.axis_size("dp")
    chips = ctx // 2
    at_ctx = lax.axis_index("ctx")
    rows, cols = feats // ctx, width // dp

    rim = vmem(RIM, feats)
    to_link, *to_chip = call_on_hbm(
        pack_kernel,
        [vmem(2, RIM, feats), rim, rim],
        k, v,
        scratch=[pltpu.SemaphoreType.DMA((4,))],
    )
    link = lax.ppermute(to_link, "ctx", over_links(ctx))
    chip_k, chip_v = (lax.ppermute(x, "ctx", swap(ctx, 1)) for x in to_chip)
    sibling_g = lax.ppermute(g, "ctx", swap(ctx, 1))
    sibling_g = pltpu.with_memory_space_constraint(sibling_g, pltpu.VMEM)

    mask = lax.dynamic_slice_in_dim(block_mask[0], at_ctx * blocks, blocks, 0)
    args = (q, k, v, g, w_out)
    own_keys = min(CAND, blocks) * BLK
    own_scores = (blocks, PAIRS, own_keys, 2 * BLK)
    rim_scores = (PAIRS, RIM, 2 * BLK)
    q, k, v, g, w_out, own_t, stats, own_exps, grad_t = call_on_hbm(
        own_kernel,
        [vmem(*x.shape) for x in args]
        + [
            vmem(blocks, feats, BLK, dtype=F32),
            vmem(2, blocks, PAIRS, 2 * BLK, dtype=F32),
            vmem(*own_scores, dtype=F32),
            vmem(blocks, feats, BLK),
        ],
        *args,
        mask=mask,
        scratch=[vmem(*own_scores), pltpu.SemaphoreType.DMA((len(args),))],
    )
    chip_t, chip_stats, chip_exps = call(
        chip_kernel,
        [
            vmem(feats, BLK, dtype=F32),
            vmem(2, PAIRS, 2 * BLK, dtype=F32),
            vmem(*rim_scores, dtype=F32),
        ],
        10**6,
        q, chip_k, chip_v, own_t, stats,
        mask=mask,
        scratch=[vmem(*rim_scores)],
    )
    attn_t, mine, other, link_exps, own_factors, rim_factors = call(
        forward_kernel,
        [
            vmem(blocks, feats, BLK),
            vmem(chips, rows, tokens),
            vmem(chips, rows, tokens),
            vmem(*rim_scores, dtype=F32),
            vmem(blocks, PAIRS, 2 * BLK, dtype=F32),
            vmem(2, PAIRS, 2 * BLK, dtype=F32),
        ],
        10**6,
        q, link, own_t, stats, chip_t, chip_stats,
        mask=mask,
        scratch=[vmem(*rim_scores)],
    )

    other = lax.ppermute(other, "ctx", swap(ctx, 1))
    other = pltpu.with_memory_space_constraint(other, pltpu.VMEM)
    (product,) = call(product_kernel, [vmem(chips * rows, width, dtype=F32)], 10**6, mine, g)
    *halves, after = call(
        halves_kernel,
        [vmem(chips, rows, cols)] * dp + [vmem(8, 128, dtype=F32)],
        10**6,
        product, other, sibling_g,
    )
    to_link, to_chip, deltas, rim_t = call(
        rim_kernel,
        [
            vmem(2, RIM, feats),
            vmem(2, RIM, feats),
            vmem(blocks, PAIRS, 2 * BLK, dtype=F32),
            vmem(blocks, feats, BLK, dtype=F32),
        ],
        10**6,
        q, link, chip_k, chip_v, grad_t, attn_t, link_exps, chip_exps, rim_factors, after,
        scratch=[vmem(2, *rim_scores, dtype=F32), vmem(2, *rim_scores), vmem(2, *rim_scores)],
    )
    grad_link = lax.ppermute(to_link, "ctx", over_links(ctx))
    grad_chip = lax.ppermute(to_chip, "ctx", swap(ctx, 1))

    q_grad, k_own, v_own, after = call(
        own_backward_kernel,
        [
            hbm(tokens, feats),
            vmem(tokens, feats, dtype=F32),
            vmem(tokens, feats, dtype=F32),
            vmem(8, 128, dtype=F32),
        ],
        10**6,
        q, k, v, grad_t, own_exps, own_factors, deltas, rim_t, after,
        scratch=[vmem(*own_scores, dtype=F32), vmem(*own_scores), vmem(*own_scores)],
    )

    halves = [halves[0]] + [lax.ppermute(halves[s], "dp", swap(dp, s)) for s in range(dp - 1, 0, -1)]
    quarters = call(chips_kernel, [vmem(rows, cols)] * chips, 10**6, *halves, after)
    (output,) = call(output_kernel, [hbm(tokens, width)], 10**6, attn_t, w_out, quarters[0])
    piece = total(
        [quarters[0]]
        + [lax.ppermute(quarters[s], "ctx", swap(ctx, 2 * s)) for s in range(chips - 1, 0, -1)]
    )
    piece = (piece * (dp * tokens * ctx) ** (-0.5)).astype(BF16)
    pieces = [piece] + [lax.ppermute(piece, "dp", swap(dp, s)) for s in range(dp - 1, 0, -1)]
    k_grad, v_grad, weight_grad = call(
        last_kernel,
        [hbm(tokens, feats), hbm(tokens, feats), hbm(rows, width, dtype=F32)],
        10**6,
        k_own, v_own, grad_link, grad_chip, *pieces,
    )
    return (output[None], q_grad[None], k_grad[None], v_grad[None], weight_grad)


def solution(mesh):
    rows = P("dp", "ctx", None)
    return jax.shard_map(
        body,
        mesh=mesh,
        in_specs=(rows, rows, rows, rows, P(), P("dp", None, None)),
        out_specs=(rows, rows, rows, rows, P("ctx", None)),
        check_vma=False,
    )
```

```python
import functools

import jax
import jax.numpy as jnp
from jax import lax
from jax.experimental import pallas as pl
from jax.experimental.pallas import tpu as pltpu
from jax.sharding import PartitionSpec as P

HEADS = 8
HD = 64
BLK = 128
RAD = 1
CAND = 2 * RAD + 1
PAIRS = HEADS // 2
PAIR = 2 * HD
RIM = RAD * BLK
BIG_NEGATIVE = -1e30
SCALE = HD ** (-0.5)
BF16 = jnp.bfloat16
F32 = jnp.float32


def dot(a, b, contract):
    return lax.dot_general(a, b, (contract, ((), ())), preferred_element_type=F32)


def two_heads(block, axis):
    feature = lax.broadcasted_iota(jnp.int32, block.shape, axis)
    zero = jnp.zeros_like(block)
    return jnp.concatenate(
        [jnp.where(feature < HD, block, zero), jnp.where(feature < HD, zero, block)], axis=1 - axis
    )


def own_features(both):
    return jnp.concatenate([both[:HD, :BLK], both[HD:, BLK:]], axis=0)


def spread(row):
    return jnp.concatenate(
        [
            jnp.broadcast_to(row[:, :BLK], (HD, BLK)),
            jnp.broadcast_to(row[:, BLK:], (HD, BLK)),
        ],
        axis=0,
    )


def own_candidates(b, blocks):
    return max(0, RAD - b), min(CAND - 1, blocks - 1 - b + RAD)


def own_rows(b, blocks):
    first, last = own_candidates(b, blocks)
    return slice((b + first - RAD) * BLK, (b + last - RAD + 1) * BLK)


def masked(bias, b, c, part):
    return part + bias[b * CAND + c]


def pairs_of(blocks):
    for b in range(blocks):
        for p in range(PAIRS):
            yield b, slice(b * BLK, (b + 1) * BLK), slice(p * PAIR, (p + 1) * PAIR), p


def at_core():
    return lax.rem(lax.axis_index("ctx"), 2)


def rim_block(blocks, over_link):
    core = at_core()
    upper = core if over_link else 1 - core
    return upper * (blocks - 1), upper * (CAND - 1)


def rows_of(b):
    return pl.ds(pl.multiple_of(b * BLK, BLK), BLK)


def pack_kernel(k, v, to_link, chip_k, chip_v, sems):
    blocks = k.shape[0] // BLK
    link_rows = rows_of(rim_block(blocks, True)[0])
    chip_rows = rows_of(rim_block(blocks, False)[0])
    pairs = (
        (k.at[link_rows], to_link.at[0]),
        (v.at[link_rows], to_link.at[1]),
        (k.at[chip_rows], chip_k),
        (v.at[chip_rows], chip_v),
    )
    copies = [pltpu.make_async_copy(x, y, sems.at[i]) for i, (x, y) in enumerate(pairs)]
    for copy in copies:
        copy.start()
    for copy in copies:
        copy.wait()


def own_kernel(
    bias, q_arg, k_arg, v_arg, g_arg, w_arg,
    q, k, v, g_low, g_high, w_out, own_t, stats, exps, grad_t, rounded, sems,
):
    half = g_low.shape[0]
    pairs = (
        (q_arg, q),
        (k_arg, k),
        (v_arg, v),
        (g_arg.at[:half], g_low),
        (g_arg.at[half:], g_high),
        (w_arg, w_out),
    )
    copies = [pltpu.make_async_copy(x, y, sems.at[i]) for i, (x, y) in enumerate(pairs)]
    for copy in copies:
        copy.start()
    copies[0].wait()
    copies[1].wait()
    blocks = q.shape[0] // BLK
    for b, rows, cols, p in pairs_of(blocks):
        first, last = own_candidates(b, blocks)
        here = own_rows(b, blocks)
        scores = dot(k[here, cols], two_heads(q[rows, cols] * SCALE, 1), ((1,), (1,)))
        for c in range(first, last + 1):
            part = slice((c - first) * BLK, (c - first + 1) * BLK)
            value = scores[part]
            exps[b, p, part] = value if c == RAD else masked(bias, b, c, value)
    for b, rows, cols, p in pairs_of(blocks):
        here = own_rows(b, blocks)
        keys = slice(0, here.stop - here.start)
        scores = exps[b, p, keys]
        top = jnp.max(scores, axis=0, keepdims=True)
        e = jnp.exp(scores - top)
        exps[b, p, keys] = e
        rounded[b, p, keys] = e.astype(BF16)
        stats[0, b, p : p + 1] = top
        stats[1, b, p : p + 1] = jnp.sum(e, axis=0, keepdims=True)
    copies[2].wait()
    for b, rows, cols, p in pairs_of(blocks):
        here = own_rows(b, blocks)
        e = rounded[b, p, : here.stop - here.start]
        own_t[b, cols] = own_features(dot(v[here, cols], e, ((0,), (0,))))
    for copy in copies[3:]:
        copy.wait()
    both = jnp.concatenate([g_low[...], g_high[...]], axis=0)
    for b in range(blocks):
        rows = slice(b * BLK, (b + 1) * BLK)
        grad_t[b] = dot(w_out[...], both[rows], ((1,), (1,))).astype(BF16)


def pair_cols(p):
    return slice(p * PAIR, (p + 1) * PAIR)


def with_rim(bias, q, rim_k, rim_v, b, c, old, exps, rounded):
    for p in range(PAIRS):
        q2 = two_heads(q[rows_of(b), pair_cols(p)] * SCALE, 1)
        scores = dot(rim_k[:, pair_cols(p)], q2, ((1,), (1,)))
        exps[p] = masked(bias, b, c, scores)
    results = []
    for p in range(PAIRS):
        old_top, old_sum = old(p)
        scores = exps[p]
        top = jnp.maximum(old_top, jnp.max(scores, axis=0, keepdims=True))
        kept = jnp.exp(old_top - top)
        e = jnp.exp(scores - top)
        exps[p] = e
        rounded[p] = e.astype(BF16)
        results.append((top, kept, old_sum * kept + jnp.sum(e, axis=0, keepdims=True)))
    parts = [
        own_features(dot(rim_v[:, pair_cols(p)], rounded[p], ((0,), (0,)))) for p in range(PAIRS)
    ]
    return [(*result, part) for result, part in zip(results, parts)]


def chip_kernel(bias, q, rim_k, rim_v, own_t, stats, chip_t, chip_stats, exps, rounded):
    blocks = q.shape[0] // BLK
    b, c = rim_block(blocks, False)

    def old(p):
        return stats[0, b, p : p + 1], stats[1, b, p : p + 1]

    results = with_rim(bias, q, rim_k, rim_v, b, c, old, exps, rounded)
    for p, (top, kept, count, part) in enumerate(results):
        at = slice(p, p + 1)
        if blocks == 1:
            chip_t[pair_cols(p)] = own_t[b, pair_cols(p)] * spread(kept) + part
            chip_stats[0, at], chip_stats[1, at] = top, count
        else:
            share = 1.0 / count
            attn = own_t[b, pair_cols(p)] * spread(kept * share) + part * spread(share)
            chip_t[pair_cols(p)] = attn
            chip_stats[0, at], chip_stats[1, at] = share, kept * share


def forward_kernel(
    bias, q, rim, own_t, stats, chip_t, chip_stats,
    attn_t, mine, other, exps, own_factors, rim_factors, rounded,
):
    blocks = q.shape[0] // BLK
    b, c = rim_block(blocks, True)
    at_chip, _ = rim_block(blocks, False)

    def old(p):
        at = slice(p, p + 1)
        if blocks == 1:
            return chip_stats[0, at], chip_stats[1, at]
        return stats[0, b, at], stats[1, b, at]

    results = with_rim(bias, q, rim.at[0], rim.at[1], b, c, old, exps, rounded)
    for p, (top, kept, count, part) in enumerate(results):
        at = slice(p, p + 1)
        cols = pair_cols(p)
        base = chip_t[cols] if blocks == 1 else own_t[b, cols]
        share = 1.0 / count
        attn_t[b, cols] = (base * spread(kept * share) + part * spread(share)).astype(BF16)
        rim_factors[0, at] = share
        if blocks == 1:
            rim_factors[1, at] = kept * share
            own_factors[0, at] = jnp.exp(stats[0, 0, at] - top) * share
        else:
            own_factors[b, at] = kept * share
            attn_t[at_chip, cols] = chip_t[cols].astype(BF16)
            rim_factors[1, at] = chip_stats[0, at]
            own_factors[at_chip, at] = chip_stats[1, at]
        for inner in range(1, blocks - 1):
            share = 1.0 / stats[1, inner, at]
            attn_t[inner, cols] = (own_t[inner, cols] * spread(share)).astype(BF16)
            own_factors[inner, at] = share
    first_core = at_core() == 0
    chips, rows, _ = mine.shape
    for i in range(chips):
        for block in range(blocks):
            tokens = slice(block * BLK, (block + 1) * BLK)
            even = attn_t[block, 2 * i * rows : (2 * i + 1) * rows]
            odd = attn_t[block, (2 * i + 1) * rows : (2 * i + 2) * rows]
            mine[i, :, tokens] = jnp.where(first_core, even, odd)
            other[i, :, tokens] = jnp.where(first_core, odd, even)


def flat_dot(attn, g_low, g_high):
    chips, rows, tokens = attn.shape
    g = jnp.concatenate([g_low[...], g_high[...]], axis=0)
    return dot(attn[...].reshape(chips * rows, tokens), g, ((1,), (0,)))


def product_kernel(mine, g_low, g_high, product):
    product[...] = flat_dot(mine, g_low, g_high)


def score_grads(probs, dprob, delta):
    return (probs * (dprob - delta)).astype(BF16), probs.astype(BF16)


def rim_kernel(
    q, link, chip_k, chip_v, grad_t, attn_t, link_exps, chip_exps, rim_factors, before,
    to_link, to_chip, deltas, query_t, dprobs, dscores, rounded,
):
    blocks = q.shape[0] // BLK
    sides = (
        (rim_block(blocks, True)[0], link.at[0], link.at[1], link_exps, to_link),
        (rim_block(blocks, False)[0], chip_k, chip_v, chip_exps, to_chip),
    )
    for i, (b, _, rim_v, _, _) in enumerate(sides):
        for p in range(PAIRS):
            g2_t = two_heads(grad_t[b, pair_cols(p)], 0)
            dprobs[i, p] = dot(rim_v[:, pair_cols(p)], g2_t, ((1,), (0,)))
    for b, _, cols, p in pairs_of(blocks):
        product = grad_t[b, cols].astype(F32) * attn_t[b, cols].astype(F32)
        deltas[b, p : p + 1] = jnp.concatenate(
            [
                jnp.sum(product[:HD], axis=0, keepdims=True),
                jnp.sum(product[HD:], axis=0, keepdims=True),
            ],
            axis=1,
        )
    query_t[...] = jnp.zeros_like(query_t)
    for i, (b, _, _, exps, _) in enumerate(sides):
        for p in range(PAIRS):
            at = slice(p, p + 1)
            dscores[i, p], rounded[i, p] = score_grads(
                exps[p] * rim_factors[i, at], dprobs[i, p], deltas[b, at]
            )
    for i, (b, rim_k, _, _, back) in enumerate(sides):
        for p in range(PAIRS):
            cols = pair_cols(p)
            q2 = two_heads(q[rows_of(b), cols] * SCALE, 1)
            g2_t = two_heads(grad_t[b, cols], 0)
            back[0, :, cols] = dot(dscores[i, p], q2, ((1,), (0,))).astype(BF16)
            back[1, :, cols] = dot(rounded[i, p], g2_t, ((1,), (1,))).astype(BF16)
            query_t[b, cols] += own_features(dot(rim_k[:, cols], dscores[i, p], ((0,), (0,))))


def own_backward_kernel(
    q, k, v, grad_t, exps, factors, deltas, rim_t, before,
    q_grad, k_own, v_own, after, dprobs, dscores, rounded,
):
    blocks = q.shape[0] // BLK
    for b, _, cols, p in pairs_of(blocks):
        here = own_rows(b, blocks)
        g2_t = two_heads(grad_t[b, cols], 0)
        dprobs[b, p, : here.stop - here.start] = dot(v[here, cols], g2_t, ((1,), (0,)))
    for b, _, _, p in pairs_of(blocks):
        here = own_rows(b, blocks)
        keys = slice(0, here.stop - here.start)
        dscores[b, p, keys], rounded[b, p, keys] = score_grads(
            exps[b, p, keys] * factors[b, p : p + 1], dprobs[b, p, keys], deltas[b, p : p + 1]
        )
    k_sums, v_sums = {}, {}
    for b, rows, cols, p in pairs_of(blocks):
        here = own_rows(b, blocks)
        keys = slice(0, here.stop - here.start)
        q2 = two_heads(q[rows, cols] * SCALE, 1)
        g2_t = two_heads(grad_t[b, cols], 0)
        dscore = dscores[b, p, keys]
        k_part = dot(dscore, q2, ((1,), (0,)))
        v_part = dot(rounded[b, p, keys], g2_t, ((1,), (1,)))
        for at in range(here.start, here.stop, BLK):
            part = slice(at - here.start, at - here.start + BLK)
            for sums, value in ((k_sums, k_part), (v_sums, v_part)):
                sums.setdefault((at, p), []).append(value[part])
        query_t = own_features(dot(k[here, cols], dscore, ((0,), (0,)))) + rim_t[b, cols]
        q_grad[rows, cols] = (query_t * SCALE).T.astype(BF16)
    for out, sums in ((k_own, k_sums), (v_own, v_sums)):
        for (at, p), values in sums.items():
            out[at : at + BLK, pair_cols(p)] = functools.reduce(jnp.add, values)
    after[...] = jnp.zeros_like(after)


def output_kernel(attn_t, w_out, before, output):
    for b in range(attn_t.shape[0]):
        part = dot(attn_t[b], w_out[...], ((0,), (0,)))
        output[b * BLK : (b + 1) * BLK] = part.astype(BF16)


def halves_kernel(product, other, g_low, g_high, *outs):
    pieces, after = outs[:-1], outs[-1]
    at_dp = lax.axis_index("dp")
    chips, rows, cols = pieces[0].shape
    both = (product[...] + flat_dot(other, g_low, g_high)).astype(BF16)
    for d in range(len(pieces)):
        value = both[:, d * cols : (d + 1) * cols].reshape(chips, rows, cols)
        for s in range(len(pieces)):

            @pl.when((at_dp ^ s) == d)
            def _(s=s, value=value):
                pieces[s][...] = value

    after[...] = jnp.zeros_like(after)


def chips_kernel(*refs):
    parts, outs = refs[: lax.axis_size("dp")], refs[lax.axis_size("dp") + 1 :]
    chip = lax.div(lax.axis_index("ctx"), 2)
    for s, out in enumerate(outs):
        out[...] = total([part[chip ^ s] for part in parts]).astype(BF16)


def last_kernel(k_own, v_own, from_link, from_chip, *refs):
    pieces, (k_grad, v_grad, weight_grad) = refs[:1] + refs[-4:0:-1], refs[-3:]
    tokens = k_own.shape[0]
    first_core = at_core() == 0
    for which, (own, grad) in enumerate(((k_own, k_grad), (v_own, v_grad))):
        link = from_link[which].astype(F32)
        chip = from_chip[which].astype(F32)
        low = jnp.where(first_core, link, chip)
        high = jnp.where(first_core, chip, link)
        if tokens == RIM:
            grad[...] = (own[...] + low + high).astype(BF16)
        else:
            grad[:RIM] = (own[:RIM] + low).astype(BF16)
            if tokens > 2 * RIM:
                grad[RIM : tokens - RIM] = own[RIM : tokens - RIM].astype(BF16)
            grad[tokens - RIM :] = (own[tokens - RIM :] + high).astype(BF16)
    at_dp = lax.axis_index("dp")
    cols = pieces[0].shape[1]
    for d in range(len(pieces)):
        value = pieces[0][...]
        for s in range(1, len(pieces)):
            value = jnp.where((at_dp ^ s) == d, pieces[s][...], value)
        weight_grad[:, d * cols : (d + 1) * cols] = value.astype(F32)


def vmem(*shape, dtype=BF16):
    return pltpu.VMEM(shape, dtype)


def hbm(*shape, dtype=BF16):
    return jax.ShapeDtypeStruct(shape, dtype)


def call(kernel, outs, flops, *args, scratch=()):
    in_vmem = pl.BlockSpec(memory_space=pltpu.VMEM)
    return pl.pallas_call(
        kernel,
        out_shape=outs,
        in_specs=[in_vmem] * len(args),
        out_specs=[in_vmem] * len(outs),
        scratch_shapes=list(scratch),
        compiler_params=pltpu.CompilerParams(vmem_limit_bytes=24 * 1024 * 1024),
        cost_estimate=pl.CostEstimate(flops=flops, bytes_accessed=flops // 250, transcendentals=0),
    )(*args)


def call_on_hbm(kernel, outs, *args, beside=(), scratch=()):
    return pl.pallas_call(
        kernel,
        out_shape=outs,
        in_specs=[pl.BlockSpec(memory_space=pltpu.VMEM)] * len(beside)
        + [pl.BlockSpec(memory_space=pltpu.HBM)] * len(args),
        out_specs=[pl.BlockSpec(memory_space=pltpu.VMEM)] * len(outs),
        scratch_shapes=list(scratch),
        compiler_params=pltpu.CompilerParams(vmem_limit_bytes=8 * 1024 * 1024),
        cost_estimate=pl.CostEstimate(flops=10**6, bytes_accessed=4096, transcendentals=0),
    )(*beside, *(pltpu.with_memory_space_constraint(x, pltpu.HBM) for x in args))


def swap(count, bits):
    return [(i, i ^ bits) for i in range(count)]


def over_links(count):
    return [(i, (i - 1 if i % 2 == 0 else i + 1) % count) for i in range(count)]


def total(parts):
    return functools.reduce(jnp.add, [p.astype(F32) for p in parts])


def body(queries, keys, values, out_grad, w_out, block_mask):
    q, k, v, g = queries[0], keys[0], values[0], out_grad[0]
    tokens, feats = q.shape
    width = g.shape[1]
    blocks = tokens // BLK
    ctx, dp = lax.axis_size("ctx"), lax.axis_size("dp")
    chips = ctx // 2
    at_ctx = lax.axis_index("ctx")
    rows, cols = feats // ctx, width // dp

    rim = vmem(RIM, feats)
    to_link, *to_chip = call_on_hbm(
        pack_kernel,
        [vmem(2, RIM, feats), rim, rim],
        k, v,
        scratch=[pltpu.SemaphoreType.DMA((4,))],
    )
    link = lax.ppermute(to_link, "ctx", over_links(ctx))
    chip_k, chip_v = (lax.ppermute(x, "ctx", swap(ctx, 1)) for x in to_chip)
    mask = lax.dynamic_slice_in_dim(block_mask[0], at_ctx * blocks, blocks, 0)
    bias = jnp.where(mask == 1, 0.0, BIG_NEGATIVE).astype(F32).reshape(blocks * CAND, 1, 1)
    bias = jnp.broadcast_to(bias, (blocks * CAND, 1, 2 * BLK))
    args = (q, k, v, g, w_out)
    own_keys = min(CAND, blocks) * BLK
    own_scores = (blocks, PAIRS, own_keys, 2 * BLK)
    rim_scores = (PAIRS, RIM, 2 * BLK)
    half = vmem(tokens // 2, width)
    q, k, v, g_low, g_high, w_out, own_t, stats, own_exps, grad_t = call_on_hbm(
        own_kernel,
        [vmem(tokens, feats)] * 3
        + [
            half,
            half,
            vmem(feats, width),
            vmem(blocks, feats, BLK, dtype=F32),
            vmem(2, blocks, PAIRS, 2 * BLK, dtype=F32),
            vmem(*own_scores, dtype=F32),
            vmem(blocks, feats, BLK),
        ],
        *args,
        beside=(bias,),
        scratch=[vmem(*own_scores), pltpu.SemaphoreType.DMA((6,))],
    )
    sibling_g = [
        pltpu.with_memory_space_constraint(lax.ppermute(x, "ctx", swap(ctx, 1)), pltpu.VMEM)
        for x in (g_low, g_high)
    ]
    chip_t, chip_stats, chip_exps = call(
        chip_kernel,
        [
            vmem(feats, BLK, dtype=F32),
            vmem(2, PAIRS, 2 * BLK, dtype=F32),
            vmem(*rim_scores, dtype=F32),
        ],
        10**6,
        bias, q, chip_k, chip_v, own_t, stats,
        scratch=[vmem(*rim_scores)],
    )
    attn_t, mine, other, link_exps, own_factors, rim_factors = call(
        forward_kernel,
        [
            vmem(blocks, feats, BLK),
            vmem(chips, rows, tokens),
            vmem(chips, rows, tokens),
            vmem(*rim_scores, dtype=F32),
            vmem(blocks, PAIRS, 2 * BLK, dtype=F32),
            vmem(2, PAIRS, 2 * BLK, dtype=F32),
        ],
        10**6,
        bias, q, link, own_t, stats, chip_t, chip_stats,
        scratch=[vmem(*rim_scores)],
    )

    other = lax.ppermute(other, "ctx", swap(ctx, 1))
    other = pltpu.with_memory_space_constraint(other, pltpu.VMEM)
    (product,) = call(product_kernel, [vmem(chips * rows, width, dtype=F32)], 10**6, mine, g_low, g_high)
    *halves, after = call(
        halves_kernel,
        [vmem(chips, rows, cols)] * dp + [vmem(8, 128, dtype=F32)],
        10**6,
        product, other, *sibling_g,
    )
    to_link, to_chip, deltas, rim_t = call(
        rim_kernel,
        [
            vmem(2, RIM, feats),
            vmem(2, RIM, feats),
            vmem(blocks, PAIRS, 2 * BLK, dtype=F32),
            vmem(blocks, feats, BLK, dtype=F32),
        ],
        10**6,
        q, link, chip_k, chip_v, grad_t, attn_t, link_exps, chip_exps, rim_factors, after,
        scratch=[vmem(2, *rim_scores, dtype=F32), vmem(2, *rim_scores), vmem(2, *rim_scores)],
    )
    grad_link = lax.ppermute(to_link, "ctx", over_links(ctx))
    grad_chip = lax.ppermute(to_chip, "ctx", swap(ctx, 1))

    q_grad, k_own, v_own, after = call(
        own_backward_kernel,
        [
            hbm(tokens, feats),
            vmem(tokens, feats, dtype=F32),
            vmem(tokens, feats, dtype=F32),
            vmem(8, 128, dtype=F32),
        ],
        10**6,
        q, k, v, grad_t, own_exps, own_factors, deltas, rim_t, after,
        scratch=[vmem(*own_scores, dtype=F32), vmem(*own_scores), vmem(*own_scores)],
    )

    halves = [halves[0]] + [lax.ppermute(halves[s], "dp", swap(dp, s)) for s in range(dp - 1, 0, -1)]
    quarters = call(chips_kernel, [vmem(rows, cols)] * chips, 10**6, *halves, after)
    (output,) = call(output_kernel, [hbm(tokens, width)], 10**6, attn_t, w_out, quarters[0])
    piece = total(
        [quarters[0]]
        + [lax.ppermute(quarters[s], "ctx", swap(ctx, 2 * s)) for s in range(chips - 1, 0, -1)]
    )
    piece = (piece * (dp * tokens * ctx) ** (-0.5)).astype(BF16)
    pieces = [piece] + [lax.ppermute(piece, "dp", swap(dp, s)) for s in range(dp - 1, 0, -1)]
    k_grad, v_grad, weight_grad = call(
        last_kernel,
        [hbm(tokens, feats), hbm(tokens, feats), hbm(rows, width, dtype=F32)],
        10**6,
        k_own, v_own, grad_link, grad_chip, *pieces,
    )
    return (output[None], q_grad[None], k_grad[None], v_grad[None], weight_grad)


def solution(mesh):
    rows = P("dp", "ctx", None)
    return jax.shard_map(
        body,
        mesh=mesh,
        in_specs=(rows, rows, rows, rows, P(), P("dp", None, None)),
        out_specs=(rows, rows, rows, rows, P("ctx", None)),
        check_vma=False,
    )
```

```python
import functools

import jax
import jax.numpy as jnp
from jax import lax
from jax.experimental import pallas as pl
from jax.experimental.pallas import tpu as pltpu
from jax.sharding import PartitionSpec as P

HEADS = 8
HD = 64
BLK = 128
RAD = 1
CAND = 2 * RAD + 1
PAIRS = HEADS // 2
PAIR = 2 * HD
RIM = RAD * BLK
BIG_NEGATIVE = -1e30
SCALE = HD ** (-0.5)
BF16 = jnp.bfloat16
F32 = jnp.float32


def dot(a, b, contract):
    return lax.dot_general(a, b, (contract, ((), ())), preferred_element_type=F32)


def two_heads(block, axis):
    feature = lax.broadcasted_iota(jnp.int32, block.shape, axis)
    zero = jnp.zeros_like(block)
    return jnp.concatenate(
        [jnp.where(feature < HD, block, zero), jnp.where(feature < HD, zero, block)], axis=1 - axis
    )


def own_features(both):
    return jnp.concatenate([both[:HD, :BLK], both[HD:, BLK:]], axis=0)


def spread(row):
    return jnp.concatenate(
        [
            jnp.broadcast_to(row[:, :BLK], (HD, BLK)),
            jnp.broadcast_to(row[:, BLK:], (HD, BLK)),
        ],
        axis=0,
    )


def own_candidates(b, blocks):
    return max(0, RAD - b), min(CAND - 1, blocks - 1 - b + RAD)


def own_rows(b, blocks):
    first, last = own_candidates(b, blocks)
    return slice((b + first - RAD) * BLK, (b + last - RAD + 1) * BLK)


def masked(bias, b, c, part):
    return part + bias[b * CAND + c]


def pairs_of(blocks):
    for b in range(blocks):
        for p in range(PAIRS):
            yield b, slice(b * BLK, (b + 1) * BLK), slice(p * PAIR, (p + 1) * PAIR), p


def at_core():
    return lax.rem(lax.axis_index("ctx"), 2)


def rim_block(blocks, over_link):
    core = at_core()
    upper = core if over_link else 1 - core
    return upper * (blocks - 1), upper * (CAND - 1)


def rows_of(b):
    return pl.ds(pl.multiple_of(b * BLK, BLK), BLK)


def pack_kernel(k, v, to_link, chip_k, chip_v, sems):
    blocks = k.shape[0] // BLK
    link_rows = rows_of(rim_block(blocks, True)[0])
    chip_rows = rows_of(rim_block(blocks, False)[0])
    pairs = (
        (k.at[link_rows], to_link.at[0]),
        (v.at[link_rows], to_link.at[1]),
        (k.at[chip_rows], chip_k),
        (v.at[chip_rows], chip_v),
    )
    copies = [pltpu.make_async_copy(x, y, sems.at[i]) for i, (x, y) in enumerate(pairs)]
    for copy in copies:
        copy.start()
    for copy in copies:
        copy.wait()


def own_kernel(
    bias, q_arg, k_arg, v_arg, g_arg, w_arg,
    q, k, v, g_low, g_high, w_out, own_t, stats, exps, grad_t, rounded, sems,
):
    half = g_low.shape[0]
    pairs = (
        (q_arg, q),
        (k_arg, k),
        (v_arg, v),
        (g_arg.at[:half], g_low),
        (g_arg.at[half:], g_high),
        (w_arg, w_out),
    )
    copies = [pltpu.make_async_copy(x, y, sems.at[i]) for i, (x, y) in enumerate(pairs)]
    for copy in copies:
        copy.start()
    copies[0].wait()
    copies[1].wait()
    blocks = q.shape[0] // BLK
    for b, rows, cols, p in pairs_of(blocks):
        first, last = own_candidates(b, blocks)
        here = own_rows(b, blocks)
        scores = dot(k[here, cols], two_heads(q[rows, cols] * SCALE, 1), ((1,), (1,)))
        for c in range(first, last + 1):
            part = slice((c - first) * BLK, (c - first + 1) * BLK)
            value = scores[part]
            exps[b, p, part] = value if c == RAD else masked(bias, b, c, value)
    for b, rows, cols, p in pairs_of(blocks):
        here = own_rows(b, blocks)
        keys = slice(0, here.stop - here.start)
        scores = exps[b, p, keys]
        top = jnp.max(scores, axis=0, keepdims=True)
        e = jnp.exp(scores - top)
        exps[b, p, keys] = e
        rounded[b, p, keys] = e.astype(BF16)
        stats[0, b, p : p + 1] = top
        stats[1, b, p : p + 1] = jnp.sum(e, axis=0, keepdims=True)
    copies[2].wait()
    for b, rows, cols, p in pairs_of(blocks):
        here = own_rows(b, blocks)
        e = rounded[b, p, : here.stop - here.start]
        own_t[b, cols] = own_features(dot(v[here, cols], e, ((0,), (0,))))
    for copy in copies[3:]:
        copy.wait()
    both = jnp.concatenate([g_low[...], g_high[...]], axis=0)
    for b in range(blocks):
        rows = slice(b * BLK, (b + 1) * BLK)
        grad_t[b] = dot(w_out[...], both[rows], ((1,), (1,))).astype(BF16)


def pair_cols(p):
    return slice(p * PAIR, (p + 1) * PAIR)


def with_rim(bias, q, rim_k, rim_v, b, c, old, exps, rounded):
    for p in range(PAIRS):
        q2 = two_heads(q[rows_of(b), pair_cols(p)] * SCALE, 1)
        scores = dot(rim_k[:, pair_cols(p)], q2, ((1,), (1,)))
        exps[p] = masked(bias, b, c, scores)
    results = []
    for p in range(PAIRS):
        old_top, old_sum = old(p)
        scores = exps[p]
        top = jnp.maximum(old_top, jnp.max(scores, axis=0, keepdims=True))
        kept = jnp.exp(old_top - top)
        e = jnp.exp(scores - top)
        exps[p] = e
        rounded[p] = e.astype(BF16)
        results.append((top, kept, old_sum * kept + jnp.sum(e, axis=0, keepdims=True)))
    parts = [
        own_features(dot(rim_v[:, pair_cols(p)], rounded[p], ((0,), (0,)))) for p in range(PAIRS)
    ]
    return [(*result, part) for result, part in zip(results, parts)]


def chip_kernel(bias, q, rim_k, rim_v, own_t, stats, chip_t, chip_stats, exps, rounded):
    blocks = q.shape[0] // BLK
    b, c = rim_block(blocks, False)

    def old(p):
        return stats[0, b, p : p + 1], stats[1, b, p : p + 1]

    results = with_rim(bias, q, rim_k, rim_v, b, c, old, exps, rounded)
    for p, (top, kept, count, part) in enumerate(results):
        at = slice(p, p + 1)
        if blocks == 1:
            chip_t[pair_cols(p)] = own_t[b, pair_cols(p)] * spread(kept) + part
            chip_stats[0, at], chip_stats[1, at] = top, count
        else:
            share = 1.0 / count
            attn = own_t[b, pair_cols(p)] * spread(kept * share) + part * spread(share)
            chip_t[pair_cols(p)] = attn
            chip_stats[0, at], chip_stats[1, at] = share, kept * share


def forward_kernel(
    bias, q, rim, own_t, stats, chip_t, chip_stats,
    attn_t, mine, other, exps, own_factors, rim_factors, rounded,
):
    blocks = q.shape[0] // BLK
    b, c = rim_block(blocks, True)
    at_chip, _ = rim_block(blocks, False)

    def old(p):
        at = slice(p, p + 1)
        if blocks == 1:
            return chip_stats[0, at], chip_stats[1, at]
        return stats[0, b, at], stats[1, b, at]

    results = with_rim(bias, q, rim.at[0], rim.at[1], b, c, old, exps, rounded)
    for p, (top, kept, count, part) in enumerate(results):
        at = slice(p, p + 1)
        cols = pair_cols(p)
        base = chip_t[cols] if blocks == 1 else own_t[b, cols]
        share = 1.0 / count
        attn_t[b, cols] = (base * spread(kept * share) + part * spread(share)).astype(BF16)
        rim_factors[0, at] = share
        if blocks == 1:
            rim_factors[1, at] = kept * share
            own_factors[0, at] = jnp.exp(stats[0, 0, at] - top) * share
        else:
            own_factors[b, at] = kept * share
            attn_t[at_chip, cols] = chip_t[cols].astype(BF16)
            rim_factors[1, at] = chip_stats[0, at]
            own_factors[at_chip, at] = chip_stats[1, at]
        for inner in range(1, blocks - 1):
            share = 1.0 / stats[1, inner, at]
            attn_t[inner, cols] = (own_t[inner, cols] * spread(share)).astype(BF16)
            own_factors[inner, at] = share
    first_core = at_core() == 0
    chips, rows, _ = mine.shape
    for i in range(chips):
        for block in range(blocks):
            tokens = slice(block * BLK, (block + 1) * BLK)
            even = attn_t[block, 2 * i * rows : (2 * i + 1) * rows]
            odd = attn_t[block, (2 * i + 1) * rows : (2 * i + 2) * rows]
            mine[i, :, tokens] = jnp.where(first_core, even, odd)
            other[i, :, tokens] = jnp.where(first_core, odd, even)


def flat_dot(attn, g_low, g_high):
    chips, rows, tokens = attn.shape
    g = jnp.concatenate([g_low[...], g_high[...]], axis=0)
    return dot(attn[...].reshape(chips * rows, tokens), g, ((1,), (0,)))


def product_kernel(mine, g_low, g_high, product):
    product[...] = flat_dot(mine, g_low, g_high)


def score_grads(probs, dprob, delta):
    return (probs * (dprob - delta)).astype(BF16), probs.astype(BF16)


def rim_kernel(
    q, link, chip_k, chip_v, grad_t, attn_t, link_exps, chip_exps, rim_factors, before,
    link_k_back, link_v_back, chip_back, deltas, query_t, dprobs, dscores, rounded,
):
    blocks = q.shape[0] // BLK
    sides = (
        (rim_block(blocks, True)[0], link.at[0], link.at[1], link_exps, link_k_back, link_v_back),
        (rim_block(blocks, False)[0], chip_k, chip_v, chip_exps, chip_back.at[0], chip_back.at[1]),
    )
    for i, (b, _, rim_v, _, _, _) in enumerate(sides):
        for p in range(PAIRS):
            g2_t = two_heads(grad_t[b, pair_cols(p)], 0)
            dprobs[i, p] = dot(rim_v[:, pair_cols(p)], g2_t, ((1,), (0,)))
    for b, _, cols, p in pairs_of(blocks):
        product = grad_t[b, cols].astype(F32) * attn_t[b, cols].astype(F32)
        deltas[b, p : p + 1] = jnp.concatenate(
            [
                jnp.sum(product[:HD], axis=0, keepdims=True),
                jnp.sum(product[HD:], axis=0, keepdims=True),
            ],
            axis=1,
        )
    query_t[...] = jnp.zeros_like(query_t)
    for i, (b, _, _, exps, _, _) in enumerate(sides):
        for p in range(PAIRS):
            at = slice(p, p + 1)
            dscores[i, p], rounded[i, p] = score_grads(
                exps[p] * rim_factors[i, at], dprobs[i, p], deltas[b, at]
            )
    for i, (b, rim_k, _, _, k_back, v_back) in enumerate(sides):
        for p in range(PAIRS):
            cols = pair_cols(p)
            q2 = two_heads(q[rows_of(b), cols] * SCALE, 1)
            g2_t = two_heads(grad_t[b, cols], 0)
            k_back[:, cols] = dot(dscores[i, p], q2, ((1,), (0,))).astype(BF16)
            v_back[:, cols] = dot(rounded[i, p], g2_t, ((1,), (1,))).astype(BF16)
            query_t[b, cols] += own_features(dot(rim_k[:, cols], dscores[i, p], ((0,), (0,))))


def own_backward_kernel(
    q, k, v, grad_t, exps, factors, deltas, rim_t,
    q_grad, k_own, v_own, after, dprobs, dscores, rounded,
):
    blocks = q.shape[0] // BLK
    for b, _, cols, p in pairs_of(blocks):
        here = own_rows(b, blocks)
        g2_t = two_heads(grad_t[b, cols], 0)
        dprobs[b, p, : here.stop - here.start] = dot(v[here, cols], g2_t, ((1,), (0,)))
    for b, _, _, p in pairs_of(blocks):
        here = own_rows(b, blocks)
        keys = slice(0, here.stop - here.start)
        dscores[b, p, keys], rounded[b, p, keys] = score_grads(
            exps[b, p, keys] * factors[b, p : p + 1], dprobs[b, p, keys], deltas[b, p : p + 1]
        )
    k_sums, v_sums = {}, {}
    for b, rows, cols, p in pairs_of(blocks):
        here = own_rows(b, blocks)
        keys = slice(0, here.stop - here.start)
        q2 = two_heads(q[rows, cols] * SCALE, 1)
        g2_t = two_heads(grad_t[b, cols], 0)
        dscore = dscores[b, p, keys]
        k_part = dot(dscore, q2, ((1,), (0,)))
        v_part = dot(rounded[b, p, keys], g2_t, ((1,), (1,)))
        for at in range(here.start, here.stop, BLK):
            part = slice(at - here.start, at - here.start + BLK)
            for sums, value in ((k_sums, k_part), (v_sums, v_part)):
                sums.setdefault((at, p), []).append(value[part])
        query_t = own_features(dot(k[here, cols], dscore, ((0,), (0,)))) + rim_t[b, cols]
        q_grad[rows, cols] = (query_t * SCALE).T.astype(BF16)
    for out, sums in ((k_own, k_sums), (v_own, v_sums)):
        for (at, p), values in sums.items():
            out[at : at + BLK, pair_cols(p)] = functools.reduce(jnp.add, values)
    after[...] = jnp.zeros_like(after)


def output_kernel(attn_t, w_out, before, output):
    for b in range(attn_t.shape[0]):
        part = dot(attn_t[b], w_out[...], ((0,), (0,)))
        output[b * BLK : (b + 1) * BLK] = part.astype(BF16)


def halves_kernel(product, other, g_low, g_high, *outs):
    pieces, after = outs[:-1], outs[-1]
    at_dp = lax.axis_index("dp")
    chips, rows, cols = pieces[0].shape
    both = (product[...] + flat_dot(other, g_low, g_high)).astype(BF16)
    for d in range(len(pieces)):
        value = both[:, d * cols : (d + 1) * cols].reshape(chips, rows, cols)
        for s in range(len(pieces)):

            @pl.when((at_dp ^ s) == d)
            def _(s=s, value=value):
                pieces[s][...] = value

    after[...] = jnp.zeros_like(after)


def chips_kernel(*refs):
    parts, outs = refs[: lax.axis_size("dp")], refs[lax.axis_size("dp") + 1 :]
    chip = lax.div(lax.axis_index("ctx"), 2)
    for s, out in enumerate(outs):
        out[...] = total([part[chip ^ s] for part in parts]).astype(BF16)


def piece_kernel(scale, count, *refs):
    refs[-1][...] = (total([part[...] for part in refs[:count]]) * scale).astype(BF16)


def last_kernel(k_own, v_own, link_k, link_v, chip_kv, *refs):
    pieces, (k_grad, v_grad, weight_grad) = refs[:1] + refs[-4:0:-1], refs[-3:]
    tokens = k_own.shape[0]
    first_core = at_core() == 0
    for i, (own, rim, grad) in enumerate(((k_own, link_k, k_grad), (v_own, link_v, v_grad))):
        link, chip = rim[...].astype(F32), chip_kv[i].astype(F32)
        low = jnp.where(first_core, link, chip)
        high = jnp.where(first_core, chip, link)
        if tokens == RIM:
            grad[...] = (own[...] + low + high).astype(BF16)
        else:
            grad[:RIM] = (own[:RIM] + low).astype(BF16)
            if tokens > 2 * RIM:
                grad[RIM : tokens - RIM] = own[RIM : tokens - RIM].astype(BF16)
            grad[tokens - RIM :] = (own[tokens - RIM :] + high).astype(BF16)
    at_dp = lax.axis_index("dp")
    cols = pieces[0].shape[1]
    for d in range(len(pieces)):
        value = pieces[0][...]
        for s in range(1, len(pieces)):
            value = jnp.where((at_dp ^ s) == d, pieces[s][...], value)
        weight_grad[:, d * cols : (d + 1) * cols] = value.astype(F32)


def vmem(*shape, dtype=BF16):
    return pltpu.VMEM(shape, dtype)


def hbm(*shape, dtype=BF16):
    return jax.ShapeDtypeStruct(shape, dtype)


def call(kernel, outs, flops, *args, scratch=()):
    in_vmem = pl.BlockSpec(memory_space=pltpu.VMEM)
    return pl.pallas_call(
        kernel,
        out_shape=outs,
        in_specs=[in_vmem] * len(args),
        out_specs=[in_vmem] * len(outs),
        scratch_shapes=list(scratch),
        compiler_params=pltpu.CompilerParams(vmem_limit_bytes=24 * 1024 * 1024),
        cost_estimate=pl.CostEstimate(flops=flops, bytes_accessed=flops // 250, transcendentals=0),
    )(*args)


def call_on_hbm(kernel, outs, *args, beside=(), scratch=()):
    return pl.pallas_call(
        kernel,
        out_shape=outs,
        in_specs=[pl.BlockSpec(memory_space=pltpu.VMEM)] * len(beside)
        + [pl.BlockSpec(memory_space=pltpu.HBM)] * len(args),
        out_specs=[pl.BlockSpec(memory_space=pltpu.VMEM)] * len(outs),
        scratch_shapes=list(scratch),
        compiler_params=pltpu.CompilerParams(vmem_limit_bytes=8 * 1024 * 1024),
        cost_estimate=pl.CostEstimate(flops=10**6, bytes_accessed=4096, transcendentals=0),
    )(*beside, *(pltpu.with_memory_space_constraint(x, pltpu.HBM) for x in args))


def swap(count, bits):
    return [(i, i ^ bits) for i in range(count)]


def over_links(count):
    return [(i, (i - 1 if i % 2 == 0 else i + 1) % count) for i in range(count)]


def total(parts):
    return functools.reduce(jnp.add, [p.astype(F32) for p in parts])


def body(queries, keys, values, out_grad, w_out, block_mask):
    q, k, v, g = queries[0], keys[0], values[0], out_grad[0]
    tokens, feats = q.shape
    width = g.shape[1]
    blocks = tokens // BLK
    ctx, dp = lax.axis_size("ctx"), lax.axis_size("dp")
    chips = ctx // 2
    at_ctx = lax.axis_index("ctx")
    rows, cols = feats // ctx, width // dp

    rim = vmem(RIM, feats)
    to_link, *to_chip = call_on_hbm(
        pack_kernel,
        [vmem(2, RIM, feats), rim, rim],
        k, v,
        scratch=[pltpu.SemaphoreType.DMA((4,))],
    )
    link = lax.ppermute(to_link, "ctx", over_links(ctx))
    chip_k, chip_v = (lax.ppermute(x, "ctx", swap(ctx, 1)) for x in to_chip)
    mask = lax.dynamic_slice_in_dim(block_mask[0], at_ctx * blocks, blocks, 0)
    bias = jnp.where(mask == 1, 0.0, BIG_NEGATIVE).astype(F32).reshape(blocks * CAND, 1, 1)
    bias = jnp.broadcast_to(bias, (blocks * CAND, 1, 2 * BLK))
    args = (q, k, v, g, w_out)
    own_keys = min(CAND, blocks) * BLK
    own_scores = (blocks, PAIRS, own_keys, 2 * BLK)
    rim_scores = (PAIRS, RIM, 2 * BLK)
    half = vmem(tokens // 2, width)
    q, k, v, g_low, g_high, w_out, own_t, stats, own_exps, grad_t = call_on_hbm(
        own_kernel,
        [vmem(tokens, feats)] * 3
        + [
            half,
            half,
            vmem(feats, width),
            vmem(blocks, feats, BLK, dtype=F32),
            vmem(2, blocks, PAIRS, 2 * BLK, dtype=F32),
            vmem(*own_scores, dtype=F32),
            vmem(blocks, feats, BLK),
        ],
        *args,
        beside=(bias,),
        scratch=[vmem(*own_scores), pltpu.SemaphoreType.DMA((6,))],
    )
    sibling_g = [
        pltpu.with_memory_space_constraint(lax.ppermute(x, "ctx", swap(ctx, 1)), pltpu.VMEM)
        for x in (g_low, g_high)
    ]
    chip_t, chip_stats, chip_exps = call(
        chip_kernel,
        [
            vmem(feats, BLK, dtype=F32),
            vmem(2, PAIRS, 2 * BLK, dtype=F32),
            vmem(*rim_scores, dtype=F32),
        ],
        10**6,
        bias, q, chip_k, chip_v, own_t, stats,
        scratch=[vmem(*rim_scores)],
    )
    attn_t, mine, other, link_exps, own_factors, rim_factors = call(
        forward_kernel,
        [
            vmem(blocks, feats, BLK),
            vmem(chips, rows, tokens),
            vmem(chips, rows, tokens),
            vmem(*rim_scores, dtype=F32),
            vmem(blocks, PAIRS, 2 * BLK, dtype=F32),
            vmem(2, PAIRS, 2 * BLK, dtype=F32),
        ],
        10**6,
        bias, q, link, own_t, stats, chip_t, chip_stats,
        scratch=[vmem(*rim_scores)],
    )

    other = lax.ppermute(other, "ctx", swap(ctx, 1))
    other = pltpu.with_memory_space_constraint(other, pltpu.VMEM)
    (product,) = call(product_kernel, [vmem(chips * rows, width, dtype=F32)], 10**6, mine, g_low, g_high)
    *halves, after = call(
        halves_kernel,
        [vmem(chips, rows, cols)] * dp + [vmem(8, 128, dtype=F32)],
        10**6,
        product, other, *sibling_g,
    )
    *back, deltas, rim_t = call(
        rim_kernel,
        [
            rim,
            rim,
            vmem(2, RIM, feats),
            vmem(blocks, PAIRS, 2 * BLK, dtype=F32),
            vmem(blocks, feats, BLK, dtype=F32),
        ],
        10**6,
        q, link, chip_k, chip_v, grad_t, attn_t, link_exps, chip_exps, rim_factors, after,
        scratch=[vmem(2, *rim_scores, dtype=F32), vmem(2, *rim_scores), vmem(2, *rim_scores)],
    )
    link_back = [lax.ppermute(x, "ctx", over_links(ctx)) for x in back[:2]]
    chip_back = lax.ppermute(back[2], "ctx", swap(ctx, 1))
    q_grad, k_own, v_own, after = call(
        own_backward_kernel,
        [
            hbm(tokens, feats),
            vmem(tokens, feats, dtype=F32),
            vmem(tokens, feats, dtype=F32),
            vmem(8, 128, dtype=F32),
        ],
        10**6,
        q, k, v, grad_t, own_exps, own_factors, deltas, rim_t,
        scratch=[vmem(*own_scores, dtype=F32), vmem(*own_scores), vmem(*own_scores)],
    )

    halves = [halves[0]] + [lax.ppermute(halves[s], "dp", swap(dp, s)) for s in range(dp - 1, 0, -1)]
    quarters = call(chips_kernel, [vmem(rows, cols)] * chips, 10**6, *halves, after)
    (output,) = call(output_kernel, [hbm(tokens, width)], 5 * 10**9, attn_t, w_out, quarters[0])
    quarters = [quarters[0]] + [
        lax.ppermute(quarters[s], "ctx", swap(ctx, 2 * s)) for s in range(chips - 1, 0, -1)
    ]
    (piece,) = call(
        functools.partial(piece_kernel, (dp * tokens * ctx) ** (-0.5), chips),
        [vmem(rows, cols)],
        10**6,
        *quarters, *link_back,
    )
    pieces = [piece] + [lax.ppermute(piece, "dp", swap(dp, s)) for s in range(dp - 1, 0, -1)]
    k_grad, v_grad, weight_grad = call(
        last_kernel,
        [hbm(tokens, feats), hbm(tokens, feats), hbm(rows, width, dtype=F32)],
        10**6,
        k_own, v_own, *link_back, chip_back, *pieces,
    )
    return (output[None], q_grad[None], k_grad[None], v_grad[None], weight_grad)


def solution(mesh):
    rows = P("dp", "ctx", None)
    return jax.shard_map(
        body,
        mesh=mesh,
        in_specs=(rows, rows, rows, rows, P(), P("dp", None, None)),
        out_specs=(rows, rows, rows, rows, P("ctx", None)),
        check_vma=False,
    )
```

```python
import functools

import jax
import jax.numpy as jnp
from jax import lax
from jax.experimental import pallas as pl
from jax.experimental.pallas import tpu as pltpu
from jax.sharding import PartitionSpec as P

HEADS = 8
HD = 64
BLK = 128
RAD = 1
CAND = 2 * RAD + 1
PAIRS = HEADS // 2
PAIR = 2 * HD
RIM = RAD * BLK
BIG_NEGATIVE = -1e30
SCALE = HD ** (-0.5)
BF16 = jnp.bfloat16
F32 = jnp.float32


def dot(a, b, contract):
    return lax.dot_general(a, b, (contract, ((), ())), preferred_element_type=F32)


def two_heads(block, axis):
    feature = lax.broadcasted_iota(jnp.int32, block.shape, axis)
    zero = jnp.zeros_like(block)
    return jnp.concatenate(
        [jnp.where(feature < HD, block, zero), jnp.where(feature < HD, zero, block)], axis=1 - axis
    )


def own_features(both):
    return jnp.concatenate([both[:HD, :BLK], both[HD:, BLK:]], axis=0)


def spread(row):
    return jnp.concatenate(
        [
            jnp.broadcast_to(row[:, :BLK], (HD, BLK)),
            jnp.broadcast_to(row[:, BLK:], (HD, BLK)),
        ],
        axis=0,
    )


def own_candidates(b, blocks):
    return max(0, RAD - b), min(CAND - 1, blocks - 1 - b + RAD)


def own_rows(b, blocks):
    first, last = own_candidates(b, blocks)
    return slice((b + first - RAD) * BLK, (b + last - RAD + 1) * BLK)


def masked(bias, b, c, part):
    return part + bias[b * CAND + c]


def pairs_of(blocks):
    for b in range(blocks):
        for p in range(PAIRS):
            yield b, slice(b * BLK, (b + 1) * BLK), slice(p * PAIR, (p + 1) * PAIR), p


def at_core():
    return lax.rem(lax.axis_index("ctx"), 2)


def rim_block(blocks, over_link):
    core = at_core()
    upper = core if over_link else 1 - core
    return upper * (blocks - 1), upper * (CAND - 1)


def rows_of(b):
    return pl.ds(pl.multiple_of(b * BLK, BLK), BLK)


def pack_kernel(k, v, to_link, chip_k, chip_v, sems):
    blocks = k.shape[0] // BLK
    link_rows = rows_of(rim_block(blocks, True)[0])
    chip_rows = rows_of(rim_block(blocks, False)[0])
    pairs = (
        (k.at[link_rows], to_link.at[0]),
        (v.at[link_rows], to_link.at[1]),
        (k.at[chip_rows], chip_k),
        (v.at[chip_rows], chip_v),
    )
    copies = [pltpu.make_async_copy(x, y, sems.at[i]) for i, (x, y) in enumerate(pairs)]
    for copy in copies:
        copy.start()
    for copy in copies:
        copy.wait()


def own_kernel(
    bias, q_arg, k_arg, v_arg, g_arg, w_arg,
    q, k, v, g_low, g_high, w_out, own_t, stats, exps, grad_t, rounded, sems,
):
    half = g_low.shape[0]
    pairs = (
        (q_arg, q),
        (k_arg, k),
        (v_arg, v),
        (g_arg.at[:half], g_low),
        (g_arg.at[half:], g_high),
        (w_arg, w_out),
    )
    copies = [pltpu.make_async_copy(x, y, sems.at[i]) for i, (x, y) in enumerate(pairs)]
    for copy in copies:
        copy.start()
    copies[0].wait()
    copies[1].wait()
    blocks = q.shape[0] // BLK
    for b, rows, cols, p in pairs_of(blocks):
        first, last = own_candidates(b, blocks)
        here = own_rows(b, blocks)
        scores = dot(k[here, cols], two_heads(q[rows, cols] * SCALE, 1), ((1,), (1,)))
        for c in range(first, last + 1):
            part = slice((c - first) * BLK, (c - first + 1) * BLK)
            value = scores[part]
            exps[b, p, part] = value if c == RAD else masked(bias, b, c, value)
    for b, rows, cols, p in pairs_of(blocks):
        here = own_rows(b, blocks)
        keys = slice(0, here.stop - here.start)
        scores = exps[b, p, keys]
        top = jnp.max(scores, axis=0, keepdims=True)
        e = jnp.exp(scores - top)
        exps[b, p, keys] = e
        rounded[b, p, keys] = e.astype(BF16)
        stats[0, b, p : p + 1] = top
        stats[1, b, p : p + 1] = jnp.sum(e, axis=0, keepdims=True)
    copies[2].wait()
    for b, rows, cols, p in pairs_of(blocks):
        here = own_rows(b, blocks)
        e = rounded[b, p, : here.stop - here.start]
        own_t[b, cols] = own_features(dot(v[here, cols], e, ((0,), (0,))))
    for copy in copies[3:]:
        copy.wait()
    both = jnp.concatenate([g_low[...], g_high[...]], axis=0)
    for b in range(blocks):
        rows = slice(b * BLK, (b + 1) * BLK)
        grad_t[b] = dot(w_out[...], both[rows], ((1,), (1,))).astype(BF16)


def pair_cols(p):
    return slice(p * PAIR, (p + 1) * PAIR)


def with_rim(bias, q, rim_k, rim_v, b, c, old, exps, rounded):
    for p in range(PAIRS):
        q2 = two_heads(q[rows_of(b), pair_cols(p)] * SCALE, 1)
        scores = dot(rim_k[:, pair_cols(p)], q2, ((1,), (1,)))
        exps[p] = masked(bias, b, c, scores)
    results = []
    for p in range(PAIRS):
        old_top, old_sum = old(p)
        scores = exps[p]
        top = jnp.maximum(old_top, jnp.max(scores, axis=0, keepdims=True))
        kept = jnp.exp(old_top - top)
        e = jnp.exp(scores - top)
        exps[p] = e
        rounded[p] = e.astype(BF16)
        results.append((top, kept, old_sum * kept + jnp.sum(e, axis=0, keepdims=True)))
    parts = [
        own_features(dot(rim_v[:, pair_cols(p)], rounded[p], ((0,), (0,)))) for p in range(PAIRS)
    ]
    return [(*result, part) for result, part in zip(results, parts)]


def chip_kernel(bias, q, rim_k, rim_v, own_t, stats, chip_t, chip_stats, exps, rounded):
    blocks = q.shape[0] // BLK
    b, c = rim_block(blocks, False)

    def old(p):
        return stats[0, b, p : p + 1], stats[1, b, p : p + 1]

    results = with_rim(bias, q, rim_k, rim_v, b, c, old, exps, rounded)
    for p, (top, kept, count, part) in enumerate(results):
        at = slice(p, p + 1)
        if blocks == 1:
            chip_t[pair_cols(p)] = own_t[b, pair_cols(p)] * spread(kept) + part
            chip_stats[0, at], chip_stats[1, at] = top, count
        else:
            share = 1.0 / count
            attn = own_t[b, pair_cols(p)] * spread(kept * share) + part * spread(share)
            chip_t[pair_cols(p)] = attn
            chip_stats[0, at], chip_stats[1, at] = share, kept * share


def forward_kernel(
    bias, q, rim, own_t, stats, chip_t, chip_stats,
    attn_t, mine, other, exps, own_factors, rim_factors, rounded,
):
    blocks = q.shape[0] // BLK
    b, c = rim_block(blocks, True)
    at_chip, _ = rim_block(blocks, False)

    def old(p):
        at = slice(p, p + 1)
        if blocks == 1:
            return chip_stats[0, at], chip_stats[1, at]
        return stats[0, b, at], stats[1, b, at]

    results = with_rim(bias, q, rim.at[0], rim.at[1], b, c, old, exps, rounded)
    for p, (top, kept, count, part) in enumerate(results):
        at = slice(p, p + 1)
        cols = pair_cols(p)
        base = chip_t[cols] if blocks == 1 else own_t[b, cols]
        share = 1.0 / count
        attn_t[b, cols] = (base * spread(kept * share) + part * spread(share)).astype(BF16)
        rim_factors[0, at] = share
        if blocks == 1:
            rim_factors[1, at] = kept * share
            own_factors[0, at] = jnp.exp(stats[0, 0, at] - top) * share
        else:
            own_factors[b, at] = kept * share
            attn_t[at_chip, cols] = chip_t[cols].astype(BF16)
            rim_factors[1, at] = chip_stats[0, at]
            own_factors[at_chip, at] = chip_stats[1, at]
        for inner in range(1, blocks - 1):
            share = 1.0 / stats[1, inner, at]
            attn_t[inner, cols] = (own_t[inner, cols] * spread(share)).astype(BF16)
            own_factors[inner, at] = share
    first_core = at_core() == 0
    chips, rows, _ = mine.shape
    for i in range(chips):
        for block in range(blocks):
            tokens = slice(block * BLK, (block + 1) * BLK)
            even = attn_t[block, 2 * i * rows : (2 * i + 1) * rows]
            odd = attn_t[block, (2 * i + 1) * rows : (2 * i + 2) * rows]
            mine[i, :, tokens] = jnp.where(first_core, even, odd)
            other[i, :, tokens] = jnp.where(first_core, odd, even)


def flat_dot(attn, g_low, g_high):
    chips, rows, tokens = attn.shape
    g = jnp.concatenate([g_low[...], g_high[...]], axis=0)
    return dot(attn[...].reshape(chips * rows, tokens), g, ((1,), (0,)))


def product_kernel(mine, g_low, g_high, product):
    product[...] = flat_dot(mine, g_low, g_high)


def score_grads(probs, dprob, delta):
    return (probs * (dprob - delta)).astype(BF16), probs.astype(BF16)


def rim_kernel(
    q, link, chip_k, chip_v, grad_t, attn_t, link_exps, chip_exps, rim_factors, before,
    link_back, chip_back, deltas, query_t, dprobs, dscores, rounded,
):
    blocks = q.shape[0] // BLK
    sides = (
        (rim_block(blocks, True)[0], link.at[0], link.at[1], link_exps, link_back.at[0], link_back.at[1]),
        (rim_block(blocks, False)[0], chip_k, chip_v, chip_exps, chip_back.at[0], chip_back.at[1]),
    )
    for i, (b, _, rim_v, _, _, _) in enumerate(sides):
        for p in range(PAIRS):
            g2_t = two_heads(grad_t[b, pair_cols(p)], 0)
            dprobs[i, p] = dot(rim_v[:, pair_cols(p)], g2_t, ((1,), (0,)))
    for b, _, cols, p in pairs_of(blocks):
        product = grad_t[b, cols].astype(F32) * attn_t[b, cols].astype(F32)
        deltas[b, p : p + 1] = jnp.concatenate(
            [
                jnp.sum(product[:HD], axis=0, keepdims=True),
                jnp.sum(product[HD:], axis=0, keepdims=True),
            ],
            axis=1,
        )
    query_t[...] = jnp.zeros_like(query_t)
    for i, (b, _, _, exps, _, _) in enumerate(sides):
        for p in range(PAIRS):
            at = slice(p, p + 1)
            dscores[i, p], rounded[i, p] = score_grads(
                exps[p] * rim_factors[i, at], dprobs[i, p], deltas[b, at]
            )
    for i, (b, rim_k, _, _, k_back, v_back) in enumerate(sides):
        for p in range(PAIRS):
            cols = pair_cols(p)
            q2 = two_heads(q[rows_of(b), cols] * SCALE, 1)
            g2_t = two_heads(grad_t[b, cols], 0)
            k_back[:, cols] = dot(dscores[i, p], q2, ((1,), (0,))).astype(BF16)
            v_back[:, cols] = dot(rounded[i, p], g2_t, ((1,), (1,))).astype(BF16)
            query_t[b, cols] += own_features(dot(rim_k[:, cols], dscores[i, p], ((0,), (0,))))


def own_backward_kernel(
    q, k, v, grad_t, exps, factors, deltas, rim_t,
    q_grad, k_own, v_own, after, dprobs, dscores, rounded,
):
    blocks = q.shape[0] // BLK
    for b, _, cols, p in pairs_of(blocks):
        here = own_rows(b, blocks)
        g2_t = two_heads(grad_t[b, cols], 0)
        dprobs[b, p, : here.stop - here.start] = dot(v[here, cols], g2_t, ((1,), (0,)))
    for b, _, _, p in pairs_of(blocks):
        here = own_rows(b, blocks)
        keys = slice(0, here.stop - here.start)
        dscores[b, p, keys], rounded[b, p, keys] = score_grads(
            exps[b, p, keys] * factors[b, p : p + 1], dprobs[b, p, keys], deltas[b, p : p + 1]
        )
    k_sums, v_sums = {}, {}
    for b, rows, cols, p in pairs_of(blocks):
        here = own_rows(b, blocks)
        keys = slice(0, here.stop - here.start)
        q2 = two_heads(q[rows, cols] * SCALE, 1)
        g2_t = two_heads(grad_t[b, cols], 0)
        dscore = dscores[b, p, keys]
        k_part = dot(dscore, q2, ((1,), (0,)))
        v_part = dot(rounded[b, p, keys], g2_t, ((1,), (1,)))
        for at in range(here.start, here.stop, BLK):
            part = slice(at - here.start, at - here.start + BLK)
            for sums, value in ((k_sums, k_part), (v_sums, v_part)):
                sums.setdefault((at, p), []).append(value[part])
        query_t = own_features(dot(k[here, cols], dscore, ((0,), (0,)))) + rim_t[b, cols]
        q_grad[rows, cols] = (query_t * SCALE).T.astype(BF16)
    for out, sums in ((k_own, k_sums), (v_own, v_sums)):
        for (at, p), values in sums.items():
            out[at : at + BLK, pair_cols(p)] = functools.reduce(jnp.add, values)
    after[...] = jnp.zeros_like(after)


def output_kernel(attn_t, w_out, before, output):
    for b in range(attn_t.shape[0]):
        part = dot(attn_t[b], w_out[...], ((0,), (0,)))
        output[b * BLK : (b + 1) * BLK] = part.astype(BF16)


def halves_kernel(product, other, g_low, g_high, *outs):
    pieces, after = outs[:-1], outs[-1]
    at_dp = lax.axis_index("dp")
    chips, rows, cols = pieces[0].shape
    both = (product[...] + flat_dot(other, g_low, g_high)).astype(BF16)
    for d in range(len(pieces)):
        value = both[:, d * cols : (d + 1) * cols].reshape(chips, rows, cols)
        for s in range(len(pieces)):

            @pl.when((at_dp ^ s) == d)
            def _(s=s, value=value):
                pieces[s][...] = value

    after[...] = jnp.zeros_like(after)


def chips_kernel(*refs):
    parts, outs = refs[: lax.axis_size("dp")], refs[lax.axis_size("dp") + 1 :]
    chip = lax.div(lax.axis_index("ctx"), 2)
    for s, out in enumerate(outs):
        out[...] = total([part[chip ^ s] for part in parts]).astype(BF16)


def piece_kernel(scale, count, *refs):
    refs[-1][...] = (total([part[...] for part in refs[:count]]) * scale).astype(BF16)


def last_kernel(k_own, v_own, link_kv, chip_kv, *refs):
    pieces, (k_grad, v_grad, weight_grad) = refs[:1] + refs[-4:0:-1], refs[-3:]
    tokens = k_own.shape[0]
    first_core = at_core() == 0
    for i, (own, grad) in enumerate(((k_own, k_grad), (v_own, v_grad))):
        link, chip = link_kv[i].astype(F32), chip_kv[i].astype(F32)
        low = jnp.where(first_core, link, chip)
        high = jnp.where(first_core, chip, link)
        if tokens == RIM:
            grad[...] = (own[...] + low + high).astype(BF16)
        else:
            grad[:RIM] = (own[:RIM] + low).astype(BF16)
            if tokens > 2 * RIM:
                grad[RIM : tokens - RIM] = own[RIM : tokens - RIM].astype(BF16)
            grad[tokens - RIM :] = (own[tokens - RIM :] + high).astype(BF16)
    at_dp = lax.axis_index("dp")
    cols = pieces[0].shape[1]
    for d in range(len(pieces)):
        value = pieces[0][...]
        for s in range(1, len(pieces)):
            value = jnp.where((at_dp ^ s) == d, pieces[s][...], value)
        weight_grad[:, d * cols : (d + 1) * cols] = value.astype(F32)


def vmem(*shape, dtype=BF16):
    return pltpu.VMEM(shape, dtype)


def hbm(*shape, dtype=BF16):
    return jax.ShapeDtypeStruct(shape, dtype)


def call(kernel, outs, flops, *args, scratch=()):
    in_vmem = pl.BlockSpec(memory_space=pltpu.VMEM)
    return pl.pallas_call(
        kernel,
        out_shape=outs,
        in_specs=[in_vmem] * len(args),
        out_specs=[in_vmem] * len(outs),
        scratch_shapes=list(scratch),
        compiler_params=pltpu.CompilerParams(vmem_limit_bytes=24 * 1024 * 1024),
        cost_estimate=pl.CostEstimate(flops=flops, bytes_accessed=flops // 250, transcendentals=0),
    )(*args)


def call_on_hbm(kernel, outs, *args, beside=(), scratch=()):
    return pl.pallas_call(
        kernel,
        out_shape=outs,
        in_specs=[pl.BlockSpec(memory_space=pltpu.VMEM)] * len(beside)
        + [pl.BlockSpec(memory_space=pltpu.HBM)] * len(args),
        out_specs=[pl.BlockSpec(memory_space=pltpu.VMEM)] * len(outs),
        scratch_shapes=list(scratch),
        compiler_params=pltpu.CompilerParams(vmem_limit_bytes=8 * 1024 * 1024),
        cost_estimate=pl.CostEstimate(flops=10**6, bytes_accessed=4096, transcendentals=0),
    )(*beside, *(pltpu.with_memory_space_constraint(x, pltpu.HBM) for x in args))


def swap(count, bits):
    return [(i, i ^ bits) for i in range(count)]


def over_links(count):
    return [(i, (i - 1 if i % 2 == 0 else i + 1) % count) for i in range(count)]


def total(parts):
    return functools.reduce(jnp.add, [p.astype(F32) for p in parts])


def body(queries, keys, values, out_grad, w_out, block_mask):
    q, k, v, g = queries[0], keys[0], values[0], out_grad[0]
    tokens, feats = q.shape
    width = g.shape[1]
    blocks = tokens // BLK
    ctx, dp = lax.axis_size("ctx"), lax.axis_size("dp")
    chips = ctx // 2
    at_ctx = lax.axis_index("ctx")
    rows, cols = feats // ctx, width // dp

    rim = vmem(RIM, feats)
    to_link, *to_chip = call_on_hbm(
        pack_kernel,
        [vmem(2, RIM, feats), rim, rim],
        k, v,
        scratch=[pltpu.SemaphoreType.DMA((4,))],
    )
    link = lax.ppermute(to_link, "ctx", over_links(ctx))
    chip_k, chip_v = (lax.ppermute(x, "ctx", swap(ctx, 1)) for x in to_chip)
    mask = lax.dynamic_slice_in_dim(block_mask[0], at_ctx * blocks, blocks, 0)
    bias = jnp.where(mask == 1, 0.0, BIG_NEGATIVE).astype(F32).reshape(blocks * CAND, 1, 1)
    bias = jnp.broadcast_to(bias, (blocks * CAND, 1, 2 * BLK))
    args = (q, k, v, g, w_out)
    own_keys = min(CAND, blocks) * BLK
    own_scores = (blocks, PAIRS, own_keys, 2 * BLK)
    rim_scores = (PAIRS, RIM, 2 * BLK)
    half = vmem(tokens // 2, width)
    q, k, v, g_low, g_high, w_out, own_t, stats, own_exps, grad_t = call_on_hbm(
        own_kernel,
        [vmem(tokens, feats)] * 3
        + [
            half,
            half,
            vmem(feats, width),
            vmem(blocks, feats, BLK, dtype=F32),
            vmem(2, blocks, PAIRS, 2 * BLK, dtype=F32),
            vmem(*own_scores, dtype=F32),
            vmem(blocks, feats, BLK),
        ],
        *args,
        beside=(bias,),
        scratch=[vmem(*own_scores), pltpu.SemaphoreType.DMA((6,))],
    )
    sibling_g = [
        pltpu.with_memory_space_constraint(lax.ppermute(x, "ctx", swap(ctx, 1)), pltpu.VMEM)
        for x in (g_low, g_high)
    ]
    chip_t, chip_stats, chip_exps = call(
        chip_kernel,
        [
            vmem(feats, BLK, dtype=F32),
            vmem(2, PAIRS, 2 * BLK, dtype=F32),
            vmem(*rim_scores, dtype=F32),
        ],
        10**6,
        bias, q, chip_k, chip_v, own_t, stats,
        scratch=[vmem(*rim_scores)],
    )
    attn_t, mine, other, link_exps, own_factors, rim_factors = call(
        forward_kernel,
        [
            vmem(blocks, feats, BLK),
            vmem(chips, rows, tokens),
            vmem(chips, rows, tokens),
            vmem(*rim_scores, dtype=F32),
            vmem(blocks, PAIRS, 2 * BLK, dtype=F32),
            vmem(2, PAIRS, 2 * BLK, dtype=F32),
        ],
        10**6,
        bias, q, link, own_t, stats, chip_t, chip_stats,
        scratch=[vmem(*rim_scores)],
    )

    other = lax.ppermute(other, "ctx", swap(ctx, 1))
    other = pltpu.with_memory_space_constraint(other, pltpu.VMEM)
    (product,) = call(product_kernel, [vmem(chips * rows, width, dtype=F32)], 10**6, mine, g_low, g_high)
    *halves, after = call(
        halves_kernel,
        [vmem(chips, rows, cols)] * dp + [vmem(8, 128, dtype=F32)],
        10**6,
        product, other, *sibling_g,
    )
    *back, deltas, rim_t = call(
        rim_kernel,
        [
            vmem(2, RIM, feats),
            vmem(2, RIM, feats),
            vmem(blocks, PAIRS, 2 * BLK, dtype=F32),
            vmem(blocks, feats, BLK, dtype=F32),
        ],
        10**6,
        q, link, chip_k, chip_v, grad_t, attn_t, link_exps, chip_exps, rim_factors, after,
        scratch=[vmem(2, *rim_scores, dtype=F32), vmem(2, *rim_scores), vmem(2, *rim_scores)],
    )
    link_back = lax.ppermute(back[0], "ctx", over_links(ctx))
    chip_back = lax.ppermute(back[1], "ctx", swap(ctx, 1))
    q_grad, k_own, v_own, after = call(
        own_backward_kernel,
        [
            hbm(tokens, feats),
            vmem(tokens, feats, dtype=F32),
            vmem(tokens, feats, dtype=F32),
            vmem(8, 128, dtype=F32),
        ],
        5 * 10**9,
        q, k, v, grad_t, own_exps, own_factors, deltas, rim_t,
        scratch=[vmem(*own_scores, dtype=F32), vmem(*own_scores), vmem(*own_scores)],
    )

    halves = [halves[0]] + [lax.ppermute(halves[s], "dp", swap(dp, s)) for s in range(dp - 1, 0, -1)]
    quarters = call(chips_kernel, [vmem(rows, cols)] * chips, 10**6, *halves, after)
    (output,) = call(output_kernel, [hbm(tokens, width)], 5 * 10**9, attn_t, w_out, quarters[0])
    quarters = [quarters[0]] + [
        lax.ppermute(quarters[s], "ctx", swap(ctx, 2 * s)) for s in range(chips - 1, 0, -1)
    ]
    (piece,) = call(
        functools.partial(piece_kernel, (dp * tokens * ctx) ** (-0.5), chips),
        [vmem(rows, cols)],
        10**6,
        *quarters, link_back,
    )
    pieces = [piece] + [lax.ppermute(piece, "dp", swap(dp, s)) for s in range(dp - 1, 0, -1)]
    k_grad, v_grad, weight_grad = call(
        last_kernel,
        [hbm(tokens, feats), hbm(tokens, feats), hbm(rows, width, dtype=F32)],
        10**6,
        k_own, v_own, link_back, chip_back, *pieces,
    )
    return (output[None], q_grad[None], k_grad[None], v_grad[None], weight_grad)


def solution(mesh):
    rows = P("dp", "ctx", None)
    return jax.shard_map(
        body,
        mesh=mesh,
        in_specs=(rows, rows, rows, rows, P(), P("dp", None, None)),
        out_specs=(rows, rows, rows, rows, P("ctx", None)),
        check_vma=False,
    )
```

```python
import functools

import jax
import jax.numpy as jnp
from jax import lax
from jax.experimental import pallas as pl
from jax.experimental.pallas import tpu as pltpu
from jax.sharding import PartitionSpec as P

HEADS = 8
HD = 64
BLK = 128
RAD = 1
CAND = 2 * RAD + 1
PAIRS = HEADS // 2
PAIR = 2 * HD
RIM = RAD * BLK
BIG_NEGATIVE = -1e30
SCALE = HD ** (-0.5)
BF16 = jnp.bfloat16
F32 = jnp.float32


def dot(a, b, contract):
    return lax.dot_general(a, b, (contract, ((), ())), preferred_element_type=F32)


def two_heads(block, axis):
    feature = lax.broadcasted_iota(jnp.int32, block.shape, axis)
    zero = jnp.zeros_like(block)
    return jnp.concatenate(
        [jnp.where(feature < HD, block, zero), jnp.where(feature < HD, zero, block)], axis=1 - axis
    )


def own_features(both):
    return jnp.concatenate([both[:HD, :BLK], both[HD:, BLK:]], axis=0)


def spread(row):
    return jnp.concatenate(
        [
            jnp.broadcast_to(row[:, :BLK], (HD, BLK)),
            jnp.broadcast_to(row[:, BLK:], (HD, BLK)),
        ],
        axis=0,
    )


def own_candidates(b, blocks):
    return max(0, RAD - b), min(CAND - 1, blocks - 1 - b + RAD)


def own_rows(b, blocks):
    first, last = own_candidates(b, blocks)
    return slice((b + first - RAD) * BLK, (b + last - RAD + 1) * BLK)


def masked(bias, b, c, part):
    return part + bias[b * CAND + c]


def pairs_of(blocks):
    for b in range(blocks):
        for p in range(PAIRS):
            yield b, slice(b * BLK, (b + 1) * BLK), slice(p * PAIR, (p + 1) * PAIR), p


def at_core():
    return lax.rem(lax.axis_index("ctx"), 2)


def rim_block(blocks, over_link):
    core = at_core()
    upper = core if over_link else 1 - core
    return upper * (blocks - 1), upper * (CAND - 1)


def rows_of(b):
    return pl.ds(pl.multiple_of(b * BLK, BLK), BLK)


def pack_kernel(k, v, to_link, chip_k, chip_v, sems):
    blocks = k.shape[0] // BLK
    link_rows = rows_of(rim_block(blocks, True)[0])
    chip_rows = rows_of(rim_block(blocks, False)[0])
    pairs = (
        (k.at[link_rows], to_link.at[0]),
        (v.at[link_rows], to_link.at[1]),
        (k.at[chip_rows], chip_k),
        (v.at[chip_rows], chip_v),
    )
    copies = [pltpu.make_async_copy(x, y, sems.at[i]) for i, (x, y) in enumerate(pairs)]
    for copy in copies:
        copy.start()
    for copy in copies:
        copy.wait()


def own_kernel(
    bias, q_arg, k_arg, v_arg, g_arg, w_arg,
    q, k, v, g_low, g_high, w_out, own_t, stats, exps, grad_t, rounded, sems,
):
    half = g_low.shape[0]
    pairs = (
        (q_arg, q),
        (k_arg, k),
        (v_arg, v),
        (g_arg.at[:half], g_low),
        (g_arg.at[half:], g_high),
        (w_arg, w_out),
    )
    copies = [pltpu.make_async_copy(x, y, sems.at[i]) for i, (x, y) in enumerate(pairs)]
    for copy in copies:
        copy.start()
    copies[0].wait()
    copies[1].wait()
    blocks = q.shape[0] // BLK
    for b, rows, cols, p in pairs_of(blocks):
        first, last = own_candidates(b, blocks)
        here = own_rows(b, blocks)
        scores = dot(k[here, cols], two_heads(q[rows, cols] * SCALE, 1), ((1,), (1,)))
        for c in range(first, last + 1):
            part = slice((c - first) * BLK, (c - first + 1) * BLK)
            value = scores[part]
            exps[b, p, part] = value if c == RAD else masked(bias, b, c, value)
    for b, rows, cols, p in pairs_of(blocks):
        here = own_rows(b, blocks)
        keys = slice(0, here.stop - here.start)
        scores = exps[b, p, keys]
        top = jnp.max(scores, axis=0, keepdims=True)
        e = jnp.exp(scores - top)
        exps[b, p, keys] = e
        rounded[b, p, keys] = e.astype(BF16)
        stats[0, b, p : p + 1] = top
        stats[1, b, p : p + 1] = jnp.sum(e, axis=0, keepdims=True)
    copies[2].wait()
    for b, rows, cols, p in pairs_of(blocks):
        here = own_rows(b, blocks)
        e = rounded[b, p, : here.stop - here.start]
        own_t[b, cols] = own_features(dot(v[here, cols], e, ((0,), (0,))))
    for copy in copies[3:]:
        copy.wait()
    both = jnp.concatenate([g_low[...], g_high[...]], axis=0)
    for b in range(blocks):
        rows = slice(b * BLK, (b + 1) * BLK)
        grad_t[b] = dot(w_out[...], both[rows], ((1,), (1,))).astype(BF16)


def pair_cols(p):
    return slice(p * PAIR, (p + 1) * PAIR)


def with_rim(bias, q, rim_k, rim_v, b, c, old, exps, rounded):
    for p in range(PAIRS):
        q2 = two_heads(q[rows_of(b), pair_cols(p)] * SCALE, 1)
        scores = dot(rim_k[:, pair_cols(p)], q2, ((1,), (1,)))
        exps[p] = masked(bias, b, c, scores)
    results = []
    for p in range(PAIRS):
        old_top, old_sum = old(p)
        scores = exps[p]
        top = jnp.maximum(old_top, jnp.max(scores, axis=0, keepdims=True))
        kept = jnp.exp(old_top - top)
        e = jnp.exp(scores - top)
        exps[p] = e
        rounded[p] = e.astype(BF16)
        results.append((top, kept, old_sum * kept + jnp.sum(e, axis=0, keepdims=True)))
    parts = [
        own_features(dot(rim_v[:, pair_cols(p)], rounded[p], ((0,), (0,)))) for p in range(PAIRS)
    ]
    return [(*result, part) for result, part in zip(results, parts)]


def chip_kernel(bias, q, rim_k, rim_v, own_t, stats, chip_t, chip_stats, exps, rounded):
    blocks = q.shape[0] // BLK
    b, c = rim_block(blocks, False)

    def old(p):
        return stats[0, b, p : p + 1], stats[1, b, p : p + 1]

    results = with_rim(bias, q, rim_k, rim_v, b, c, old, exps, rounded)
    for p, (top, kept, count, part) in enumerate(results):
        at = slice(p, p + 1)
        if blocks == 1:
            chip_t[pair_cols(p)] = own_t[b, pair_cols(p)] * spread(kept) + part
            chip_stats[0, at], chip_stats[1, at] = top, count
        else:
            share = 1.0 / count
            attn = own_t[b, pair_cols(p)] * spread(kept * share) + part * spread(share)
            chip_t[pair_cols(p)] = attn
            chip_stats[0, at], chip_stats[1, at] = share, kept * share


def forward_kernel(
    bias, q, rim, own_t, stats, chip_t, chip_stats,
    attn_t, mine, other, exps, own_factors, rim_factors, rounded,
):
    blocks = q.shape[0] // BLK
    b, c = rim_block(blocks, True)
    at_chip, _ = rim_block(blocks, False)

    def old(p):
        at = slice(p, p + 1)
        if blocks == 1:
            return chip_stats[0, at], chip_stats[1, at]
        return stats[0, b, at], stats[1, b, at]

    results = with_rim(bias, q, rim.at[0], rim.at[1], b, c, old, exps, rounded)
    for p, (top, kept, count, part) in enumerate(results):
        at = slice(p, p + 1)
        cols = pair_cols(p)
        base = chip_t[cols] if blocks == 1 else own_t[b, cols]
        share = 1.0 / count
        attn_t[b, cols] = (base * spread(kept * share) + part * spread(share)).astype(BF16)
        rim_factors[0, at] = share
        if blocks == 1:
            rim_factors[1, at] = kept * share
            own_factors[0, at] = jnp.exp(stats[0, 0, at] - top) * share
        else:
            own_factors[b, at] = kept * share
            attn_t[at_chip, cols] = chip_t[cols].astype(BF16)
            rim_factors[1, at] = chip_stats[0, at]
            own_factors[at_chip, at] = chip_stats[1, at]
        for inner in range(1, blocks - 1):
            share = 1.0 / stats[1, inner, at]
            attn_t[inner, cols] = (own_t[inner, cols] * spread(share)).astype(BF16)
            own_factors[inner, at] = share
    first_core = at_core() == 0
    chips, rows, _ = mine.shape
    for i in range(chips):
        for block in range(blocks):
            tokens = slice(block * BLK, (block + 1) * BLK)
            even = attn_t[block, 2 * i * rows : (2 * i + 1) * rows]
            odd = attn_t[block, (2 * i + 1) * rows : (2 * i + 2) * rows]
            mine[i, :, tokens] = jnp.where(first_core, even, odd)
            other[i, :, tokens] = jnp.where(first_core, odd, even)


def flat_dot(attn, g_low, g_high):
    chips, rows, tokens = attn.shape
    g = jnp.concatenate([g_low[...], g_high[...]], axis=0)
    return dot(attn[...].reshape(chips * rows, tokens), g, ((1,), (0,)))


def product_kernel(mine, g_low, g_high, product):
    product[...] = flat_dot(mine, g_low, g_high)


def score_grads(probs, dprob, delta):
    return (probs * (dprob - delta)).astype(BF16), probs.astype(BF16)


def rim_kernel(
    q, link, chip_k, chip_v, grad_t, attn_t, link_exps, chip_exps, rim_factors, before,
    link_back, chip_back, deltas, query_t, dprobs, dscores, rounded,
):
    blocks = q.shape[0] // BLK
    sides = (
        (rim_block(blocks, True)[0], link.at[0], link.at[1], link_exps, link_back.at[0], link_back.at[1]),
        (rim_block(blocks, False)[0], chip_k, chip_v, chip_exps, chip_back.at[0], chip_back.at[1]),
    )
    for i, (b, _, rim_v, _, _, _) in enumerate(sides):
        for p in range(PAIRS):
            g2_t = two_heads(grad_t[b, pair_cols(p)], 0)
            dprobs[i, p] = dot(rim_v[:, pair_cols(p)], g2_t, ((1,), (0,)))
    for b, _, cols, p in pairs_of(blocks):
        product = grad_t[b, cols].astype(F32) * attn_t[b, cols].astype(F32)
        deltas[b, p : p + 1] = jnp.concatenate(
            [
                jnp.sum(product[:HD], axis=0, keepdims=True),
                jnp.sum(product[HD:], axis=0, keepdims=True),
            ],
            axis=1,
        )
    query_t[...] = jnp.zeros_like(query_t)
    for i, (b, _, _, exps, _, _) in enumerate(sides):
        for p in range(PAIRS):
            at = slice(p, p + 1)
            dscores[i, p], rounded[i, p] = score_grads(
                exps[p] * rim_factors[i, at], dprobs[i, p], deltas[b, at]
            )
    for i, (b, rim_k, _, _, k_back, v_back) in enumerate(sides):
        for p in range(PAIRS):
            cols = pair_cols(p)
            q2 = two_heads(q[rows_of(b), cols] * SCALE, 1)
            g2_t = two_heads(grad_t[b, cols], 0)
            k_back[:, cols] = dot(dscores[i, p], q2, ((1,), (0,))).astype(BF16)
            v_back[:, cols] = dot(rounded[i, p], g2_t, ((1,), (1,))).astype(BF16)
            query_t[b, cols] += own_features(dot(rim_k[:, cols], dscores[i, p], ((0,), (0,))))


def own_backward_kernel(
    q, k, v, grad_t, exps, factors, deltas, rim_t,
    q_grad, k_own, v_own, after, dprobs, dscores, rounded,
):
    blocks = q.shape[0] // BLK
    for b, _, cols, p in pairs_of(blocks):
        here = own_rows(b, blocks)
        g2_t = two_heads(grad_t[b, cols], 0)
        dprobs[b, p, : here.stop - here.start] = dot(v[here, cols], g2_t, ((1,), (0,)))
    for b, _, _, p in pairs_of(blocks):
        here = own_rows(b, blocks)
        keys = slice(0, here.stop - here.start)
        dscores[b, p, keys], rounded[b, p, keys] = score_grads(
            exps[b, p, keys] * factors[b, p : p + 1], dprobs[b, p, keys], deltas[b, p : p + 1]
        )
    k_sums, v_sums = {}, {}
    for b, rows, cols, p in pairs_of(blocks):
        here = own_rows(b, blocks)
        keys = slice(0, here.stop - here.start)
        q2 = two_heads(q[rows, cols] * SCALE, 1)
        g2_t = two_heads(grad_t[b, cols], 0)
        dscore = dscores[b, p, keys]
        k_part = dot(dscore, q2, ((1,), (0,)))
        v_part = dot(rounded[b, p, keys], g2_t, ((1,), (1,)))
        for at in range(here.start, here.stop, BLK):
            part = slice(at - here.start, at - here.start + BLK)
            for sums, value in ((k_sums, k_part), (v_sums, v_part)):
                sums.setdefault((at, p), []).append(value[part])
        query_t = own_features(dot(k[here, cols], dscore, ((0,), (0,)))) + rim_t[b, cols]
        q_grad[rows, cols] = (query_t * SCALE).T.astype(BF16)
    for out, sums in ((k_own, k_sums), (v_own, v_sums)):
        for (at, p), values in sums.items():
            out[at : at + BLK, pair_cols(p)] = functools.reduce(jnp.add, values)
    after[...] = jnp.zeros_like(after)


def output_kernel(attn_t, w_out, before, output):
    for b in range(attn_t.shape[0]):
        part = dot(attn_t[b], w_out[...], ((0,), (0,)))
        output[b * BLK : (b + 1) * BLK] = part.astype(BF16)


def halves_kernel(product, other, g_low, g_high, *outs):
    pieces, after = outs[:-1], outs[-1]
    at_dp = lax.axis_index("dp")
    chips, rows, cols = pieces[0].shape
    if cols % BLK == 0:
        flat = other[...].reshape(chips * rows, other.shape[2])
        for s in range(len(pieces)):
            at = pl.ds(pl.multiple_of((at_dp ^ s) * cols, BLK), cols)
            g = jnp.concatenate([g_low[:, at], g_high[:, at]], axis=0)
            value = product[:, at] + dot(flat, g, ((1,), (0,)))
            pieces[s][...] = value.astype(BF16).reshape(chips, rows, cols)
    else:
        both = (product[...] + flat_dot(other, g_low, g_high)).astype(BF16)
        for d in range(len(pieces)):
            value = both[:, d * cols : (d + 1) * cols].reshape(chips, rows, cols)
            for s in range(len(pieces)):

                @pl.when((at_dp ^ s) == d)
                def _(s=s, value=value):
                    pieces[s][...] = value

    after[...] = jnp.zeros_like(after)


def chips_kernel(*refs):
    parts, outs = refs[: lax.axis_size("dp")], refs[lax.axis_size("dp") + 1 :]
    chip = lax.div(lax.axis_index("ctx"), 2)
    for s, out in enumerate(outs):
        out[...] = total([part[chip ^ s] for part in parts]).astype(BF16)


def piece_kernel(scale, count, *refs):
    refs[-1][...] = (total([part[...] for part in refs[:count]]) * scale).astype(BF16)


def rim_sum_kernel(k_own, v_own, link_kv, chip_kv, k_grad, v_grad):
    tokens = k_own.shape[0]
    first_core = at_core() == 0
    for i, (own, grad) in enumerate(((k_own, k_grad), (v_own, v_grad))):
        link, chip = link_kv[i].astype(F32), chip_kv[i].astype(F32)
        low = jnp.where(first_core, link, chip)
        high = jnp.where(first_core, chip, link)
        if tokens == RIM:
            grad[...] = (own[...] + low + high).astype(BF16)
        else:
            grad[:RIM] = (own[:RIM] + low).astype(BF16)
            if tokens > 2 * RIM:
                grad[RIM : tokens - RIM] = own[RIM : tokens - RIM].astype(BF16)
            grad[tokens - RIM :] = (own[tokens - RIM :] + high).astype(BF16)


def columns_kernel(*refs):
    pieces, weight_grad = refs[:1] + refs[-2:0:-1], refs[-1]
    at_dp = lax.axis_index("dp")
    cols = pieces[0].shape[1]
    for d in range(len(pieces)):
        value = pieces[0][...]
        for s in range(1, len(pieces)):
            value = jnp.where((at_dp ^ s) == d, pieces[s][...], value)
        weight_grad[:, d * cols : (d + 1) * cols] = value.astype(F32)


def vmem(*shape, dtype=BF16):
    return pltpu.VMEM(shape, dtype)


def hbm(*shape, dtype=BF16):
    return jax.ShapeDtypeStruct(shape, dtype)


def call(kernel, outs, flops, *args, scratch=()):
    in_vmem = pl.BlockSpec(memory_space=pltpu.VMEM)
    return pl.pallas_call(
        kernel,
        out_shape=outs,
        in_specs=[in_vmem] * len(args),
        out_specs=[in_vmem] * len(outs),
        scratch_shapes=list(scratch),
        compiler_params=pltpu.CompilerParams(vmem_limit_bytes=24 * 1024 * 1024),
        cost_estimate=pl.CostEstimate(flops=flops, bytes_accessed=flops // 250, transcendentals=0),
    )(*args)


def call_on_hbm(kernel, outs, *args, beside=(), scratch=()):
    return pl.pallas_call(
        kernel,
        out_shape=outs,
        in_specs=[pl.BlockSpec(memory_space=pltpu.VMEM)] * len(beside)
        + [pl.BlockSpec(memory_space=pltpu.HBM)] * len(args),
        out_specs=[pl.BlockSpec(memory_space=pltpu.VMEM)] * len(outs),
        scratch_shapes=list(scratch),
        compiler_params=pltpu.CompilerParams(vmem_limit_bytes=8 * 1024 * 1024),
        cost_estimate=pl.CostEstimate(flops=10**6, bytes_accessed=4096, transcendentals=0),
    )(*beside, *(pltpu.with_memory_space_constraint(x, pltpu.HBM) for x in args))


def swap(count, bits):
    return [(i, i ^ bits) for i in range(count)]


def over_links(count):
    return [(i, (i - 1 if i % 2 == 0 else i + 1) % count) for i in range(count)]


def total(parts):
    return functools.reduce(jnp.add, [p.astype(F32) for p in parts])


def body(queries, keys, values, out_grad, w_out, block_mask):
    q, k, v, g = queries[0], keys[0], values[0], out_grad[0]
    tokens, feats = q.shape
    width = g.shape[1]
    blocks = tokens // BLK
    ctx, dp = lax.axis_size("ctx"), lax.axis_size("dp")
    chips = ctx // 2
    at_ctx = lax.axis_index("ctx")
    rows, cols = feats // ctx, width // dp

    rim = vmem(RIM, feats)
    to_link, *to_chip = call_on_hbm(
        pack_kernel,
        [vmem(2, RIM, feats), rim, rim],
        k, v,
        scratch=[pltpu.SemaphoreType.DMA((4,))],
    )
    link = lax.ppermute(to_link, "ctx", over_links(ctx))
    chip_k, chip_v = (lax.ppermute(x, "ctx", swap(ctx, 1)) for x in to_chip)
    mask = lax.dynamic_slice_in_dim(block_mask[0], at_ctx * blocks, blocks, 0)
    bias = jnp.where(mask == 1, 0.0, BIG_NEGATIVE).astype(F32).reshape(blocks * CAND, 1, 1)
    bias = jnp.broadcast_to(bias, (blocks * CAND, 1, 2 * BLK))
    args = (q, k, v, g, w_out)
    own_keys = min(CAND, blocks) * BLK
    own_scores = (blocks, PAIRS, own_keys, 2 * BLK)
    rim_scores = (PAIRS, RIM, 2 * BLK)
    half = vmem(tokens // 2, width)
    q, k, v, g_low, g_high, w_out, own_t, stats, own_exps, grad_t = call_on_hbm(
        own_kernel,
        [vmem(tokens, feats)] * 3
        + [
            half,
            half,
            vmem(feats, width),
            vmem(blocks, feats, BLK, dtype=F32),
            vmem(2, blocks, PAIRS, 2 * BLK, dtype=F32),
            vmem(*own_scores, dtype=F32),
            vmem(blocks, feats, BLK),
        ],
        *args,
        beside=(bias,),
        scratch=[vmem(*own_scores), pltpu.SemaphoreType.DMA((6,))],
    )
    sibling_g = [
        pltpu.with_memory_space_constraint(lax.ppermute(x, "ctx", swap(ctx, 1)), pltpu.VMEM)
        for x in (g_low, g_high)
    ]
    chip_t, chip_stats, chip_exps = call(
        chip_kernel,
        [
            vmem(feats, BLK, dtype=F32),
            vmem(2, PAIRS, 2 * BLK, dtype=F32),
            vmem(*rim_scores, dtype=F32),
        ],
        10**6,
        bias, q, chip_k, chip_v, own_t, stats,
        scratch=[vmem(*rim_scores)],
    )
    attn_t, mine, other, link_exps, own_factors, rim_factors = call(
        forward_kernel,
        [
            vmem(blocks, feats, BLK),
            vmem(chips, rows, tokens),
            vmem(chips, rows, tokens),
            vmem(*rim_scores, dtype=F32),
            vmem(blocks, PAIRS, 2 * BLK, dtype=F32),
            vmem(2, PAIRS, 2 * BLK, dtype=F32),
        ],
        10**6,
        bias, q, link, own_t, stats, chip_t, chip_stats,
        scratch=[vmem(*rim_scores)],
    )

    other = lax.ppermute(other, "ctx", swap(ctx, 1))
    other = pltpu.with_memory_space_constraint(other, pltpu.VMEM)
    (product,) = call(product_kernel, [vmem(chips * rows, width, dtype=F32)], 10**6, mine, g_low, g_high)
    *halves, after = call(
        halves_kernel,
        [vmem(chips, rows, cols)] * dp + [vmem(8, 128, dtype=F32)],
        10**6,
        product, other, *sibling_g,
    )
    *back, deltas, rim_t = call(
        rim_kernel,
        [
            vmem(2, RIM, feats),
            vmem(2, RIM, feats),
            vmem(blocks, PAIRS, 2 * BLK, dtype=F32),
            vmem(blocks, feats, BLK, dtype=F32),
        ],
        10**6,
        q, link, chip_k, chip_v, grad_t, attn_t, link_exps, chip_exps, rim_factors, after,
        scratch=[vmem(2, *rim_scores, dtype=F32), vmem(2, *rim_scores), vmem(2, *rim_scores)],
    )
    link_back = lax.ppermute(back[0], "ctx", over_links(ctx))
    chip_back = lax.ppermute(back[1], "ctx", swap(ctx, 1))
    q_grad, k_own, v_own, after = call(
        own_backward_kernel,
        [
            hbm(tokens, feats),
            vmem(tokens, feats, dtype=F32),
            vmem(tokens, feats, dtype=F32),
            vmem(8, 128, dtype=F32),
        ],
        5 * 10**9,
        q, k, v, grad_t, own_exps, own_factors, deltas, rim_t,
        scratch=[vmem(*own_scores, dtype=F32), vmem(*own_scores), vmem(*own_scores)],
    )

    halves = [halves[0]] + [lax.ppermute(halves[s], "dp", swap(dp, s)) for s in range(dp - 1, 0, -1)]
    quarters = call(chips_kernel, [vmem(rows, cols)] * chips, 10**6, *halves, after)
    (output,) = call(output_kernel, [hbm(tokens, width)], 5 * 10**9, attn_t, w_out, quarters[0])
    quarters = [quarters[0]] + [
        lax.ppermute(quarters[s], "ctx", swap(ctx, 2 * s)) for s in range(chips - 1, 0, -1)
    ]
    (piece,) = call(
        functools.partial(piece_kernel, (dp * tokens * ctx) ** (-0.5), chips),
        [vmem(rows, cols)],
        10**6,
        *quarters, link_back,
    )
    pieces = [piece] + [lax.ppermute(piece, "dp", swap(dp, s)) for s in range(dp - 1, 0, -1)]
    k_grad, v_grad = call(
        rim_sum_kernel, [hbm(tokens, feats)] * 2, 10**6, k_own, v_own, link_back, chip_back
    )
    (weight_grad,) = call(columns_kernel, [hbm(rows, width, dtype=F32)], 10**6, *pieces)
    return (output[None], q_grad[None], k_grad[None], v_grad[None], weight_grad)


def solution(mesh):
    rows = P("dp", "ctx", None)
    return jax.shard_map(
        body,
        mesh=mesh,
        in_specs=(rows, rows, rows, rows, P(), P("dp", None, None)),
        out_specs=(rows, rows, rows, rows, P("ctx", None)),
        check_vma=False,
    )
```

```python
import functools

import jax
import jax.numpy as jnp
from jax import lax
from jax.experimental import pallas as pl
from jax.experimental.pallas import tpu as pltpu
from jax.sharding import PartitionSpec as P

HEADS = 8
HD = 64
BLK = 128
RAD = 1
CAND = 2 * RAD + 1
PAIRS = HEADS // 2
PAIR = 2 * HD
RIM = RAD * BLK
BIG_NEGATIVE = -1e30
SCALE = HD ** (-0.5)
BF16 = jnp.bfloat16
F32 = jnp.float32


def dot(a, b, contract):
    return lax.dot_general(a, b, (contract, ((), ())), preferred_element_type=F32)


def two_heads(block, axis):
    feature = lax.broadcasted_iota(jnp.int32, block.shape, axis)
    zero = jnp.zeros_like(block)
    return jnp.concatenate(
        [jnp.where(feature < HD, block, zero), jnp.where(feature < HD, zero, block)], axis=1 - axis
    )


def own_features(both):
    return jnp.concatenate([both[:HD, :BLK], both[HD:, BLK:]], axis=0)


def spread(row):
    return jnp.concatenate(
        [
            jnp.broadcast_to(row[:, :BLK], (HD, BLK)),
            jnp.broadcast_to(row[:, BLK:], (HD, BLK)),
        ],
        axis=0,
    )


def own_candidates(b, blocks):
    return max(0, RAD - b), min(CAND - 1, blocks - 1 - b + RAD)


def own_rows(b, blocks):
    first, last = own_candidates(b, blocks)
    return slice((b + first - RAD) * BLK, (b + last - RAD + 1) * BLK)


def masked(bias, b, c, part):
    return part + bias[b * CAND + c]


def pairs_of(blocks):
    for b in range(blocks):
        for p in range(PAIRS):
            yield b, slice(b * BLK, (b + 1) * BLK), slice(p * PAIR, (p + 1) * PAIR), p


def at_core():
    return lax.rem(lax.axis_index("ctx"), 2)


def rim_block(blocks, over_link):
    core = at_core()
    upper = core if over_link else 1 - core
    return upper * (blocks - 1), upper * (CAND - 1)


def rows_of(b):
    return pl.ds(pl.multiple_of(b * BLK, BLK), BLK)


def copy_all(pairs, sems):
    copies = [pltpu.make_async_copy(x, y, sems.at[i]) for i, (x, y) in enumerate(pairs)]
    for copy in copies:
        copy.start()
    for copy in copies:
        copy.wait()


def pack_link_kernel(k, v, out, sems):
    rows = rows_of(rim_block(k.shape[0] // BLK, True)[0])
    copy_all(((k.at[rows], out.at[0]), (v.at[rows], out.at[1])), sems)


def pack_chip_kernel(k, v, k_out, v_out, sems):
    rows = rows_of(rim_block(k.shape[0] // BLK, False)[0])
    copy_all(((k.at[rows], k_out), (v.at[rows], v_out)), sems)


def own_kernel(
    bias, q_arg, k_arg, v_arg, g_arg, w_arg,
    q, k, v, g_low, g_high, w_out, own_t, stats, exps, grad_t, rounded, sems,
):
    half = g_low.shape[0]
    pairs = (
        (q_arg, q),
        (k_arg, k),
        (v_arg, v),
        (g_arg.at[:half], g_low),
        (g_arg.at[half:], g_high),
        (w_arg, w_out),
    )
    copies = [pltpu.make_async_copy(x, y, sems.at[i]) for i, (x, y) in enumerate(pairs)]
    for copy in copies:
        copy.start()
    copies[0].wait()
    copies[1].wait()
    blocks = q.shape[0] // BLK
    for b, rows, cols, p in pairs_of(blocks):
        first, last = own_candidates(b, blocks)
        here = own_rows(b, blocks)
        scores = dot(k[here, cols], two_heads(q[rows, cols] * SCALE, 1), ((1,), (1,)))
        for c in range(first, last + 1):
            part = slice((c - first) * BLK, (c - first + 1) * BLK)
            value = scores[part]
            exps[b, p, part] = value if c == RAD else masked(bias, b, c, value)
    for b, rows, cols, p in pairs_of(blocks):
        here = own_rows(b, blocks)
        keys = slice(0, here.stop - here.start)
        scores = exps[b, p, keys]
        top = jnp.max(scores, axis=0, keepdims=True)
        e = jnp.exp(scores - top)
        exps[b, p, keys] = e
        rounded[b, p, keys] = e.astype(BF16)
        stats[0, b, p : p + 1] = top
        stats[1, b, p : p + 1] = jnp.sum(e, axis=0, keepdims=True)
    copies[2].wait()
    for b, rows, cols, p in pairs_of(blocks):
        here = own_rows(b, blocks)
        e = rounded[b, p, : here.stop - here.start]
        own_t[b, cols] = own_features(dot(v[here, cols], e, ((0,), (0,))))
    for copy in copies[3:]:
        copy.wait()
    both = jnp.concatenate([g_low[...], g_high[...]], axis=0)
    for b in range(blocks):
        rows = slice(b * BLK, (b + 1) * BLK)
        grad_t[b] = dot(w_out[...], both[rows], ((1,), (1,))).astype(BF16)


def pair_cols(p):
    return slice(p * PAIR, (p + 1) * PAIR)


def with_rim(bias, q, rim_k, rim_v, b, c, old, exps, rounded):
    for p in range(PAIRS):
        q2 = two_heads(q[rows_of(b), pair_cols(p)] * SCALE, 1)
        scores = dot(rim_k[:, pair_cols(p)], q2, ((1,), (1,)))
        exps[p] = masked(bias, b, c, scores)
    results = []
    for p in range(PAIRS):
        old_top, old_sum = old(p)
        scores = exps[p]
        top = jnp.maximum(old_top, jnp.max(scores, axis=0, keepdims=True))
        kept = jnp.exp(old_top - top)
        e = jnp.exp(scores - top)
        exps[p] = e
        rounded[p] = e.astype(BF16)
        results.append((top, kept, old_sum * kept + jnp.sum(e, axis=0, keepdims=True)))
    parts = [
        own_features(dot(rim_v[:, pair_cols(p)], rounded[p], ((0,), (0,)))) for p in range(PAIRS)
    ]
    return [(*result, part) for result, part in zip(results, parts)]


def chip_kernel(bias, q, rim_k, rim_v, own_t, stats, chip_t, chip_stats, exps, rounded):
    blocks = q.shape[0] // BLK
    b, c = rim_block(blocks, False)

    def old(p):
        return stats[0, b, p : p + 1], stats[1, b, p : p + 1]

    results = with_rim(bias, q, rim_k, rim_v, b, c, old, exps, rounded)
    for p, (top, kept, count, part) in enumerate(results):
        at = slice(p, p + 1)
        if blocks == 1:
            chip_t[pair_cols(p)] = own_t[b, pair_cols(p)] * spread(kept) + part
            chip_stats[0, at], chip_stats[1, at] = top, count
        else:
            share = 1.0 / count
            attn = own_t[b, pair_cols(p)] * spread(kept * share) + part * spread(share)
            chip_t[pair_cols(p)] = attn
            chip_stats[0, at], chip_stats[1, at] = share, kept * share


def forward_kernel(
    bias, q, rim, own_t, stats, chip_t, chip_stats,
    attn_t, mine, other, exps, own_factors, rim_factors, rounded,
):
    blocks = q.shape[0] // BLK
    b, c = rim_block(blocks, True)
    at_chip, _ = rim_block(blocks, False)

    def old(p):
        at = slice(p, p + 1)
        if blocks == 1:
            return chip_stats[0, at], chip_stats[1, at]
        return stats[0, b, at], stats[1, b, at]

    results = with_rim(bias, q, rim.at[0], rim.at[1], b, c, old, exps, rounded)
    for p, (top, kept, count, part) in enumerate(results):
        at = slice(p, p + 1)
        cols = pair_cols(p)
        base = chip_t[cols] if blocks == 1 else own_t[b, cols]
        share = 1.0 / count
        attn_t[b, cols] = (base * spread(kept * share) + part * spread(share)).astype(BF16)
        rim_factors[0, at] = share
        if blocks == 1:
            rim_factors[1, at] = kept * share
            own_factors[0, at] = jnp.exp(stats[0, 0, at] - top) * share
        else:
            own_factors[b, at] = kept * share
            attn_t[at_chip, cols] = chip_t[cols].astype(BF16)
            rim_factors[1, at] = chip_stats[0, at]
            own_factors[at_chip, at] = chip_stats[1, at]
        for inner in range(1, blocks - 1):
            share = 1.0 / stats[1, inner, at]
            attn_t[inner, cols] = (own_t[inner, cols] * spread(share)).astype(BF16)
            own_factors[inner, at] = share
    first_core = at_core() == 0
    chips, rows, _ = mine.shape
    for i in range(chips):
        for block in range(blocks):
            tokens = slice(block * BLK, (block + 1) * BLK)
            even = attn_t[block, 2 * i * rows : (2 * i + 1) * rows]
            odd = attn_t[block, (2 * i + 1) * rows : (2 * i + 2) * rows]
            mine[i, :, tokens] = jnp.where(first_core, even, odd)
            other[i, :, tokens] = jnp.where(first_core, odd, even)


def flat_dot(attn, g_low, g_high):
    chips, rows, tokens = attn.shape
    g = jnp.concatenate([g_low[...], g_high[...]], axis=0)
    return dot(attn[...].reshape(chips * rows, tokens), g, ((1,), (0,)))


def product_kernel(mine, g_low, g_high, product):
    product[...] = flat_dot(mine, g_low, g_high)


def score_grads(probs, dprob, delta):
    return (probs * (dprob - delta)).astype(BF16), probs.astype(BF16)


def rim_kernel(
    q, link, chip_k, chip_v, grad_t, attn_t, link_exps, chip_exps, rim_factors, before,
    link_back, chip_back, deltas, query_t, dprobs, dscores, rounded,
):
    blocks = q.shape[0] // BLK
    sides = (
        (rim_block(blocks, True)[0], link.at[0], link.at[1], link_exps, link_back.at[0], link_back.at[1]),
        (rim_block(blocks, False)[0], chip_k, chip_v, chip_exps, chip_back.at[0], chip_back.at[1]),
    )
    for i, (b, _, rim_v, _, _, _) in enumerate(sides):
        for p in range(PAIRS):
            g2_t = two_heads(grad_t[b, pair_cols(p)], 0)
            dprobs[i, p] = dot(rim_v[:, pair_cols(p)], g2_t, ((1,), (0,)))
    for b, _, cols, p in pairs_of(blocks):
        product = grad_t[b, cols].astype(F32) * attn_t[b, cols].astype(F32)
        deltas[b, p : p + 1] = jnp.concatenate(
            [
                jnp.sum(product[:HD], axis=0, keepdims=True),
                jnp.sum(product[HD:], axis=0, keepdims=True),
            ],
            axis=1,
        )
    query_t[...] = jnp.zeros_like(query_t)
    for i, (b, _, _, exps, _, _) in enumerate(sides):
        for p in range(PAIRS):
            at = slice(p, p + 1)
            dscores[i, p], rounded[i, p] = score_grads(
                exps[p] * rim_factors[i, at], dprobs[i, p], deltas[b, at]
            )
    for i, (b, rim_k, _, _, k_back, v_back) in enumerate(sides):
        for p in range(PAIRS):
            cols = pair_cols(p)
            q2 = two_heads(q[rows_of(b), cols] * SCALE, 1)
            g2_t = two_heads(grad_t[b, cols], 0)
            k_back[:, cols] = dot(dscores[i, p], q2, ((1,), (0,))).astype(BF16)
            v_back[:, cols] = dot(rounded[i, p], g2_t, ((1,), (1,))).astype(BF16)
            query_t[b, cols] += own_features(dot(rim_k[:, cols], dscores[i, p], ((0,), (0,))))


def own_backward_kernel(
    q, k, v, grad_t, exps, factors, deltas, rim_t,
    q_grad, k_own, v_own, after, dprobs, dscores, rounded,
):
    blocks = q.shape[0] // BLK
    for b, _, cols, p in pairs_of(blocks):
        here = own_rows(b, blocks)
        g2_t = two_heads(grad_t[b, cols], 0)
        dprobs[b, p, : here.stop - here.start] = dot(v[here, cols], g2_t, ((1,), (0,)))
    for b, _, _, p in pairs_of(blocks):
        here = own_rows(b, blocks)
        keys = slice(0, here.stop - here.start)
        dscores[b, p, keys], rounded[b, p, keys] = score_grads(
            exps[b, p, keys] * factors[b, p : p + 1], dprobs[b, p, keys], deltas[b, p : p + 1]
        )
    k_sums, v_sums = {}, {}
    for b, rows, cols, p in pairs_of(blocks):
        here = own_rows(b, blocks)
        keys = slice(0, here.stop - here.start)
        q2 = two_heads(q[rows, cols] * SCALE, 1)
        g2_t = two_heads(grad_t[b, cols], 0)
        dscore = dscores[b, p, keys]
        k_part = dot(dscore, q2, ((1,), (0,)))
        v_part = dot(rounded[b, p, keys], g2_t, ((1,), (1,)))
        for at in range(here.start, here.stop, BLK):
            part = slice(at - here.start, at - here.start + BLK)
            for sums, value in ((k_sums, k_part), (v_sums, v_part)):
                sums.setdefault((at, p), []).append(value[part])
        query_t = own_features(dot(k[here, cols], dscore, ((0,), (0,)))) + rim_t[b, cols]
        q_grad[rows, cols] = (query_t * SCALE).T.astype(BF16)
    for out, sums in ((k_own, k_sums), (v_own, v_sums)):
        for (at, p), values in sums.items():
            out[at : at + BLK, pair_cols(p)] = functools.reduce(jnp.add, values)
    after[...] = jnp.zeros_like(after)


def output_kernel(attn_t, w_out, before, output):
    for b in range(attn_t.shape[0]):
        part = dot(attn_t[b], w_out[...], ((0,), (0,)))
        output[b * BLK : (b + 1) * BLK] = part.astype(BF16)


def halves_kernel(product, other, g_low, g_high, *outs):
    pieces, after = outs[:-1], outs[-1]
    at_dp = lax.axis_index("dp")
    chips, rows, cols = pieces[0].shape
    if cols % BLK == 0:
        flat = other[...].reshape(chips * rows, other.shape[2])
        for s in range(len(pieces)):
            at = pl.ds(pl.multiple_of((at_dp ^ s) * cols, BLK), cols)
            g = jnp.concatenate([g_low[:, at], g_high[:, at]], axis=0)
            value = product[:, at] + dot(flat, g, ((1,), (0,)))
            pieces[s][...] = value.astype(BF16).reshape(chips, rows, cols)
    else:
        both = (product[...] + flat_dot(other, g_low, g_high)).astype(BF16)
        for d in range(len(pieces)):
            value = both[:, d * cols : (d + 1) * cols].reshape(chips, rows, cols)
            for s in range(len(pieces)):

                @pl.when((at_dp ^ s) == d)
                def _(s=s, value=value):
                    pieces[s][...] = value

    after[...] = jnp.zeros_like(after)


def chips_kernel(*refs):
    parts, outs = refs[: lax.axis_size("dp")], refs[lax.axis_size("dp") + 1 :]
    chip = lax.div(lax.axis_index("ctx"), 2)
    for s, out in enumerate(outs):
        out[...] = total([part[chip ^ s] for part in parts]).astype(BF16)


def piece_kernel(scale, count, *refs):
    refs[-1][...] = (total([part[...] for part in refs[:count]]) * scale).astype(BF16)


def rim_sum_kernel(k_own, v_own, link_kv, chip_kv, k_grad, v_grad):
    tokens = k_own.shape[0]
    first_core = at_core() == 0
    for i, (own, grad) in enumerate(((k_own, k_grad), (v_own, v_grad))):
        link, chip = link_kv[i].astype(F32), chip_kv[i].astype(F32)
        low = jnp.where(first_core, link, chip)
        high = jnp.where(first_core, chip, link)
        if tokens == RIM:
            grad[...] = (own[...] + low + high).astype(BF16)
        else:
            grad[:RIM] = (own[:RIM] + low).astype(BF16)
            if tokens > 2 * RIM:
                grad[RIM : tokens - RIM] = own[RIM : tokens - RIM].astype(BF16)
            grad[tokens - RIM :] = (own[tokens - RIM :] + high).astype(BF16)


def columns_kernel(*refs):
    pieces, weight_grad = refs[:1] + refs[-2:0:-1], refs[-1]
    at_dp = lax.axis_index("dp")
    cols = pieces[0].shape[1]
    for d in range(len(pieces)):
        value = pieces[0][...]
        for s in range(1, len(pieces)):
            value = jnp.where((at_dp ^ s) == d, pieces[s][...], value)
        weight_grad[:, d * cols : (d + 1) * cols] = value.astype(F32)


def vmem(*shape, dtype=BF16):
    return pltpu.VMEM(shape, dtype)


def hbm(*shape, dtype=BF16):
    return jax.ShapeDtypeStruct(shape, dtype)


def call(kernel, outs, flops, *args, scratch=()):
    in_vmem = pl.BlockSpec(memory_space=pltpu.VMEM)
    return pl.pallas_call(
        kernel,
        out_shape=outs,
        in_specs=[in_vmem] * len(args),
        out_specs=[in_vmem] * len(outs),
        scratch_shapes=list(scratch),
        compiler_params=pltpu.CompilerParams(vmem_limit_bytes=24 * 1024 * 1024),
        cost_estimate=pl.CostEstimate(flops=flops, bytes_accessed=flops // 250, transcendentals=0),
    )(*args)


def call_on_hbm(kernel, outs, *args, beside=(), scratch=()):
    return pl.pallas_call(
        kernel,
        out_shape=outs,
        in_specs=[pl.BlockSpec(memory_space=pltpu.VMEM)] * len(beside)
        + [pl.BlockSpec(memory_space=pltpu.HBM)] * len(args),
        out_specs=[pl.BlockSpec(memory_space=pltpu.VMEM)] * len(outs),
        scratch_shapes=list(scratch),
        compiler_params=pltpu.CompilerParams(vmem_limit_bytes=8 * 1024 * 1024),
        cost_estimate=pl.CostEstimate(flops=10**6, bytes_accessed=4096, transcendentals=0),
    )(*beside, *(pltpu.with_memory_space_constraint(x, pltpu.HBM) for x in args))


def swap(count, bits):
    return [(i, i ^ bits) for i in range(count)]


def over_links(count):
    return [(i, (i - 1 if i % 2 == 0 else i + 1) % count) for i in range(count)]


def total(parts):
    return functools.reduce(jnp.add, [p.astype(F32) for p in parts])


def body(queries, keys, values, out_grad, w_out, block_mask):
    q, k, v, g = queries[0], keys[0], values[0], out_grad[0]
    tokens, feats = q.shape
    width = g.shape[1]
    blocks = tokens // BLK
    ctx, dp = lax.axis_size("ctx"), lax.axis_size("dp")
    chips = ctx // 2
    at_ctx = lax.axis_index("ctx")
    rows, cols = feats // ctx, width // dp

    rim = vmem(RIM, feats)
    sems = [pltpu.SemaphoreType.DMA((2,))]
    (to_link,) = call_on_hbm(pack_link_kernel, [vmem(2, RIM, feats)], k, v, scratch=sems)
    to_chip = call_on_hbm(pack_chip_kernel, [rim, rim], k, v, scratch=sems)
    link = lax.ppermute(to_link, "ctx", over_links(ctx))
    chip_k, chip_v = (lax.ppermute(x, "ctx", swap(ctx, 1)) for x in to_chip)
    mask = lax.dynamic_slice_in_dim(block_mask[0], at_ctx * blocks, blocks, 0)
    bias = jnp.where(mask == 1, 0.0, BIG_NEGATIVE).astype(F32).reshape(blocks * CAND, 1, 1)
    bias = jnp.broadcast_to(bias, (blocks * CAND, 1, 2 * BLK))
    args = (q, k, v, g, w_out)
    own_keys = min(CAND, blocks) * BLK
    own_scores = (blocks, PAIRS, own_keys, 2 * BLK)
    rim_scores = (PAIRS, RIM, 2 * BLK)
    half = vmem(tokens // 2, width)
    q, k, v, g_low, g_high, w_out, own_t, stats, own_exps, grad_t = call_on_hbm(
        own_kernel,
        [vmem(tokens, feats)] * 3
        + [
            half,
            half,
            vmem(feats, width),
            vmem(blocks, feats, BLK, dtype=F32),
            vmem(2, blocks, PAIRS, 2 * BLK, dtype=F32),
            vmem(*own_scores, dtype=F32),
            vmem(blocks, feats, BLK),
        ],
        *args,
        beside=(bias,),
        scratch=[vmem(*own_scores), pltpu.SemaphoreType.DMA((6,))],
    )
    sibling_g = [
        pltpu.with_memory_space_constraint(lax.ppermute(x, "ctx", swap(ctx, 1)), pltpu.VMEM)
        for x in (g_low, g_high)
    ]
    chip_t, chip_stats, chip_exps = call(
        chip_kernel,
        [
            vmem(feats, BLK, dtype=F32),
            vmem(2, PAIRS, 2 * BLK, dtype=F32),
            vmem(*rim_scores, dtype=F32),
        ],
        10**6,
        bias, q, chip_k, chip_v, own_t, stats,
        scratch=[vmem(*rim_scores)],
    )
    attn_t, mine, other, link_exps, own_factors, rim_factors = call(
        forward_kernel,
        [
            vmem(blocks, feats, BLK),
            vmem(chips, rows, tokens),
            vmem(chips, rows, tokens),
            vmem(*rim_scores, dtype=F32),
            vmem(blocks, PAIRS, 2 * BLK, dtype=F32),
            vmem(2, PAIRS, 2 * BLK, dtype=F32),
        ],
        10**6,
        bias, q, link, own_t, stats, chip_t, chip_stats,
        scratch=[vmem(*rim_scores)],
    )

    other = lax.ppermute(other, "ctx", swap(ctx, 1))
    other = pltpu.with_memory_space_constraint(other, pltpu.VMEM)
    (product,) = call(product_kernel, [vmem(chips * rows, width, dtype=F32)], 10**6, mine, g_low, g_high)
    *halves, after = call(
        halves_kernel,
        [vmem(chips, rows, cols)] * dp + [vmem(8, 128, dtype=F32)],
        10**6,
        product, other, *sibling_g,
    )
    *back, deltas, rim_t = call(
        rim_kernel,
        [
            vmem(2, RIM, feats),
            vmem(2, RIM, feats),
            vmem(blocks, PAIRS, 2 * BLK, dtype=F32),
            vmem(blocks, feats, BLK, dtype=F32),
        ],
        10**6,
        q, link, chip_k, chip_v, grad_t, attn_t, link_exps, chip_exps, rim_factors, after,
        scratch=[vmem(2, *rim_scores, dtype=F32), vmem(2, *rim_scores), vmem(2, *rim_scores)],
    )
    link_back = lax.ppermute(back[0], "ctx", over_links(ctx))
    chip_back = lax.ppermute(back[1], "ctx", swap(ctx, 1))
    q_grad, k_own, v_own, after = call(
        own_backward_kernel,
        [
            hbm(tokens, feats),
            vmem(tokens, feats, dtype=F32),
            vmem(tokens, feats, dtype=F32),
            vmem(8, 128, dtype=F32),
        ],
        5 * 10**9,
        q, k, v, grad_t, own_exps, own_factors, deltas, rim_t,
        scratch=[vmem(*own_scores, dtype=F32), vmem(*own_scores), vmem(*own_scores)],
    )

    halves = [halves[0]] + [lax.ppermute(halves[s], "dp", swap(dp, s)) for s in range(dp - 1, 0, -1)]
    quarters = call(chips_kernel, [vmem(rows, cols)] * chips, 10**6, *halves, after)
    (output,) = call(output_kernel, [hbm(tokens, width)], 5 * 10**9, attn_t, w_out, quarters[0])
    quarters = [quarters[0]] + [
        lax.ppermute(quarters[s], "ctx", swap(ctx, 2 * s)) for s in range(chips - 1, 0, -1)
    ]
    (piece,) = call(
        functools.partial(piece_kernel, (dp * tokens * ctx) ** (-0.5), chips),
        [vmem(rows, cols)],
        10**6,
        *quarters, link_back,
    )
    pieces = [piece] + [lax.ppermute(piece, "dp", swap(dp, s)) for s in range(dp - 1, 0, -1)]
    k_grad, v_grad = call(
        rim_sum_kernel, [hbm(tokens, feats)] * 2, 10**6, k_own, v_own, link_back, chip_back
    )
    (weight_grad,) = call(columns_kernel, [hbm(rows, width, dtype=F32)], 10**6, *pieces)
    return (output[None], q_grad[None], k_grad[None], v_grad[None], weight_grad)


def solution(mesh):
    rows = P("dp", "ctx", None)
    return jax.shard_map(
        body,
        mesh=mesh,
        in_specs=(rows, rows, rows, rows, P(), P("dp", None, None)),
        out_specs=(rows, rows, rows, rows, P("ctx", None)),
        check_vma=False,
    )
```

```python
import functools

import jax
import jax.numpy as jnp
from jax import lax
from jax.experimental import pallas as pl
from jax.experimental.pallas import tpu as pltpu
from jax.sharding import PartitionSpec as P

HEADS = 8
HD = 64
BLK = 128
RAD = 1
CAND = 2 * RAD + 1
PAIRS = HEADS // 2
PAIR = 2 * HD
RIM = RAD * BLK
BIG_NEGATIVE = -1e30
SCALE = HD ** (-0.5)
BF16 = jnp.bfloat16
F32 = jnp.float32


def dot(a, b, contract):
    return lax.dot_general(a, b, (contract, ((), ())), preferred_element_type=F32)


def two_heads(block, axis):
    feature = lax.broadcasted_iota(jnp.int32, block.shape, axis)
    zero = jnp.zeros_like(block)
    return jnp.concatenate(
        [jnp.where(feature < HD, block, zero), jnp.where(feature < HD, zero, block)], axis=1 - axis
    )


def own_features(both):
    return jnp.concatenate([both[:HD, :BLK], both[HD:, BLK:]], axis=0)


def spread(row):
    return jnp.concatenate(
        [
            jnp.broadcast_to(row[:, :BLK], (HD, BLK)),
            jnp.broadcast_to(row[:, BLK:], (HD, BLK)),
        ],
        axis=0,
    )


def own_candidates(b, blocks):
    return max(0, RAD - b), min(CAND - 1, blocks - 1 - b + RAD)


def own_rows(b, blocks):
    first, last = own_candidates(b, blocks)
    return slice((b + first - RAD) * BLK, (b + last - RAD + 1) * BLK)


def masked(bias, b, c, part):
    return part + bias[b * CAND + c]


def pairs_of(blocks):
    for b in range(blocks):
        for p in range(PAIRS):
            yield b, slice(b * BLK, (b + 1) * BLK), slice(p * PAIR, (p + 1) * PAIR), p


def at_core():
    return lax.rem(lax.axis_index("ctx"), 2)


def rim_block(blocks, over_link):
    core = at_core()
    upper = core if over_link else 1 - core
    return upper * (blocks - 1), upper * (CAND - 1)


def rows_of(b):
    return pl.ds(pl.multiple_of(b * BLK, BLK), BLK)


def copy_all(pairs, sems):
    copies = [pltpu.make_async_copy(x, y, sems.at[i]) for i, (x, y) in enumerate(pairs)]
    for copy in copies:
        copy.start()
    for copy in copies:
        copy.wait()


def pack_link_kernel(k, v, out, sems):
    rows = rows_of(rim_block(k.shape[0] // BLK, True)[0])
    copy_all(((k.at[rows], out.at[0]), (v.at[rows], out.at[1])), sems)


def pack_chip_kernel(k, v, k_out, v_out, sems):
    rows = rows_of(rim_block(k.shape[0] // BLK, False)[0])
    copy_all(((k.at[rows], k_out), (v.at[rows], v_out)), sems)


def own_kernel(
    bias, q_arg, k_arg, v_arg, g_arg, w_arg,
    q, k, v, g_low, g_high, w_out, own_t, stats, exps, grad_t, rounded, sems,
):
    half = g_low.shape[0]
    pairs = (
        (q_arg, q),
        (k_arg, k),
        (v_arg, v),
        (g_arg.at[:half], g_low),
        (g_arg.at[half:], g_high),
        (w_arg, w_out),
    )
    copies = [pltpu.make_async_copy(x, y, sems.at[i]) for i, (x, y) in enumerate(pairs)]
    for copy in copies:
        copy.start()
    copies[0].wait()
    copies[1].wait()
    blocks = q.shape[0] // BLK
    for b, rows, cols, p in pairs_of(blocks):
        first, last = own_candidates(b, blocks)
        here = own_rows(b, blocks)
        scores = dot(k[here, cols], two_heads(q[rows, cols] * SCALE, 1), ((1,), (1,)))
        for c in range(first, last + 1):
            part = slice((c - first) * BLK, (c - first + 1) * BLK)
            value = scores[part]
            exps[b, p, part] = value if c == RAD else masked(bias, b, c, value)
    for b, rows, cols, p in pairs_of(blocks):
        here = own_rows(b, blocks)
        keys = slice(0, here.stop - here.start)
        scores = exps[b, p, keys]
        top = jnp.max(scores, axis=0, keepdims=True)
        e = jnp.exp(scores - top)
        exps[b, p, keys] = e
        rounded[b, p, keys] = e.astype(BF16)
        stats[0, b, p : p + 1] = top
        stats[1, b, p : p + 1] = jnp.sum(e, axis=0, keepdims=True)
    copies[2].wait()
    for b, rows, cols, p in pairs_of(blocks):
        here = own_rows(b, blocks)
        e = rounded[b, p, : here.stop - here.start]
        own_t[b, cols] = own_features(dot(v[here, cols], e, ((0,), (0,))))
    for copy in copies[3:]:
        copy.wait()
    both = jnp.concatenate([g_low[...], g_high[...]], axis=0)
    for b in range(blocks):
        rows = slice(b * BLK, (b + 1) * BLK)
        grad_t[b] = dot(w_out[...], both[rows], ((1,), (1,))).astype(BF16)


def pair_cols(p):
    return slice(p * PAIR, (p + 1) * PAIR)


def with_rim(bias, q, rim_k, rim_v, b, c, old, exps, rounded):
    for p in range(PAIRS):
        q2 = two_heads(q[rows_of(b), pair_cols(p)] * SCALE, 1)
        scores = dot(rim_k[:, pair_cols(p)], q2, ((1,), (1,)))
        exps[p] = masked(bias, b, c, scores)
    results = []
    for p in range(PAIRS):
        old_top, old_sum = old(p)
        scores = exps[p]
        top = jnp.maximum(old_top, jnp.max(scores, axis=0, keepdims=True))
        kept = jnp.exp(old_top - top)
        e = jnp.exp(scores - top)
        exps[p] = e
        rounded[p] = e.astype(BF16)
        results.append((top, kept, old_sum * kept + jnp.sum(e, axis=0, keepdims=True)))
    parts = [
        own_features(dot(rim_v[:, pair_cols(p)], rounded[p], ((0,), (0,)))) for p in range(PAIRS)
    ]
    return [(*result, part) for result, part in zip(results, parts)]


def chip_kernel(bias, q, rim_k, rim_v, own_t, stats, chip_t, chip_stats, exps, rounded):
    blocks = q.shape[0] // BLK
    b, c = rim_block(blocks, False)

    def old(p):
        return stats[0, b, p : p + 1], stats[1, b, p : p + 1]

    results = with_rim(bias, q, rim_k, rim_v, b, c, old, exps, rounded)
    for p, (top, kept, count, part) in enumerate(results):
        at = slice(p, p + 1)
        if blocks == 1:
            chip_t[pair_cols(p)] = own_t[b, pair_cols(p)] * spread(kept) + part
            chip_stats[0, at], chip_stats[1, at] = top, count
        else:
            share = 1.0 / count
            attn = own_t[b, pair_cols(p)] * spread(kept * share) + part * spread(share)
            chip_t[pair_cols(p)] = attn
            chip_stats[0, at], chip_stats[1, at] = share, kept * share


def forward_kernel(
    bias, q, rim, own_t, stats, chip_t, chip_stats,
    attn_t, mine, other, exps, own_factors, rim_factors, rounded,
):
    blocks = q.shape[0] // BLK
    b, c = rim_block(blocks, True)
    at_chip, _ = rim_block(blocks, False)

    def old(p):
        at = slice(p, p + 1)
        if blocks == 1:
            return chip_stats[0, at], chip_stats[1, at]
        return stats[0, b, at], stats[1, b, at]

    results = with_rim(bias, q, rim.at[0], rim.at[1], b, c, old, exps, rounded)
    for p, (top, kept, count, part) in enumerate(results):
        at = slice(p, p + 1)
        cols = pair_cols(p)
        base = chip_t[cols] if blocks == 1 else own_t[b, cols]
        share = 1.0 / count
        attn_t[b, cols] = (base * spread(kept * share) + part * spread(share)).astype(BF16)
        rim_factors[0, at] = share
        if blocks == 1:
            rim_factors[1, at] = kept * share
            own_factors[0, at] = jnp.exp(stats[0, 0, at] - top) * share
        else:
            own_factors[b, at] = kept * share
            attn_t[at_chip, cols] = chip_t[cols].astype(BF16)
            rim_factors[1, at] = chip_stats[0, at]
            own_factors[at_chip, at] = chip_stats[1, at]
        for inner in range(1, blocks - 1):
            share = 1.0 / stats[1, inner, at]
            attn_t[inner, cols] = (own_t[inner, cols] * spread(share)).astype(BF16)
            own_factors[inner, at] = share
    first_core = at_core() == 0
    chips, rows, _ = mine.shape
    for i in range(chips):
        for block in range(blocks):
            tokens = slice(block * BLK, (block + 1) * BLK)
            even = attn_t[block, 2 * i * rows : (2 * i + 1) * rows]
            odd = attn_t[block, (2 * i + 1) * rows : (2 * i + 2) * rows]
            mine[i, :, tokens] = jnp.where(first_core, even, odd)
            other[i, :, tokens] = jnp.where(first_core, odd, even)


def flat_dot(attn, g_low, g_high):
    chips, rows, tokens = attn.shape
    g = jnp.concatenate([g_low[...], g_high[...]], axis=0)
    return dot(attn[...].reshape(chips * rows, tokens), g, ((1,), (0,)))


def product_kernel(mine, g_low, g_high, product):
    product[...] = flat_dot(mine, g_low, g_high)


def score_grads(probs, dprob, delta):
    return (probs * (dprob - delta)).astype(BF16), probs.astype(BF16)


def rim_kernel(
    q, link, chip_k, chip_v, grad_t, attn_t, link_exps, chip_exps, rim_factors, before,
    link_back, chip_back, deltas, query_t, dprobs, dscores, rounded,
):
    blocks = q.shape[0] // BLK
    sides = (
        (rim_block(blocks, True)[0], link.at[0], link.at[1], link_exps, link_back.at[0], link_back.at[1]),
        (rim_block(blocks, False)[0], chip_k, chip_v, chip_exps, chip_back.at[0], chip_back.at[1]),
    )
    for i, (b, _, rim_v, _, _, _) in enumerate(sides):
        for p in range(PAIRS):
            g2_t = two_heads(grad_t[b, pair_cols(p)], 0)
            dprobs[i, p] = dot(rim_v[:, pair_cols(p)], g2_t, ((1,), (0,)))
    for b, _, cols, p in pairs_of(blocks):
        product = grad_t[b, cols].astype(F32) * attn_t[b, cols].astype(F32)
        deltas[b, p : p + 1] = jnp.concatenate(
            [
                jnp.sum(product[:HD], axis=0, keepdims=True),
                jnp.sum(product[HD:], axis=0, keepdims=True),
            ],
            axis=1,
        )
    query_t[...] = jnp.zeros_like(query_t)
    for i, (b, _, _, exps, _, _) in enumerate(sides):
        for p in range(PAIRS):
            at = slice(p, p + 1)
            dscores[i, p], rounded[i, p] = score_grads(
                exps[p] * rim_factors[i, at], dprobs[i, p], deltas[b, at]
            )
    for i, (b, rim_k, _, _, k_back, v_back) in enumerate(sides):
        for p in range(PAIRS):
            cols = pair_cols(p)
            q2 = two_heads(q[rows_of(b), cols] * SCALE, 1)
            g2_t = two_heads(grad_t[b, cols], 0)
            k_back[:, cols] = dot(dscores[i, p], q2, ((1,), (0,))).astype(BF16)
            v_back[:, cols] = dot(rounded[i, p], g2_t, ((1,), (1,))).astype(BF16)
            query_t[b, cols] += own_features(dot(rim_k[:, cols], dscores[i, p], ((0,), (0,))))


def own_backward_kernel(
    q, k, v, grad_t, exps, factors, deltas, rim_t,
    q_grad, k_own, v_own, after, dprobs, dscores, rounded,
):
    blocks = q.shape[0] // BLK
    for b, _, cols, p in pairs_of(blocks):
        here = own_rows(b, blocks)
        g2_t = two_heads(grad_t[b, cols], 0)
        dprobs[b, p, : here.stop - here.start] = dot(v[here, cols], g2_t, ((1,), (0,)))
    for b, _, _, p in pairs_of(blocks):
        here = own_rows(b, blocks)
        keys = slice(0, here.stop - here.start)
        dscores[b, p, keys], rounded[b, p, keys] = score_grads(
            exps[b, p, keys] * factors[b, p : p + 1], dprobs[b, p, keys], deltas[b, p : p + 1]
        )
    k_sums, v_sums = {}, {}
    for b, rows, cols, p in pairs_of(blocks):
        here = own_rows(b, blocks)
        keys = slice(0, here.stop - here.start)
        q2 = two_heads(q[rows, cols] * SCALE, 1)
        g2_t = two_heads(grad_t[b, cols], 0)
        dscore = dscores[b, p, keys]
        k_part = dot(dscore, q2, ((1,), (0,)))
        v_part = dot(rounded[b, p, keys], g2_t, ((1,), (1,)))
        for at in range(here.start, here.stop, BLK):
            part = slice(at - here.start, at - here.start + BLK)
            for sums, value in ((k_sums, k_part), (v_sums, v_part)):
                sums.setdefault((at, p), []).append(value[part])
        query_t = own_features(dot(k[here, cols], dscore, ((0,), (0,)))) + rim_t[b, cols]
        q_grad[rows, cols] = (query_t * SCALE).T.astype(BF16)
    for out, sums in ((k_own, k_sums), (v_own, v_sums)):
        for (at, p), values in sums.items():
            out[at : at + BLK, pair_cols(p)] = functools.reduce(jnp.add, values)
    after[...] = jnp.zeros_like(after)


def output_kernel(attn_t, w_out, before, output):
    for b in range(attn_t.shape[0]):
        part = dot(attn_t[b], w_out[...], ((0,), (0,)))
        output[b * BLK : (b + 1) * BLK] = part.astype(BF16)


def halves_kernel(product, other, g_low, g_high, *outs):
    pieces, after = outs[:-1], outs[-1]
    at_dp = lax.axis_index("dp")
    chips, rows, cols = pieces[0].shape
    if cols % BLK == 0:
        flat = other[...].reshape(chips * rows, other.shape[2])
        for s in range(len(pieces)):
            at = pl.ds(pl.multiple_of((at_dp ^ s) * cols, BLK), cols)
            g = jnp.concatenate([g_low[:, at], g_high[:, at]], axis=0)
            value = product[:, at] + dot(flat, g, ((1,), (0,)))
            pieces[s][...] = value.astype(BF16).reshape(chips, rows, cols)
    else:
        both = (product[...] + flat_dot(other, g_low, g_high)).astype(BF16)
        for d in range(len(pieces)):
            value = both[:, d * cols : (d + 1) * cols].reshape(chips, rows, cols)
            for s in range(len(pieces)):

                @pl.when((at_dp ^ s) == d)
                def _(s=s, value=value):
                    pieces[s][...] = value

    after[...] = jnp.zeros_like(after)


def chips_kernel(*refs):
    parts, outs = refs[: lax.axis_size("dp")], refs[lax.axis_size("dp") + 1 :]
    chip = lax.div(lax.axis_index("ctx"), 2)
    for s, out in enumerate(outs):
        out[...] = total([part[chip ^ s] for part in parts]).astype(BF16)


def piece_kernel(scale, count, *refs):
    refs[-1][...] = (total([part[...] for part in refs[:count]]) * scale).astype(BF16)


def rim_sum_kernel(k_own, v_own, link_kv, chip_kv, k_grad, v_grad):
    tokens = k_own.shape[0]
    first_core = at_core() == 0
    for i, (own, grad) in enumerate(((k_own, k_grad), (v_own, v_grad))):
        link, chip = link_kv[i].astype(F32), chip_kv[i].astype(F32)
        low = jnp.where(first_core, link, chip)
        high = jnp.where(first_core, chip, link)
        if tokens == RIM:
            grad[...] = (own[...] + low + high).astype(BF16)
        else:
            grad[:RIM] = (own[:RIM] + low).astype(BF16)
            if tokens > 2 * RIM:
                grad[RIM : tokens - RIM] = own[RIM : tokens - RIM].astype(BF16)
            grad[tokens - RIM :] = (own[tokens - RIM :] + high).astype(BF16)


def columns_kernel(*refs):
    pieces, weight_grad = refs[:1] + refs[-2:0:-1], refs[-1]
    at_dp = lax.axis_index("dp")
    cols = pieces[0].shape[1]
    for d in range(len(pieces)):
        value = pieces[0][...]
        for s in range(1, len(pieces)):
            value = jnp.where((at_dp ^ s) == d, pieces[s][...], value)
        weight_grad[:, d * cols : (d + 1) * cols] = value.astype(F32)


def vmem(*shape, dtype=BF16):
    return pltpu.VMEM(shape, dtype)


def hbm(*shape, dtype=BF16):
    return jax.ShapeDtypeStruct(shape, dtype)


def call(kernel, outs, flops, *args, scratch=()):
    in_vmem = pl.BlockSpec(memory_space=pltpu.VMEM)
    return pl.pallas_call(
        kernel,
        out_shape=outs,
        in_specs=[in_vmem] * len(args),
        out_specs=[in_vmem] * len(outs),
        scratch_shapes=list(scratch),
        compiler_params=pltpu.CompilerParams(vmem_limit_bytes=24 * 1024 * 1024),
        cost_estimate=pl.CostEstimate(flops=flops, bytes_accessed=flops // 250, transcendentals=0),
    )(*args)


def call_on_hbm(kernel, outs, *args, beside=(), scratch=()):
    return pl.pallas_call(
        kernel,
        out_shape=outs,
        in_specs=[pl.BlockSpec(memory_space=pltpu.VMEM)] * len(beside)
        + [pl.BlockSpec(memory_space=pltpu.HBM)] * len(args),
        out_specs=[pl.BlockSpec(memory_space=pltpu.VMEM)] * len(outs),
        scratch_shapes=list(scratch),
        compiler_params=pltpu.CompilerParams(vmem_limit_bytes=8 * 1024 * 1024),
        cost_estimate=pl.CostEstimate(flops=10**6, bytes_accessed=4096, transcendentals=0),
    )(*beside, *(pltpu.with_memory_space_constraint(x, pltpu.HBM) for x in args))


def swap(count, bits):
    return [(i, i ^ bits) for i in range(count)]


def over_links(count):
    return [(i, (i - 1 if i % 2 == 0 else i + 1) % count) for i in range(count)]


def total(parts):
    return functools.reduce(jnp.add, [p.astype(F32) for p in parts])


def body(queries, keys, values, out_grad, w_out, block_mask):
    q, k, v, g = queries[0], keys[0], values[0], out_grad[0]
    tokens, feats = q.shape
    width = g.shape[1]
    blocks = tokens // BLK
    ctx, dp = lax.axis_size("ctx"), lax.axis_size("dp")
    chips = ctx // 2
    at_ctx = lax.axis_index("ctx")
    rows, cols = feats // ctx, width // dp

    rim = vmem(RIM, feats)
    sems = [pltpu.SemaphoreType.DMA((2,))]
    (to_link,) = call_on_hbm(pack_link_kernel, [vmem(2, RIM, feats)], k, v, scratch=sems)
    to_chip = call_on_hbm(pack_chip_kernel, [rim, rim], k, v, scratch=sems)
    link = lax.ppermute(to_link, "ctx", over_links(ctx))
    chip_k, chip_v = (lax.ppermute(x, "ctx", swap(ctx, 1)) for x in to_chip)
    mask = lax.dynamic_slice_in_dim(block_mask[0], at_ctx * blocks, blocks, 0)
    bias = jnp.where(mask == 1, 0.0, BIG_NEGATIVE).astype(F32).reshape(blocks * CAND, 1, 1)
    bias = jnp.broadcast_to(bias, (blocks * CAND, 1, 2 * BLK))
    args = (q, k, v, g, w_out)
    own_keys = min(CAND, blocks) * BLK
    own_scores = (blocks, PAIRS, own_keys, 2 * BLK)
    rim_scores = (PAIRS, RIM, 2 * BLK)
    half = vmem(tokens // 2, width)
    q, k, v, g_low, g_high, w_out, own_t, stats, own_exps, grad_t = call_on_hbm(
        own_kernel,
        [vmem(tokens, feats)] * 3
        + [
            half,
            half,
            vmem(feats, width),
            vmem(blocks, feats, BLK, dtype=F32),
            vmem(2, blocks, PAIRS, 2 * BLK, dtype=F32),
            vmem(*own_scores, dtype=F32),
            vmem(blocks, feats, BLK),
        ],
        *args,
        beside=(bias,),
        scratch=[vmem(*own_scores), pltpu.SemaphoreType.DMA((6,))],
    )
    sibling_g = [
        pltpu.with_memory_space_constraint(lax.ppermute(x, "ctx", swap(ctx, 1)), pltpu.VMEM)
        for x in (g_low, g_high)
    ]
    chip_t, chip_stats, chip_exps = call(
        chip_kernel,
        [
            vmem(feats, BLK, dtype=F32),
            vmem(2, PAIRS, 2 * BLK, dtype=F32),
            vmem(*rim_scores, dtype=F32),
        ],
        10**6,
        bias, q, chip_k, chip_v, own_t, stats,
        scratch=[vmem(*rim_scores)],
    )
    attn_t, mine, other, link_exps, own_factors, rim_factors = call(
        forward_kernel,
        [
            vmem(blocks, feats, BLK),
            vmem(chips, rows, tokens),
            vmem(chips, rows, tokens),
            vmem(*rim_scores, dtype=F32),
            vmem(blocks, PAIRS, 2 * BLK, dtype=F32),
            vmem(2, PAIRS, 2 * BLK, dtype=F32),
        ],
        10**6,
        bias, q, link, own_t, stats, chip_t, chip_stats,
        scratch=[vmem(*rim_scores)],
    )

    other = lax.ppermute(other, "ctx", swap(ctx, 1))
    other = pltpu.with_memory_space_constraint(other, pltpu.VMEM)
    (product,) = call(product_kernel, [vmem(chips * rows, width, dtype=F32)], 10**6, mine, g_low, g_high)
    *halves, after = call(
        halves_kernel,
        [vmem(chips, rows, cols)] * dp + [vmem(8, 128, dtype=F32)],
        10**6,
        product, other, *sibling_g,
    )
    *back, deltas, rim_t = call(
        rim_kernel,
        [
            vmem(2, RIM, feats),
            vmem(2, RIM, feats),
            vmem(blocks, PAIRS, 2 * BLK, dtype=F32),
            vmem(blocks, feats, BLK, dtype=F32),
        ],
        10**6,
        q, link, chip_k, chip_v, grad_t, attn_t, link_exps, chip_exps, rim_factors, after,
        scratch=[vmem(2, *rim_scores, dtype=F32), vmem(2, *rim_scores), vmem(2, *rim_scores)],
    )
    link_back = lax.ppermute(back[0], "ctx", over_links(ctx))
    chip_back = lax.ppermute(back[1], "ctx", swap(ctx, 1))
    q_grad, k_own, v_own, after = call(
        own_backward_kernel,
        [
            hbm(tokens, feats),
            vmem(tokens, feats, dtype=F32),
            vmem(tokens, feats, dtype=F32),
            vmem(8, 128, dtype=F32),
        ],
        5 * 10**9,
        q, k, v, grad_t, own_exps, own_factors, deltas, rim_t,
        scratch=[vmem(*own_scores, dtype=F32), vmem(*own_scores), vmem(*own_scores)],
    )

    halves = [halves[0]] + [lax.ppermute(halves[s], "dp", swap(dp, s)) for s in range(1, dp)]
    quarters = call(chips_kernel, [vmem(rows, cols)] * chips, 10**6, *halves, after)
    (output,) = call(output_kernel, [hbm(tokens, width)], 5 * 10**9, attn_t, w_out, quarters[0])
    quarters = [quarters[0]] + [
        lax.ppermute(quarters[s], "ctx", swap(ctx, 2 * s)) for s in range(chips - 1, 0, -1)
    ]
    (piece,) = call(
        functools.partial(piece_kernel, (dp * tokens * ctx) ** (-0.5), chips),
        [vmem(rows, cols)],
        10**6,
        *quarters, link_back,
    )
    pieces = [piece] + [lax.ppermute(piece, "dp", swap(dp, s)) for s in range(dp - 1, 0, -1)]
    k_grad, v_grad = call(
        rim_sum_kernel, [hbm(tokens, feats)] * 2, 10**6, k_own, v_own, link_back, chip_back
    )
    (weight_grad,) = call(columns_kernel, [hbm(rows, width, dtype=F32)], 10**6, *pieces)
    return (output[None], q_grad[None], k_grad[None], v_grad[None], weight_grad)


def solution(mesh):
    rows = P("dp", "ctx", None)
    return jax.shard_map(
        body,
        mesh=mesh,
        in_specs=(rows, rows, rows, rows, P(), P("dp", None, None)),
        out_specs=(rows, rows, rows, rows, P("ctx", None)),
        check_vma=False,
    )
```

```python
import functools

import jax
import jax.numpy as jnp
from jax import lax
from jax.experimental import pallas as pl
from jax.experimental.pallas import tpu as pltpu
from jax.sharding import PartitionSpec as P

HEADS = 8
HD = 64
BLK = 128
RAD = 1
CAND = 2 * RAD + 1
PAIRS = HEADS // 2
PAIR = 2 * HD
RIM = RAD * BLK
BIG_NEGATIVE = -1e30
SCALE = HD ** (-0.5)
BF16 = jnp.bfloat16
F32 = jnp.float32


def dot(a, b, contract):
    return lax.dot_general(a, b, (contract, ((), ())), preferred_element_type=F32)


def two_heads(block, axis):
    feature = lax.broadcasted_iota(jnp.int32, block.shape, axis)
    zero = jnp.zeros_like(block)
    return jnp.concatenate(
        [jnp.where(feature < HD, block, zero), jnp.where(feature < HD, zero, block)], axis=1 - axis
    )


def own_features(both):
    return jnp.concatenate([both[:HD, :BLK], both[HD:, BLK:]], axis=0)


def spread(row):
    return jnp.concatenate(
        [
            jnp.broadcast_to(row[:, :BLK], (HD, BLK)),
            jnp.broadcast_to(row[:, BLK:], (HD, BLK)),
        ],
        axis=0,
    )


def own_candidates(b, blocks):
    return max(0, RAD - b), min(CAND - 1, blocks - 1 - b + RAD)


def own_rows(b, blocks):
    first, last = own_candidates(b, blocks)
    return slice((b + first - RAD) * BLK, (b + last - RAD + 1) * BLK)


def masked(bias, b, c, part):
    return part + bias[b * CAND + c]


def pairs_of(blocks):
    for b in range(blocks):
        for p in range(PAIRS):
            yield b, slice(b * BLK, (b + 1) * BLK), slice(p * PAIR, (p + 1) * PAIR), p


def at_core():
    return lax.rem(lax.axis_index("ctx"), 2)


def rim_block(blocks, over_link):
    core = at_core()
    upper = core if over_link else 1 - core
    return upper * (blocks - 1), upper * (CAND - 1)


def rows_of(b):
    return pl.ds(pl.multiple_of(b * BLK, BLK), BLK)


def copy_all(pairs, sems):
    copies = [pltpu.make_async_copy(x, y, sems.at[i]) for i, (x, y) in enumerate(pairs)]
    for copy in copies:
        copy.start()
    for copy in copies:
        copy.wait()


def pack_link_kernel(k, v, out, sems):
    rows = rows_of(rim_block(k.shape[0] // BLK, True)[0])
    copy_all(((k.at[rows], out.at[0]), (v.at[rows], out.at[1])), sems)


def pack_chip_kernel(k, v, k_out, v_out, sems):
    rows = rows_of(rim_block(k.shape[0] // BLK, False)[0])
    copy_all(((k.at[rows], k_out), (v.at[rows], v_out)), sems)


def own_kernel(
    bias, q_arg, k_arg, v_arg, g_arg, w_arg,
    q, k, v, g_low, g_high, w_out, own_t, stats, exps, grad_t, rounded, sems,
):
    half = g_low.shape[0]
    pairs = (
        (q_arg, q),
        (k_arg, k),
        (v_arg, v),
        (g_arg.at[:half], g_low),
        (g_arg.at[half:], g_high),
        (w_arg, w_out),
    )
    copies = [pltpu.make_async_copy(x, y, sems.at[i]) for i, (x, y) in enumerate(pairs)]
    for copy in copies:
        copy.start()
    copies[0].wait()
    copies[1].wait()
    blocks = q.shape[0] // BLK
    for b, rows, cols, p in pairs_of(blocks):
        first, last = own_candidates(b, blocks)
        here = own_rows(b, blocks)
        scores = dot(k[here, cols], two_heads(q[rows, cols] * SCALE, 1), ((1,), (1,)))
        for c in range(first, last + 1):
            part = slice((c - first) * BLK, (c - first + 1) * BLK)
            value = scores[part]
            exps[b, p, part] = value if c == RAD else masked(bias, b, c, value)
    for b, rows, cols, p in pairs_of(blocks):
        here = own_rows(b, blocks)
        keys = slice(0, here.stop - here.start)
        scores = exps[b, p, keys]
        top = jnp.max(scores, axis=0, keepdims=True)
        e = jnp.exp(scores - top)
        exps[b, p, keys] = e
        rounded[b, p, keys] = e.astype(BF16)
        stats[0, b, p : p + 1] = top
        stats[1, b, p : p + 1] = jnp.sum(e, axis=0, keepdims=True)
    copies[2].wait()
    for b, rows, cols, p in pairs_of(blocks):
        here = own_rows(b, blocks)
        e = rounded[b, p, : here.stop - here.start]
        own_t[b, cols] = own_features(dot(v[here, cols], e, ((0,), (0,))))
    for copy in copies[3:]:
        copy.wait()
    both = jnp.concatenate([g_low[...], g_high[...]], axis=0)
    for b in range(blocks):
        rows = slice(b * BLK, (b + 1) * BLK)
        grad_t[b] = dot(w_out[...], both[rows], ((1,), (1,))).astype(BF16)


def pair_cols(p):
    return slice(p * PAIR, (p + 1) * PAIR)


def with_rim(bias, q, rim_k, rim_v, b, c, old, exps, rounded):
    for p in range(PAIRS):
        q2 = two_heads(q[rows_of(b), pair_cols(p)] * SCALE, 1)
        scores = dot(rim_k[:, pair_cols(p)], q2, ((1,), (1,)))
        exps[p] = masked(bias, b, c, scores)
    results = []
    for p in range(PAIRS):
        old_top, old_sum = old(p)
        scores = exps[p]
        top = jnp.maximum(old_top, jnp.max(scores, axis=0, keepdims=True))
        kept = jnp.exp(old_top - top)
        e = jnp.exp(scores - top)
        exps[p] = e
        rounded[p] = e.astype(BF16)
        results.append((top, kept, old_sum * kept + jnp.sum(e, axis=0, keepdims=True)))
    parts = [
        own_features(dot(rim_v[:, pair_cols(p)], rounded[p], ((0,), (0,)))) for p in range(PAIRS)
    ]
    return [(*result, part) for result, part in zip(results, parts)]


def chip_kernel(bias, q, rim_k, rim_v, own_t, stats, chip_t, chip_stats, exps, rounded):
    blocks = q.shape[0] // BLK
    b, c = rim_block(blocks, False)

    def old(p):
        return stats[0, b, p : p + 1], stats[1, b, p : p + 1]

    results = with_rim(bias, q, rim_k, rim_v, b, c, old, exps, rounded)
    for p, (top, kept, count, part) in enumerate(results):
        at = slice(p, p + 1)
        if blocks == 1:
            chip_t[pair_cols(p)] = own_t[b, pair_cols(p)] * spread(kept) + part
            chip_stats[0, at], chip_stats[1, at] = top, count
        else:
            share = 1.0 / count
            attn = own_t[b, pair_cols(p)] * spread(kept * share) + part * spread(share)
            chip_t[pair_cols(p)] = attn
            chip_stats[0, at], chip_stats[1, at] = share, kept * share


def forward_kernel(
    bias, q, rim, own_t, stats, chip_t, chip_stats,
    attn_t, mine, other, exps, own_factors, rim_factors, rounded,
):
    blocks = q.shape[0] // BLK
    b, c = rim_block(blocks, True)
    at_chip, _ = rim_block(blocks, False)

    def old(p):
        at = slice(p, p + 1)
        if blocks == 1:
            return chip_stats[0, at], chip_stats[1, at]
        return stats[0, b, at], stats[1, b, at]

    results = with_rim(bias, q, rim.at[0], rim.at[1], b, c, old, exps, rounded)
    for p, (top, kept, count, part) in enumerate(results):
        at = slice(p, p + 1)
        cols = pair_cols(p)
        base = chip_t[cols] if blocks == 1 else own_t[b, cols]
        share = 1.0 / count
        attn_t[b, cols] = (base * spread(kept * share) + part * spread(share)).astype(BF16)
        rim_factors[0, at] = share
        if blocks == 1:
            rim_factors[1, at] = kept * share
            own_factors[0, at] = jnp.exp(stats[0, 0, at] - top) * share
        else:
            own_factors[b, at] = kept * share
            attn_t[at_chip, cols] = chip_t[cols].astype(BF16)
            rim_factors[1, at] = chip_stats[0, at]
            own_factors[at_chip, at] = chip_stats[1, at]
        for inner in range(1, blocks - 1):
            share = 1.0 / stats[1, inner, at]
            attn_t[inner, cols] = (own_t[inner, cols] * spread(share)).astype(BF16)
            own_factors[inner, at] = share
    first_core = at_core() == 0
    chips, rows, _ = mine.shape
    for i in range(chips):
        for block in range(blocks):
            tokens = slice(block * BLK, (block + 1) * BLK)
            even = attn_t[block, 2 * i * rows : (2 * i + 1) * rows]
            odd = attn_t[block, (2 * i + 1) * rows : (2 * i + 2) * rows]
            mine[i, :, tokens] = jnp.where(first_core, even, odd)
            other[i, :, tokens] = jnp.where(first_core, odd, even)


def flat_dot(attn, g_low, g_high):
    chips, rows, tokens = attn.shape
    g = jnp.concatenate([g_low[...], g_high[...]], axis=0)
    return dot(attn[...].reshape(chips * rows, tokens), g, ((1,), (0,)))


def product_kernel(mine, g_low, g_high, product):
    product[...] = flat_dot(mine, g_low, g_high)


def score_grads(probs, dprob, delta):
    return (probs * (dprob - delta)).astype(BF16), probs.astype(BF16)


def rim_kernel(
    q, link, chip_k, chip_v, grad_t, attn_t, link_exps, chip_exps, rim_factors, before,
    link_back, chip_back, deltas, query_t, dprobs, dscores, rounded,
):
    blocks = q.shape[0] // BLK
    sides = (
        (rim_block(blocks, True)[0], link.at[0], link.at[1], link_exps, link_back.at[0], link_back.at[1]),
        (rim_block(blocks, False)[0], chip_k, chip_v, chip_exps, chip_back.at[0], chip_back.at[1]),
    )
    for i, (b, _, rim_v, _, _, _) in enumerate(sides):
        for p in range(PAIRS):
            g2_t = two_heads(grad_t[b, pair_cols(p)], 0)
            dprobs[i, p] = dot(rim_v[:, pair_cols(p)], g2_t, ((1,), (0,)))
    for b, _, cols, p in pairs_of(blocks):
        product = grad_t[b, cols].astype(F32) * attn_t[b, cols].astype(F32)
        deltas[b, p : p + 1] = jnp.concatenate(
            [
                jnp.sum(product[:HD], axis=0, keepdims=True),
                jnp.sum(product[HD:], axis=0, keepdims=True),
            ],
            axis=1,
        )
    query_t[...] = jnp.zeros_like(query_t)
    for i, (b, _, _, exps, _, _) in enumerate(sides):
        for p in range(PAIRS):
            at = slice(p, p + 1)
            dscores[i, p], rounded[i, p] = score_grads(
                exps[p] * rim_factors[i, at], dprobs[i, p], deltas[b, at]
            )
    for i, (b, rim_k, _, _, k_back, v_back) in enumerate(sides):
        for p in range(PAIRS):
            cols = pair_cols(p)
            q2 = two_heads(q[rows_of(b), cols] * SCALE, 1)
            g2_t = two_heads(grad_t[b, cols], 0)
            k_back[:, cols] = dot(dscores[i, p], q2, ((1,), (0,))).astype(BF16)
            v_back[:, cols] = dot(rounded[i, p], g2_t, ((1,), (1,))).astype(BF16)
            query_t[b, cols] += own_features(dot(rim_k[:, cols], dscores[i, p], ((0,), (0,))))


def own_backward_kernel(
    q, k, v, grad_t, exps, factors, deltas, rim_t,
    q_grad, k_own, v_own, after, dprobs, dscores, rounded,
):
    blocks = q.shape[0] // BLK
    for b, _, cols, p in pairs_of(blocks):
        here = own_rows(b, blocks)
        g2_t = two_heads(grad_t[b, cols], 0)
        dprobs[b, p, : here.stop - here.start] = dot(v[here, cols], g2_t, ((1,), (0,)))
    for b, _, _, p in pairs_of(blocks):
        here = own_rows(b, blocks)
        keys = slice(0, here.stop - here.start)
        dscores[b, p, keys], rounded[b, p, keys] = score_grads(
            exps[b, p, keys] * factors[b, p : p + 1], dprobs[b, p, keys], deltas[b, p : p + 1]
        )
    k_sums, v_sums = {}, {}
    for b, rows, cols, p in pairs_of(blocks):
        here = own_rows(b, blocks)
        keys = slice(0, here.stop - here.start)
        q2 = two_heads(q[rows, cols] * SCALE, 1)
        g2_t = two_heads(grad_t[b, cols], 0)
        dscore = dscores[b, p, keys]
        k_part = dot(dscore, q2, ((1,), (0,)))
        v_part = dot(rounded[b, p, keys], g2_t, ((1,), (1,)))
        for at in range(here.start, here.stop, BLK):
            part = slice(at - here.start, at - here.start + BLK)
            for sums, value in ((k_sums, k_part), (v_sums, v_part)):
                sums.setdefault((at, p), []).append(value[part])
        query_t = own_features(dot(k[here, cols], dscore, ((0,), (0,)))) + rim_t[b, cols]
        q_grad[rows, cols] = (query_t * SCALE).T.astype(BF16)
    for out, sums in ((k_own, k_sums), (v_own, v_sums)):
        for (at, p), values in sums.items():
            out[at : at + BLK, pair_cols(p)] = functools.reduce(jnp.add, values)
    after[...] = jnp.zeros_like(after)


def output_kernel(attn_t, w_out, before, output):
    for b in range(attn_t.shape[0]):
        part = dot(attn_t[b], w_out[...], ((0,), (0,)))
        output[b * BLK : (b + 1) * BLK] = part.astype(BF16)


def halves_kernel(product, other, g_low, g_high, *outs):
    pieces, after = outs[:-1], outs[-1]
    at_dp = lax.axis_index("dp")
    chips, rows, cols = pieces[0].shape
    if cols % BLK == 0:
        flat = other[...].reshape(chips * rows, other.shape[2])
        for s in range(len(pieces)):
            at = pl.ds(pl.multiple_of((at_dp ^ s) * cols, BLK), cols)
            g = jnp.concatenate([g_low[:, at], g_high[:, at]], axis=0)
            value = product[:, at] + dot(flat, g, ((1,), (0,)))
            pieces[s][...] = value.astype(BF16).reshape(chips, rows, cols)
    else:
        both = (product[...] + flat_dot(other, g_low, g_high)).astype(BF16)
        for d in range(len(pieces)):
            value = both[:, d * cols : (d + 1) * cols].reshape(chips, rows, cols)
            for s in range(len(pieces)):

                @pl.when((at_dp ^ s) == d)
                def _(s=s, value=value):
                    pieces[s][...] = value

    after[...] = jnp.zeros_like(after)


def chips_kernel(*refs):
    parts, outs = refs[: lax.axis_size("dp")], refs[lax.axis_size("dp") + 1 :]
    chip = lax.div(lax.axis_index("ctx"), 2)
    for s, out in enumerate(outs):
        out[...] = total([part[chip ^ s] for part in parts]).astype(BF16)


def piece_kernel(scale, count, *refs):
    refs[-1][...] = (total([part[...] for part in refs[:count]]) * scale).astype(BF16)


def rim_sum_kernel(k_own, v_own, link_kv, chip_kv, k_grad, v_grad):
    tokens = k_own.shape[0]
    first_core = at_core() == 0
    for i, (own, grad) in enumerate(((k_own, k_grad), (v_own, v_grad))):
        link, chip = link_kv[i].astype(F32), chip_kv[i].astype(F32)
        low = jnp.where(first_core, link, chip)
        high = jnp.where(first_core, chip, link)
        if tokens == RIM:
            grad[...] = (own[...] + low + high).astype(BF16)
        else:
            grad[:RIM] = (own[:RIM] + low).astype(BF16)
            if tokens > 2 * RIM:
                grad[RIM : tokens - RIM] = own[RIM : tokens - RIM].astype(BF16)
            grad[tokens - RIM :] = (own[tokens - RIM :] + high).astype(BF16)


def columns_kernel(*refs):
    pieces, weight_grad = refs[:-1], refs[-1]
    at_dp = lax.axis_index("dp")
    cols = pieces[0].shape[1]
    for d in range(len(pieces)):
        value = pieces[0][...]
        for s in range(1, len(pieces)):
            value = jnp.where((at_dp ^ s) == d, pieces[s][...], value)
        weight_grad[:, d * cols : (d + 1) * cols] = value.astype(F32)


def vmem(*shape, dtype=BF16):
    return pltpu.VMEM(shape, dtype)


def hbm(*shape, dtype=BF16):
    return jax.ShapeDtypeStruct(shape, dtype)


def call(kernel, outs, flops, *args, scratch=()):
    in_vmem = pl.BlockSpec(memory_space=pltpu.VMEM)
    return pl.pallas_call(
        kernel,
        out_shape=outs,
        in_specs=[in_vmem] * len(args),
        out_specs=[in_vmem] * len(outs),
        scratch_shapes=list(scratch),
        compiler_params=pltpu.CompilerParams(vmem_limit_bytes=24 * 1024 * 1024),
        cost_estimate=pl.CostEstimate(flops=flops, bytes_accessed=flops // 250, transcendentals=0),
    )(*args)


def call_on_hbm(kernel, outs, *args, beside=(), scratch=()):
    return pl.pallas_call(
        kernel,
        out_shape=outs,
        in_specs=[pl.BlockSpec(memory_space=pltpu.VMEM)] * len(beside)
        + [pl.BlockSpec(memory_space=pltpu.HBM)] * len(args),
        out_specs=[pl.BlockSpec(memory_space=pltpu.VMEM)] * len(outs),
        scratch_shapes=list(scratch),
        compiler_params=pltpu.CompilerParams(vmem_limit_bytes=8 * 1024 * 1024),
        cost_estimate=pl.CostEstimate(flops=10**6, bytes_accessed=4096, transcendentals=0),
    )(*beside, *(pltpu.with_memory_space_constraint(x, pltpu.HBM) for x in args))


def swap(count, bits):
    return [(i, i ^ bits) for i in range(count)]


def over_links(count):
    return [(i, (i - 1 if i % 2 == 0 else i + 1) % count) for i in range(count)]


def total(parts):
    return functools.reduce(jnp.add, [p.astype(F32) for p in parts])


def body(queries, keys, values, out_grad, w_out, block_mask):
    q, k, v, g = queries[0], keys[0], values[0], out_grad[0]
    tokens, feats = q.shape
    width = g.shape[1]
    blocks = tokens // BLK
    ctx, dp = lax.axis_size("ctx"), lax.axis_size("dp")
    chips = ctx // 2
    at_ctx = lax.axis_index("ctx")
    rows, cols = feats // ctx, width // dp

    rim = vmem(RIM, feats)
    sems = [pltpu.SemaphoreType.DMA((2,))]
    (to_link,) = call_on_hbm(pack_link_kernel, [vmem(2, RIM, feats)], k, v, scratch=sems)
    to_chip = call_on_hbm(pack_chip_kernel, [rim, rim], k, v, scratch=sems)
    link = lax.ppermute(to_link, "ctx", over_links(ctx))
    chip_k, chip_v = (lax.ppermute(x, "ctx", swap(ctx, 1)) for x in to_chip)
    mask = lax.dynamic_slice_in_dim(block_mask[0], at_ctx * blocks, blocks, 0)
    bias = jnp.where(mask == 1, 0.0, BIG_NEGATIVE).astype(F32).reshape(blocks * CAND, 1, 1)
    bias = jnp.broadcast_to(bias, (blocks * CAND, 1, 2 * BLK))
    args = (q, k, v, g, w_out)
    own_keys = min(CAND, blocks) * BLK
    own_scores = (blocks, PAIRS, own_keys, 2 * BLK)
    rim_scores = (PAIRS, RIM, 2 * BLK)
    half = vmem(tokens // 2, width)
    q, k, v, g_low, g_high, w_out, own_t, stats, own_exps, grad_t = call_on_hbm(
        own_kernel,
        [vmem(tokens, feats)] * 3
        + [
            half,
            half,
            vmem(feats, width),
            vmem(blocks, feats, BLK, dtype=F32),
            vmem(2, blocks, PAIRS, 2 * BLK, dtype=F32),
            vmem(*own_scores, dtype=F32),
            vmem(blocks, feats, BLK),
        ],
        *args,
        beside=(bias,),
        scratch=[vmem(*own_scores), pltpu.SemaphoreType.DMA((6,))],
    )
    sibling_g = [
        pltpu.with_memory_space_constraint(lax.ppermute(x, "ctx", swap(ctx, 1)), pltpu.VMEM)
        for x in (g_low, g_high)
    ]
    chip_t, chip_stats, chip_exps = call(
        chip_kernel,
        [
            vmem(feats, BLK, dtype=F32),
            vmem(2, PAIRS, 2 * BLK, dtype=F32),
            vmem(*rim_scores, dtype=F32),
        ],
        10**6,
        bias, q, chip_k, chip_v, own_t, stats,
        scratch=[vmem(*rim_scores)],
    )
    attn_t, mine, other, link_exps, own_factors, rim_factors = call(
        forward_kernel,
        [
            vmem(blocks, feats, BLK),
            vmem(chips, rows, tokens),
            vmem(chips, rows, tokens),
            vmem(*rim_scores, dtype=F32),
            vmem(blocks, PAIRS, 2 * BLK, dtype=F32),
            vmem(2, PAIRS, 2 * BLK, dtype=F32),
        ],
        10**6,
        bias, q, link, own_t, stats, chip_t, chip_stats,
        scratch=[vmem(*rim_scores)],
    )

    other = lax.ppermute(other, "ctx", swap(ctx, 1))
    other = pltpu.with_memory_space_constraint(other, pltpu.VMEM)
    (product,) = call(product_kernel, [vmem(chips * rows, width, dtype=F32)], 10**6, mine, g_low, g_high)
    *halves, after = call(
        halves_kernel,
        [vmem(chips, rows, cols)] * dp + [vmem(8, 128, dtype=F32)],
        10**6,
        product, other, *sibling_g,
    )
    *back, deltas, rim_t = call(
        rim_kernel,
        [
            vmem(2, RIM, feats),
            vmem(2, RIM, feats),
            vmem(blocks, PAIRS, 2 * BLK, dtype=F32),
            vmem(blocks, feats, BLK, dtype=F32),
        ],
        10**6,
        q, link, chip_k, chip_v, grad_t, attn_t, link_exps, chip_exps, rim_factors, after,
        scratch=[vmem(2, *rim_scores, dtype=F32), vmem(2, *rim_scores), vmem(2, *rim_scores)],
    )
    link_back = lax.ppermute(back[0], "ctx", over_links(ctx))
    chip_back = lax.ppermute(back[1], "ctx", swap(ctx, 1))
    q_grad, k_own, v_own, after = call(
        own_backward_kernel,
        [
            hbm(tokens, feats),
            vmem(tokens, feats, dtype=F32),
            vmem(tokens, feats, dtype=F32),
            vmem(8, 128, dtype=F32),
        ],
        5 * 10**9,
        q, k, v, grad_t, own_exps, own_factors, deltas, rim_t,
        scratch=[vmem(*own_scores, dtype=F32), vmem(*own_scores), vmem(*own_scores)],
    )

    halves = [halves[0]] + [lax.ppermute(halves[s], "dp", swap(dp, s)) for s in range(1, dp)]
    quarters = call(chips_kernel, [vmem(rows, cols)] * chips, 10**6, *halves, after)
    (output,) = call(output_kernel, [hbm(tokens, width)], 5 * 10**9, attn_t, w_out, quarters[0])
    quarters = [quarters[0]] + [
        lax.ppermute(quarters[s], "ctx", swap(ctx, 2 * s)) for s in range(chips - 1, 0, -1)
    ]
    (piece,) = call(
        functools.partial(piece_kernel, (dp * tokens * ctx) ** (-0.5), chips),
        [vmem(rows, cols)],
        10**6,
        *quarters, link_back,
    )
    pieces = [piece] + [lax.ppermute(piece, "dp", swap(dp, s)) for s in range(1, dp)]
    k_grad, v_grad = call(
        rim_sum_kernel, [hbm(tokens, feats)] * 2, 10**6, k_own, v_own, link_back, chip_back
    )
    (weight_grad,) = call(columns_kernel, [hbm(rows, width, dtype=F32)], 10**6, *pieces)
    return (output[None], q_grad[None], k_grad[None], v_grad[None], weight_grad)


def solution(mesh):
    rows = P("dp", "ctx", None)
    return jax.shard_map(
        body,
        mesh=mesh,
        in_specs=(rows, rows, rows, rows, P(), P("dp", None, None)),
        out_specs=(rows, rows, rows, rows, P("ctx", None)),
        check_vma=False,
    )
```

```python
import functools

import jax
import jax.numpy as jnp
from jax import lax
from jax.experimental import pallas as pl
from jax.experimental.pallas import tpu as pltpu
from jax.sharding import PartitionSpec as P

HEADS = 8
HD = 64
BLK = 128
RAD = 1
CAND = 2 * RAD + 1
PAIRS = HEADS // 2
PAIR = 2 * HD
RIM = RAD * BLK
BIG_NEGATIVE = -1e30
SCALE = HD ** (-0.5)
BF16 = jnp.bfloat16
F32 = jnp.float32


def dot(a, b, contract):
    return lax.dot_general(a, b, (contract, ((), ())), preferred_element_type=F32)


def two_heads(block, axis):
    feature = lax.broadcasted_iota(jnp.int32, block.shape, axis)
    zero = jnp.zeros_like(block)
    return jnp.concatenate(
        [jnp.where(feature < HD, block, zero), jnp.where(feature < HD, zero, block)], axis=1 - axis
    )


def own_features(both):
    return jnp.concatenate([both[:HD, :BLK], both[HD:, BLK:]], axis=0)


def spread(row):
    return jnp.concatenate(
        [
            jnp.broadcast_to(row[:, :BLK], (HD, BLK)),
            jnp.broadcast_to(row[:, BLK:], (HD, BLK)),
        ],
        axis=0,
    )


def own_candidates(b, blocks):
    return max(0, RAD - b), min(CAND - 1, blocks - 1 - b + RAD)


def own_rows(b, blocks):
    first, last = own_candidates(b, blocks)
    return slice((b + first - RAD) * BLK, (b + last - RAD + 1) * BLK)


def masked(bias, b, c, part):
    return part + bias[b * CAND + c]


def pairs_of(blocks):
    for b in range(blocks):
        for p in range(PAIRS):
            yield b, slice(b * BLK, (b + 1) * BLK), slice(p * PAIR, (p + 1) * PAIR), p


def at_core():
    return lax.rem(lax.axis_index("ctx"), 2)


def rim_block(blocks, over_link):
    core = at_core()
    upper = core if over_link else 1 - core
    return upper * (blocks - 1), upper * (CAND - 1)


def rows_of(b):
    return pl.ds(pl.multiple_of(b * BLK, BLK), BLK)


def copy_all(pairs, sems):
    copies = [pltpu.make_async_copy(x, y, sems.at[i]) for i, (x, y) in enumerate(pairs)]
    for copy in copies:
        copy.start()
    for copy in copies:
        copy.wait()


def pack_link_kernel(k, v, out, sems):
    rows = rows_of(rim_block(k.shape[0] // BLK, True)[0])
    copy_all(((k.at[rows], out.at[0]), (v.at[rows], out.at[1])), sems)


def pack_chip_kernel(k, v, k_out, v_out, sems):
    rows = rows_of(rim_block(k.shape[0] // BLK, False)[0])
    copy_all(((k.at[rows], k_out), (v.at[rows], v_out)), sems)


def own_kernel(
    bias, q_arg, k_arg, v_arg, g_arg, w_arg,
    q, k, v, g_low, g_high, w_out, own_t, stats, exps, grad_t, rounded, sems,
):
    half = g_low.shape[0]
    pairs = (
        (q_arg, q),
        (k_arg, k),
        (v_arg, v),
        (g_arg.at[:half], g_low),
        (g_arg.at[half:], g_high),
        (w_arg, w_out),
    )
    copies = [pltpu.make_async_copy(x, y, sems.at[i]) for i, (x, y) in enumerate(pairs)]
    for copy in copies:
        copy.start()
    copies[0].wait()
    copies[1].wait()
    blocks = q.shape[0] // BLK
    for b, rows, cols, p in pairs_of(blocks):
        first, last = own_candidates(b, blocks)
        here = own_rows(b, blocks)
        scores = dot(k[here, cols], two_heads(q[rows, cols] * SCALE, 1), ((1,), (1,)))
        for c in range(first, last + 1):
            part = slice((c - first) * BLK, (c - first + 1) * BLK)
            value = scores[part]
            exps[b, p, part] = value if c == RAD else masked(bias, b, c, value)
    for b, rows, cols, p in pairs_of(blocks):
        here = own_rows(b, blocks)
        keys = slice(0, here.stop - here.start)
        scores = exps[b, p, keys]
        top = jnp.max(scores, axis=0, keepdims=True)
        e = jnp.exp(scores - top)
        exps[b, p, keys] = e
        rounded[b, p, keys] = e.astype(BF16)
        stats[0, b, p : p + 1] = top
        stats[1, b, p : p + 1] = jnp.sum(e, axis=0, keepdims=True)
    copies[2].wait()
    for b, rows, cols, p in pairs_of(blocks):
        here = own_rows(b, blocks)
        e = rounded[b, p, : here.stop - here.start]
        own_t[b, cols] = own_features(dot(v[here, cols], e, ((0,), (0,))))
    for copy in copies[3:]:
        copy.wait()
    both = jnp.concatenate([g_low[...], g_high[...]], axis=0)
    for b in range(blocks):
        rows = slice(b * BLK, (b + 1) * BLK)
        grad_t[b] = dot(w_out[...], both[rows], ((1,), (1,))).astype(BF16)


def pair_cols(p):
    return slice(p * PAIR, (p + 1) * PAIR)


def with_rim(bias, q, rim_k, rim_v, b, c, old, exps, rounded):
    for p in range(PAIRS):
        q2 = two_heads(q[rows_of(b), pair_cols(p)] * SCALE, 1)
        scores = dot(rim_k[:, pair_cols(p)], q2, ((1,), (1,)))
        exps[p] = masked(bias, b, c, scores)
    results = []
    for p in range(PAIRS):
        old_top, old_sum = old(p)
        scores = exps[p]
        top = jnp.maximum(old_top, jnp.max(scores, axis=0, keepdims=True))
        kept = jnp.exp(old_top - top)
        e = jnp.exp(scores - top)
        exps[p] = e
        rounded[p] = e.astype(BF16)
        results.append((top, kept, old_sum * kept + jnp.sum(e, axis=0, keepdims=True)))
    parts = [
        own_features(dot(rim_v[:, pair_cols(p)], rounded[p], ((0,), (0,)))) for p in range(PAIRS)
    ]
    return [(*result, part) for result, part in zip(results, parts)]


def chip_kernel(bias, q, rim_k, rim_v, own_t, stats, chip_t, chip_stats, exps, rounded):
    blocks = q.shape[0] // BLK
    b, c = rim_block(blocks, False)

    def old(p):
        return stats[0, b, p : p + 1], stats[1, b, p : p + 1]

    results = with_rim(bias, q, rim_k, rim_v, b, c, old, exps, rounded)
    for p, (top, kept, count, part) in enumerate(results):
        at = slice(p, p + 1)
        if blocks == 1:
            chip_t[pair_cols(p)] = own_t[b, pair_cols(p)] * spread(kept) + part
            chip_stats[0, at], chip_stats[1, at] = top, count
        else:
            share = 1.0 / count
            attn = own_t[b, pair_cols(p)] * spread(kept * share) + part * spread(share)
            chip_t[pair_cols(p)] = attn
            chip_stats[0, at], chip_stats[1, at] = share, kept * share


def forward_kernel(
    bias, q, rim, own_t, stats, chip_t, chip_stats,
    attn_t, mine, other, exps, own_factors, rim_factors, rounded,
):
    blocks = q.shape[0] // BLK
    b, c = rim_block(blocks, True)
    at_chip, _ = rim_block(blocks, False)

    def old(p):
        at = slice(p, p + 1)
        if blocks == 1:
            return chip_stats[0, at], chip_stats[1, at]
        return stats[0, b, at], stats[1, b, at]

    results = with_rim(bias, q, rim.at[0], rim.at[1], b, c, old, exps, rounded)
    for p, (top, kept, count, part) in enumerate(results):
        at = slice(p, p + 1)
        cols = pair_cols(p)
        base = chip_t[cols] if blocks == 1 else own_t[b, cols]
        share = 1.0 / count
        attn_t[b, cols] = (base * spread(kept * share) + part * spread(share)).astype(BF16)
        rim_factors[0, at] = share
        if blocks == 1:
            rim_factors[1, at] = kept * share
            own_factors[0, at] = jnp.exp(stats[0, 0, at] - top) * share
        else:
            own_factors[b, at] = kept * share
            attn_t[at_chip, cols] = chip_t[cols].astype(BF16)
            rim_factors[1, at] = chip_stats[0, at]
            own_factors[at_chip, at] = chip_stats[1, at]
        for inner in range(1, blocks - 1):
            share = 1.0 / stats[1, inner, at]
            attn_t[inner, cols] = (own_t[inner, cols] * spread(share)).astype(BF16)
            own_factors[inner, at] = share
    first_core = at_core() == 0
    chips, rows, _ = mine.shape
    for i in range(chips):
        for block in range(blocks):
            tokens = slice(block * BLK, (block + 1) * BLK)
            even = attn_t[block, 2 * i * rows : (2 * i + 1) * rows]
            odd = attn_t[block, (2 * i + 1) * rows : (2 * i + 2) * rows]
            mine[i, :, tokens] = jnp.where(first_core, even, odd)
            other[i, :, tokens] = jnp.where(first_core, odd, even)


def flat_dot(attn, g_low, g_high):
    chips, rows, tokens = attn.shape
    g = jnp.concatenate([g_low[...], g_high[...]], axis=0)
    return dot(attn[...].reshape(chips * rows, tokens), g, ((1,), (0,)))


def product_kernel(mine, g_low, g_high, product):
    product[...] = flat_dot(mine, g_low, g_high)


def score_grads(probs, dprob, delta):
    return (probs * (dprob - delta)).astype(BF16), probs.astype(BF16)


def rim_kernel(
    q, link, chip_k, chip_v, grad_t, attn_t, link_exps, chip_exps, rim_factors, before,
    link_back, chip_back, deltas, query_t, dprobs, dscores, rounded,
):
    blocks = q.shape[0] // BLK
    sides = (
        (rim_block(blocks, True)[0], link.at[0], link.at[1], link_exps, link_back.at[0], link_back.at[1]),
        (rim_block(blocks, False)[0], chip_k, chip_v, chip_exps, chip_back.at[0], chip_back.at[1]),
    )
    for i, (b, _, rim_v, _, _, _) in enumerate(sides):
        for p in range(PAIRS):
            g2_t = two_heads(grad_t[b, pair_cols(p)], 0)
            dprobs[i, p] = dot(rim_v[:, pair_cols(p)], g2_t, ((1,), (0,)))
    for b, _, cols, p in pairs_of(blocks):
        product = grad_t[b, cols].astype(F32) * attn_t[b, cols].astype(F32)
        deltas[b, p : p + 1] = jnp.concatenate(
            [
                jnp.sum(product[:HD], axis=0, keepdims=True),
                jnp.sum(product[HD:], axis=0, keepdims=True),
            ],
            axis=1,
        )
    query_t[...] = jnp.zeros_like(query_t)
    for i, (b, _, _, exps, _, _) in enumerate(sides):
        for p in range(PAIRS):
            at = slice(p, p + 1)
            dscores[i, p], rounded[i, p] = score_grads(
                exps[p] * rim_factors[i, at], dprobs[i, p], deltas[b, at]
            )
    for i, (b, rim_k, _, _, k_back, v_back) in enumerate(sides):
        for p in range(PAIRS):
            cols = pair_cols(p)
            q2 = two_heads(q[rows_of(b), cols] * SCALE, 1)
            g2_t = two_heads(grad_t[b, cols], 0)
            k_back[:, cols] = dot(dscores[i, p], q2, ((1,), (0,))).astype(BF16)
            v_back[:, cols] = dot(rounded[i, p], g2_t, ((1,), (1,))).astype(BF16)
            query_t[b, cols] += own_features(dot(rim_k[:, cols], dscores[i, p], ((0,), (0,))))


def own_backward_kernel(
    q, k, v, grad_t, exps, factors, deltas, rim_t,
    q_grad, k_own, v_own, after, dprobs, dscores, rounded,
):
    blocks = q.shape[0] // BLK
    for b, _, cols, p in pairs_of(blocks):
        here = own_rows(b, blocks)
        g2_t = two_heads(grad_t[b, cols], 0)
        dprobs[b, p, : here.stop - here.start] = dot(v[here, cols], g2_t, ((1,), (0,)))
    for b, _, _, p in pairs_of(blocks):
        here = own_rows(b, blocks)
        keys = slice(0, here.stop - here.start)
        dscores[b, p, keys], rounded[b, p, keys] = score_grads(
            exps[b, p, keys] * factors[b, p : p + 1], dprobs[b, p, keys], deltas[b, p : p + 1]
        )
    k_sums, v_sums = {}, {}
    for b, rows, cols, p in pairs_of(blocks):
        here = own_rows(b, blocks)
        keys = slice(0, here.stop - here.start)
        q2 = two_heads(q[rows, cols] * SCALE, 1)
        g2_t = two_heads(grad_t[b, cols], 0)
        dscore = dscores[b, p, keys]
        k_part = dot(dscore, q2, ((1,), (0,)))
        v_part = dot(rounded[b, p, keys], g2_t, ((1,), (1,)))
        for at in range(here.start, here.stop, BLK):
            part = slice(at - here.start, at - here.start + BLK)
            for sums, value in ((k_sums, k_part), (v_sums, v_part)):
                sums.setdefault((at, p), []).append(value[part])
        query_t = own_features(dot(k[here, cols], dscore, ((0,), (0,)))) + rim_t[b, cols]
        q_grad[rows, cols] = (query_t * SCALE).T.astype(BF16)
    for out, sums in ((k_own, k_sums), (v_own, v_sums)):
        for (at, p), values in sums.items():
            out[at : at + BLK, pair_cols(p)] = functools.reduce(jnp.add, values)
    after[...] = jnp.zeros_like(after)


def output_kernel(attn_t, w_out, before, output):
    for b in range(attn_t.shape[0]):
        part = dot(attn_t[b], w_out[...], ((0,), (0,)))
        output[b * BLK : (b + 1) * BLK] = part.astype(BF16)


def halves_kernel(product, other, g_low, g_high, *outs):
    pieces, after = outs[:-1], outs[-1]
    at_dp = lax.axis_index("dp")
    chips, rows, cols = pieces[0].shape
    if cols % BLK == 0:
        flat = other[...].reshape(chips * rows, other.shape[2])
        for s in range(len(pieces)):
            at = pl.ds(pl.multiple_of((at_dp ^ s) * cols, BLK), cols)
            g = jnp.concatenate([g_low[:, at], g_high[:, at]], axis=0)
            value = product[:, at] + dot(flat, g, ((1,), (0,)))
            pieces[s][...] = value.astype(BF16).reshape(chips, rows, cols)
    else:
        both = (product[...] + flat_dot(other, g_low, g_high)).astype(BF16)
        for d in range(len(pieces)):
            value = both[:, d * cols : (d + 1) * cols].reshape(chips, rows, cols)
            for s in range(len(pieces)):

                @pl.when((at_dp ^ s) == d)
                def _(s=s, value=value):
                    pieces[s][...] = value

    after[...] = jnp.zeros_like(after)


def chips_kernel(*refs):
    parts, outs = refs[: lax.axis_size("dp")], refs[lax.axis_size("dp") + 1 :]
    chip = lax.div(lax.axis_index("ctx"), 2)
    for s, out in enumerate(outs):
        out[...] = total([part[chip ^ s] for part in parts]).astype(BF16)


def piece_kernel(scale, count, *refs):
    refs[-1][...] = (total([part[...] for part in refs[:count]]) * scale).astype(BF16)


def rim_sum_kernel(k_own, v_own, link_kv, chip_kv, k_grad, v_grad):
    tokens = k_own.shape[0]
    first_core = at_core() == 0
    for i, (own, grad) in enumerate(((k_own, k_grad), (v_own, v_grad))):
        link, chip = link_kv[i].astype(F32), chip_kv[i].astype(F32)
        low = jnp.where(first_core, link, chip)
        high = jnp.where(first_core, chip, link)
        if tokens == RIM:
            grad[...] = (own[...] + low + high).astype(BF16)
        else:
            grad[:RIM] = (own[:RIM] + low).astype(BF16)
            if tokens > 2 * RIM:
                grad[RIM : tokens - RIM] = own[RIM : tokens - RIM].astype(BF16)
            grad[tokens - RIM :] = (own[tokens - RIM :] + high).astype(BF16)


def columns_kernel(*refs):
    pieces, weight_grad = refs[:1] + refs[-2:0:-1], refs[-1]
    at_dp = lax.axis_index("dp")
    cols = pieces[0].shape[1]
    for d in range(len(pieces)):
        value = pieces[0][...]
        for s in range(1, len(pieces)):
            value = jnp.where((at_dp ^ s) == d, pieces[s][...], value)
        weight_grad[:, d * cols : (d + 1) * cols] = value.astype(F32)


def vmem(*shape, dtype=BF16):
    return pltpu.VMEM(shape, dtype)


def hbm(*shape, dtype=BF16):
    return jax.ShapeDtypeStruct(shape, dtype)


def call(kernel, outs, flops, *args, scratch=()):
    in_vmem = pl.BlockSpec(memory_space=pltpu.VMEM)
    return pl.pallas_call(
        kernel,
        out_shape=outs,
        in_specs=[in_vmem] * len(args),
        out_specs=[in_vmem] * len(outs),
        scratch_shapes=list(scratch),
        compiler_params=pltpu.CompilerParams(vmem_limit_bytes=24 * 1024 * 1024),
        cost_estimate=pl.CostEstimate(flops=flops, bytes_accessed=flops // 250, transcendentals=0),
    )(*args)


def call_on_hbm(kernel, outs, *args, beside=(), scratch=()):
    return pl.pallas_call(
        kernel,
        out_shape=outs,
        in_specs=[pl.BlockSpec(memory_space=pltpu.VMEM)] * len(beside)
        + [pl.BlockSpec(memory_space=pltpu.HBM)] * len(args),
        out_specs=[pl.BlockSpec(memory_space=pltpu.VMEM)] * len(outs),
        scratch_shapes=list(scratch),
        compiler_params=pltpu.CompilerParams(vmem_limit_bytes=8 * 1024 * 1024),
        cost_estimate=pl.CostEstimate(flops=10**6, bytes_accessed=4096, transcendentals=0),
    )(*beside, *(pltpu.with_memory_space_constraint(x, pltpu.HBM) for x in args))


def swap(count, bits):
    return [(i, i ^ bits) for i in range(count)]


def over_links(count):
    return [(i, (i - 1 if i % 2 == 0 else i + 1) % count) for i in range(count)]


def total(parts):
    return functools.reduce(jnp.add, [p.astype(F32) for p in parts])


def body(queries, keys, values, out_grad, w_out, block_mask):
    q, k, v, g = queries[0], keys[0], values[0], out_grad[0]
    tokens, feats = q.shape
    width = g.shape[1]
    blocks = tokens // BLK
    ctx, dp = lax.axis_size("ctx"), lax.axis_size("dp")
    chips = ctx // 2
    at_ctx = lax.axis_index("ctx")
    rows, cols = feats // ctx, width // dp

    rim = vmem(RIM, feats)
    sems = [pltpu.SemaphoreType.DMA((2,))]
    (to_link,) = call_on_hbm(pack_link_kernel, [vmem(2, RIM, feats)], k, v, scratch=sems)
    to_chip = call_on_hbm(pack_chip_kernel, [rim, rim], k, v, scratch=sems)
    link = lax.ppermute(to_link, "ctx", over_links(ctx))
    chip_k, chip_v = (lax.ppermute(x, "ctx", swap(ctx, 1)) for x in to_chip)
    mask = lax.dynamic_slice_in_dim(block_mask[0], at_ctx * blocks, blocks, 0)
    bias = jnp.where(mask == 1, 0.0, BIG_NEGATIVE).astype(F32).reshape(blocks * CAND, 1, 1)
    bias = jnp.broadcast_to(bias, (blocks * CAND, 1, 2 * BLK))
    args = (q, k, v, g, w_out)
    own_keys = min(CAND, blocks) * BLK
    own_scores = (blocks, PAIRS, own_keys, 2 * BLK)
    rim_scores = (PAIRS, RIM, 2 * BLK)
    half = vmem(tokens // 2, width)
    q, k, v, g_low, g_high, w_out, own_t, stats, own_exps, grad_t = call_on_hbm(
        own_kernel,
        [vmem(tokens, feats)] * 3
        + [
            half,
            half,
            vmem(feats, width),
            vmem(blocks, feats, BLK, dtype=F32),
            vmem(2, blocks, PAIRS, 2 * BLK, dtype=F32),
            vmem(*own_scores, dtype=F32),
            vmem(blocks, feats, BLK),
        ],
        *args,
        beside=(bias,),
        scratch=[vmem(*own_scores), pltpu.SemaphoreType.DMA((6,))],
    )
    sibling_g = [
        pltpu.with_memory_space_constraint(lax.ppermute(x, "ctx", swap(ctx, 1)), pltpu.VMEM)
        for x in (g_low, g_high)
    ]
    chip_t, chip_stats, chip_exps = call(
        chip_kernel,
        [
            vmem(feats, BLK, dtype=F32),
            vmem(2, PAIRS, 2 * BLK, dtype=F32),
            vmem(*rim_scores, dtype=F32),
        ],
        10**6,
        bias, q, chip_k, chip_v, own_t, stats,
        scratch=[vmem(*rim_scores)],
    )
    attn_t, mine, other, link_exps, own_factors, rim_factors = call(
        forward_kernel,
        [
            vmem(blocks, feats, BLK),
            vmem(chips, rows, tokens),
            vmem(chips, rows, tokens),
            vmem(*rim_scores, dtype=F32),
            vmem(blocks, PAIRS, 2 * BLK, dtype=F32),
            vmem(2, PAIRS, 2 * BLK, dtype=F32),
        ],
        10**6,
        bias, q, link, own_t, stats, chip_t, chip_stats,
        scratch=[vmem(*rim_scores)],
    )

    other = lax.ppermute(other, "ctx", swap(ctx, 1))
    other = pltpu.with_memory_space_constraint(other, pltpu.VMEM)
    (product,) = call(product_kernel, [vmem(chips * rows, width, dtype=F32)], 10**6, mine, g_low, g_high)
    *halves, after = call(
        halves_kernel,
        [vmem(chips, rows, cols)] * dp + [vmem(8, 128, dtype=F32)],
        10**6,
        product, other, *sibling_g,
    )
    *back, deltas, rim_t = call(
        rim_kernel,
        [
            vmem(2, RIM, feats),
            vmem(2, RIM, feats),
            vmem(blocks, PAIRS, 2 * BLK, dtype=F32),
            vmem(blocks, feats, BLK, dtype=F32),
        ],
        10**6,
        q, link, chip_k, chip_v, grad_t, attn_t, link_exps, chip_exps, rim_factors, after,
        scratch=[vmem(2, *rim_scores, dtype=F32), vmem(2, *rim_scores), vmem(2, *rim_scores)],
    )
    link_back = lax.ppermute(back[0], "ctx", over_links(ctx))
    chip_back = lax.ppermute(back[1], "ctx", swap(ctx, 1))
    q_grad, k_own, v_own, after = call(
        own_backward_kernel,
        [
            hbm(tokens, feats),
            vmem(tokens, feats, dtype=F32),
            vmem(tokens, feats, dtype=F32),
            vmem(8, 128, dtype=F32),
        ],
        5 * 10**9,
        q, k, v, grad_t, own_exps, own_factors, deltas, rim_t,
        scratch=[vmem(*own_scores, dtype=F32), vmem(*own_scores), vmem(*own_scores)],
    )

    halves = [halves[0]] + [lax.ppermute(halves[s], "dp", swap(dp, s)) for s in range(1, dp)]
    quarters = call(chips_kernel, [vmem(rows, cols)] * chips, 10**6, *halves, after)
    (output,) = call(output_kernel, [hbm(tokens, width)], 5 * 10**9, attn_t, w_out, quarters[0])
    quarters = [quarters[0]] + [
        lax.ppermute(quarters[s], "ctx", swap(ctx, 2 * s))
        for s in (*range(chips // 2, chips), *range(chips // 2 - 1, 0, -1))
    ]
    (piece,) = call(
        functools.partial(piece_kernel, (dp * tokens * ctx) ** (-0.5), chips),
        [vmem(rows, cols)],
        10**6,
        *quarters, link_back,
    )
    pieces = [piece] + [lax.ppermute(piece, "dp", swap(dp, s)) for s in range(dp - 1, 0, -1)]
    k_grad, v_grad = call(
        rim_sum_kernel, [hbm(tokens, feats)] * 2, 10**6, k_own, v_own, link_back, chip_back
    )
    (weight_grad,) = call(columns_kernel, [hbm(rows, width, dtype=F32)], 10**6, *pieces)
    return (output[None], q_grad[None], k_grad[None], v_grad[None], weight_grad)


def solution(mesh):
    rows = P("dp", "ctx", None)
    return jax.shard_map(
        body,
        mesh=mesh,
        in_specs=(rows, rows, rows, rows, P(), P("dp", None, None)),
        out_specs=(rows, rows, rows, rows, P("ctx", None)),
        check_vma=False,
    )
```

```python
import functools

import jax
import jax.numpy as jnp
from jax import lax
from jax.experimental import pallas as pl
from jax.experimental.pallas import tpu as pltpu
from jax.sharding import PartitionSpec as P

HEADS = 8
HD = 64
BLK = 128
RAD = 1
CAND = 2 * RAD + 1
PAIRS = HEADS // 2
PAIR = 2 * HD
RIM = RAD * BLK
BIG_NEGATIVE = -1e30
SCALE = HD ** (-0.5)
BF16 = jnp.bfloat16
F32 = jnp.float32


def dot(a, b, contract):
    return lax.dot_general(a, b, (contract, ((), ())), preferred_element_type=F32)


def two_heads(block, axis):
    feature = lax.broadcasted_iota(jnp.int32, block.shape, axis)
    zero = jnp.zeros_like(block)
    return jnp.concatenate(
        [jnp.where(feature < HD, block, zero), jnp.where(feature < HD, zero, block)], axis=1 - axis
    )


def own_features(both):
    return jnp.concatenate([both[:HD, :BLK], both[HD:, BLK:]], axis=0)


def spread(row):
    return jnp.concatenate(
        [
            jnp.broadcast_to(row[:, :BLK], (HD, BLK)),
            jnp.broadcast_to(row[:, BLK:], (HD, BLK)),
        ],
        axis=0,
    )


def own_candidates(b, blocks):
    return max(0, RAD - b), min(CAND - 1, blocks - 1 - b + RAD)


def own_rows(b, blocks):
    first, last = own_candidates(b, blocks)
    return slice((b + first - RAD) * BLK, (b + last - RAD + 1) * BLK)


def masked(bias, b, c, part):
    return part + bias[b * CAND + c]


def pairs_of(blocks):
    for b in range(blocks):
        for p in range(PAIRS):
            yield b, slice(b * BLK, (b + 1) * BLK), slice(p * PAIR, (p + 1) * PAIR), p


def at_core():
    return lax.rem(lax.axis_index("ctx"), 2)


def rim_block(blocks, over_link):
    core = at_core()
    upper = core if over_link else 1 - core
    return upper * (blocks - 1), upper * (CAND - 1)


def rows_of(b):
    return pl.ds(pl.multiple_of(b * BLK, BLK), BLK)


def copy_all(pairs, sems):
    copies = [pltpu.make_async_copy(x, y, sems.at[i]) for i, (x, y) in enumerate(pairs)]
    for copy in copies:
        copy.start()
    for copy in copies:
        copy.wait()


def pack_link_kernel(k, v, out, sems):
    rows = rows_of(rim_block(k.shape[0] // BLK, True)[0])
    copy_all(((k.at[rows], out.at[0]), (v.at[rows], out.at[1])), sems)


def pack_chip_kernel(k, v, k_out, v_out, sems):
    rows = rows_of(rim_block(k.shape[0] // BLK, False)[0])
    copy_all(((k.at[rows], k_out), (v.at[rows], v_out)), sems)


def own_kernel(
    bias, q_arg, k_arg, v_arg, g_arg, w_arg,
    q, k, v, g_low, g_high, w_out, own_t, stats, exps, grad_t, rounded, sems,
):
    half = g_low.shape[0]
    pairs = (
        (q_arg, q),
        (k_arg, k),
        (v_arg, v),
        (g_arg.at[:half], g_low),
        (g_arg.at[half:], g_high),
        (w_arg, w_out),
    )
    copies = [pltpu.make_async_copy(x, y, sems.at[i]) for i, (x, y) in enumerate(pairs)]
    for copy in copies:
        copy.start()
    copies[0].wait()
    copies[1].wait()
    blocks = q.shape[0] // BLK
    for b, rows, cols, p in pairs_of(blocks):
        first, last = own_candidates(b, blocks)
        here = own_rows(b, blocks)
        scores = dot(k[here, cols], two_heads(q[rows, cols] * SCALE, 1), ((1,), (1,)))
        for c in range(first, last + 1):
            part = slice((c - first) * BLK, (c - first + 1) * BLK)
            value = scores[part]
            exps[b, p, part] = value if c == RAD else masked(bias, b, c, value)
    for b, rows, cols, p in pairs_of(blocks):
        here = own_rows(b, blocks)
        keys = slice(0, here.stop - here.start)
        scores = exps[b, p, keys]
        top = jnp.max(scores, axis=0, keepdims=True)
        e = jnp.exp(scores - top)
        exps[b, p, keys] = e
        rounded[b, p, keys] = e.astype(BF16)
        stats[0, b, p : p + 1] = top
        stats[1, b, p : p + 1] = jnp.sum(e, axis=0, keepdims=True)
    copies[2].wait()
    for b, rows, cols, p in pairs_of(blocks):
        here = own_rows(b, blocks)
        e = rounded[b, p, : here.stop - here.start]
        own_t[b, cols] = own_features(dot(v[here, cols], e, ((0,), (0,))))
    for copy in copies[3:]:
        copy.wait()
    both = jnp.concatenate([g_low[...], g_high[...]], axis=0)
    for b in range(blocks):
        rows = slice(b * BLK, (b + 1) * BLK)
        grad_t[b] = dot(w_out[...], both[rows], ((1,), (1,))).astype(BF16)


def pair_cols(p):
    return slice(p * PAIR, (p + 1) * PAIR)


def with_rim(bias, q, rim_k, rim_v, b, c, old, exps, rounded):
    for p in range(PAIRS):
        q2 = two_heads(q[rows_of(b), pair_cols(p)] * SCALE, 1)
        scores = dot(rim_k[:, pair_cols(p)], q2, ((1,), (1,)))
        exps[p] = masked(bias, b, c, scores)
    results = []
    for p in range(PAIRS):
        old_top, old_sum = old(p)
        scores = exps[p]
        top = jnp.maximum(old_top, jnp.max(scores, axis=0, keepdims=True))
        kept = jnp.exp(old_top - top)
        e = jnp.exp(scores - top)
        exps[p] = e
        rounded[p] = e.astype(BF16)
        results.append((top, kept, old_sum * kept + jnp.sum(e, axis=0, keepdims=True)))
    parts = [
        own_features(dot(rim_v[:, pair_cols(p)], rounded[p], ((0,), (0,)))) for p in range(PAIRS)
    ]
    return [(*result, part) for result, part in zip(results, parts)]


def chip_kernel(bias, q, rim_k, rim_v, own_t, stats, chip_t, chip_stats, exps, rounded):
    blocks = q.shape[0] // BLK
    b, c = rim_block(blocks, False)

    def old(p):
        return stats[0, b, p : p + 1], stats[1, b, p : p + 1]

    results = with_rim(bias, q, rim_k, rim_v, b, c, old, exps, rounded)
    for p, (top, kept, count, part) in enumerate(results):
        at = slice(p, p + 1)
        if blocks == 1:
            chip_t[pair_cols(p)] = own_t[b, pair_cols(p)] * spread(kept) + part
            chip_stats[0, at], chip_stats[1, at] = top, count
        else:
            share = 1.0 / count
            attn = own_t[b, pair_cols(p)] * spread(kept * share) + part * spread(share)
            chip_t[pair_cols(p)] = attn
            chip_stats[0, at], chip_stats[1, at] = share, kept * share


def forward_kernel(
    bias, q, rim, own_t, stats, chip_t, chip_stats,
    attn_t, mine, other, exps, own_factors, rim_factors, rounded,
):
    blocks = q.shape[0] // BLK
    b, c = rim_block(blocks, True)
    at_chip, _ = rim_block(blocks, False)

    def old(p):
        at = slice(p, p + 1)
        if blocks == 1:
            return chip_stats[0, at], chip_stats[1, at]
        return stats[0, b, at], stats[1, b, at]

    results = with_rim(bias, q, rim.at[0], rim.at[1], b, c, old, exps, rounded)
    for p, (top, kept, count, part) in enumerate(results):
        at = slice(p, p + 1)
        cols = pair_cols(p)
        base = chip_t[cols] if blocks == 1 else own_t[b, cols]
        share = 1.0 / count
        attn_t[b, cols] = (base * spread(kept * share) + part * spread(share)).astype(BF16)
        rim_factors[0, at] = share
        if blocks == 1:
            rim_factors[1, at] = kept * share
            own_factors[0, at] = jnp.exp(stats[0, 0, at] - top) * share
        else:
            own_factors[b, at] = kept * share
            attn_t[at_chip, cols] = chip_t[cols].astype(BF16)
            rim_factors[1, at] = chip_stats[0, at]
            own_factors[at_chip, at] = chip_stats[1, at]
        for inner in range(1, blocks - 1):
            share = 1.0 / stats[1, inner, at]
            attn_t[inner, cols] = (own_t[inner, cols] * spread(share)).astype(BF16)
            own_factors[inner, at] = share
    first_core = at_core() == 0
    chips, rows, _ = mine.shape
    for i in range(chips):
        for block in range(blocks):
            tokens = slice(block * BLK, (block + 1) * BLK)
            even = attn_t[block, 2 * i * rows : (2 * i + 1) * rows]
            odd = attn_t[block, (2 * i + 1) * rows : (2 * i + 2) * rows]
            mine[i, :, tokens] = jnp.where(first_core, even, odd)
            other[i, :, tokens] = jnp.where(first_core, odd, even)


def flat_dot(attn, g_low, g_high):
    chips, rows, tokens = attn.shape
    g = jnp.concatenate([g_low[...], g_high[...]], axis=0)
    return dot(attn[...].reshape(chips * rows, tokens), g, ((1,), (0,)))


def product_kernel(mine, g_low, g_high, product):
    product[...] = flat_dot(mine, g_low, g_high)


def score_grads(probs, dprob, delta):
    return (probs * (dprob - delta)).astype(BF16), probs.astype(BF16)


def rim_kernel(
    q, link, chip_k, chip_v, grad_t, attn_t, link_exps, chip_exps, rim_factors,
    link_back, chip_back, deltas, query_t, dprobs, dscores, rounded,
):
    blocks = q.shape[0] // BLK
    sides = (
        (rim_block(blocks, True)[0], link.at[0], link.at[1], link_exps, link_back.at[0], link_back.at[1]),
        (rim_block(blocks, False)[0], chip_k, chip_v, chip_exps, chip_back.at[0], chip_back.at[1]),
    )
    for i, (b, _, rim_v, _, _, _) in enumerate(sides):
        for p in range(PAIRS):
            g2_t = two_heads(grad_t[b, pair_cols(p)], 0)
            dprobs[i, p] = dot(rim_v[:, pair_cols(p)], g2_t, ((1,), (0,)))
    for b, _, cols, p in pairs_of(blocks):
        product = grad_t[b, cols].astype(F32) * attn_t[b, cols].astype(F32)
        deltas[b, p : p + 1] = jnp.concatenate(
            [
                jnp.sum(product[:HD], axis=0, keepdims=True),
                jnp.sum(product[HD:], axis=0, keepdims=True),
            ],
            axis=1,
        )
    query_t[...] = jnp.zeros_like(query_t)
    for i, (b, _, _, exps, _, _) in enumerate(sides):
        for p in range(PAIRS):
            at = slice(p, p + 1)
            dscores[i, p], rounded[i, p] = score_grads(
                exps[p] * rim_factors[i, at], dprobs[i, p], deltas[b, at]
            )
    for i, (b, rim_k, _, _, k_back, v_back) in enumerate(sides):
        for p in range(PAIRS):
            cols = pair_cols(p)
            q2 = two_heads(q[rows_of(b), cols] * SCALE, 1)
            g2_t = two_heads(grad_t[b, cols], 0)
            k_back[:, cols] = dot(dscores[i, p], q2, ((1,), (0,))).astype(BF16)
            v_back[:, cols] = dot(rounded[i, p], g2_t, ((1,), (1,))).astype(BF16)
            query_t[b, cols] += own_features(dot(rim_k[:, cols], dscores[i, p], ((0,), (0,))))


def own_backward_kernel(
    q, k, v, grad_t, exps, factors, deltas, rim_t, before,
    q_grad, k_own, v_own, after, dprobs, dscores, rounded,
):
    blocks = q.shape[0] // BLK
    for b, _, cols, p in pairs_of(blocks):
        here = own_rows(b, blocks)
        g2_t = two_heads(grad_t[b, cols], 0)
        dprobs[b, p, : here.stop - here.start] = dot(v[here, cols], g2_t, ((1,), (0,)))
    for b, _, _, p in pairs_of(blocks):
        here = own_rows(b, blocks)
        keys = slice(0, here.stop - here.start)
        dscores[b, p, keys], rounded[b, p, keys] = score_grads(
            exps[b, p, keys] * factors[b, p : p + 1], dprobs[b, p, keys], deltas[b, p : p + 1]
        )
    k_sums, v_sums = {}, {}
    for b, rows, cols, p in pairs_of(blocks):
        here = own_rows(b, blocks)
        keys = slice(0, here.stop - here.start)
        q2 = two_heads(q[rows, cols] * SCALE, 1)
        g2_t = two_heads(grad_t[b, cols], 0)
        dscore = dscores[b, p, keys]
        k_part = dot(dscore, q2, ((1,), (0,)))
        v_part = dot(rounded[b, p, keys], g2_t, ((1,), (1,)))
        for at in range(here.start, here.stop, BLK):
            part = slice(at - here.start, at - here.start + BLK)
            for sums, value in ((k_sums, k_part), (v_sums, v_part)):
                sums.setdefault((at, p), []).append(value[part])
        query_t = own_features(dot(k[here, cols], dscore, ((0,), (0,)))) + rim_t[b, cols]
        q_grad[rows, cols] = (query_t * SCALE).T.astype(BF16)
    for out, sums in ((k_own, k_sums), (v_own, v_sums)):
        for (at, p), values in sums.items():
            out[at : at + BLK, pair_cols(p)] = functools.reduce(jnp.add, values)
    after[...] = jnp.zeros_like(after)


def send_kernel(back, before, out):
    out[...] = back[...]


def output_kernel(attn_t, w_out, before, output):
    for b in range(attn_t.shape[0]):
        part = dot(attn_t[b], w_out[...], ((0,), (0,)))
        output[b * BLK : (b + 1) * BLK] = part.astype(BF16)


def halves_kernel(product, other, g_low, g_high, before, *outs):
    pieces, after = outs[:-1], outs[-1]
    at_dp = lax.axis_index("dp")
    chips, rows, cols = pieces[0].shape
    if cols % BLK == 0:
        flat = other[...].reshape(chips * rows, other.shape[2])
        for s in range(len(pieces)):
            at = pl.ds(pl.multiple_of((at_dp ^ s) * cols, BLK), cols)
            g = jnp.concatenate([g_low[:, at], g_high[:, at]], axis=0)
            value = product[:, at] + dot(flat, g, ((1,), (0,)))
            pieces[s][...] = value.astype(BF16).reshape(chips, rows, cols)
    else:
        both = (product[...] + flat_dot(other, g_low, g_high)).astype(BF16)
        for d in range(len(pieces)):
            value = both[:, d * cols : (d + 1) * cols].reshape(chips, rows, cols)
            for s in range(len(pieces)):

                @pl.when((at_dp ^ s) == d)
                def _(s=s, value=value):
                    pieces[s][...] = value

    after[...] = jnp.zeros_like(after)


def chips_kernel(*refs):
    parts, outs = refs[: lax.axis_size("dp")], refs[lax.axis_size("dp") + 1 :]
    chip = lax.div(lax.axis_index("ctx"), 2)
    for s, out in enumerate(outs):
        out[...] = total([part[chip ^ s] for part in parts]).astype(BF16)


def piece_kernel(scale, count, *refs):
    refs[-1][...] = (total([part[...] for part in refs[:count]]) * scale).astype(BF16)


def rim_sum_kernel(k_own, v_own, link_kv, chip_kv, k_grad, v_grad):
    tokens = k_own.shape[0]
    first_core = at_core() == 0
    for i, (own, grad) in enumerate(((k_own, k_grad), (v_own, v_grad))):
        link, chip = link_kv[i].astype(F32), chip_kv[i].astype(F32)
        low = jnp.where(first_core, link, chip)
        high = jnp.where(first_core, chip, link)
        if tokens == RIM:
            grad[...] = (own[...] + low + high).astype(BF16)
        else:
            grad[:RIM] = (own[:RIM] + low).astype(BF16)
            if tokens > 2 * RIM:
                grad[RIM : tokens - RIM] = own[RIM : tokens - RIM].astype(BF16)
            grad[tokens - RIM :] = (own[tokens - RIM :] + high).astype(BF16)


def columns_kernel(*refs):
    pieces, weight_grad = refs[:1] + refs[-2:0:-1], refs[-1]
    at_dp = lax.axis_index("dp")
    cols = pieces[0].shape[1]
    for d in range(len(pieces)):
        value = pieces[0][...]
        for s in range(1, len(pieces)):
            value = jnp.where((at_dp ^ s) == d, pieces[s][...], value)
        weight_grad[:, d * cols : (d + 1) * cols] = value.astype(F32)


def vmem(*shape, dtype=BF16):
    return pltpu.VMEM(shape, dtype)


def hbm(*shape, dtype=BF16):
    return jax.ShapeDtypeStruct(shape, dtype)


def call(kernel, outs, flops, *args, scratch=()):
    in_vmem = pl.BlockSpec(memory_space=pltpu.VMEM)
    return pl.pallas_call(
        kernel,
        out_shape=outs,
        in_specs=[in_vmem] * len(args),
        out_specs=[in_vmem] * len(outs),
        scratch_shapes=list(scratch),
        compiler_params=pltpu.CompilerParams(vmem_limit_bytes=24 * 1024 * 1024),
        cost_estimate=pl.CostEstimate(flops=flops, bytes_accessed=flops // 250, transcendentals=0),
    )(*args)


def call_on_hbm(kernel, outs, *args, beside=(), scratch=()):
    return pl.pallas_call(
        kernel,
        out_shape=outs,
        in_specs=[pl.BlockSpec(memory_space=pltpu.VMEM)] * len(beside)
        + [pl.BlockSpec(memory_space=pltpu.HBM)] * len(args),
        out_specs=[pl.BlockSpec(memory_space=pltpu.VMEM)] * len(outs),
        scratch_shapes=list(scratch),
        compiler_params=pltpu.CompilerParams(vmem_limit_bytes=8 * 1024 * 1024),
        cost_estimate=pl.CostEstimate(flops=10**6, bytes_accessed=4096, transcendentals=0),
    )(*beside, *(pltpu.with_memory_space_constraint(x, pltpu.HBM) for x in args))


def swap(count, bits):
    return [(i, i ^ bits) for i in range(count)]


def over_links(count):
    return [(i, (i - 1 if i % 2 == 0 else i + 1) % count) for i in range(count)]


def total(parts):
    return functools.reduce(jnp.add, [p.astype(F32) for p in parts])


def body(queries, keys, values, out_grad, w_out, block_mask):
    q, k, v, g = queries[0], keys[0], values[0], out_grad[0]
    tokens, feats = q.shape
    width = g.shape[1]
    blocks = tokens // BLK
    ctx, dp = lax.axis_size("ctx"), lax.axis_size("dp")
    chips = ctx // 2
    at_ctx = lax.axis_index("ctx")
    rows, cols = feats // ctx, width // dp

    rim = vmem(RIM, feats)
    sems = [pltpu.SemaphoreType.DMA((2,))]
    (to_link,) = call_on_hbm(pack_link_kernel, [vmem(2, RIM, feats)], k, v, scratch=sems)
    to_chip = call_on_hbm(pack_chip_kernel, [rim, rim], k, v, scratch=sems)
    link = lax.ppermute(to_link, "ctx", over_links(ctx))
    chip_k, chip_v = (lax.ppermute(x, "ctx", swap(ctx, 1)) for x in to_chip)
    mask = lax.dynamic_slice_in_dim(block_mask[0], at_ctx * blocks, blocks, 0)
    bias = jnp.where(mask == 1, 0.0, BIG_NEGATIVE).astype(F32).reshape(blocks * CAND, 1, 1)
    bias = jnp.broadcast_to(bias, (blocks * CAND, 1, 2 * BLK))
    args = (q, k, v, g, w_out)
    own_keys = min(CAND, blocks) * BLK
    own_scores = (blocks, PAIRS, own_keys, 2 * BLK)
    rim_scores = (PAIRS, RIM, 2 * BLK)
    half = vmem(tokens // 2, width)
    q, k, v, g_low, g_high, w_out, own_t, stats, own_exps, grad_t = call_on_hbm(
        own_kernel,
        [vmem(tokens, feats)] * 3
        + [
            half,
            half,
            vmem(feats, width),
            vmem(blocks, feats, BLK, dtype=F32),
            vmem(2, blocks, PAIRS, 2 * BLK, dtype=F32),
            vmem(*own_scores, dtype=F32),
            vmem(blocks, feats, BLK),
        ],
        *args,
        beside=(bias,),
        scratch=[vmem(*own_scores), pltpu.SemaphoreType.DMA((6,))],
    )
    sibling_g = [
        pltpu.with_memory_space_constraint(lax.ppermute(x, "ctx", swap(ctx, 1)), pltpu.VMEM)
        for x in (g_low, g_high)
    ]
    chip_t, chip_stats, chip_exps = call(
        chip_kernel,
        [
            vmem(feats, BLK, dtype=F32),
            vmem(2, PAIRS, 2 * BLK, dtype=F32),
            vmem(*rim_scores, dtype=F32),
        ],
        10**6,
        bias, q, chip_k, chip_v, own_t, stats,
        scratch=[vmem(*rim_scores)],
    )
    attn_t, mine, other, link_exps, own_factors, rim_factors = call(
        forward_kernel,
        [
            vmem(blocks, feats, BLK),
            vmem(chips, rows, tokens),
            vmem(chips, rows, tokens),
            vmem(*rim_scores, dtype=F32),
            vmem(blocks, PAIRS, 2 * BLK, dtype=F32),
            vmem(2, PAIRS, 2 * BLK, dtype=F32),
        ],
        10**6,
        bias, q, link, own_t, stats, chip_t, chip_stats,
        scratch=[vmem(*rim_scores)],
    )

    other = lax.ppermute(other, "ctx", swap(ctx, 1))
    other = pltpu.with_memory_space_constraint(other, pltpu.VMEM)
    (product,) = call(product_kernel, [vmem(chips * rows, width, dtype=F32)], 10**6, mine, g_low, g_high)
    *back, deltas, rim_t = call(
        rim_kernel,
        [
            vmem(2, RIM, feats),
            vmem(2, RIM, feats),
            vmem(blocks, PAIRS, 2 * BLK, dtype=F32),
            vmem(blocks, feats, BLK, dtype=F32),
        ],
        10**6,
        q, link, chip_k, chip_v, grad_t, attn_t, link_exps, chip_exps, rim_factors,
        scratch=[vmem(2, *rim_scores, dtype=F32), vmem(2, *rim_scores), vmem(2, *rim_scores)],
    )
    *halves, after = call(
        halves_kernel,
        [vmem(chips, rows, cols)] * dp + [vmem(8, 128, dtype=F32)],
        10**6,
        product, other, *sibling_g, deltas,
    )
    (to_link,) = call(send_kernel, [vmem(2, RIM, feats)], 10**6, back[0], after)
    link_back = lax.ppermute(to_link, "ctx", over_links(ctx))
    chip_back = lax.ppermute(back[1], "ctx", swap(ctx, 1))
    q_grad, k_own, v_own, after = call(
        own_backward_kernel,
        [
            hbm(tokens, feats),
            vmem(tokens, feats, dtype=F32),
            vmem(tokens, feats, dtype=F32),
            vmem(8, 128, dtype=F32),
        ],
        5 * 10**9,
        q, k, v, grad_t, own_exps, own_factors, deltas, rim_t, to_link,
        scratch=[vmem(*own_scores, dtype=F32), vmem(*own_scores), vmem(*own_scores)],
    )

    halves = [halves[0]] + [lax.ppermute(halves[s], "dp", swap(dp, s)) for s in range(1, dp)]
    quarters = call(chips_kernel, [vmem(rows, cols)] * chips, 10**6, *halves, after)
    (output,) = call(output_kernel, [hbm(tokens, width)], 5 * 10**9, attn_t, w_out, quarters[0])
    quarters = [quarters[0]] + [
        lax.ppermute(quarters[s], "ctx", swap(ctx, 2 * s))
        for s in (*range(chips // 2, chips), *range(chips // 2 - 1, 0, -1))
    ]
    (piece,) = call(
        functools.partial(piece_kernel, (dp * tokens * ctx) ** (-0.5), chips),
        [vmem(rows, cols)],
        10**6,
        *quarters, link_back,
    )
    pieces = [piece] + [lax.ppermute(piece, "dp", swap(dp, s)) for s in range(dp - 1, 0, -1)]
    k_grad, v_grad = call(
        rim_sum_kernel, [hbm(tokens, feats)] * 2, 10**6, k_own, v_own, link_back, chip_back
    )
    (weight_grad,) = call(columns_kernel, [hbm(rows, width, dtype=F32)], 10**6, *pieces)
    return (output[None], q_grad[None], k_grad[None], v_grad[None], weight_grad)


def solution(mesh):
    rows = P("dp", "ctx", None)
    return jax.shard_map(
        body,
        mesh=mesh,
        in_specs=(rows, rows, rows, rows, P(), P("dp", None, None)),
        out_specs=(rows, rows, rows, rows, P("ctx", None)),
        check_vma=False,
    )
```

```python
import functools

import jax
import jax.numpy as jnp
from jax import lax
from jax.experimental import pallas as pl
from jax.experimental.pallas import tpu as pltpu
from jax.sharding import PartitionSpec as P

HEADS = 8
HD = 64
BLK = 128
RAD = 1
CAND = 2 * RAD + 1
PAIRS = HEADS // 2
PAIR = 2 * HD
RIM = RAD * BLK
BIG_NEGATIVE = -1e30
SCALE = HD ** (-0.5)
BF16 = jnp.bfloat16
F32 = jnp.float32


def dot(a, b, contract):
    return lax.dot_general(a, b, (contract, ((), ())), preferred_element_type=F32)


def two_heads(block, axis):
    feature = lax.broadcasted_iota(jnp.int32, block.shape, axis)
    zero = jnp.zeros_like(block)
    return jnp.concatenate(
        [jnp.where(feature < HD, block, zero), jnp.where(feature < HD, zero, block)], axis=1 - axis
    )


def own_features(both):
    return jnp.concatenate([both[:HD, :BLK], both[HD:, BLK:]], axis=0)


def spread(row):
    return jnp.concatenate(
        [
            jnp.broadcast_to(row[:, :BLK], (HD, BLK)),
            jnp.broadcast_to(row[:, BLK:], (HD, BLK)),
        ],
        axis=0,
    )


def own_candidates(b, blocks):
    return max(0, RAD - b), min(CAND - 1, blocks - 1 - b + RAD)


def own_rows(b, blocks):
    first, last = own_candidates(b, blocks)
    return slice((b + first - RAD) * BLK, (b + last - RAD + 1) * BLK)


def masked(bias, b, c, part):
    return part + bias[b * CAND + c]


def pairs_of(blocks):
    for b in range(blocks):
        for p in range(PAIRS):
            yield b, slice(b * BLK, (b + 1) * BLK), slice(p * PAIR, (p + 1) * PAIR), p


def at_core():
    return lax.rem(lax.axis_index("ctx"), 2)


def rim_block(blocks, over_link):
    core = at_core()
    upper = core if over_link else 1 - core
    return upper * (blocks - 1), upper * (CAND - 1)


def rows_of(b):
    return pl.ds(pl.multiple_of(b * BLK, BLK), BLK)


def copy_all(pairs, sems):
    copies = [pltpu.make_async_copy(x, y, sems.at[i]) for i, (x, y) in enumerate(pairs)]
    for copy in copies:
        copy.start()
    for copy in copies:
        copy.wait()


def pack_link_kernel(k, v, out, sems):
    rows = rows_of(rim_block(k.shape[0] // BLK, True)[0])
    copy_all(((k.at[rows], out.at[0]), (v.at[rows], out.at[1])), sems)


def pack_chip_kernel(k, v, k_out, v_out, sems):
    rows = rows_of(rim_block(k.shape[0] // BLK, False)[0])
    copy_all(((k.at[rows], k_out), (v.at[rows], v_out)), sems)


def own_kernel(
    bias, q_arg, k_arg, v_arg, g_arg, w_arg,
    q, k, v, g_low, g_high, w_out, own_t, stats, exps, grad_t, rounded, sems,
):
    half = g_low.shape[0]
    pairs = (
        (q_arg, q),
        (k_arg, k),
        (v_arg, v),
        (g_arg.at[:half], g_low),
        (g_arg.at[half:], g_high),
        (w_arg, w_out),
    )
    copies = [pltpu.make_async_copy(x, y, sems.at[i]) for i, (x, y) in enumerate(pairs)]
    for copy in copies:
        copy.start()
    copies[0].wait()
    copies[1].wait()
    blocks = q.shape[0] // BLK
    for b, rows, cols, p in pairs_of(blocks):
        first, last = own_candidates(b, blocks)
        here = own_rows(b, blocks)
        scores = dot(k[here, cols], two_heads(q[rows, cols] * SCALE, 1), ((1,), (1,)))
        for c in range(first, last + 1):
            part = slice((c - first) * BLK, (c - first + 1) * BLK)
            value = scores[part]
            exps[b, p, part] = value if c == RAD else masked(bias, b, c, value)
    for b, rows, cols, p in pairs_of(blocks):
        here = own_rows(b, blocks)
        keys = slice(0, here.stop - here.start)
        scores = exps[b, p, keys]
        top = jnp.max(scores, axis=0, keepdims=True)
        e = jnp.exp(scores - top)
        exps[b, p, keys] = e
        rounded[b, p, keys] = e.astype(BF16)
        stats[0, b, p : p + 1] = top
        stats[1, b, p : p + 1] = jnp.sum(e, axis=0, keepdims=True)
    copies[2].wait()
    for b, rows, cols, p in pairs_of(blocks):
        here = own_rows(b, blocks)
        e = rounded[b, p, : here.stop - here.start]
        own_t[b, cols] = own_features(dot(v[here, cols], e, ((0,), (0,))))
    for copy in copies[3:]:
        copy.wait()
    both = jnp.concatenate([g_low[...], g_high[...]], axis=0)
    for b in range(blocks):
        rows = slice(b * BLK, (b + 1) * BLK)
        grad_t[b] = dot(w_out[...], both[rows], ((1,), (1,))).astype(BF16)


def pair_cols(p):
    return slice(p * PAIR, (p + 1) * PAIR)


def with_rim(bias, q, rim_k, rim_v, b, c, old, exps, rounded):
    for p in range(PAIRS):
        q2 = two_heads(q[rows_of(b), pair_cols(p)] * SCALE, 1)
        scores = dot(rim_k[:, pair_cols(p)], q2, ((1,), (1,)))
        exps[p] = masked(bias, b, c, scores)
    results = []
    for p in range(PAIRS):
        old_top, old_sum = old(p)
        scores = exps[p]
        top = jnp.maximum(old_top, jnp.max(scores, axis=0, keepdims=True))
        kept = jnp.exp(old_top - top)
        e = jnp.exp(scores - top)
        exps[p] = e
        rounded[p] = e.astype(BF16)
        results.append((top, kept, old_sum * kept + jnp.sum(e, axis=0, keepdims=True)))
    parts = [
        own_features(dot(rim_v[:, pair_cols(p)], rounded[p], ((0,), (0,)))) for p in range(PAIRS)
    ]
    return [(*result, part) for result, part in zip(results, parts)]


def chip_kernel(bias, q, rim_k, rim_v, own_t, stats, chip_t, chip_stats, exps, rounded):
    blocks = q.shape[0] // BLK
    b, c = rim_block(blocks, False)

    def old(p):
        return stats[0, b, p : p + 1], stats[1, b, p : p + 1]

    results = with_rim(bias, q, rim_k, rim_v, b, c, old, exps, rounded)
    for p, (top, kept, count, part) in enumerate(results):
        at = slice(p, p + 1)
        if blocks == 1:
            chip_t[pair_cols(p)] = own_t[b, pair_cols(p)] * spread(kept) + part
            chip_stats[0, at], chip_stats[1, at] = top, count
        else:
            share = 1.0 / count
            attn = own_t[b, pair_cols(p)] * spread(kept * share) + part * spread(share)
            chip_t[pair_cols(p)] = attn
            chip_stats[0, at], chip_stats[1, at] = share, kept * share


def forward_kernel(
    bias, q, rim, own_t, stats, chip_t, chip_stats,
    attn_t, mine, other, exps, own_factors, rim_factors, rounded,
):
    blocks = q.shape[0] // BLK
    b, c = rim_block(blocks, True)
    at_chip, _ = rim_block(blocks, False)

    def old(p):
        at = slice(p, p + 1)
        if blocks == 1:
            return chip_stats[0, at], chip_stats[1, at]
        return stats[0, b, at], stats[1, b, at]

    results = with_rim(bias, q, rim.at[0], rim.at[1], b, c, old, exps, rounded)
    for p, (top, kept, count, part) in enumerate(results):
        at = slice(p, p + 1)
        cols = pair_cols(p)
        base = chip_t[cols] if blocks == 1 else own_t[b, cols]
        share = 1.0 / count
        attn_t[b, cols] = (base * spread(kept * share) + part * spread(share)).astype(BF16)
        rim_factors[0, at] = share
        if blocks == 1:
            rim_factors[1, at] = kept * share
            own_factors[0, at] = jnp.exp(stats[0, 0, at] - top) * share
        else:
            own_factors[b, at] = kept * share
            attn_t[at_chip, cols] = chip_t[cols].astype(BF16)
            rim_factors[1, at] = chip_stats[0, at]
            own_factors[at_chip, at] = chip_stats[1, at]
        for inner in range(1, blocks - 1):
            share = 1.0 / stats[1, inner, at]
            attn_t[inner, cols] = (own_t[inner, cols] * spread(share)).astype(BF16)
            own_factors[inner, at] = share
    first_core = at_core() == 0
    chips, rows, _ = mine.shape
    for i in range(chips):
        for block in range(blocks):
            tokens = slice(block * BLK, (block + 1) * BLK)
            even = attn_t[block, 2 * i * rows : (2 * i + 1) * rows]
            odd = attn_t[block, (2 * i + 1) * rows : (2 * i + 2) * rows]
            mine[i, :, tokens] = jnp.where(first_core, even, odd)
            other[i, :, tokens] = jnp.where(first_core, odd, even)


def flat_dot(attn, g_low, g_high):
    chips, rows, tokens = attn.shape
    g = jnp.concatenate([g_low[...], g_high[...]], axis=0)
    return dot(attn[...].reshape(chips * rows, tokens), g, ((1,), (0,)))


def product_kernel(mine, g_low, g_high, product):
    product[...] = flat_dot(mine, g_low, g_high)


def score_grads(probs, dprob, delta):
    return (probs * (dprob - delta)).astype(BF16), probs.astype(BF16)


def rim_kernel(
    q, link, chip_k, chip_v, grad_t, attn_t, link_exps, chip_exps, rim_factors, before,
    link_back, chip_back, deltas, query_t, dprobs, dscores, rounded,
):
    blocks = q.shape[0] // BLK
    sides = (
        (rim_block(blocks, True)[0], link.at[0], link.at[1], link_exps, link_back.at[0], link_back.at[1]),
        (rim_block(blocks, False)[0], chip_k, chip_v, chip_exps, chip_back.at[0], chip_back.at[1]),
    )
    for i, (b, _, rim_v, _, _, _) in enumerate(sides):
        for p in range(PAIRS):
            g2_t = two_heads(grad_t[b, pair_cols(p)], 0)
            dprobs[i, p] = dot(rim_v[:, pair_cols(p)], g2_t, ((1,), (0,)))
    for b, _, cols, p in pairs_of(blocks):
        product = grad_t[b, cols].astype(F32) * attn_t[b, cols].astype(F32)
        deltas[b, p : p + 1] = jnp.concatenate(
            [
                jnp.sum(product[:HD], axis=0, keepdims=True),
                jnp.sum(product[HD:], axis=0, keepdims=True),
            ],
            axis=1,
        )
    query_t[...] = jnp.zeros_like(query_t)
    for i, (b, _, _, exps, _, _) in enumerate(sides):
        for p in range(PAIRS):
            at = slice(p, p + 1)
            dscores[i, p], rounded[i, p] = score_grads(
                exps[p] * rim_factors[i, at], dprobs[i, p], deltas[b, at]
            )
    for i, (b, rim_k, _, _, k_back, v_back) in enumerate(sides):
        for p in range(PAIRS):
            cols = pair_cols(p)
            q2 = two_heads(q[rows_of(b), cols] * SCALE, 1)
            g2_t = two_heads(grad_t[b, cols], 0)
            k_back[:, cols] = dot(dscores[i, p], q2, ((1,), (0,))).astype(BF16)
            v_back[:, cols] = dot(rounded[i, p], g2_t, ((1,), (1,))).astype(BF16)
            query_t[b, cols] += own_features(dot(rim_k[:, cols], dscores[i, p], ((0,), (0,))))


def own_backward_kernel(
    q, k, v, grad_t, exps, factors, deltas, rim_t,
    q_grad, k_own, v_own, after, dprobs, dscores, rounded,
):
    blocks = q.shape[0] // BLK
    for b, _, cols, p in pairs_of(blocks):
        here = own_rows(b, blocks)
        g2_t = two_heads(grad_t[b, cols], 0)
        dprobs[b, p, : here.stop - here.start] = dot(v[here, cols], g2_t, ((1,), (0,)))
    for b, _, _, p in pairs_of(blocks):
        here = own_rows(b, blocks)
        keys = slice(0, here.stop - here.start)
        dscores[b, p, keys], rounded[b, p, keys] = score_grads(
            exps[b, p, keys] * factors[b, p : p + 1], dprobs[b, p, keys], deltas[b, p : p + 1]
        )
    k_sums, v_sums = {}, {}
    for b, rows, cols, p in pairs_of(blocks):
        here = own_rows(b, blocks)
        keys = slice(0, here.stop - here.start)
        q2 = two_heads(q[rows, cols] * SCALE, 1)
        g2_t = two_heads(grad_t[b, cols], 0)
        dscore = dscores[b, p, keys]
        k_part = dot(dscore, q2, ((1,), (0,)))
        v_part = dot(rounded[b, p, keys], g2_t, ((1,), (1,)))
        for at in range(here.start, here.stop, BLK):
            part = slice(at - here.start, at - here.start + BLK)
            for sums, value in ((k_sums, k_part), (v_sums, v_part)):
                sums.setdefault((at, p), []).append(value[part])
        query_t = own_features(dot(k[here, cols], dscore, ((0,), (0,)))) + rim_t[b, cols]
        q_grad[rows, cols] = (query_t * SCALE).T.astype(BF16)
    for out, sums in ((k_own, k_sums), (v_own, v_sums)):
        for (at, p), values in sums.items():
            out[at : at + BLK, pair_cols(p)] = functools.reduce(jnp.add, values)
    after[...] = jnp.zeros_like(after)


def output_kernel(attn_t, w_out, before, output):
    for b in range(attn_t.shape[0]):
        part = dot(attn_t[b], w_out[...], ((0,), (0,)))
        output[b * BLK : (b + 1) * BLK] = part.astype(BF16)


def halves_kernel(product, other, g_low, g_high, *outs):
    pieces, after = outs[:-1], outs[-1]
    at_dp = lax.axis_index("dp")
    chips, rows, cols = pieces[0].shape
    if cols % BLK == 0:
        flat = other[...].reshape(chips * rows, other.shape[2])
        for s in range(len(pieces)):
            at = pl.ds(pl.multiple_of((at_dp ^ s) * cols, BLK), cols)
            g = jnp.concatenate([g_low[:, at], g_high[:, at]], axis=0)
            value = product[:, at] + dot(flat, g, ((1,), (0,)))
            pieces[s][...] = value.astype(BF16).reshape(chips, rows, cols)
    else:
        both = (product[...] + flat_dot(other, g_low, g_high)).astype(BF16)
        for d in range(len(pieces)):
            value = both[:, d * cols : (d + 1) * cols].reshape(chips, rows, cols)
            for s in range(len(pieces)):

                @pl.when((at_dp ^ s) == d)
                def _(s=s, value=value):
                    pieces[s][...] = value

    after[...] = jnp.zeros_like(after)


def chips_kernel(*refs):
    parts, outs = refs[: lax.axis_size("dp")], refs[lax.axis_size("dp") + 1 :]
    chip = lax.div(lax.axis_index("ctx"), 2)
    for s, out in enumerate(outs):
        out[...] = total([part[chip ^ s] for part in parts]).astype(BF16)


def piece_kernel(scale, count, *refs):
    refs[-1][...] = (total([part[...] for part in refs[:count]]) * scale).astype(BF16)


def rim_sum_kernel(k_own, v_own, link_kv, chip_kv, k_grad, v_grad):
    tokens = k_own.shape[0]
    first_core = at_core() == 0
    for i, (own, grad) in enumerate(((k_own, k_grad), (v_own, v_grad))):
        link, chip = link_kv[i].astype(F32), chip_kv[i].astype(F32)
        low = jnp.where(first_core, link, chip)
        high = jnp.where(first_core, chip, link)
        if tokens == RIM:
            grad[...] = (own[...] + low + high).astype(BF16)
        else:
            grad[:RIM] = (own[:RIM] + low).astype(BF16)
            if tokens > 2 * RIM:
                grad[RIM : tokens - RIM] = own[RIM : tokens - RIM].astype(BF16)
            grad[tokens - RIM :] = (own[tokens - RIM :] + high).astype(BF16)


def columns_kernel(*refs):
    pieces, weight_grad = refs[:1] + refs[2:-1] + refs[1:2], refs[-1]
    at_dp = lax.axis_index("dp")
    cols = pieces[0].shape[1]
    for d in range(len(pieces)):
        value = pieces[0][...]
        for s in range(1, len(pieces)):
            value = jnp.where((at_dp ^ s) == d, pieces[s][...], value)
        weight_grad[:, d * cols : (d + 1) * cols] = value.astype(F32)


def vmem(*shape, dtype=BF16):
    return pltpu.VMEM(shape, dtype)


def hbm(*shape, dtype=BF16):
    return jax.ShapeDtypeStruct(shape, dtype)


def call(kernel, outs, flops, *args, scratch=()):
    in_vmem = pl.BlockSpec(memory_space=pltpu.VMEM)
    return pl.pallas_call(
        kernel,
        out_shape=outs,
        in_specs=[in_vmem] * len(args),
        out_specs=[in_vmem] * len(outs),
        scratch_shapes=list(scratch),
        compiler_params=pltpu.CompilerParams(vmem_limit_bytes=24 * 1024 * 1024),
        cost_estimate=pl.CostEstimate(flops=flops, bytes_accessed=flops // 250, transcendentals=0),
    )(*args)


def call_on_hbm(kernel, outs, *args, beside=(), scratch=()):
    return pl.pallas_call(
        kernel,
        out_shape=outs,
        in_specs=[pl.BlockSpec(memory_space=pltpu.VMEM)] * len(beside)
        + [pl.BlockSpec(memory_space=pltpu.HBM)] * len(args),
        out_specs=[pl.BlockSpec(memory_space=pltpu.VMEM)] * len(outs),
        scratch_shapes=list(scratch),
        compiler_params=pltpu.CompilerParams(vmem_limit_bytes=8 * 1024 * 1024),
        cost_estimate=pl.CostEstimate(flops=10**6, bytes_accessed=4096, transcendentals=0),
    )(*beside, *(pltpu.with_memory_space_constraint(x, pltpu.HBM) for x in args))


def swap(count, bits):
    return [(i, i ^ bits) for i in range(count)]


def over_links(count):
    return [(i, (i - 1 if i % 2 == 0 else i + 1) % count) for i in range(count)]


def total(parts):
    return functools.reduce(jnp.add, [p.astype(F32) for p in parts])


def body(queries, keys, values, out_grad, w_out, block_mask):
    q, k, v, g = queries[0], keys[0], values[0], out_grad[0]
    tokens, feats = q.shape
    width = g.shape[1]
    blocks = tokens // BLK
    ctx, dp = lax.axis_size("ctx"), lax.axis_size("dp")
    chips = ctx // 2
    at_ctx = lax.axis_index("ctx")
    rows, cols = feats // ctx, width // dp

    rim = vmem(RIM, feats)
    sems = [pltpu.SemaphoreType.DMA((2,))]
    (to_link,) = call_on_hbm(pack_link_kernel, [vmem(2, RIM, feats)], k, v, scratch=sems)
    to_chip = call_on_hbm(pack_chip_kernel, [rim, rim], k, v, scratch=sems)
    link = lax.ppermute(to_link, "ctx", over_links(ctx))
    chip_k, chip_v = (lax.ppermute(x, "ctx", swap(ctx, 1)) for x in to_chip)
    mask = lax.dynamic_slice_in_dim(block_mask[0], at_ctx * blocks, blocks, 0)
    bias = jnp.where(mask == 1, 0.0, BIG_NEGATIVE).astype(F32).reshape(blocks * CAND, 1, 1)
    bias = jnp.broadcast_to(bias, (blocks * CAND, 1, 2 * BLK))
    args = (q, k, v, g, w_out)
    own_keys = min(CAND, blocks) * BLK
    own_scores = (blocks, PAIRS, own_keys, 2 * BLK)
    rim_scores = (PAIRS, RIM, 2 * BLK)
    half = vmem(tokens // 2, width)
    q, k, v, g_low, g_high, w_out, own_t, stats, own_exps, grad_t = call_on_hbm(
        own_kernel,
        [vmem(tokens, feats)] * 3
        + [
            half,
            half,
            vmem(feats, width),
            vmem(blocks, feats, BLK, dtype=F32),
            vmem(2, blocks, PAIRS, 2 * BLK, dtype=F32),
            vmem(*own_scores, dtype=F32),
            vmem(blocks, feats, BLK),
        ],
        *args,
        beside=(bias,),
        scratch=[vmem(*own_scores), pltpu.SemaphoreType.DMA((6,))],
    )
    sibling_g = [
        pltpu.with_memory_space_constraint(lax.ppermute(x, "ctx", swap(ctx, 1)), pltpu.VMEM)
        for x in (g_low, g_high)
    ]
    chip_t, chip_stats, chip_exps = call(
        chip_kernel,
        [
            vmem(feats, BLK, dtype=F32),
            vmem(2, PAIRS, 2 * BLK, dtype=F32),
            vmem(*rim_scores, dtype=F32),
        ],
        10**6,
        bias, q, chip_k, chip_v, own_t, stats,
        scratch=[vmem(*rim_scores)],
    )
    attn_t, mine, other, link_exps, own_factors, rim_factors = call(
        forward_kernel,
        [
            vmem(blocks, feats, BLK),
            vmem(chips, rows, tokens),
            vmem(chips, rows, tokens),
            vmem(*rim_scores, dtype=F32),
            vmem(blocks, PAIRS, 2 * BLK, dtype=F32),
            vmem(2, PAIRS, 2 * BLK, dtype=F32),
        ],
        10**6,
        bias, q, link, own_t, stats, chip_t, chip_stats,
        scratch=[vmem(*rim_scores)],
    )

    other = lax.ppermute(other, "ctx", swap(ctx, 1))
    other = pltpu.with_memory_space_constraint(other, pltpu.VMEM)
    (product,) = call(product_kernel, [vmem(chips * rows, width, dtype=F32)], 10**6, mine, g_low, g_high)
    *halves, after = call(
        halves_kernel,
        [vmem(chips, rows, cols)] * dp + [vmem(8, 128, dtype=F32)],
        10**6,
        product, other, *sibling_g,
    )
    *back, deltas, rim_t = call(
        rim_kernel,
        [
            vmem(2, RIM, feats),
            vmem(2, RIM, feats),
            vmem(blocks, PAIRS, 2 * BLK, dtype=F32),
            vmem(blocks, feats, BLK, dtype=F32),
        ],
        10**6,
        q, link, chip_k, chip_v, grad_t, attn_t, link_exps, chip_exps, rim_factors, after,
        scratch=[vmem(2, *rim_scores, dtype=F32), vmem(2, *rim_scores), vmem(2, *rim_scores)],
    )
    link_back = lax.ppermute(back[0], "ctx", over_links(ctx))
    chip_back = lax.ppermute(back[1], "ctx", swap(ctx, 1))
    q_grad, k_own, v_own, after = call(
        own_backward_kernel,
        [
            hbm(tokens, feats),
            vmem(tokens, feats, dtype=F32),
            vmem(tokens, feats, dtype=F32),
            vmem(8, 128, dtype=F32),
        ],
        5 * 10**9,
        q, k, v, grad_t, own_exps, own_factors, deltas, rim_t,
        scratch=[vmem(*own_scores, dtype=F32), vmem(*own_scores), vmem(*own_scores)],
    )

    halves = [halves[0]] + [lax.ppermute(halves[s], "dp", swap(dp, s)) for s in range(1, dp)]
    quarters = call(chips_kernel, [vmem(rows, cols)] * chips, 10**6, *halves, after)
    (output,) = call(output_kernel, [hbm(tokens, width)], 5 * 10**9, attn_t, w_out, quarters[0])
    quarters = [quarters[0]] + [
        lax.ppermute(quarters[s], "ctx", swap(ctx, 2 * s))
        for s in (*range(chips // 2, chips), *range(chips // 2 - 1, 0, -1))
    ]
    (piece,) = call(
        functools.partial(piece_kernel, (dp * tokens * ctx) ** (-0.5), chips),
        [vmem(rows, cols)],
        10**6,
        *quarters, link_back,
    )
    order = (dp - 1, *range(1, dp - 1))
    pieces = [piece] + [lax.ppermute(piece, "dp", swap(dp, s)) for s in order]
    k_grad, v_grad = call(
        rim_sum_kernel, [hbm(tokens, feats)] * 2, 10**6, k_own, v_own, link_back, chip_back
    )
    (weight_grad,) = call(columns_kernel, [hbm(rows, width, dtype=F32)], 10**6, *pieces)
    return (output[None], q_grad[None], k_grad[None], v_grad[None], weight_grad)


def solution(mesh):
    rows = P("dp", "ctx", None)
    return jax.shard_map(
        body,
        mesh=mesh,
        in_specs=(rows, rows, rows, rows, P(), P("dp", None, None)),
        out_specs=(rows, rows, rows, rows, P("ctx", None)),
        check_vma=False,
    )
```

```python
import functools

import jax
import jax.numpy as jnp
from jax import lax
from jax.experimental import pallas as pl
from jax.experimental.pallas import tpu as pltpu
from jax.sharding import PartitionSpec as P

HEADS = 8
HD = 64
BLK = 128
RAD = 1
CAND = 2 * RAD + 1
PAIRS = HEADS // 2
PAIR = 2 * HD
RIM = RAD * BLK
BIG_NEGATIVE = -1e30
SCALE = HD ** (-0.5)
BF16 = jnp.bfloat16
F32 = jnp.float32


def dot(a, b, contract):
    return lax.dot_general(a, b, (contract, ((), ())), preferred_element_type=F32)


def two_heads(block, axis):
    feature = lax.broadcasted_iota(jnp.int32, block.shape, axis)
    zero = jnp.zeros_like(block)
    return jnp.concatenate(
        [jnp.where(feature < HD, block, zero), jnp.where(feature < HD, zero, block)], axis=1 - axis
    )


def own_features(both):
    return jnp.concatenate([both[:HD, :BLK], both[HD:, BLK:]], axis=0)


def spread(row):
    return jnp.concatenate(
        [
            jnp.broadcast_to(row[:, :BLK], (HD, BLK)),
            jnp.broadcast_to(row[:, BLK:], (HD, BLK)),
        ],
        axis=0,
    )


def own_candidates(b, blocks):
    return max(0, RAD - b), min(CAND - 1, blocks - 1 - b + RAD)


def own_rows(b, blocks):
    first, last = own_candidates(b, blocks)
    return slice((b + first - RAD) * BLK, (b + last - RAD + 1) * BLK)


def masked(bias, b, c, part):
    return part + bias[b * CAND + c]


def pairs_of(blocks):
    for b in range(blocks):
        for p in range(PAIRS):
            yield b, slice(b * BLK, (b + 1) * BLK), slice(p * PAIR, (p + 1) * PAIR), p


def at_core():
    return lax.rem(lax.axis_index("ctx"), 2)


def rim_block(blocks, over_link):
    core = at_core()
    upper = core if over_link else 1 - core
    return upper * (blocks - 1), upper * (CAND - 1)


def rows_of(b):
    return pl.ds(pl.multiple_of(b * BLK, BLK), BLK)


def copy_all(pairs, sems):
    copies = [pltpu.make_async_copy(x, y, sems.at[i]) for i, (x, y) in enumerate(pairs)]
    for copy in copies:
        copy.start()
    for copy in copies:
        copy.wait()


def pack_link_kernel(k, v, out, sems):
    rows = rows_of(rim_block(k.shape[0] // BLK, True)[0])
    copy_all(((k.at[rows], out.at[0]), (v.at[rows], out.at[1])), sems)


def pack_chip_kernel(k, v, k_out, v_out, sems):
    rows = rows_of(rim_block(k.shape[0] // BLK, False)[0])
    copy_all(((k.at[rows], k_out), (v.at[rows], v_out)), sems)


def own_kernel(
    bias, q_arg, k_arg, v_arg, g_arg, w_arg,
    q, k, v, g_low, g_high, w_out, own_t, stats, exps, grad_t, rounded, sems,
):
    half = g_low.shape[0]
    pairs = (
        (q_arg, q),
        (k_arg, k),
        (v_arg, v),
        (g_arg.at[:half], g_low),
        (g_arg.at[half:], g_high),
        (w_arg, w_out),
    )
    copies = [pltpu.make_async_copy(x, y, sems.at[i]) for i, (x, y) in enumerate(pairs)]
    for copy in copies:
        copy.start()
    copies[0].wait()
    copies[1].wait()
    blocks = q.shape[0] // BLK
    for b, rows, cols, p in pairs_of(blocks):
        first, last = own_candidates(b, blocks)
        here = own_rows(b, blocks)
        scores = dot(k[here, cols], two_heads(q[rows, cols] * SCALE, 1), ((1,), (1,)))
        for c in range(first, last + 1):
            part = slice((c - first) * BLK, (c - first + 1) * BLK)
            value = scores[part]
            exps[b, p, part] = value if c == RAD else masked(bias, b, c, value)
    for b, rows, cols, p in pairs_of(blocks):
        here = own_rows(b, blocks)
        keys = slice(0, here.stop - here.start)
        scores = exps[b, p, keys]
        top = jnp.max(scores, axis=0, keepdims=True)
        e = jnp.exp(scores - top)
        exps[b, p, keys] = e
        rounded[b, p, keys] = e.astype(BF16)
        stats[0, b, p : p + 1] = top
        stats[1, b, p : p + 1] = jnp.sum(e, axis=0, keepdims=True)
    copies[2].wait()
    for b, rows, cols, p in pairs_of(blocks):
        here = own_rows(b, blocks)
        e = rounded[b, p, : here.stop - here.start]
        own_t[b, cols] = own_features(dot(v[here, cols], e, ((0,), (0,))))
    for copy in copies[3:]:
        copy.wait()
    both = jnp.concatenate([g_low[...], g_high[...]], axis=0)
    for b in range(blocks):
        rows = slice(b * BLK, (b + 1) * BLK)
        grad_t[b] = dot(w_out[...], both[rows], ((1,), (1,))).astype(BF16)


def pair_cols(p):
    return slice(p * PAIR, (p + 1) * PAIR)


def with_rim(bias, q, rim_k, rim_v, b, c, old, exps, rounded):
    for p in range(PAIRS):
        q2 = two_heads(q[rows_of(b), pair_cols(p)] * SCALE, 1)
        scores = dot(rim_k[:, pair_cols(p)], q2, ((1,), (1,)))
        exps[p] = masked(bias, b, c, scores)
    results = []
    for p in range(PAIRS):
        old_top, old_sum = old(p)
        scores = exps[p]
        top = jnp.maximum(old_top, jnp.max(scores, axis=0, keepdims=True))
        kept = jnp.exp(old_top - top)
        e = jnp.exp(scores - top)
        exps[p] = e
        rounded[p] = e.astype(BF16)
        results.append((top, kept, old_sum * kept + jnp.sum(e, axis=0, keepdims=True)))
    parts = [
        own_features(dot(rim_v[:, pair_cols(p)], rounded[p], ((0,), (0,)))) for p in range(PAIRS)
    ]
    return [(*result, part) for result, part in zip(results, parts)]


def chip_kernel(bias, q, rim_k, rim_v, own_t, stats, chip_t, chip_stats, exps, rounded):
    blocks = q.shape[0] // BLK
    b, c = rim_block(blocks, False)

    def old(p):
        return stats[0, b, p : p + 1], stats[1, b, p : p + 1]

    results = with_rim(bias, q, rim_k, rim_v, b, c, old, exps, rounded)
    for p, (top, kept, count, part) in enumerate(results):
        at = slice(p, p + 1)
        if blocks == 1:
            chip_t[pair_cols(p)] = own_t[b, pair_cols(p)] * spread(kept) + part
            chip_stats[0, at], chip_stats[1, at] = top, count
        else:
            share = 1.0 / count
            attn = own_t[b, pair_cols(p)] * spread(kept * share) + part * spread(share)
            chip_t[pair_cols(p)] = attn
            chip_stats[0, at], chip_stats[1, at] = share, kept * share


def forward_kernel(
    bias, q, rim, own_t, stats, chip_t, chip_stats,
    attn_t, mine, other, exps, own_factors, rim_factors, rounded,
):
    blocks = q.shape[0] // BLK
    b, c = rim_block(blocks, True)
    at_chip, _ = rim_block(blocks, False)

    def old(p):
        at = slice(p, p + 1)
        if blocks == 1:
            return chip_stats[0, at], chip_stats[1, at]
        return stats[0, b, at], stats[1, b, at]

    results = with_rim(bias, q, rim.at[0], rim.at[1], b, c, old, exps, rounded)
    for p, (top, kept, count, part) in enumerate(results):
        at = slice(p, p + 1)
        cols = pair_cols(p)
        base = chip_t[cols] if blocks == 1 else own_t[b, cols]
        share = 1.0 / count
        attn_t[b, cols] = (base * spread(kept * share) + part * spread(share)).astype(BF16)
        rim_factors[0, at] = share
        if blocks == 1:
            rim_factors[1, at] = kept * share
            own_factors[0, at] = jnp.exp(stats[0, 0, at] - top) * share
        else:
            own_factors[b, at] = kept * share
            attn_t[at_chip, cols] = chip_t[cols].astype(BF16)
            rim_factors[1, at] = chip_stats[0, at]
            own_factors[at_chip, at] = chip_stats[1, at]
        for inner in range(1, blocks - 1):
            share = 1.0 / stats[1, inner, at]
            attn_t[inner, cols] = (own_t[inner, cols] * spread(share)).astype(BF16)
            own_factors[inner, at] = share
    first_core = at_core() == 0
    chips, rows, _ = mine.shape
    for i in range(chips):
        for block in range(blocks):
            tokens = slice(block * BLK, (block + 1) * BLK)
            even = attn_t[block, 2 * i * rows : (2 * i + 1) * rows]
            odd = attn_t[block, (2 * i + 1) * rows : (2 * i + 2) * rows]
            mine[i, :, tokens] = jnp.where(first_core, even, odd)
            other[i, :, tokens] = jnp.where(first_core, odd, even)


def flat_dot(attn, g_low, g_high):
    chips, rows, tokens = attn.shape
    g = jnp.concatenate([g_low[...], g_high[...]], axis=0)
    return dot(attn[...].reshape(chips * rows, tokens), g, ((1,), (0,)))


def product_kernel(mine, g_low, g_high, product):
    product[...] = flat_dot(mine, g_low, g_high)


def score_grads(probs, dprob, delta):
    return (probs * (dprob - delta)).astype(BF16), probs.astype(BF16)


def rim_kernel(
    q, link, chip_k, chip_v, grad_t, attn_t, link_exps, chip_exps, rim_factors, before,
    link_back, chip_back, deltas, query_t, dprobs, dscores, rounded,
):
    blocks = q.shape[0] // BLK
    sides = (
        (rim_block(blocks, True)[0], link.at[0], link.at[1], link_exps, link_back.at[0], link_back.at[1]),
        (rim_block(blocks, False)[0], chip_k, chip_v, chip_exps, chip_back.at[0], chip_back.at[1]),
    )
    for i, (b, _, rim_v, _, _, _) in enumerate(sides):
        for p in range(PAIRS):
            g2_t = two_heads(grad_t[b, pair_cols(p)], 0)
            dprobs[i, p] = dot(rim_v[:, pair_cols(p)], g2_t, ((1,), (0,)))
    for b, _, cols, p in pairs_of(blocks):
        product = grad_t[b, cols].astype(F32) * attn_t[b, cols].astype(F32)
        deltas[b, p : p + 1] = jnp.concatenate(
            [
                jnp.sum(product[:HD], axis=0, keepdims=True),
                jnp.sum(product[HD:], axis=0, keepdims=True),
            ],
            axis=1,
        )
    query_t[...] = jnp.zeros_like(query_t)
    for i, (b, _, _, exps, _, _) in enumerate(sides):
        for p in range(PAIRS):
            at = slice(p, p + 1)
            dscores[i, p], rounded[i, p] = score_grads(
                exps[p] * rim_factors[i, at], dprobs[i, p], deltas[b, at]
            )
    for i, (b, rim_k, _, _, k_back, v_back) in enumerate(sides):
        for p in range(PAIRS):
            cols = pair_cols(p)
            q2 = two_heads(q[rows_of(b), cols] * SCALE, 1)
            g2_t = two_heads(grad_t[b, cols], 0)
            k_back[:, cols] = dot(dscores[i, p], q2, ((1,), (0,))).astype(BF16)
            v_back[:, cols] = dot(rounded[i, p], g2_t, ((1,), (1,))).astype(BF16)
            query_t[b, cols] += own_features(dot(rim_k[:, cols], dscores[i, p], ((0,), (0,))))


def own_backward_kernel(
    q, k, v, grad_t, exps, factors, deltas, rim_t,
    q_grad, k_own, v_own, after, dprobs, dscores, rounded,
):
    blocks = q.shape[0] // BLK
    for b, _, cols, p in pairs_of(blocks):
        here = own_rows(b, blocks)
        g2_t = two_heads(grad_t[b, cols], 0)
        dprobs[b, p, : here.stop - here.start] = dot(v[here, cols], g2_t, ((1,), (0,)))
    for b, _, _, p in pairs_of(blocks):
        here = own_rows(b, blocks)
        keys = slice(0, here.stop - here.start)
        dscores[b, p, keys], rounded[b, p, keys] = score_grads(
            exps[b, p, keys] * factors[b, p : p + 1], dprobs[b, p, keys], deltas[b, p : p + 1]
        )
    k_sums, v_sums = {}, {}
    for b, rows, cols, p in pairs_of(blocks):
        here = own_rows(b, blocks)
        keys = slice(0, here.stop - here.start)
        q2 = two_heads(q[rows, cols] * SCALE, 1)
        g2_t = two_heads(grad_t[b, cols], 0)
        dscore = dscores[b, p, keys]
        k_part = dot(dscore, q2, ((1,), (0,)))
        v_part = dot(rounded[b, p, keys], g2_t, ((1,), (1,)))
        for at in range(here.start, here.stop, BLK):
            part = slice(at - here.start, at - here.start + BLK)
            for sums, value in ((k_sums, k_part), (v_sums, v_part)):
                sums.setdefault((at, p), []).append(value[part])
        query_t = own_features(dot(k[here, cols], dscore, ((0,), (0,)))) + rim_t[b, cols]
        q_grad[rows, cols] = (query_t * SCALE).T.astype(BF16)
    for out, sums in ((k_own, k_sums), (v_own, v_sums)):
        for (at, p), values in sums.items():
            out[at : at + BLK, pair_cols(p)] = functools.reduce(jnp.add, values)
    after[...] = jnp.zeros_like(after)


def send_kernel(back, before, out):
    out[...] = back[...]


def output_kernel(attn_t, w_out, before, output):
    for b in range(attn_t.shape[0]):
        part = dot(attn_t[b], w_out[...], ((0,), (0,)))
        output[b * BLK : (b + 1) * BLK] = part.astype(BF16)


def halves_kernel(product, other, g_low, g_high, *outs):
    pieces, after = outs[:-1], outs[-1]
    at_dp = lax.axis_index("dp")
    chips, rows, cols = pieces[0].shape
    if cols % BLK == 0:
        flat = other[...].reshape(chips * rows, other.shape[2])
        for s in range(len(pieces)):
            at = pl.ds(pl.multiple_of((at_dp ^ s) * cols, BLK), cols)
            g = jnp.concatenate([g_low[:, at], g_high[:, at]], axis=0)
            value = product[:, at] + dot(flat, g, ((1,), (0,)))
            pieces[s][...] = value.astype(BF16).reshape(chips, rows, cols)
    else:
        both = (product[...] + flat_dot(other, g_low, g_high)).astype(BF16)
        for d in range(len(pieces)):
            value = both[:, d * cols : (d + 1) * cols].reshape(chips, rows, cols)
            for s in range(len(pieces)):

                @pl.when((at_dp ^ s) == d)
                def _(s=s, value=value):
                    pieces[s][...] = value

    after[...] = jnp.zeros_like(after)


def chips_kernel(*refs):
    parts, outs = refs[: lax.axis_size("dp")], refs[lax.axis_size("dp") + 1 :]
    chip = lax.div(lax.axis_index("ctx"), 2)
    for s, out in enumerate(outs):
        out[...] = total([part[chip ^ s] for part in parts]).astype(BF16)


def piece_kernel(scale, count, *refs):
    refs[-1][...] = (total([part[...] for part in refs[:count]]) * scale).astype(BF16)


def rim_sum_kernel(k_own, v_own, link_kv, chip_kv, k_grad, v_grad, after):
    tokens = k_own.shape[0]
    first_core = at_core() == 0
    for i, (own, grad) in enumerate(((k_own, k_grad), (v_own, v_grad))):
        link, chip = link_kv[i].astype(F32), chip_kv[i].astype(F32)
        low = jnp.where(first_core, link, chip)
        high = jnp.where(first_core, chip, link)
        if tokens == RIM:
            grad[...] = (own[...] + low + high).astype(BF16)
        else:
            grad[:RIM] = (own[:RIM] + low).astype(BF16)
            if tokens > 2 * RIM:
                grad[RIM : tokens - RIM] = own[RIM : tokens - RIM].astype(BF16)
            grad[tokens - RIM :] = (own[tokens - RIM :] + high).astype(BF16)
    after[...] = jnp.zeros_like(after)


def columns_kernel(before, *refs):
    pieces, weight_grad = refs[:1] + refs[-2:0:-1], refs[-1]
    at_dp = lax.axis_index("dp")
    cols = pieces[0].shape[1]
    for d in range(len(pieces)):
        value = pieces[0][...]
        for s in range(1, len(pieces)):
            value = jnp.where((at_dp ^ s) == d, pieces[s][...], value)
        weight_grad[:, d * cols : (d + 1) * cols] = value.astype(F32)


def vmem(*shape, dtype=BF16):
    return pltpu.VMEM(shape, dtype)


def hbm(*shape, dtype=BF16):
    return jax.ShapeDtypeStruct(shape, dtype)


def call(kernel, outs, flops, *args, scratch=()):
    in_vmem = pl.BlockSpec(memory_space=pltpu.VMEM)
    return pl.pallas_call(
        kernel,
        out_shape=outs,
        in_specs=[in_vmem] * len(args),
        out_specs=[in_vmem] * len(outs),
        scratch_shapes=list(scratch),
        compiler_params=pltpu.CompilerParams(vmem_limit_bytes=24 * 1024 * 1024),
        cost_estimate=pl.CostEstimate(flops=flops, bytes_accessed=flops // 250, transcendentals=0),
    )(*args)


def call_on_hbm(kernel, outs, *args, beside=(), scratch=()):
    return pl.pallas_call(
        kernel,
        out_shape=outs,
        in_specs=[pl.BlockSpec(memory_space=pltpu.VMEM)] * len(beside)
        + [pl.BlockSpec(memory_space=pltpu.HBM)] * len(args),
        out_specs=[pl.BlockSpec(memory_space=pltpu.VMEM)] * len(outs),
        scratch_shapes=list(scratch),
        compiler_params=pltpu.CompilerParams(vmem_limit_bytes=8 * 1024 * 1024),
        cost_estimate=pl.CostEstimate(flops=10**6, bytes_accessed=4096, transcendentals=0),
    )(*beside, *(pltpu.with_memory_space_constraint(x, pltpu.HBM) for x in args))


def swap(count, bits):
    return [(i, i ^ bits) for i in range(count)]


def over_links(count):
    return [(i, (i - 1 if i % 2 == 0 else i + 1) % count) for i in range(count)]


def total(parts):
    return functools.reduce(jnp.add, [p.astype(F32) for p in parts])


def body(queries, keys, values, out_grad, w_out, block_mask):
    q, k, v, g = queries[0], keys[0], values[0], out_grad[0]
    tokens, feats = q.shape
    width = g.shape[1]
    blocks = tokens // BLK
    ctx, dp = lax.axis_size("ctx"), lax.axis_size("dp")
    chips = ctx // 2
    at_ctx = lax.axis_index("ctx")
    rows, cols = feats // ctx, width // dp

    rim = vmem(RIM, feats)
    sems = [pltpu.SemaphoreType.DMA((2,))]
    (to_link,) = call_on_hbm(pack_link_kernel, [vmem(2, RIM, feats)], k, v, scratch=sems)
    to_chip = call_on_hbm(pack_chip_kernel, [rim, rim], k, v, scratch=sems)
    link = lax.ppermute(to_link, "ctx", over_links(ctx))
    chip_k, chip_v = (lax.ppermute(x, "ctx", swap(ctx, 1)) for x in to_chip)
    mask = lax.dynamic_slice_in_dim(block_mask[0], at_ctx * blocks, blocks, 0)
    bias = jnp.where(mask == 1, 0.0, BIG_NEGATIVE).astype(F32).reshape(blocks * CAND, 1, 1)
    bias = jnp.broadcast_to(bias, (blocks * CAND, 1, 2 * BLK))
    args = (q, k, v, g, w_out)
    own_keys = min(CAND, blocks) * BLK
    own_scores = (blocks, PAIRS, own_keys, 2 * BLK)
    rim_scores = (PAIRS, RIM, 2 * BLK)
    half = vmem(tokens // 2, width)
    q, k, v, g_low, g_high, w_out, own_t, stats, own_exps, grad_t = call_on_hbm(
        own_kernel,
        [vmem(tokens, feats)] * 3
        + [
            half,
            half,
            vmem(feats, width),
            vmem(blocks, feats, BLK, dtype=F32),
            vmem(2, blocks, PAIRS, 2 * BLK, dtype=F32),
            vmem(*own_scores, dtype=F32),
            vmem(blocks, feats, BLK),
        ],
        *args,
        beside=(bias,),
        scratch=[vmem(*own_scores), pltpu.SemaphoreType.DMA((6,))],
    )
    sibling_g = [
        pltpu.with_memory_space_constraint(lax.ppermute(x, "ctx", swap(ctx, 1)), pltpu.VMEM)
        for x in (g_low, g_high)
    ]
    chip_t, chip_stats, chip_exps = call(
        chip_kernel,
        [
            vmem(feats, BLK, dtype=F32),
            vmem(2, PAIRS, 2 * BLK, dtype=F32),
            vmem(*rim_scores, dtype=F32),
        ],
        10**6,
        bias, q, chip_k, chip_v, own_t, stats,
        scratch=[vmem(*rim_scores)],
    )
    attn_t, mine, other, link_exps, own_factors, rim_factors = call(
        forward_kernel,
        [
            vmem(blocks, feats, BLK),
            vmem(chips, rows, tokens),
            vmem(chips, rows, tokens),
            vmem(*rim_scores, dtype=F32),
            vmem(blocks, PAIRS, 2 * BLK, dtype=F32),
            vmem(2, PAIRS, 2 * BLK, dtype=F32),
        ],
        10**6,
        bias, q, link, own_t, stats, chip_t, chip_stats,
        scratch=[vmem(*rim_scores)],
    )

    other = lax.ppermute(other, "ctx", swap(ctx, 1))
    other = pltpu.with_memory_space_constraint(other, pltpu.VMEM)
    (product,) = call(product_kernel, [vmem(chips * rows, width, dtype=F32)], 10**6, mine, g_low, g_high)
    *halves, after = call(
        halves_kernel,
        [vmem(chips, rows, cols)] * dp + [vmem(8, 128, dtype=F32)],
        10**6,
        product, other, *sibling_g,
    )
    *back, deltas, rim_t = call(
        rim_kernel,
        [
            vmem(2, RIM, feats),
            vmem(2, RIM, feats),
            vmem(blocks, PAIRS, 2 * BLK, dtype=F32),
            vmem(blocks, feats, BLK, dtype=F32),
        ],
        10**6,
        q, link, chip_k, chip_v, grad_t, attn_t, link_exps, chip_exps, rim_factors, after,
        scratch=[vmem(2, *rim_scores, dtype=F32), vmem(2, *rim_scores), vmem(2, *rim_scores)],
    )
    link_back = lax.ppermute(back[0], "ctx", over_links(ctx))
    q_grad, k_own, v_own, after = call(
        own_backward_kernel,
        [
            hbm(tokens, feats),
            vmem(tokens, feats, dtype=F32),
            vmem(tokens, feats, dtype=F32),
            vmem(8, 128, dtype=F32),
        ],
        5 * 10**9,
        q, k, v, grad_t, own_exps, own_factors, deltas, rim_t,
        scratch=[vmem(*own_scores, dtype=F32), vmem(*own_scores), vmem(*own_scores)],
    )

    halves = [halves[0]] + [lax.ppermute(halves[s], "dp", swap(dp, s)) for s in range(1, dp)]
    quarters = call(chips_kernel, [vmem(rows, cols)] * chips, 10**6, *halves, after)
    (output,) = call(output_kernel, [hbm(tokens, width)], 5 * 10**9, attn_t, w_out, quarters[0])
    quarters = [quarters[0]] + [
        lax.ppermute(quarters[s], "ctx", swap(ctx, 2 * s))
        for s in (*range(chips // 2, chips), *range(chips // 2 - 1, 0, -1))
    ]
    (piece,) = call(
        functools.partial(piece_kernel, (dp * tokens * ctx) ** (-0.5), chips),
        [vmem(rows, cols)],
        10**6,
        *quarters, link_back,
    )
    pieces = [piece] + [lax.ppermute(piece, "dp", swap(dp, s)) for s in range(dp - 1, 0, -1)]
    (to_chip,) = call(send_kernel, [vmem(2, RIM, feats)], 10**6, back[1], piece)
    chip_back = lax.ppermute(to_chip, "ctx", swap(ctx, 1))
    k_grad, v_grad, after = call(
        rim_sum_kernel,
        [hbm(tokens, feats), hbm(tokens, feats), vmem(8, 128, dtype=F32)],
        10**6,
        k_own, v_own, link_back, chip_back,
    )
    (weight_grad,) = call(columns_kernel, [hbm(rows, width, dtype=F32)], 10**6, after, *pieces)
    return (output[None], q_grad[None], k_grad[None], v_grad[None], weight_grad)


def solution(mesh):
    rows = P("dp", "ctx", None)
    return jax.shard_map(
        body,
        mesh=mesh,
        in_specs=(rows, rows, rows, rows, P(), P("dp", None, None)),
        out_specs=(rows, rows, rows, rows, P("ctx", None)),
        check_vma=False,
    )
```

```python
import functools

import jax
import jax.numpy as jnp
from jax import lax
from jax.experimental import pallas as pl
from jax.experimental.pallas import tpu as pltpu
from jax.sharding import PartitionSpec as P

HEADS = 8
HD = 64
BLK = 128
RAD = 1
CAND = 2 * RAD + 1
PAIRS = HEADS // 2
PAIR = 2 * HD
RIM = RAD * BLK
BIG_NEGATIVE = -1e30
SCALE = HD ** (-0.5)
BF16 = jnp.bfloat16
F32 = jnp.float32


def dot(a, b, contract):
    return lax.dot_general(a, b, (contract, ((), ())), preferred_element_type=F32)


def two_heads(block, axis):
    feature = lax.broadcasted_iota(jnp.int32, block.shape, axis)
    zero = jnp.zeros_like(block)
    return jnp.concatenate(
        [jnp.where(feature < HD, block, zero), jnp.where(feature < HD, zero, block)], axis=1 - axis
    )


def own_features(both):
    return jnp.concatenate([both[:HD, :BLK], both[HD:, BLK:]], axis=0)


def spread(row):
    return jnp.concatenate(
        [
            jnp.broadcast_to(row[:, :BLK], (HD, BLK)),
            jnp.broadcast_to(row[:, BLK:], (HD, BLK)),
        ],
        axis=0,
    )


def own_candidates(b, blocks):
    return max(0, RAD - b), min(CAND - 1, blocks - 1 - b + RAD)


def own_rows(b, blocks):
    first, last = own_candidates(b, blocks)
    return slice((b + first - RAD) * BLK, (b + last - RAD + 1) * BLK)


def masked(bias, b, c, part):
    return part + bias[b * CAND + c]


def pairs_of(blocks):
    for b in range(blocks):
        for p in range(PAIRS):
            yield b, slice(b * BLK, (b + 1) * BLK), slice(p * PAIR, (p + 1) * PAIR), p


def at_core():
    return lax.rem(lax.axis_index("ctx"), 2)


def rim_block(blocks, over_link):
    core = at_core()
    upper = core if over_link else 1 - core
    return upper * (blocks - 1), upper * (CAND - 1)


def rows_of(b):
    return pl.ds(pl.multiple_of(b * BLK, BLK), BLK)


def copy_all(pairs, sems):
    copies = [pltpu.make_async_copy(x, y, sems.at[i]) for i, (x, y) in enumerate(pairs)]
    for copy in copies:
        copy.start()
    for copy in copies:
        copy.wait()


def pack_link_kernel(k, v, out, sems):
    rows = rows_of(rim_block(k.shape[0] // BLK, True)[0])
    copy_all(((k.at[rows], out.at[0]), (v.at[rows], out.at[1])), sems)


def pack_chip_kernel(k, v, k_out, v_out, sems):
    rows = rows_of(rim_block(k.shape[0] // BLK, False)[0])
    copy_all(((k.at[rows], k_out), (v.at[rows], v_out)), sems)


def own_kernel(
    bias, q_arg, k_arg, v_arg, g_arg, w_arg,
    q, k, v, g_low, g_high, w_out, own_t, stats, exps, grad_t, rounded, sems,
):
    half = g_low.shape[0]
    pairs = (
        (q_arg, q),
        (k_arg, k),
        (v_arg, v),
        (g_arg.at[:half], g_low),
        (g_arg.at[half:], g_high),
        (w_arg, w_out),
    )
    copies = [pltpu.make_async_copy(x, y, sems.at[i]) for i, (x, y) in enumerate(pairs)]
    for copy in copies:
        copy.start()
    copies[0].wait()
    copies[1].wait()
    blocks = q.shape[0] // BLK
    for b, rows, cols, p in pairs_of(blocks):
        first, last = own_candidates(b, blocks)
        here = own_rows(b, blocks)
        scores = dot(k[here, cols], two_heads(q[rows, cols] * SCALE, 1), ((1,), (1,)))
        for c in range(first, last + 1):
            part = slice((c - first) * BLK, (c - first + 1) * BLK)
            value = scores[part]
            exps[b, p, part] = value if c == RAD else masked(bias, b, c, value)
    for b, rows, cols, p in pairs_of(blocks):
        here = own_rows(b, blocks)
        keys = slice(0, here.stop - here.start)
        scores = exps[b, p, keys]
        top = jnp.max(scores, axis=0, keepdims=True)
        e = jnp.exp(scores - top)
        exps[b, p, keys] = e
        rounded[b, p, keys] = e.astype(BF16)
        stats[0, b, p : p + 1] = top
        stats[1, b, p : p + 1] = jnp.sum(e, axis=0, keepdims=True)
    copies[2].wait()
    for b, rows, cols, p in pairs_of(blocks):
        here = own_rows(b, blocks)
        e = rounded[b, p, : here.stop - here.start]
        own_t[b, cols] = own_features(dot(v[here, cols], e, ((0,), (0,))))
    for copy in copies[3:]:
        copy.wait()
    both = jnp.concatenate([g_low[...], g_high[...]], axis=0)
    for b in range(blocks):
        rows = slice(b * BLK, (b + 1) * BLK)
        grad_t[b] = dot(w_out[...], both[rows], ((1,), (1,))).astype(BF16)


def pair_cols(p):
    return slice(p * PAIR, (p + 1) * PAIR)


def with_rim(bias, q, rim_k, rim_v, b, c, old, exps, rounded):
    for p in range(PAIRS):
        q2 = two_heads(q[rows_of(b), pair_cols(p)] * SCALE, 1)
        scores = dot(rim_k[:, pair_cols(p)], q2, ((1,), (1,)))
        exps[p] = masked(bias, b, c, scores)
    results = []
    for p in range(PAIRS):
        old_top, old_sum = old(p)
        scores = exps[p]
        top = jnp.maximum(old_top, jnp.max(scores, axis=0, keepdims=True))
        kept = jnp.exp(old_top - top)
        e = jnp.exp(scores - top)
        exps[p] = e
        rounded[p] = e.astype(BF16)
        results.append((top, kept, old_sum * kept + jnp.sum(e, axis=0, keepdims=True)))
    parts = [
        own_features(dot(rim_v[:, pair_cols(p)], rounded[p], ((0,), (0,)))) for p in range(PAIRS)
    ]
    return [(*result, part) for result, part in zip(results, parts)]


def chip_kernel(bias, q, rim_k, rim_v, own_t, stats, chip_t, chip_stats, exps, rounded):
    blocks = q.shape[0] // BLK
    b, c = rim_block(blocks, False)

    def old(p):
        return stats[0, b, p : p + 1], stats[1, b, p : p + 1]

    results = with_rim(bias, q, rim_k, rim_v, b, c, old, exps, rounded)
    for p, (top, kept, count, part) in enumerate(results):
        at = slice(p, p + 1)
        if blocks == 1:
            chip_t[pair_cols(p)] = own_t[b, pair_cols(p)] * spread(kept) + part
            chip_stats[0, at], chip_stats[1, at] = top, count
        else:
            share = 1.0 / count
            attn = own_t[b, pair_cols(p)] * spread(kept * share) + part * spread(share)
            chip_t[pair_cols(p)] = attn
            chip_stats[0, at], chip_stats[1, at] = share, kept * share


def forward_kernel(
    bias, q, rim, own_t, stats, chip_t, chip_stats,
    attn_t, mine, other, exps, own_factors, rim_factors, rounded,
):
    blocks = q.shape[0] // BLK
    b, c = rim_block(blocks, True)
    at_chip, _ = rim_block(blocks, False)

    def old(p):
        at = slice(p, p + 1)
        if blocks == 1:
            return chip_stats[0, at], chip_stats[1, at]
        return stats[0, b, at], stats[1, b, at]

    results = with_rim(bias, q, rim.at[0], rim.at[1], b, c, old, exps, rounded)
    for p, (top, kept, count, part) in enumerate(results):
        at = slice(p, p + 1)
        cols = pair_cols(p)
        base = chip_t[cols] if blocks == 1 else own_t[b, cols]
        share = 1.0 / count
        attn_t[b, cols] = (base * spread(kept * share) + part * spread(share)).astype(BF16)
        rim_factors[0, at] = share
        if blocks == 1:
            rim_factors[1, at] = kept * share
            own_factors[0, at] = jnp.exp(stats[0, 0, at] - top) * share
        else:
            own_factors[b, at] = kept * share
            attn_t[at_chip, cols] = chip_t[cols].astype(BF16)
            rim_factors[1, at] = chip_stats[0, at]
            own_factors[at_chip, at] = chip_stats[1, at]
        for inner in range(1, blocks - 1):
            share = 1.0 / stats[1, inner, at]
            attn_t[inner, cols] = (own_t[inner, cols] * spread(share)).astype(BF16)
            own_factors[inner, at] = share
    first_core = at_core() == 0
    chips, rows, _ = mine.shape
    for i in range(chips):
        for block in range(blocks):
            tokens = slice(block * BLK, (block + 1) * BLK)
            even = attn_t[block, 2 * i * rows : (2 * i + 1) * rows]
            odd = attn_t[block, (2 * i + 1) * rows : (2 * i + 2) * rows]
            mine[i, :, tokens] = jnp.where(first_core, even, odd)
            other[i, :, tokens] = jnp.where(first_core, odd, even)


def flat_dot(attn, g_low, g_high):
    chips, rows, tokens = attn.shape
    g = jnp.concatenate([g_low[...], g_high[...]], axis=0)
    return dot(attn[...].reshape(chips * rows, tokens), g, ((1,), (0,)))


def product_kernel(mine, g_low, g_high, product):
    product[...] = flat_dot(mine, g_low, g_high)


def score_grads(probs, dprob, delta):
    return (probs * (dprob - delta)).astype(BF16), probs.astype(BF16)


def rim_kernel(
    q, link, chip_k, chip_v, grad_t, attn_t, link_exps, chip_exps, rim_factors,
    link_back, chip_back, deltas, query_t, dprobs, dscores, rounded,
):
    blocks = q.shape[0] // BLK
    sides = (
        (rim_block(blocks, True)[0], link.at[0], link.at[1], link_exps, link_back.at[0], link_back.at[1]),
        (rim_block(blocks, False)[0], chip_k, chip_v, chip_exps, chip_back.at[0], chip_back.at[1]),
    )
    for i, (b, _, rim_v, _, _, _) in enumerate(sides):
        for p in range(PAIRS):
            g2_t = two_heads(grad_t[b, pair_cols(p)], 0)
            dprobs[i, p] = dot(rim_v[:, pair_cols(p)], g2_t, ((1,), (0,)))
    for b, _, cols, p in pairs_of(blocks):
        product = grad_t[b, cols].astype(F32) * attn_t[b, cols].astype(F32)
        deltas[b, p : p + 1] = jnp.concatenate(
            [
                jnp.sum(product[:HD], axis=0, keepdims=True),
                jnp.sum(product[HD:], axis=0, keepdims=True),
            ],
            axis=1,
        )
    query_t[...] = jnp.zeros_like(query_t)
    for i, (b, _, _, exps, _, _) in enumerate(sides):
        for p in range(PAIRS):
            at = slice(p, p + 1)
            dscores[i, p], rounded[i, p] = score_grads(
                exps[p] * rim_factors[i, at], dprobs[i, p], deltas[b, at]
            )
    for i, (b, rim_k, _, _, k_back, v_back) in enumerate(sides):
        for p in range(PAIRS):
            cols = pair_cols(p)
            q2 = two_heads(q[rows_of(b), cols] * SCALE, 1)
            g2_t = two_heads(grad_t[b, cols], 0)
            k_back[:, cols] = dot(dscores[i, p], q2, ((1,), (0,))).astype(BF16)
            v_back[:, cols] = dot(rounded[i, p], g2_t, ((1,), (1,))).astype(BF16)
            query_t[b, cols] += own_features(dot(rim_k[:, cols], dscores[i, p], ((0,), (0,))))


def own_backward_kernel(
    q, k, v, grad_t, exps, factors, deltas, rim_t, before,
    q_grad, k_own, v_own, after, dprobs, dscores, rounded,
):
    blocks = q.shape[0] // BLK
    for b, _, cols, p in pairs_of(blocks):
        here = own_rows(b, blocks)
        g2_t = two_heads(grad_t[b, cols], 0)
        dprobs[b, p, : here.stop - here.start] = dot(v[here, cols], g2_t, ((1,), (0,)))
    for b, _, _, p in pairs_of(blocks):
        here = own_rows(b, blocks)
        keys = slice(0, here.stop - here.start)
        dscores[b, p, keys], rounded[b, p, keys] = score_grads(
            exps[b, p, keys] * factors[b, p : p + 1], dprobs[b, p, keys], deltas[b, p : p + 1]
        )
    k_sums, v_sums = {}, {}
    for b, rows, cols, p in pairs_of(blocks):
        here = own_rows(b, blocks)
        keys = slice(0, here.stop - here.start)
        q2 = two_heads(q[rows, cols] * SCALE, 1)
        g2_t = two_heads(grad_t[b, cols], 0)
        dscore = dscores[b, p, keys]
        k_part = dot(dscore, q2, ((1,), (0,)))
        v_part = dot(rounded[b, p, keys], g2_t, ((1,), (1,)))
        for at in range(here.start, here.stop, BLK):
            part = slice(at - here.start, at - here.start + BLK)
            for sums, value in ((k_sums, k_part), (v_sums, v_part)):
                sums.setdefault((at, p), []).append(value[part])
        query_t = own_features(dot(k[here, cols], dscore, ((0,), (0,)))) + rim_t[b, cols]
        q_grad[rows, cols] = (query_t * SCALE).T.astype(BF16)
    for out, sums in ((k_own, k_sums), (v_own, v_sums)):
        for (at, p), values in sums.items():
            out[at : at + BLK, pair_cols(p)] = functools.reduce(jnp.add, values)
    after[...] = jnp.zeros_like(after)


def send_kernel(back, before, out):
    out[...] = back[...]


def output_kernel(attn_t, w_out, before, output):
    for b in range(attn_t.shape[0]):
        part = dot(attn_t[b], w_out[...], ((0,), (0,)))
        output[b * BLK : (b + 1) * BLK] = part.astype(BF16)


def halves_kernel(product, other, g_low, g_high, before, *outs):
    pieces, after = outs[:-1], outs[-1]
    at_dp = lax.axis_index("dp")
    chips, rows, cols = pieces[0].shape
    if cols % BLK == 0:
        flat = other[...].reshape(chips * rows, other.shape[2])
        for s in range(len(pieces)):
            at = pl.ds(pl.multiple_of((at_dp ^ s) * cols, BLK), cols)
            g = jnp.concatenate([g_low[:, at], g_high[:, at]], axis=0)
            value = product[:, at] + dot(flat, g, ((1,), (0,)))
            pieces[s][...] = value.astype(BF16).reshape(chips, rows, cols)
    else:
        both = (product[...] + flat_dot(other, g_low, g_high)).astype(BF16)
        for d in range(len(pieces)):
            value = both[:, d * cols : (d + 1) * cols].reshape(chips, rows, cols)
            for s in range(len(pieces)):

                @pl.when((at_dp ^ s) == d)
                def _(s=s, value=value):
                    pieces[s][...] = value

    after[...] = jnp.zeros_like(after)


def chips_kernel(*refs):
    parts, outs = refs[: lax.axis_size("dp")], refs[lax.axis_size("dp") + 1 :]
    chip = lax.div(lax.axis_index("ctx"), 2)
    for s, out in enumerate(outs):
        out[...] = total([part[chip ^ s] for part in parts]).astype(BF16)


def piece_kernel(scale, count, *refs):
    refs[-1][...] = (total([part[...] for part in refs[:count]]) * scale).astype(BF16)


def rim_sum_kernel(k_own, v_own, link_kv, chip_kv, k_grad, v_grad, after):
    tokens = k_own.shape[0]
    first_core = at_core() == 0
    for i, (own, grad) in enumerate(((k_own, k_grad), (v_own, v_grad))):
        link, chip = link_kv[i].astype(F32), chip_kv[i].astype(F32)
        low = jnp.where(first_core, link, chip)
        high = jnp.where(first_core, chip, link)
        if tokens == RIM:
            grad[...] = (own[...] + low + high).astype(BF16)
        else:
            grad[:RIM] = (own[:RIM] + low).astype(BF16)
            if tokens > 2 * RIM:
                grad[RIM : tokens - RIM] = own[RIM : tokens - RIM].astype(BF16)
            grad[tokens - RIM :] = (own[tokens - RIM :] + high).astype(BF16)
    after[...] = jnp.zeros_like(after)


def columns_kernel(before, *refs):
    pieces, weight_grad = refs[:1] + refs[-2:0:-1], refs[-1]
    at_dp = lax.axis_index("dp")
    cols = pieces[0].shape[1]
    for d in range(len(pieces)):
        value = pieces[0][...]
        for s in range(1, len(pieces)):
            value = jnp.where((at_dp ^ s) == d, pieces[s][...], value)
        weight_grad[:, d * cols : (d + 1) * cols] = value.astype(F32)


def vmem(*shape, dtype=BF16):
    return pltpu.VMEM(shape, dtype)


def hbm(*shape, dtype=BF16):
    return jax.ShapeDtypeStruct(shape, dtype)


def call(kernel, outs, flops, *args, scratch=()):
    in_vmem = pl.BlockSpec(memory_space=pltpu.VMEM)
    return pl.pallas_call(
        kernel,
        out_shape=outs,
        in_specs=[in_vmem] * len(args),
        out_specs=[in_vmem] * len(outs),
        scratch_shapes=list(scratch),
        compiler_params=pltpu.CompilerParams(vmem_limit_bytes=24 * 1024 * 1024),
        cost_estimate=pl.CostEstimate(flops=flops, bytes_accessed=flops // 250, transcendentals=0),
    )(*args)


def call_on_hbm(kernel, outs, *args, beside=(), scratch=()):
    return pl.pallas_call(
        kernel,
        out_shape=outs,
        in_specs=[pl.BlockSpec(memory_space=pltpu.VMEM)] * len(beside)
        + [pl.BlockSpec(memory_space=pltpu.HBM)] * len(args),
        out_specs=[pl.BlockSpec(memory_space=pltpu.VMEM)] * len(outs),
        scratch_shapes=list(scratch),
        compiler_params=pltpu.CompilerParams(vmem_limit_bytes=8 * 1024 * 1024),
        cost_estimate=pl.CostEstimate(flops=10**6, bytes_accessed=4096, transcendentals=0),
    )(*beside, *(pltpu.with_memory_space_constraint(x, pltpu.HBM) for x in args))


def swap(count, bits):
    return [(i, i ^ bits) for i in range(count)]


def over_links(count):
    return [(i, (i - 1 if i % 2 == 0 else i + 1) % count) for i in range(count)]


def total(parts):
    return functools.reduce(jnp.add, [p.astype(F32) for p in parts])


def body(queries, keys, values, out_grad, w_out, block_mask):
    q, k, v, g = queries[0], keys[0], values[0], out_grad[0]
    tokens, feats = q.shape
    width = g.shape[1]
    blocks = tokens // BLK
    ctx, dp = lax.axis_size("ctx"), lax.axis_size("dp")
    chips = ctx // 2
    at_ctx = lax.axis_index("ctx")
    rows, cols = feats // ctx, width // dp

    rim = vmem(RIM, feats)
    sems = [pltpu.SemaphoreType.DMA((2,))]
    (to_link,) = call_on_hbm(pack_link_kernel, [vmem(2, RIM, feats)], k, v, scratch=sems)
    to_chip = call_on_hbm(pack_chip_kernel, [rim, rim], k, v, scratch=sems)
    link = lax.ppermute(to_link, "ctx", over_links(ctx))
    chip_k, chip_v = (lax.ppermute(x, "ctx", swap(ctx, 1)) for x in to_chip)
    mask = lax.dynamic_slice_in_dim(block_mask[0], at_ctx * blocks, blocks, 0)
    bias = jnp.where(mask == 1, 0.0, BIG_NEGATIVE).astype(F32).reshape(blocks * CAND, 1, 1)
    bias = jnp.broadcast_to(bias, (blocks * CAND, 1, 2 * BLK))
    args = (q, k, v, g, w_out)
    own_keys = min(CAND, blocks) * BLK
    own_scores = (blocks, PAIRS, own_keys, 2 * BLK)
    rim_scores = (PAIRS, RIM, 2 * BLK)
    half = vmem(tokens // 2, width)
    q, k, v, g_low, g_high, w_out, own_t, stats, own_exps, grad_t = call_on_hbm(
        own_kernel,
        [vmem(tokens, feats)] * 3
        + [
            half,
            half,
            vmem(feats, width),
            vmem(blocks, feats, BLK, dtype=F32),
            vmem(2, blocks, PAIRS, 2 * BLK, dtype=F32),
            vmem(*own_scores, dtype=F32),
            vmem(blocks, feats, BLK),
        ],
        *args,
        beside=(bias,),
        scratch=[vmem(*own_scores), pltpu.SemaphoreType.DMA((6,))],
    )
    sibling_g = [
        pltpu.with_memory_space_constraint(lax.ppermute(x, "ctx", swap(ctx, 1)), pltpu.VMEM)
        for x in (g_low, g_high)
    ]
    chip_t, chip_stats, chip_exps = call(
        chip_kernel,
        [
            vmem(feats, BLK, dtype=F32),
            vmem(2, PAIRS, 2 * BLK, dtype=F32),
            vmem(*rim_scores, dtype=F32),
        ],
        10**6,
        bias, q, chip_k, chip_v, own_t, stats,
        scratch=[vmem(*rim_scores)],
    )
    attn_t, mine, other, link_exps, own_factors, rim_factors = call(
        forward_kernel,
        [
            vmem(blocks, feats, BLK),
            vmem(chips, rows, tokens),
            vmem(chips, rows, tokens),
            vmem(*rim_scores, dtype=F32),
            vmem(blocks, PAIRS, 2 * BLK, dtype=F32),
            vmem(2, PAIRS, 2 * BLK, dtype=F32),
        ],
        10**6,
        bias, q, link, own_t, stats, chip_t, chip_stats,
        scratch=[vmem(*rim_scores)],
    )

    other = lax.ppermute(other, "ctx", swap(ctx, 1))
    other = pltpu.with_memory_space_constraint(other, pltpu.VMEM)
    (product,) = call(product_kernel, [vmem(chips * rows, width, dtype=F32)], 10**6, mine, g_low, g_high)
    *back, deltas, rim_t = call(
        rim_kernel,
        [
            vmem(2, RIM, feats),
            vmem(2, RIM, feats),
            vmem(blocks, PAIRS, 2 * BLK, dtype=F32),
            vmem(blocks, feats, BLK, dtype=F32),
        ],
        10**6,
        q, link, chip_k, chip_v, grad_t, attn_t, link_exps, chip_exps, rim_factors,
        scratch=[vmem(2, *rim_scores, dtype=F32), vmem(2, *rim_scores), vmem(2, *rim_scores)],
    )
    *halves, after = call(
        halves_kernel,
        [vmem(chips, rows, cols)] * dp + [vmem(8, 128, dtype=F32)],
        10**6,
        product, other, *sibling_g, deltas,
    )
    (to_link,) = call(send_kernel, [vmem(2, RIM, feats)], 10**6, back[0], after)
    link_back = lax.ppermute(to_link, "ctx", over_links(ctx))
    q_grad, k_own, v_own, after = call(
        own_backward_kernel,
        [
            hbm(tokens, feats),
            vmem(tokens, feats, dtype=F32),
            vmem(tokens, feats, dtype=F32),
            vmem(8, 128, dtype=F32),
        ],
        5 * 10**9,
        q, k, v, grad_t, own_exps, own_factors, deltas, rim_t, to_link,
        scratch=[vmem(*own_scores, dtype=F32), vmem(*own_scores), vmem(*own_scores)],
    )

    halves = [halves[0]] + [lax.ppermute(halves[s], "dp", swap(dp, s)) for s in range(1, dp)]
    quarters = call(chips_kernel, [vmem(rows, cols)] * chips, 10**6, *halves, after)
    (output,) = call(output_kernel, [hbm(tokens, width)], 5 * 10**9, attn_t, w_out, quarters[0])
    quarters = [quarters[0]] + [
        lax.ppermute(quarters[s], "ctx", swap(ctx, 2 * s))
        for s in (*range(chips // 2, chips), *range(chips // 2 - 1, 0, -1))
    ]
    (piece,) = call(
        functools.partial(piece_kernel, (dp * tokens * ctx) ** (-0.5), chips),
        [vmem(rows, cols)],
        10**6,
        *quarters, link_back,
    )
    pieces = [piece] + [lax.ppermute(piece, "dp", swap(dp, s)) for s in range(dp - 1, 0, -1)]
    (to_chip,) = call(send_kernel, [vmem(2, RIM, feats)], 10**6, back[1], piece)
    chip_back = lax.ppermute(to_chip, "ctx", swap(ctx, 1))
    k_grad, v_grad, after = call(
        rim_sum_kernel,
        [hbm(tokens, feats), hbm(tokens, feats), vmem(8, 128, dtype=F32)],
        10**6,
        k_own, v_own, link_back, chip_back,
    )
    (weight_grad,) = call(columns_kernel, [hbm(rows, width, dtype=F32)], 10**6, after, *pieces)
    return (output[None], q_grad[None], k_grad[None], v_grad[None], weight_grad)


def solution(mesh):
    rows = P("dp", "ctx", None)
    return jax.shard_map(
        body,
        mesh=mesh,
        in_specs=(rows, rows, rows, rows, P(), P("dp", None, None)),
        out_specs=(rows, rows, rows, rows, P("ctx", None)),
        check_vma=False,
    )
```

```python
import functools

import jax
import jax.numpy as jnp
from jax import lax
from jax.experimental import pallas as pl
from jax.experimental.pallas import tpu as pltpu
from jax.sharding import PartitionSpec as P

HEADS = 8
HD = 64
BLK = 128
RAD = 1
CAND = 2 * RAD + 1
PAIRS = HEADS // 2
PAIR = 2 * HD
RIM = RAD * BLK
BIG_NEGATIVE = -1e30
SCALE = HD ** (-0.5)
BF16 = jnp.bfloat16
F32 = jnp.float32


def dot(a, b, contract):
    return lax.dot_general(a, b, (contract, ((), ())), preferred_element_type=F32)


def two_heads(block, axis):
    feature = lax.broadcasted_iota(jnp.int32, block.shape, axis)
    zero = jnp.zeros_like(block)
    return jnp.concatenate(
        [jnp.where(feature < HD, block, zero), jnp.where(feature < HD, zero, block)], axis=1 - axis
    )


def own_features(both):
    return jnp.concatenate([both[:HD, :BLK], both[HD:, BLK:]], axis=0)


def spread(row):
    return jnp.concatenate(
        [
            jnp.broadcast_to(row[:, :BLK], (HD, BLK)),
            jnp.broadcast_to(row[:, BLK:], (HD, BLK)),
        ],
        axis=0,
    )


def own_candidates(b, blocks):
    return max(0, RAD - b), min(CAND - 1, blocks - 1 - b + RAD)


def own_rows(b, blocks):
    first, last = own_candidates(b, blocks)
    return slice((b + first - RAD) * BLK, (b + last - RAD + 1) * BLK)


def masked(bias, b, c, part):
    return part + bias[b * CAND + c]


def pairs_of(blocks):
    for b in range(blocks):
        for p in range(PAIRS):
            yield b, slice(b * BLK, (b + 1) * BLK), slice(p * PAIR, (p + 1) * PAIR), p


def at_core():
    return lax.rem(lax.axis_index("ctx"), 2)


def rim_block(blocks, over_link):
    core = at_core()
    upper = core if over_link else 1 - core
    return upper * (blocks - 1), upper * (CAND - 1)


def rows_of(b):
    return pl.ds(pl.multiple_of(b * BLK, BLK), BLK)


def copy_all(pairs, sems):
    copies = [pltpu.make_async_copy(x, y, sems.at[i]) for i, (x, y) in enumerate(pairs)]
    for copy in copies:
        copy.start()
    for copy in copies:
        copy.wait()


def pack_link_kernel(k, v, out, sems):
    rows = rows_of(rim_block(k.shape[0] // BLK, True)[0])
    copy_all(((k.at[rows], out.at[0]), (v.at[rows], out.at[1])), sems)


def pack_chip_kernel(k, v, k_out, v_out, sems):
    rows = rows_of(rim_block(k.shape[0] // BLK, False)[0])
    copy_all(((k.at[rows], k_out), (v.at[rows], v_out)), sems)


def own_kernel(
    bias, q_arg, k_arg, v_arg, g_arg, w_arg,
    q, k, v, g_low, g_high, w_out, own_t, stats, exps, grad_t, rounded, sems,
):
    half = g_low.shape[0]
    pairs = (
        (q_arg, q),
        (k_arg, k),
        (v_arg, v),
        (g_arg.at[:half], g_low),
        (g_arg.at[half:], g_high),
        (w_arg, w_out),
    )
    copies = [pltpu.make_async_copy(x, y, sems.at[i]) for i, (x, y) in enumerate(pairs)]
    for copy in copies:
        copy.start()
    copies[0].wait()
    copies[1].wait()
    blocks = q.shape[0] // BLK
    for b, rows, cols, p in pairs_of(blocks):
        first, last = own_candidates(b, blocks)
        here = own_rows(b, blocks)
        scores = dot(k[here, cols], two_heads(q[rows, cols] * SCALE, 1), ((1,), (1,)))
        for c in range(first, last + 1):
            part = slice((c - first) * BLK, (c - first + 1) * BLK)
            value = scores[part]
            exps[b, p, part] = value if c == RAD else masked(bias, b, c, value)
    for b, rows, cols, p in pairs_of(blocks):
        here = own_rows(b, blocks)
        keys = slice(0, here.stop - here.start)
        scores = exps[b, p, keys]
        top = jnp.max(scores, axis=0, keepdims=True)
        e = jnp.exp(scores - top)
        exps[b, p, keys] = e
        rounded[b, p, keys] = e.astype(BF16)
        stats[0, b, p : p + 1] = top
        stats[1, b, p : p + 1] = jnp.sum(e, axis=0, keepdims=True)
    copies[2].wait()
    for b, rows, cols, p in pairs_of(blocks):
        here = own_rows(b, blocks)
        e = rounded[b, p, : here.stop - here.start]
        own_t[b, cols] = own_features(dot(v[here, cols], e, ((0,), (0,))))
    for copy in copies[3:]:
        copy.wait()
    both = jnp.concatenate([g_low[...], g_high[...]], axis=0)
    for b in range(blocks):
        rows = slice(b * BLK, (b + 1) * BLK)
        grad_t[b] = dot(w_out[...], both[rows], ((1,), (1,))).astype(BF16)


def pair_cols(p):
    return slice(p * PAIR, (p + 1) * PAIR)


def with_rim(bias, q, rim_k, rim_v, b, c, old, exps, rounded):
    for p in range(PAIRS):
        q2 = two_heads(q[rows_of(b), pair_cols(p)] * SCALE, 1)
        scores = dot(rim_k[:, pair_cols(p)], q2, ((1,), (1,)))
        exps[p] = masked(bias, b, c, scores)
    results = []
    for p in range(PAIRS):
        old_top, old_sum = old(p)
        scores = exps[p]
        top = jnp.maximum(old_top, jnp.max(scores, axis=0, keepdims=True))
        kept = jnp.exp(old_top - top)
        e = jnp.exp(scores - top)
        exps[p] = e
        rounded[p] = e.astype(BF16)
        results.append((top, kept, old_sum * kept + jnp.sum(e, axis=0, keepdims=True)))
    parts = [
        own_features(dot(rim_v[:, pair_cols(p)], rounded[p], ((0,), (0,)))) for p in range(PAIRS)
    ]
    return [(*result, part) for result, part in zip(results, parts)]


def chip_kernel(bias, q, rim_k, rim_v, own_t, stats, chip_t, chip_stats, exps, rounded):
    blocks = q.shape[0] // BLK
    b, c = rim_block(blocks, False)

    def old(p):
        return stats[0, b, p : p + 1], stats[1, b, p : p + 1]

    results = with_rim(bias, q, rim_k, rim_v, b, c, old, exps, rounded)
    for p, (top, kept, count, part) in enumerate(results):
        at = slice(p, p + 1)
        if blocks == 1:
            chip_t[pair_cols(p)] = own_t[b, pair_cols(p)] * spread(kept) + part
            chip_stats[0, at], chip_stats[1, at] = top, count
        else:
            share = 1.0 / count
            attn = own_t[b, pair_cols(p)] * spread(kept * share) + part * spread(share)
            chip_t[pair_cols(p)] = attn
            chip_stats[0, at], chip_stats[1, at] = share, kept * share


def forward_kernel(
    bias, q, rim, own_t, stats, chip_t, chip_stats,
    attn_t, mine, other, exps, own_factors, rim_factors, rounded,
):
    blocks = q.shape[0] // BLK
    b, c = rim_block(blocks, True)
    at_chip, _ = rim_block(blocks, False)

    def old(p):
        at = slice(p, p + 1)
        if blocks == 1:
            return chip_stats[0, at], chip_stats[1, at]
        return stats[0, b, at], stats[1, b, at]

    results = with_rim(bias, q, rim.at[0], rim.at[1], b, c, old, exps, rounded)
    for p, (top, kept, count, part) in enumerate(results):
        at = slice(p, p + 1)
        cols = pair_cols(p)
        base = chip_t[cols] if blocks == 1 else own_t[b, cols]
        share = 1.0 / count
        attn_t[b, cols] = (base * spread(kept * share) + part * spread(share)).astype(BF16)
        rim_factors[0, at] = share
        if blocks == 1:
            rim_factors[1, at] = kept * share
            own_factors[0, at] = jnp.exp(stats[0, 0, at] - top) * share
        else:
            own_factors[b, at] = kept * share
            attn_t[at_chip, cols] = chip_t[cols].astype(BF16)
            rim_factors[1, at] = chip_stats[0, at]
            own_factors[at_chip, at] = chip_stats[1, at]
        for inner in range(1, blocks - 1):
            share = 1.0 / stats[1, inner, at]
            attn_t[inner, cols] = (own_t[inner, cols] * spread(share)).astype(BF16)
            own_factors[inner, at] = share
    first_core = at_core() == 0
    chips, rows, _ = mine.shape
    for i in range(chips):
        for block in range(blocks):
            tokens = slice(block * BLK, (block + 1) * BLK)
            even = attn_t[block, 2 * i * rows : (2 * i + 1) * rows]
            odd = attn_t[block, (2 * i + 1) * rows : (2 * i + 2) * rows]
            mine[i, :, tokens] = jnp.where(first_core, even, odd)
            other[i, :, tokens] = jnp.where(first_core, odd, even)


def flat_dot(attn, g_low, g_high):
    chips, rows, tokens = attn.shape
    g = jnp.concatenate([g_low[...], g_high[...]], axis=0)
    return dot(attn[...].reshape(chips * rows, tokens), g, ((1,), (0,)))


def product_kernel(mine, g_low, g_high, product):
    product[...] = flat_dot(mine, g_low, g_high)


def score_grads(probs, dprob, delta):
    return (probs * (dprob - delta)).astype(BF16), probs.astype(BF16)


def rim_kernel(
    q, link, chip_k, chip_v, grad_t, attn_t, link_exps, chip_exps, rim_factors, before,
    link_back, chip_back, deltas, query_t, dprobs, dscores, rounded,
):
    blocks = q.shape[0] // BLK
    sides = (
        (rim_block(blocks, True)[0], link.at[0], link.at[1], link_exps, link_back.at[0], link_back.at[1]),
        (rim_block(blocks, False)[0], chip_k, chip_v, chip_exps, chip_back.at[0], chip_back.at[1]),
    )
    for i, (b, _, rim_v, _, _, _) in enumerate(sides):
        for p in range(PAIRS):
            g2_t = two_heads(grad_t[b, pair_cols(p)], 0)
            dprobs[i, p] = dot(rim_v[:, pair_cols(p)], g2_t, ((1,), (0,)))
    for b, _, cols, p in pairs_of(blocks):
        product = grad_t[b, cols].astype(F32) * attn_t[b, cols].astype(F32)
        deltas[b, p : p + 1] = jnp.concatenate(
            [
                jnp.sum(product[:HD], axis=0, keepdims=True),
                jnp.sum(product[HD:], axis=0, keepdims=True),
            ],
            axis=1,
        )
    query_t[...] = jnp.zeros_like(query_t)
    for i, (b, _, _, exps, _, _) in enumerate(sides):
        for p in range(PAIRS):
            at = slice(p, p + 1)
            dscores[i, p], rounded[i, p] = score_grads(
                exps[p] * rim_factors[i, at], dprobs[i, p], deltas[b, at]
            )
    for i, (b, rim_k, _, _, k_back, v_back) in enumerate(sides):
        for p in range(PAIRS):
            cols = pair_cols(p)
            q2 = two_heads(q[rows_of(b), cols] * SCALE, 1)
            g2_t = two_heads(grad_t[b, cols], 0)
            k_back[:, cols] = dot(dscores[i, p], q2, ((1,), (0,))).astype(BF16)
            v_back[:, cols] = dot(rounded[i, p], g2_t, ((1,), (1,))).astype(BF16)
            query_t[b, cols] += own_features(dot(rim_k[:, cols], dscores[i, p], ((0,), (0,))))


def own_backward_kernel(
    q, k, v, grad_t, exps, factors, deltas, rim_t,
    q_grad, k_own, v_own, after, dprobs, dscores, rounded,
):
    blocks = q.shape[0] // BLK
    for b, _, cols, p in pairs_of(blocks):
        here = own_rows(b, blocks)
        g2_t = two_heads(grad_t[b, cols], 0)
        dprobs[b, p, : here.stop - here.start] = dot(v[here, cols], g2_t, ((1,), (0,)))
    for b, _, _, p in pairs_of(blocks):
        here = own_rows(b, blocks)
        keys = slice(0, here.stop - here.start)
        dscores[b, p, keys], rounded[b, p, keys] = score_grads(
            exps[b, p, keys] * factors[b, p : p + 1], dprobs[b, p, keys], deltas[b, p : p + 1]
        )
    k_sums, v_sums = {}, {}
    for b, rows, cols, p in pairs_of(blocks):
        here = own_rows(b, blocks)
        keys = slice(0, here.stop - here.start)
        q2 = two_heads(q[rows, cols] * SCALE, 1)
        g2_t = two_heads(grad_t[b, cols], 0)
        dscore = dscores[b, p, keys]
        k_part = dot(dscore, q2, ((1,), (0,)))
        v_part = dot(rounded[b, p, keys], g2_t, ((1,), (1,)))
        for at in range(here.start, here.stop, BLK):
            part = slice(at - here.start, at - here.start + BLK)
            for sums, value in ((k_sums, k_part), (v_sums, v_part)):
                sums.setdefault((at, p), []).append(value[part])
        query_t = own_features(dot(k[here, cols], dscore, ((0,), (0,)))) + rim_t[b, cols]
        q_grad[rows, cols] = (query_t * SCALE).T.astype(BF16)
    for out, sums in ((k_own, k_sums), (v_own, v_sums)):
        for (at, p), values in sums.items():
            out[at : at + BLK, pair_cols(p)] = functools.reduce(jnp.add, values)
    after[...] = jnp.zeros_like(after)


def output_kernel(attn_t, w_out, before, output):
    for b in range(attn_t.shape[0]):
        part = dot(attn_t[b], w_out[...], ((0,), (0,)))
        output[b * BLK : (b + 1) * BLK] = part.astype(BF16)


def halves_kernel(product, other, g_low, g_high, *outs):
    pieces, after = outs[:-1], outs[-1]
    at_dp = lax.axis_index("dp")
    chips, rows, cols = pieces[0].shape
    if cols % BLK == 0:
        flat = other[...].reshape(chips * rows, other.shape[2])
        for s in range(len(pieces)):
            at = pl.ds(pl.multiple_of((at_dp ^ s) * cols, BLK), cols)
            g = jnp.concatenate([g_low[:, at], g_high[:, at]], axis=0)
            value = product[:, at] + dot(flat, g, ((1,), (0,)))
            pieces[s][...] = value.astype(BF16).reshape(chips, rows, cols)
    else:
        both = (product[...] + flat_dot(other, g_low, g_high)).astype(BF16)
        for d in range(len(pieces)):
            value = both[:, d * cols : (d + 1) * cols].reshape(chips, rows, cols)
            for s in range(len(pieces)):

                @pl.when((at_dp ^ s) == d)
                def _(s=s, value=value):
                    pieces[s][...] = value

    after[...] = jnp.zeros_like(after)


def chips_kernel(*refs):
    parts, outs = refs[: lax.axis_size("dp")], refs[lax.axis_size("dp") + 1 :]
    chip = lax.div(lax.axis_index("ctx"), 2)
    for s, out in enumerate(outs):
        out[...] = total([part[chip ^ s] for part in parts]).astype(BF16)


def piece_kernel(scale, count, *refs):
    refs[-1][...] = (total([part[...] for part in refs[:count]]) * scale).astype(BF16)


def rim_sum_kernel(k_own, v_own, link_kv, chip_kv, k_grad, v_grad):
    tokens = k_own.shape[0]
    first_core = at_core() == 0
    for i, (own, grad) in enumerate(((k_own, k_grad), (v_own, v_grad))):
        link, chip = link_kv[i].astype(F32), chip_kv[i].astype(F32)
        low = jnp.where(first_core, link, chip)
        high = jnp.where(first_core, chip, link)
        if tokens == RIM:
            grad[...] = (own[...] + low + high).astype(BF16)
        else:
            grad[:RIM] = (own[:RIM] + low).astype(BF16)
            if tokens > 2 * RIM:
                grad[RIM : tokens - RIM] = own[RIM : tokens - RIM].astype(BF16)
            grad[tokens - RIM :] = (own[tokens - RIM :] + high).astype(BF16)


def columns_kernel(*refs):
    pieces, weight_grad = refs[:1] + refs[-2:0:-1], refs[-1]
    at_dp = lax.axis_index("dp")
    cols = pieces[0].shape[1]
    for d in range(len(pieces)):
        value = pieces[0][...]
        for s in range(1, len(pieces)):
            value = jnp.where((at_dp ^ s) == d, pieces[s][...], value)
        weight_grad[:, d * cols : (d + 1) * cols] = value.astype(F32)


def vmem(*shape, dtype=BF16):
    return pltpu.VMEM(shape, dtype)


def hbm(*shape, dtype=BF16):
    return jax.ShapeDtypeStruct(shape, dtype)


def call(kernel, outs, flops, *args, scratch=()):
    in_vmem = pl.BlockSpec(memory_space=pltpu.VMEM)
    return pl.pallas_call(
        kernel,
        out_shape=outs,
        in_specs=[in_vmem] * len(args),
        out_specs=[in_vmem] * len(outs),
        scratch_shapes=list(scratch),
        compiler_params=pltpu.CompilerParams(vmem_limit_bytes=24 * 1024 * 1024),
        cost_estimate=pl.CostEstimate(flops=flops, bytes_accessed=flops // 250, transcendentals=0),
    )(*args)


def call_on_hbm(kernel, outs, *args, beside=(), scratch=()):
    return pl.pallas_call(
        kernel,
        out_shape=outs,
        in_specs=[pl.BlockSpec(memory_space=pltpu.VMEM)] * len(beside)
        + [pl.BlockSpec(memory_space=pltpu.HBM)] * len(args),
        out_specs=[pl.BlockSpec(memory_space=pltpu.VMEM)] * len(outs),
        scratch_shapes=list(scratch),
        compiler_params=pltpu.CompilerParams(vmem_limit_bytes=8 * 1024 * 1024),
        cost_estimate=pl.CostEstimate(flops=10**6, bytes_accessed=4096, transcendentals=0),
    )(*beside, *(pltpu.with_memory_space_constraint(x, pltpu.HBM) for x in args))


def swap(count, bits):
    return [(i, i ^ bits) for i in range(count)]


def over_links(count):
    return [(i, (i - 1 if i % 2 == 0 else i + 1) % count) for i in range(count)]


def total(parts):
    return functools.reduce(jnp.add, [p.astype(F32) for p in parts])


def body(queries, keys, values, out_grad, w_out, block_mask):
    q, k, v, g = queries[0], keys[0], values[0], out_grad[0]
    tokens, feats = q.shape
    width = g.shape[1]
    blocks = tokens // BLK
    ctx, dp = lax.axis_size("ctx"), lax.axis_size("dp")
    chips = ctx // 2
    at_ctx = lax.axis_index("ctx")
    rows, cols = feats // ctx, width // dp

    rim = vmem(RIM, feats)
    sems = [pltpu.SemaphoreType.DMA((2,))]
    (to_link,) = call_on_hbm(pack_link_kernel, [vmem(2, RIM, feats)], k, v, scratch=sems)
    to_chip = call_on_hbm(pack_chip_kernel, [rim, rim], k, v, scratch=sems)
    link = lax.ppermute(to_link, "ctx", over_links(ctx))
    chip_k, chip_v = (lax.ppermute(x, "ctx", swap(ctx, 1)) for x in to_chip)
    mask = lax.dynamic_slice_in_dim(block_mask[0], at_ctx * blocks, blocks, 0)
    bias = jnp.where(mask == 1, 0.0, BIG_NEGATIVE).astype(F32).reshape(blocks * CAND, 1, 1)
    bias = jnp.broadcast_to(bias, (blocks * CAND, 1, 2 * BLK))
    args = (q, k, v, g, w_out)
    own_keys = min(CAND, blocks) * BLK
    own_scores = (blocks, PAIRS, own_keys, 2 * BLK)
    rim_scores = (PAIRS, RIM, 2 * BLK)
    half = vmem(tokens // 2, width)
    q, k, v, g_low, g_high, w_out, own_t, stats, own_exps, grad_t = call_on_hbm(
        own_kernel,
        [vmem(tokens, feats)] * 3
        + [
            half,
            half,
            vmem(feats, width),
            vmem(blocks, feats, BLK, dtype=F32),
            vmem(2, blocks, PAIRS, 2 * BLK, dtype=F32),
            vmem(*own_scores, dtype=F32),
            vmem(blocks, feats, BLK),
        ],
        *args,
        beside=(bias,),
        scratch=[vmem(*own_scores), pltpu.SemaphoreType.DMA((6,))],
    )
    sibling_g = [
        pltpu.with_memory_space_constraint(lax.ppermute(x, "ctx", swap(ctx, 1)), pltpu.VMEM)
        for x in (g_low, g_high)
    ]
    chip_t, chip_stats, chip_exps = call(
        chip_kernel,
        [
            vmem(feats, BLK, dtype=F32),
            vmem(2, PAIRS, 2 * BLK, dtype=F32),
            vmem(*rim_scores, dtype=F32),
        ],
        10**6,
        bias, q, chip_k, chip_v, own_t, stats,
        scratch=[vmem(*rim_scores)],
    )
    attn_t, mine, other, link_exps, own_factors, rim_factors = call(
        forward_kernel,
        [
            vmem(blocks, feats, BLK),
            vmem(chips, rows, tokens),
            vmem(chips, rows, tokens),
            vmem(*rim_scores, dtype=F32),
            vmem(blocks, PAIRS, 2 * BLK, dtype=F32),
            vmem(2, PAIRS, 2 * BLK, dtype=F32),
        ],
        10**6,
        bias, q, link, own_t, stats, chip_t, chip_stats,
        scratch=[vmem(*rim_scores)],
    )

    other = lax.ppermute(other, "ctx", swap(ctx, 1))
    other = pltpu.with_memory_space_constraint(other, pltpu.VMEM)
    (product,) = call(product_kernel, [vmem(chips * rows, width, dtype=F32)], 10**6, mine, g_low, g_high)
    *halves, after = call(
        halves_kernel,
        [vmem(chips, rows, cols)] * dp + [vmem(8, 128, dtype=F32)],
        10**6,
        product, other, *sibling_g,
    )
    *back, deltas, rim_t = call(
        rim_kernel,
        [
            vmem(2, RIM, feats),
            vmem(2, RIM, feats),
            vmem(blocks, PAIRS, 2 * BLK, dtype=F32),
            vmem(blocks, feats, BLK, dtype=F32),
        ],
        10**6,
        q, link, chip_k, chip_v, grad_t, attn_t, link_exps, chip_exps, rim_factors, after,
        scratch=[vmem(2, *rim_scores, dtype=F32), vmem(2, *rim_scores), vmem(2, *rim_scores)],
    )
    link_back = lax.ppermute(back[0], "ctx", over_links(ctx))
    chip_back = lax.ppermute(back[1], "ctx", swap(ctx, 1))
    q_grad, k_own, v_own, after = call(
        own_backward_kernel,
        [
            hbm(tokens, feats),
            vmem(tokens, feats, dtype=F32),
            vmem(tokens, feats, dtype=F32),
            vmem(8, 128, dtype=F32),
        ],
        5 * 10**9,
        q, k, v, grad_t, own_exps, own_factors, deltas, rim_t,
        scratch=[vmem(*own_scores, dtype=F32), vmem(*own_scores), vmem(*own_scores)],
    )

    halves = [halves[0]] + [lax.ppermute(halves[s], "dp", swap(dp, s)) for s in (dp - 1, *range(1, dp - 1))]
    quarters = call(chips_kernel, [vmem(rows, cols)] * chips, 10**6, *halves, after)
    (output,) = call(output_kernel, [hbm(tokens, width)], 5 * 10**9, attn_t, w_out, quarters[0])
    quarters = [quarters[0]] + [
        lax.ppermute(quarters[s], "ctx", swap(ctx, 2 * s))
        for s in (*range(chips // 2, chips), *range(chips // 2 - 1, 0, -1))
    ]
    (piece,) = call(
        functools.partial(piece_kernel, (dp * tokens * ctx) ** (-0.5), chips),
        [vmem(rows, cols)],
        10**6,
        *quarters, link_back,
    )
    pieces = [piece] + [lax.ppermute(piece, "dp", swap(dp, s)) for s in range(dp - 1, 0, -1)]
    k_grad, v_grad = call(
        rim_sum_kernel, [hbm(tokens, feats)] * 2, 10**6, k_own, v_own, link_back, chip_back
    )
    (weight_grad,) = call(columns_kernel, [hbm(rows, width, dtype=F32)], 10**6, *pieces)
    return (output[None], q_grad[None], k_grad[None], v_grad[None], weight_grad)


def solution(mesh):
    rows = P("dp", "ctx", None)
    return jax.shard_map(
        body,
        mesh=mesh,
        in_specs=(rows, rows, rows, rows, P(), P("dp", None, None)),
        out_specs=(rows, rows, rows, rows, P("ctx", None)),
        check_vma=False,
    )
```
